32 devices in a mesh: dp: 8 (over z, y), expert: 4 (over x, core).
Axes of the slice: x: 2, y: 2, z: 4, core: 2. Of those that a mesh axis runs over, the one named last changes fastest.
Arguments:
- tokens: bfloat16 [2, 16704, 768], P(None, ('dp', 'expert')), may hold values from -6 to 6
- cotangent: bfloat16 [2, 16704, 768], P(None, ('dp', 'expert')), may hold values from -6 to 6
- item_group: int32 [2, 16704], P(None, ('dp', 'expert')), may hold values from 0 to 1, as said below
- routes: int32 [2, 16704], P(None, ('dp', 'expert')), may hold values from 0 to 2, as said below
- slot_order: int32 [2, 32, 522], P(None, ('dp', 'expert')), may hold values from 0 to 521, each once within a row
- attn_gain: float32 [768], replicated, may hold values from 0.1 to 1.9
- ffn_gain: float32 [768], replicated, may hold values from 0.1 to 1.9
- qkv_weight: bfloat16 [768, 2304], replicated, may hold values from -0.21875 to 0.21875
- out_weight: bfloat16 [768, 768], replicated, may hold values from -0.875 to 0.875
- expert_in: bfloat16 [3, 768, 3072], P(None, None, 'dp'), may hold values from -0.21875 to 0.21875
- expert_out: bfloat16 [3, 3072, 768], P(None, 'dp'), may hold values from -0.109375 to 0.109375
Outputs:
- result: bfloat16 [2, 16704, 768], P(None, ('dp', 'expert'))
- token_grad: bfloat16 [2, 16704, 768], P(None, ('dp', 'expert'))
- attn_gain_grad: float32 [768], replicated
- ffn_gain_grad: float32 [768], replicated
- qkv_grad: float32 [768, 2304], replicated
- out_grad: float32 [768, 768], replicated
- expert_in_grad: float32 [3, 768, 3072], P(None, None, 'dp')
- expert_out_grad: float32 [3, 3072, 768], P(None, 'dp')
The draws below stay inside these ranges and needn't reach their ends.
Inputs may be any that keep to these rules, and one draw needn't show every extreme that they name: `item_group`: within one device's 522 rows of a micro-batch the first 394 rows are 2 images of 197 tokens numbered 0 to 1 in order, and the rest are 2 captions of 64 tokens, each caption numbered as a different image. `routes`: 0 is the vision expert, 1 the language expert, 2 the vision-language expert. All tokens of one item (an image and its caption) take 2, or none of them does; otherwise image tokens take 0 and caption tokens 1. `slot_order`: each device's 522 entries of a micro-batch are a permutation of 0 to 521.
All inputs are finite; a program needn't handle non-finite values.
Results may differ from the reference program's by a relative error of at most 0.013.
Values may be sent and summed in bfloat16 or wider, within the bound.
A program may use at most 384 MiB of HBM per device.

```python
import jax
import jax.numpy as jnp
from jax import lax

D = 768
HEADS = 12
HEAD_DIM = 64
FF = 3072
PATCHES = 197
CAPTION = 64
ITEMS_DEV = 2
MICRO = 2
TOK_MB = 522
TOKENS = 16704
CAP = 261
N_DP = 8
N_EXPERT = 4


def item_layout(key):
    blocks = MICRO * N_DP * N_EXPERT
    pairing = jax.vmap(lambda k: jax.random.permutation(k, ITEMS_DEV))(jax.random.split(jax.random.fold_in(key, 11), blocks))
    merging = jax.random.randint(jax.random.fold_in(key, 12), (blocks, ITEMS_DEV), 0, 3) == 0
    position = jnp.arange(TOK_MB, dtype=jnp.int32)
    image_rows = ITEMS_DEV * PATCHES
    caption_item = jnp.clip((position - image_rows) // CAPTION, 0, ITEMS_DEV - 1)
    is_image = position[None, :] < image_rows
    grouping = jnp.where(is_image, position[None, :] // PATCHES, pairing[:, caption_item]).astype(jnp.int32)
    merged_rows = jnp.take_along_axis(merging, grouping, axis=1)
    routing = jnp.where(merged_rows, 2, jnp.where(is_image, 0, 1)).astype(jnp.int32)
    return (grouping, routing)


def draw_item_group(key, part):
    grouping, routing = item_layout(key)
    return grouping.reshape(MICRO, N_DP * N_EXPERT * TOK_MB)


def draw_routes(key, part):
    grouping, routing = item_layout(key)
    return routing.reshape(MICRO, N_DP * N_EXPERT * TOK_MB)


def shard_levels(stream_key, dims, cuts, low, top_value):
    def one(dim, shards_of):
        steps = jax.random.uniform(jax.random.fold_in(jax.random.fold_in(stream_key, 6), dim), (shards_of,), jnp.float32, low / len(cuts), top_value / len(cuts))
        return jnp.repeat(jnp.exp(steps), dims[dim] // shards_of).reshape((-1,) + (1,) * (len(dims) - dim - 1))

    level = one(*cuts[0])
    for cut in cuts[1:]:
        level = level * one(*cut)
    return level


def noise(rng, extent, deviation, reach, cuts=(), kind=jnp.bfloat16):
    drawn = jax.random.normal(rng, extent, jnp.float32) * deviation
    if len(cuts) > 0:
        drawn = shard_levels(rng, extent, cuts, -0.22, 0.18) * drawn
    return jnp.clip(drawn, min=-reach, max=reach).astype(kind)


def setup_inputs(seed: int = 0) -> dict:
    streams_of = jax.random.split(jax.random.key(seed), 12)
    tokens = noise(streams_of[0], (MICRO, TOKENS, D), 1.0, 6.0, ((1, 32),))
    cotangent = noise(streams_of[1], (MICRO, TOKENS, D), 1.0, 6.0, ((1, 32),))
    item_group = draw_item_group(jax.random.fold_in(streams_of[11], 71), 0)
    routes = draw_routes(jax.random.fold_in(streams_of[11], 71), 0)
    slot_order = jax.vmap(lambda own: jax.random.permutation(own, TOK_MB))(jax.random.split(streams_of[4], MICRO * (N_DP * N_EXPERT))).reshape((MICRO, N_DP * N_EXPERT, TOK_MB)).astype(jnp.int32)
    attn_gain = jnp.clip(1.0 + 0.18 * jax.random.normal(streams_of[5], (D,), jnp.float32), 0.1, 1.9)
    ffn_gain = jnp.clip(1.0 + 0.18 * jax.random.normal(streams_of[6], (D,), jnp.float32), 0.1, 1.9)
    qkv_weight = noise(streams_of[7], (D, 3 * D), D ** -0.5, 0.21875)
    out_weight = noise(streams_of[8], (D, D), (D // 16) ** -0.5, 0.875)
    expert_in = noise(streams_of[9], (3, D, FF), D ** -0.5, 0.21875, ((2, 8),))
    expert_out = noise(streams_of[10], (3, FF, D), FF ** -0.5, 0.109375, ((1, 8),))
    return {"tokens": tokens, "cotangent": cotangent, "item_group": item_group, "routes": routes, "slot_order": slot_order, "attn_gain": attn_gain, "ffn_gain": ffn_gain, "qkv_weight": qkv_weight, "out_weight": out_weight, "expert_in": expert_in, "expert_out": expert_out}


@jax.custom_vjp
def low(v):
    return lax.optimization_barrier(v.astype(jnp.bfloat16)).astype(jnp.float32)

@jax.custom_vjp
def low_back(v):
    return v

def low_keep(v):
    return (low(v), None)

def low_pass(kept, grad):
    return (grad,)

def back_keep(v):
    return (v, None)

def back_low(kept, grad):
    return (low(grad),)
low.defvjp(low_keep, low_pass)
low_back.defvjp(back_keep, back_low)
EPSILON = 1e-05
EXACTLY = lax.Precision.HIGHEST

def normalize(v, gain):
    centred = v - lax.optimization_barrier(jnp.mean(v, axis=-1, keepdims=True))
    spread_sq = lax.optimization_barrier(jnp.mean(centred * centred, axis=-1, keepdims=True))
    return centred * lax.rsqrt(spread_sq + EPSILON) * gain

def slot_ranks(routing, priority):
    length = routing.shape[0]
    position = jnp.zeros((length,), jnp.int32).at[priority].set(jnp.arange(length, dtype=jnp.int32))
    ordered = routing[priority]
    chosen = (ordered[:, None] == jnp.arange(3, dtype=jnp.int32)[None, :]).astype(jnp.int32)
    running = jnp.cumsum(chosen, axis=0).astype(jnp.int32) - chosen
    earlier = lax.optimization_barrier(jnp.sum(running * chosen, axis=1)).astype(jnp.int32)
    return earlier[position]

def layer_block(x, grouping, routing, priority, params):
    attn_gain, ffn_gain, qkv_weight, out_weight, expert_in, expert_out = params
    length = x.shape[0]
    a = low(normalize(x, attn_gain))
    qkv = low_back(low(jnp.dot(a, qkv_weight, precision=EXACTLY)))
    queries = qkv[:, :D].reshape(length, HEADS, HEAD_DIM)
    keyset = qkv[:, D:2 * D].reshape(length, HEADS, HEAD_DIM)
    valueset = qkv[:, 2 * D:].reshape(length, HEADS, HEAD_DIM)
    scores = low_back(jnp.einsum('qhd,khd->hqk', queries, keyset, precision=EXACTLY) * HEAD_DIM ** (-0.5))
    within = (grouping[:, None] == grouping[None, :])[None]
    scores = jnp.where(within, scores, -1e+30)
    highest = lax.optimization_barrier(jnp.max(scores, axis=-1, keepdims=True))
    expons = jnp.exp(scores - highest)
    weights = low(expons / lax.optimization_barrier(jnp.sum(expons, axis=-1, keepdims=True)))
    attended = jnp.einsum('hqk,khd->qhd', weights, valueset, precision=EXACTLY).reshape(length, D)
    attended = low_back(low(attended))
    y = x + low_back(jnp.dot(attended, out_weight, precision=EXACTLY))
    b = low_back(low(normalize(y, ffn_gain)))
    hidden = low_back(jnp.einsum('td,mdf->mtf', b, expert_in, precision=EXACTLY))
    activated = low(jax.nn.gelu(hidden, approximate=False))
    branch = low_back(low(jnp.einsum('mtf,mfd->mtd', activated, expert_out, precision=EXACTLY)))
    earlier = slot_ranks(routing, priority)
    replicas = (N_EXPERT - routing + 2) // 3
    keeping = earlier // replicas < CAP
    select = ((routing[None, :] == jnp.arange(3, dtype=jnp.int32)[:, None]) & keeping[None, :]).astype(x.dtype)
    return y + lax.optimization_barrier(jnp.sum(select[:, :, None] * branch, axis=0))

def reference(tokens, cotangent, item_group, routes, slot_order, attn_gain, ffn_gain, qkv_weight, out_weight, expert_in, expert_out):
    blocks = MICRO * N_DP * N_EXPERT
    inputs = tokens.astype(jnp.float32).reshape(blocks, TOK_MB, D)
    grouping = item_group.reshape(blocks, TOK_MB)
    routing = routes.reshape(blocks, TOK_MB)
    priority = slot_order.reshape(blocks, TOK_MB)
    params = (attn_gain.astype(jnp.float32), ffn_gain.astype(jnp.float32), qkv_weight.astype(jnp.float32), out_weight.astype(jnp.float32), expert_in.astype(jnp.float32), expert_out.astype(jnp.float32))

    def forward(values, weights):

        def single(pieces):
            return layer_block(pieces[0], pieces[1], pieces[2], pieces[3], weights)
        return lax.map(jax.checkpoint(single), (values, grouping, routing, priority))
    output, pullback = jax.vjp(forward, inputs, params)
    input_grad, weight_grads = pullback(cotangent.astype(jnp.float32).reshape(blocks, TOK_MB, D))
    whole = (MICRO, TOKENS, D)
    return (output.reshape(whole).astype(jnp.bfloat16), input_grad.reshape(whole).astype(jnp.bfloat16), weight_grads[0], weight_grads[1], weight_grads[2], weight_grads[3], weight_grads[4], weight_grads[5])
```

```python
import functools

import jax
import jax.numpy as jnp
from jax import lax
from jax.experimental import pallas as pl
from jax.experimental.pallas import tpu as pltpu
from jax.sharding import PartitionSpec as P

HEADS = 12
EPSILON = 1e-05
PATCHES = 197
CAPTION = 64
ITEMS = 2
IMAGE_ROWS = 208
ITEM_ROWS = IMAGE_ROWS + CAPTION
ROWS = ITEMS * ITEM_ROWS
FLAG_ROWS = 16
TILE = 256
VMEM_LIMIT = 60 * 1024 * 1024
F32 = jnp.float32
BF16 = jnp.bfloat16


def dot(a, b, a_dim, b_dim):
    return lax.dot_general(
        a, b, (((a_dim,), (b_dim,)), ((), ())), preferred_element_type=F32
    )


def normalize_parts(v):
    centred = v - jnp.mean(v, axis=-1, keepdims=True)
    inverse = lax.rsqrt(jnp.mean(centred * centred, axis=-1, keepdims=True) + EPSILON)
    return centred * inverse, inverse


def normalize_back(grad_unit, unit_rows, inverse):
    return inverse * (
        grad_unit
        - jnp.mean(grad_unit, axis=-1, keepdims=True)
        - unit_rows * jnp.mean(grad_unit * unit_rows, axis=-1, keepdims=True)
    )


def gelu_and_slope(h):
    bell = jnp.exp(-0.5 * h * h)
    t = 1.0 / (1.0 + (0.3275911 * 0.7071067811865476) * jnp.abs(h))
    poly = t * (
        0.254829592
        + t * (-0.284496736 + t * (1.421413741 + t * (-1.453152027 + t * 1.061405429)))
    )
    below = 0.5 * poly * bell
    phi = jnp.where(h > 0, 1.0 - below, below)
    return h * phi, phi + h * (0.3989422804014327 * bell)


class Partners:
    def __init__(self):
        dp, expert = lax.axis_index("dp"), lax.axis_index("expert")
        self.core = (dp, expert + 1 - 2 * (expert % 2))
        self.x = (dp, (expert + 2) % 4)
        self.y = (dp + 1 - 2 * (dp % 2), expert)
        self.z = {shift: ((dp + 2 * shift) % 8, expert) for shift in (1, 2, 3)}
        self.z_pair = (dp + 2 - 4 * (dp // 2 % 2), expert)

    def greet(self):
        barrier = pltpu.get_barrier_semaphore()
        everyone = [self.core, self.x, self.y, self.z[1], self.z[2], self.z[3]]
        for other in everyone:
            pl.semaphore_signal(
                barrier, inc=1, device_id=other, device_id_type=pl.DeviceIdType.MESH
            )
        pl.semaphore_wait(barrier, len(everyone))


class Copies:
    def __init__(self, send_sem, recv_sem, local_sem):
        self.send_sem, self.recv_sem, self.local_sem = send_sem, recv_sem, local_sem
        self.sent, self.kept, self.locals = [], [], 0

    def send(self, src, dst, device):
        at = len(self.sent)
        copy = pltpu.make_async_remote_copy(
            src_ref=src,
            dst_ref=dst,
            send_sem=self.send_sem.at[at],
            recv_sem=self.recv_sem.at[at],
            device_id=device,
            device_id_type=pl.DeviceIdType.MESH,
        )
        copy.start()
        self.sent.append(copy)
        return copy

    def keep(self, src, dst):
        copy = self.load(src, dst)
        self.kept.append(copy)
        return copy

    def load(self, src, dst):
        copy = pltpu.make_async_copy(src, dst, self.local_sem.at[self.locals])
        self.locals += 1
        copy.start()
        return copy

    def finish(self):
        for copy in self.sent:
            copy.wait_send()
        for copy in self.kept:
            copy.wait()


def pick_rows(index_ref, m, length, rows=slice(0, ROWS)):
    token = lax.broadcasted_iota(jnp.int32, (rows.stop - rows.start, length), 1)
    return index_ref[m, rows] == token


def front_kernel(direct, batches, *refs):
    (own_ref, tokens_ref, cot_ref, index_ref, keep_ref, flags_ref, gain1_ref, gain2_ref) = refs[:8]
    wqkv_ref, wo_ref, w_all, gz_all, flags_all, b_all, x_out, qkv_out, p_out, o_out, y_out = refs[
        8:19
    ]
    gz_scr, b_scr, x_scr, qkv_scr, p_scr, o_scr, y_scr, send_sem, recv_sem, local_sem = refs[19:]
    length, width = tokens_ref.shape[1:]
    head_dim = width // HEADS
    pair = 2 * head_dim
    copies = Copies(send_sem, recv_sem, local_sem)

    def spread(src, slots):
        copies.keep(src, slots(0))
        if not direct:
            return None
        near = copies.send(src, slots(1), near_by.core)
        return near, copies.send(src, slots(2), near_by.x)

    def pass_on(pair_of, slots):
        near, far = pair_of
        far.wait_recv()
        return near, copies.send(slots(2), slots(3), near_by.core)

    if direct:
        near_by = Partners()
        near_by.greet()
        y0 = copies.send(own_ref, w_all.at[0], near_by.y)
        z1 = copies.send(own_ref, w_all.at[1], near_by.z[1])
    flags = spread(flags_ref, lambda i: flags_all.at[i])

    for m in range(batches):
        chosen = pick_rows(index_ref, m, length) & (keep_ref[m] > 0)
        gz_scr[m] = dot(chosen.astype(BF16), cot_ref[m], 1, 0).astype(BF16)
    gz = spread(gz_scr, lambda i: gz_all.at[i])

    left = lax.broadcasted_iota(jnp.int32, (ITEM_ROWS, pair), 1) < head_dim
    key = lax.broadcasted_iota(jnp.int32, (1, ITEM_ROWS), 1)
    bias = jnp.where((key >= PATCHES) & (key < IMAGE_ROWS), -1e30, 0.0).astype(F32)
    b_sent = []
    for m in range(batches):
        xb = dot(pick_rows(index_ref, m, length).astype(BF16), tokens_ref[m], 1, 0)
        x_scr[m] = xb.astype(BF16)
        unit, _ = normalize_parts(xb)
        a = (unit * gain1_ref[...]).astype(BF16)
        for part in range(3):
            cols = slice(part * width, (part + 1) * width)
            qkv_scr[m, :, cols] = dot(a, wqkv_ref[:, cols], 1, 0).astype(BF16)

        def heads(hp, carry, m=m):
            at_q = pl.ds(pl.multiple_of(hp * pair, pair), pair)
            at_k = pl.ds(pl.multiple_of(width + hp * pair, pair), pair)
            at_v = pl.ds(pl.multiple_of(2 * width + hp * pair, pair), pair)
            for item in range(ITEMS):
                rows = slice(item * ITEM_ROWS, (item + 1) * ITEM_ROWS)
                q, k, v = qkv_scr[m, rows, at_q], qkv_scr[m, rows, at_k], qkv_scr[m, rows, at_v]
                outs = []
                for half in range(2):
                    mine = left if half == 0 else ~left
                    s = dot(jnp.where(mine, q, 0), k, 1, 1) * (head_dim**-0.5) + bias
                    e = jnp.exp(s - jnp.max(s, axis=-1, keepdims=True))
                    p = (e * (1.0 / jnp.sum(e, axis=-1, keepdims=True))).astype(BF16)
                    p_scr[m, item, hp * 2 + half] = p
                    outs.append(dot(p, v, 1, 0))
                o_scr[m, rows, at_q] = jnp.where(left, outs[0], outs[1]).astype(BF16)
            return carry

        lax.fori_loop(0, HEADS // 2, heads, 0)
        y = x_scr[m].astype(F32) + dot(o_scr[m], wo_ref[...], 1, 0)
        y_scr[m] = y
        unit2, _ = normalize_parts(y)
        b_scr[m] = (unit2 * gain2_ref[...]).astype(BF16)
        b_sent.append(spread(b_scr.at[m], lambda i, m=m: b_all.at[i, m]))
        for scr, out in (
            (x_scr, x_out), (qkv_scr, qkv_out), (p_scr, p_out), (o_scr, o_out), (y_scr, y_out)
        ):
            copies.keep(scr.at[m], out.at[m])
        if direct and m == 0:
            z1.wait_recv()
            y1 = copies.send(w_all.at[1], w_all.at[2], near_by.y)
            z3 = copies.send(own_ref, w_all.at[3], near_by.z[3])
            flags = pass_on(flags, lambda i: flags_all.at[i])

    if direct:
        z3.wait_recv()
        y3 = copies.send(w_all.at[3], w_all.at[4], near_by.y)
        z2 = [copies.send(own_ref.at[:, i], w_all.at[5, :, i], near_by.z[2]) for i in range(2)]
        gz = pass_on(gz, lambda i: gz_all.at[i])
        b_sent[0] = pass_on(b_sent[0], lambda i: b_all.at[i, 0])
        y2 = []
        for i in range(2):
            z2[i].wait_recv()
            y2.append(copies.send(w_all.at[5, :, i], w_all.at[6, :, i], near_by.y))
        for m in range(1, batches):
            b_sent[m] = pass_on(b_sent[m], lambda i, m=m: b_all.at[i, m])
        for copy in [y0, y1, y3, *y2, *flags, *gz] + [c for pair_of in b_sent for c in pair_of]:
            copy.wait_recv()
    copies.finish()


def front(direct, own, tokens, cot, index, keep, flags, gain1, gain2, wqkv, wo):
    batches, length, width = tokens.shape
    groups = 4 if direct else 1
    out = jax.ShapeDtypeStruct
    vmem = pl.BlockSpec(memory_space=pltpu.VMEM)
    anywhere = pl.BlockSpec(memory_space=pl.ANY)
    kept = [
        ((batches, ROWS, width), BF16),
        ((batches, ROWS, 3 * width), BF16),
        ((batches, ITEMS, HEADS, ITEM_ROWS, ITEM_ROWS), BF16),
        ((batches, ROWS, width), BF16),
        ((batches, ROWS, width), F32),
    ]
    scratch = [pltpu.VMEM((batches, ROWS, width), BF16)] * 2
    return pl.pallas_call(
        functools.partial(front_kernel, direct, batches),
        in_specs=[anywhere] + [vmem] * 9,
        out_specs=[anywhere] * 9,
        out_shape=[
            out((7 if direct else 1,) + (own.shape if direct else (8, 128)), BF16),
            out((groups, batches, ROWS, width), BF16),
            out((groups,) + flags.shape, flags.dtype),
            out((groups, batches, ROWS, width), BF16),
        ]
        + [out(*k) for k in kept],
        scratch_shapes=scratch
        + [pltpu.VMEM(*k) for k in kept]
        + [
            pltpu.SemaphoreType.DMA((32,)),
            pltpu.SemaphoreType.DMA((32,)),
            pltpu.SemaphoreType.DMA((24,)),
        ],
        compiler_params=pltpu.CompilerParams(
            vmem_limit_bytes=VMEM_LIMIT,
            has_side_effects=direct,
            collective_id=0 if direct else None,
        ),
        cost_estimate=pl.CostEstimate(
            flops=batches
            * (2 * ROWS * width * width * 4 + 8 * HEADS * ITEMS * ITEM_ROWS**2 * 128),
            bytes_accessed=60_000_000,
            transcendentals=batches * HEADS * ITEMS * ITEM_ROWS**2,
        ),
        name="front",
    )(own, tokens, cot, index, keep, flags, gain1, gain2, wqkv, wo)


def head_gradients(qkv_at, go_at, p_of, gqkv_ref, row0, hp, width, left):
    head_dim = width // HEADS
    pair = 2 * head_dim
    scaling = head_dim**-0.5
    at_q = pl.ds(pl.multiple_of(hp * pair, pair), pair)
    at_k = pl.ds(pl.multiple_of(width + hp * pair, pair), pair)
    at_v = pl.ds(pl.multiple_of(2 * width + hp * pair, pair), pair)
    for item in range(ITEMS):
        rows = slice(item * ITEM_ROWS, (item + 1) * ITEM_ROWS)
        out_rows = slice(row0 + rows.start, row0 + rows.stop)
        q, k, v = qkv_at(rows, at_q), qkv_at(rows, at_k), qkv_at(rows, at_v)
        go = go_at(rows, at_q)
        gq, gk, gv = [], [], []
        for half in range(2):
            mine = left if half == 0 else ~left
            p = p_of(item, half)
            pf = p.astype(F32)
            gp = dot(jnp.where(mine, go, 0), v, 1, 1)
            gs = (pf * (gp - jnp.sum(pf * gp, axis=-1, keepdims=True))).astype(BF16)
            gv.append(dot(p, go, 0, 0))
            gq.append(dot(gs, k, 1, 0))
            gk.append(dot(gs, q, 0, 0))
        gqkv_ref[out_rows, at_q] = (jnp.where(left, gq[0], gq[1]) * scaling).astype(BF16)
        gqkv_ref[out_rows, at_k] = (jnp.where(left, gk[0], gk[1]) * scaling).astype(BF16)
        gqkv_ref[out_rows, at_v] = jnp.where(left, gv[0], gv[1]).astype(BF16)


def back_kernel(batches, *refs):
    gb_parts, z_parts, gw, cot_in, index_ref, keep_ref, x_in, o_in, y_in, qkv_in, p_in = refs[:11]
    gain1_ref, gain2_ref, wqkv_in, wo_in = refs[11:15]
    result_out, tg_out, gall, wsum, gains_out, z_core, z_far, rs_z = refs[15:23]
    (
        wqkv, wo, x, o, y, cot, qkv, p, gb_own, gb_far, gb_core, gb_cross, gb_x,
        gy, ga, go, gqkv, grads, r_core, r_one, r_two, r_z, final,
        held, r_y, gsum, gain_in, tok, send_sem, recv_sem, local_sem, p_sem,
    ) = refs[23:]
    width = x.shape[1]
    head_dim = width // HEADS
    pair = 2 * head_dim
    length = cot.shape[0]
    dp, expert = lax.axis_index("dp"), lax.axis_index("expert")
    core, xi, yi, zi = expert % 2, expert // 2, dp % 2, dp // 2
    copies = Copies(send_sem, recv_sem, local_sem)
    near_by = Partners()
    near_by.greet()
    load, send = copies.load, copies.send

    def add(*terms):
        total = terms[0].astype(F32)
        for term in terms[1:]:
            total = total + term.astype(F32)
        return total.astype(BF16)

    crossed, nearer = [], []
    for m in range(batches):
        crossed.append(send(gb_parts.at[3, m], gb_cross.at[m], near_by.core))
        nearer.append(send(gb_parts.at[1, m], gb_core.at[m], near_by.core))
    order = ((6, 2), (2, 3), (4, 1), (0, 0))
    pieces = [send(gw.at[order[0][0] + 1], r_y.at[0], near_by.y)]
    far_loads = [load(gb_parts.at[2, m], gb_far.at[m]) for m in range(batches)]
    own_loads = [load(gb_parts.at[0, m], gb_own.at[m]) for m in range(batches)]
    first_loads = [load(y_in.at[0], y), load(cot_in.at[0], cot)]
    held_loads = [load(gw.at[order[i][0]], held.at[i]) for i in range(4)]
    late_loads = [load(o_in, o), load(wo_in, wo), load(qkv_in.at[0], qkv)]
    last_loads = [load(x_in, x), load(wqkv_in, wqkv)]
    along = []
    for m in range(batches):
        far_loads[m].wait()
        crossed[m].wait_recv()
        gb_far[m] = add(gb_far[m], gb_cross[m])
        along.append(send(gb_far.at[m], gb_x.at[m], near_by.x))
    z_crossed = [send(z_parts.at[3, m], z_core.at[1, m], near_by.core) for m in range(batches)]
    z_nearer = [send(z_parts.at[1, m], z_core.at[0, m], near_by.core) for m in range(batches)]

    sent_z = []

    def reduce_piece(i):
        pieces[i].wait_recv()
        if i < 3:
            pieces.append(send(gw.at[order[i + 1][0] + 1], r_y.at[i + 1], near_by.y))
        held_loads[i].wait()
        held[i] = add(held[i], r_y[i])
        if i < 3:
            sent_z.append(send(held.at[i], rs_z.at[i], near_by.z[order[i][1]]))

    left = lax.broadcasted_iota(jnp.int32, (ITEM_ROWS, pair), 1) < head_dim
    reduce_piece(0)
    for copy in first_loads + late_loads:
        copy.wait()
    gain2_grad = jnp.zeros((1, width), F32)
    items = [slice(i * ITEM_ROWS, (i + 1) * ITEM_ROWS) for i in range(ITEMS)]
    for m in range(batches):
        row0 = m * ROWS

        def p_load(hp, m=m):
            return pltpu.make_async_copy(
                p_in.at[m, :, pl.ds(2 * hp, 2)], p.at[hp % 2], p_sem.at[hp % 2]
            )

        p_load(0).start()
        own_loads[m].wait()
        nearer[m].wait_recv()
        along[m].wait_recv()
        for rows in items:
            at = slice(row0 + rows.start, row0 + rows.stop)
            gb = (
                gb_own[m, rows].astype(F32)
                + gb_core[m, rows].astype(F32)
                + gb_x[m, rows].astype(F32)
            )
            unit2, inverse2 = normalize_parts(y[rows])
            gain2_grad = gain2_grad + jnp.sum(gb * unit2, axis=0, keepdims=True)
            g = dot(pick_rows(index_ref, m, length, rows).astype(BF16), cot[...], 1, 0)
            gy_rows = g + normalize_back(gb * gain2_ref[...], unit2, inverse2)
            gy[at] = gy_rows
            ga[at] = gy_rows.astype(BF16)
            go[rows] = dot(ga[at], wo[...], 1, 1).astype(BF16)
        if m + 1 < batches:
            first_loads = [load(y_in.at[m + 1], y), load(cot_in.at[m + 1], cot)]

        def heads(hp, carry, row0=row0, p_load=p_load):
            @pl.when(hp + 1 < HEADS // 2)
            def _():
                p_load(hp + 1).start()

            p_load(hp).wait()
            slot = hp % 2
            head_gradients(
                lambda rows, cols: qkv[rows, cols],
                lambda rows, cols: go[rows, cols],
                lambda item, half: p[slot, item, half],
                gqkv, row0, hp, width, left,
            )
            return carry

        lax.fori_loop(0, HEADS // 2, heads, 0)
        if m + 1 < batches:
            first_loads.append(load(qkv_in.at[m + 1], qkv))
            reduce_piece(1 + m)
            for copy in first_loads:
                copy.wait()

    z_along = []
    for m in range(batches):
        loads = [load(z_parts.at[2, m], gb_own.at[m])]
        z_crossed[m].wait_recv()
        loads.append(load(z_core.at[1, m], gb_core.at[m]))
        for copy in loads:
            copy.wait()
        gb_cross[m] = add(gb_own[m], gb_core[m])
        z_along.append(send(gb_cross.at[m], z_far.at[m], near_by.x))
    reduce_piece(2)

    for copy in last_loads:
        copy.wait()
    for part in range(2):
        cols = slice(part * width // 2, (part + 1) * width // 2)
        grads[:, 3 * width + cols.start : 3 * width + cols.stop] = dot(
            o[...], ga[:, cols], 0, 0
        ).astype(BF16)
    a = ga
    for m in range(batches):
        at = slice(m * ROWS, (m + 1) * ROWS)
        unit, _ = normalize_parts(x[at].astype(F32))
        a[at] = (unit * gain1_ref[...]).astype(BF16)
    for part in range(6):
        cols = slice(part * width // 2, (part + 1) * width // 2)
        grads[:, cols] = dot(a[...], gqkv[:, cols], 0, 0).astype(BF16)

    half = width // 2
    wide = grads.shape[1] // 2
    a_cols, b_cols = pl.ds(0, wide), pl.ds(wide, wide)

    def rows_at(start, size):
        return pl.ds(pl.multiple_of(start, 32), size)

    row_c = core * half
    copy_c = send(grads.at[rows_at(half - row_c, half)], r_core, near_by.core)

    gain1_grad = jnp.zeros((1, width), F32)
    token_stores = []
    for m in range(batches):
        for rows in items:
            at = slice(m * ROWS + rows.start, m * ROWS + rows.stop)
            unit, inverse = normalize_parts(x[at].astype(F32))
            gnorm = dot(gqkv[at], wqkv[...], 1, 1)
            gain1_grad = gain1_grad + jnp.sum(gnorm * unit, axis=0, keepdims=True)
            go[rows] = (gy[at] + normalize_back(gnorm * gain1_ref[...], unit, inverse)).astype(BF16)
        tok[m] = dot(pick_rows(index_ref, m, length).astype(BF16), go[...], 0, 0).astype(BF16)
        token_stores.append(load(tok.at[m], tg_out.at[m]))
        if m == 0:
            copy_c.wait_recv()
            for part in range(8):
                cols = pl.ds(part * width // 2, width // 2)
                grads[rows_at(row_c, half), cols] = add(
                    grads[rows_at(row_c, half), cols], r_core[:, cols]
                )
            quarter = half // 2
            row_a, row_b = row_c + xi * quarter, row_c + yi * quarter
            one = [
                send(
                    grads.at[rows_at(row_c + (1 - xi) * quarter, quarter), a_cols],
                    r_one.at[0], near_by.x,
                ),
                send(
                    grads.at[rows_at(row_c + (1 - yi) * quarter, quarter), b_cols],
                    r_one.at[1], near_by.y,
                ),
            ]
    gsum[0] = jnp.concatenate([gain1_grad, gain2_grad, jnp.zeros((6, width), F32)], axis=0)
    gain_partners = [near_by.core, near_by.x, near_by.y, near_by.z_pair, near_by.z[2]]
    gain_sent = [send(gsum.at[0], gain_in.at[0], gain_partners[0])]

    def gain_step():
        at = len(gain_sent)
        gain_sent[-1].wait_recv()
        gsum[at] = gsum[at - 1] + gain_in[at - 1]
        if at < len(gain_partners):
            gain_sent.append(send(gsum.at[at], gain_in.at[at], gain_partners[at]))

    gain_step()
    reduce_piece(3)
    for i, (row, cols) in enumerate(((row_a, a_cols), (row_b, b_cols))):
        one[i].wait_recv()
        grads[rows_at(row, quarter), cols] = add(grads[rows_at(row, quarter), cols], r_one[i])
    eighth = quarter // 2
    two = [
        send(
            grads.at[rows_at(row_a + (1 - yi) * eighth, eighth), a_cols], r_two.at[0], near_by.y
        ),
        send(
            grads.at[rows_at(row_b + (1 - xi) * eighth, eighth), b_cols], r_two.at[1], near_by.x
        ),
    ]
    row_a2, row_b2 = row_a + yi * eighth, row_b + xi * eighth
    gain_step()

    for m in range(batches):
        z_nearer[m].wait_recv()
        z_along[m].wait_recv()
        loads = [
            load(z_parts.at[0, m], gb_own.at[m]),
            load(z_core.at[0, m], gb_core.at[m]),
            load(z_far.at[m], gb_x.at[m]),
            load(y_in.at[m], y),
        ]
        for copy in loads:
            copy.wait()
        for rows in items:
            chosen = pick_rows(index_ref, m, length, rows)
            keep = jnp.sum(jnp.where(chosen, keep_ref[m], 0.0), axis=1, keepdims=True)
            z = (
                gb_own[m, rows].astype(F32)
                + gb_core[m, rows].astype(F32)
                + gb_x[m, rows].astype(F32)
            )
            go[rows] = (y[rows] + jnp.where(keep > 0, z, 0.0)).astype(BF16)
        token_stores[m].wait()
        tok[m] = dot(pick_rows(index_ref, m, length).astype(BF16), go[...], 0, 0).astype(BF16)
        copies.keep(tok.at[m], result_out.at[m])

    for i, (row, cols) in enumerate(((row_a2, a_cols), (row_b2, b_cols))):
        two[i].wait_recv()
        grads[rows_at(row, eighth), cols] = add(grads[rows_at(row, eighth), cols], r_two[i])
    chunk = wide // 4
    ends = ((row_a2, 0), (row_b2, wide))

    def z_cols(first, z):
        return pl.ds(pl.multiple_of(first + z * chunk, 128), chunk)

    three = [
        [
            send(
                grads.at[rows_at(row, eighth), z_cols(first, (zi + shift) % 4)],
                r_z.at[i, shift - 1], near_by.z[shift],
            )
            for shift in (1, 2, 3)
        ]
        for i, (row, first) in enumerate(ends)
    ]
    gain_step()

    z_loads = []
    for i in range(3):
        sent_z[i].wait_recv()
        z_loads.append(load(rs_z.at[i], r_y.at[i]))
    for copy in z_loads:
        copy.wait()
    held[3] = add(held[3], r_y[0], r_y[1], r_y[2])
    copies.keep(held.at[3], wsum.at[expert])
    join_near = send(held.at[3], wsum.at[expert], near_by.core)
    join_far = send(held.at[3], wsum.at[expert], near_by.x)

    spread = []
    for i, (row, first) in enumerate(ends):
        for copy in three[i]:
            copy.wait_recv()
        mine = z_cols(first, zi)
        final[i] = add(grads[rows_at(row, eighth), mine], r_z[i, 0], r_z[i, 1], r_z[i, 2])
        place = gall.at[rows_at(row, eighth), mine]
        spread.append(
            (
                load(final.at[i], place),
                [send(final.at[i], place, near_by.z[shift]) for shift in (1, 2, 3)],
            )
        )
    gain_step()
    join_far.wait_recv()
    opposite = (expert + 2) % 4
    join_last = send(wsum.at[opposite], wsum.at[opposite], near_by.core)

    def block(row, size, cols):
        return gall.at[rows_at(row, size), cols]

    back_two = []
    for i, (row, cols, to) in enumerate(
        ((row_a2, a_cols, near_by.y), (row_b2, b_cols, near_by.x))
    ):
        own, others = spread[i]
        own.wait()
        for copy in others:
            copy.wait_recv()
        back_two.append(send(block(row, eighth, cols), block(row, eighth, cols), to))
    gain_step()
    copies.keep(gsum.at[len(gain_partners)], gains_out)
    back_one = []
    for i, (row, cols, to) in enumerate(((row_a, a_cols, near_by.x), (row_b, b_cols, near_by.y))):
        back_two[i].wait_recv()
        back_one.append(send(block(row, quarter, cols), block(row, quarter, cols), to))
    back_core = []
    for i, cols in enumerate((a_cols, b_cols)):
        back_one[i].wait_recv()
        back_core.append(send(block(row_c, half, cols), block(row_c, half, cols), near_by.core))
    for copy in [join_near, join_last] + back_core:
        copy.wait_recv()
    copies.finish()


def back(gb_parts, z_parts, gw, cot, index, keep, x, o, y, qkv, p, gain1, gain2, wqkv, wo):
    batches, rows, width = x.shape
    length = cot.shape[1]
    out = jax.ShapeDtypeStruct
    vmem = pl.BlockSpec(memory_space=pltpu.VMEM)
    anywhere = pl.BlockSpec(memory_space=pl.ANY)
    piece = gw.shape[1:]
    both = batches * rows
    half, wide = width // 2, 2 * width
    tokens_shape = (batches, rows, width)
    slots = [tokens_shape] * 5
    scratch = [
        ((width, 3 * width), BF16),
        ((width, width), BF16),
        ((both, width), BF16),
        ((both, width), BF16),
        ((rows, width), F32),
        ((length, width), BF16),
        ((rows, 3 * width), BF16),
        ((2, ITEMS, 2, ITEM_ROWS, ITEM_ROWS), BF16),
        *[(slot, BF16) for slot in slots],
        ((both, width), F32),
        ((both, width), BF16),
        ((rows, width), BF16),
        ((both, 3 * width), BF16),
        ((width, 4 * width), BF16),
        ((half, 4 * width), BF16),
        ((2, half // 2, wide), BF16),
        ((2, half // 4, wide), BF16),
        ((2, 3, half // 4, wide // 4), BF16),
        ((2, half // 4, wide // 4), BF16),
        ((4,) + piece, BF16),
        ((4,) + piece, BF16),
        ((6, 8, width), F32),
        ((5, 8, width), F32),
        ((batches, length, width), BF16),
    ]
    return pl.pallas_call(
        functools.partial(back_kernel, batches),
        in_specs=[anywhere] * 4 + [vmem] * 2 + [anywhere] * 5 + [vmem] * 2 + [anywhere] * 2,
        out_specs=[anywhere] * 8,
        out_shape=[
            out(cot.shape, BF16),
            out(cot.shape, BF16),
            out((width, 4 * width), BF16),
            out((4,) + piece, BF16),
            out((8, width), F32),
            out((2,) + tokens_shape, BF16),
            out(tokens_shape, BF16),
            out((3,) + piece, BF16),
        ],
        scratch_shapes=[pltpu.VMEM(*k) for k in scratch]
        + [
            pltpu.SemaphoreType.DMA((64,)),
            pltpu.SemaphoreType.DMA((64,)),
            pltpu.SemaphoreType.DMA((64,)),
            pltpu.SemaphoreType.DMA((2,)),
        ],
        compiler_params=pltpu.CompilerParams(
            vmem_limit_bytes=VMEM_LIMIT, has_side_effects=True, collective_id=1
        ),
        cost_estimate=pl.CostEstimate(
            flops=batches
            * (2 * rows * width * width * 8 + 16 * HEADS * ITEMS * ITEM_ROWS**2 * 128),
            bytes_accessed=80_000_000,
            transcendentals=0,
        ),
        name="back",
    )(
        gb_parts, z_parts, gw, cot, index, keep,
        x.reshape(both, width), o.reshape(both, width), y, qkv, p, gain1, gain2, wqkv, wo,
    )


def attention_backward_kernel(n_parts, n_carry, *refs):
    parts = refs[:n_parts]
    (cot_ref, x_ref, y_ref, qkv_ref, p_ref, o_ref, gain1_ref, gain2_ref, wqkv_ref, wo_ref) = refs[
        n_parts : n_parts + 10
    ]
    carried = refs[n_parts + 10 : n_parts + 10 + n_carry]
    tg_ref, gwqkv_ref, gwo_ref, ggain_ref, gmix_ref, gqkv_ref = refs[n_parts + 10 + n_carry :]
    width = x_ref.shape[1]
    head_dim = width // HEADS
    gb = parts[0][...].astype(F32)
    for part in parts[1:]:
        gb = gb + part[...].astype(F32)
    unit2, inverse2 = normalize_parts(y_ref[...])
    gain2_grad = jnp.sum(gb * unit2, axis=0, keepdims=True)
    gy = cot_ref[...].astype(F32) + normalize_back(gb * gain2_ref[...], unit2, inverse2)
    ga = gy.astype(BF16)
    gwo = dot(o_ref[...], ga, 0, 0)
    if n_carry:
        gwo = gwo + carried[1][...]
    gwo_ref[...] = gwo
    gmix_ref[...] = dot(ga, wo_ref[...], 1, 1).astype(BF16)
    pair = 2 * head_dim
    left = lax.broadcasted_iota(jnp.int32, (ITEM_ROWS, pair), 1) < head_dim

    def heads(hp, carry):
        head_gradients(
            lambda rows, cols: qkv_ref[rows, cols],
            lambda rows, cols: gmix_ref[rows, cols],
            lambda item, half: p_ref[item, hp * 2 + half],
            gqkv_ref, 0, hp, width, left,
        )
        return carry

    lax.fori_loop(0, HEADS // 2, heads, 0)
    unit, inverse = normalize_parts(x_ref[...].astype(F32))
    a = (unit * gain1_ref[...]).astype(BF16)
    for part in range(3):
        cols = slice(part * width, (part + 1) * width)
        gw = dot(a, gqkv_ref[:, cols], 0, 0)
        if n_carry:
            gw = gw + carried[0][:, cols]
        gwqkv_ref[:, cols] = gw
    gnorm = dot(gqkv_ref[...], wqkv_ref[...], 1, 1)
    gain1_grad = jnp.sum(gnorm * unit, axis=0, keepdims=True)
    gains = jnp.concatenate([gain1_grad, gain2_grad, jnp.zeros((6, width), F32)], axis=0)
    if n_carry:
        gains = gains + carried[2][...]
    ggain_ref[...] = gains
    tg_ref[...] = (gy + normalize_back(gnorm * gain1_ref[...], unit, inverse)).astype(BF16)


def attention_backward(parts, cot, x, y, qkv, p, o, gain1, gain2, wqkv, wo, carried):
    rows, width = x.shape
    out = jax.ShapeDtypeStruct
    return pl.pallas_call(
        functools.partial(attention_backward_kernel, len(parts), len(carried)),
        out_shape=(
            out((rows, width), BF16),
            out((width, 3 * width), F32),
            out((width, width), F32),
            out((8, width), F32),
        ),
        scratch_shapes=[pltpu.VMEM((rows, width), BF16), pltpu.VMEM((rows, 3 * width), BF16)],
        compiler_params=pltpu.CompilerParams(vmem_limit_bytes=VMEM_LIMIT),
        cost_estimate=pl.CostEstimate(
            flops=2 * rows * width * width * 8 + 16 * HEADS * ITEMS * ITEM_ROWS**2 * 128,
            bytes_accessed=30_000_000,
            transcendentals=0,
        ),
        name="attention_backward",
    )(*parts, cot, x, y, qkv, p, o, gain1, gain2, wqkv, wo, *carried)


def expert_kernel(groups, batches, pieces, *refs):
    flags, own_ref, more_ref, b_in, g_in, z_out, gb_out, gw_out = refs[:8]
    rows_b, rows_g, w, grads, in_sem, w_sem, out_sem, gw_sem = refs[8:]
    part = own_ref.shape[2]

    def rounded(rows):
        return (rows + TILE - 1) // TILE * TILE

    merged = [
        flags[g, 0, micro * ITEMS + item]
        for g in range(groups)
        for micro in range(batches)
        for item in range(ITEMS)
    ]
    n_merged = sum(merged)
    n_plain = len(merged) - n_merged
    sizes = [n_plain * IMAGE_ROWS, n_plain * CAPTION, n_merged * ITEM_ROWS]
    starts = [0, rounded(sizes[0]), rounded(sizes[0]) + rounded(sizes[1])]
    ends = [start + rounded(size) for start, size in zip(starts, sizes)]
    blocks = []
    plain, joined = 0, 0
    for flat, flag in enumerate(merged):
        g, micro, item = flat // (batches * ITEMS), flat // ITEMS % batches, flat % ITEMS
        base = item * ITEM_ROWS
        image = jnp.where(flag == 1, starts[2] + joined * ITEM_ROWS, plain * IMAGE_ROWS)
        caption = jnp.where(
            flag == 1, image + IMAGE_ROWS, starts[1] + plain * CAPTION
        )
        blocks.append((g, micro, base, IMAGE_ROWS, image, flag, 0))
        blocks.append((g, micro, base + IMAGE_ROWS, CAPTION, caption, flag, 1))
        plain, joined = plain + 1 - flag, joined + flag

    def copy_of(which, number, outward):
        g, micro, base, size, at, _, _ = blocks[number]
        held = (rows_b, rows_g)[which].at[pl.ds(pl.multiple_of(at, 16), size)]
        if outward:
            far = (gb_out, z_out)[which].at[g, micro, pl.ds(base, size)]
            return pltpu.make_async_copy(held, far, out_sem.at[which, number])
        far = (b_in, g_in)[which].at[g, micro, pl.ds(base, size)]
        return pltpu.make_async_copy(far, held, in_sem.at[which, number])

    def of_expert(expert, act):
        for number, (_, _, _, _, _, flag, kind) in enumerate(blocks):
            if expert == 2 or kind == expert:
                @pl.when(flag == (1 if expert == 2 else 0))
                def _(number=number):
                    for which in range(2):
                        act(which, number)

    def weight_copy(k, i):
        piece = own_ref if i == 0 else more_ref.at[i - 1]
        return pltpu.make_async_copy(
            piece.at[k], w.at[k, :, pl.ds(i * part, part), :], w_sem.at[k, i]
        )

    for k in range(3):
        tail = pl.multiple_of(jnp.maximum(ends[k] - TILE, 0), TILE)
        rows_b[pl.ds(tail, TILE), :] = jnp.zeros((TILE, rows_b.shape[1]), BF16)
        rows_g[pl.ds(tail, TILE), :] = jnp.zeros((TILE, rows_g.shape[1]), BF16)
    for k in range(3):
        of_expert(k, lambda which, number: copy_of(which, number, False).start())
        for i in range(pieces):
            weight_copy(k, i).start()

    third = w.shape[2] // 3
    for k in range(3):
        grads[...] = jnp.zeros(grads.shape, F32)
        of_expert(k, lambda which, number: copy_of(which, number, False).wait())
        for i in range(pieces):
            weight_copy(k, i).wait()

        def tile(t, carry, k=k):
            at = pl.ds(pl.multiple_of(t * TILE, TILE), TILE)
            b, gz = rows_b[at, :], rows_g[at, :]
            z = gb = None
            for c in range(3):
                cols = slice(c * third, (c + 1) * third)
                w1, w2 = w[k, 0, cols], w[k, 1, cols]
                u, slope = gelu_and_slope(dot(b, w1, 1, 1))
                gh = (dot(gz, w2, 1, 1) * slope).astype(BF16)
                u = u.astype(BF16)
                more_z, more_gb = dot(u, w2, 1, 0), dot(gh, w1, 1, 0)
                z = more_z if c == 0 else z + more_z
                gb = more_gb if c == 0 else gb + more_gb
                grads[0, cols] += dot(gh, b, 0, 0)
                grads[1, cols] += dot(u, gz, 0, 0)
            rows_b[at, :] = gb.astype(BF16)
            rows_g[at, :] = z.astype(BF16)
            return carry

        lax.fori_loop(starts[k] // TILE, ends[k] // TILE, tile, 0)
        of_expert(k, lambda which, number: copy_of(which, number, True).start())
        w[k] = grads[...].astype(BF16)
        for i in range(pieces):
            pltpu.make_async_copy(
                w.at[k, :, pl.ds(i * part, part), :], gw_out.at[i, k], gw_sem.at[k, i]
            ).start()
    for number in range(len(blocks)):
        for which in range(2):
            copy_of(which, number, True).wait()
    for k in range(3):
        for i in range(pieces):
            pltpu.make_async_copy(
                w.at[k, :, pl.ds(i * part, part), :], gw_out.at[i, k], gw_sem.at[k, i]
            ).wait()


def experts(flags, own, more, b_groups, g_groups):
    groups, batches, rows, width = b_groups.shape
    part = own.shape[2]
    pieces = 1 + (more.shape[0] if more.ndim == 5 else 0)
    hidden = part * pieces
    count = groups * batches * ITEMS
    capacity = (count * ITEM_ROWS // TILE + 4) * TILE
    out = jax.ShapeDtypeStruct
    anywhere = pl.BlockSpec(memory_space=pl.ANY)
    return pl.pallas_call(
        functools.partial(expert_kernel, groups, batches, pieces),
        in_specs=[pl.BlockSpec(memory_space=pltpu.SMEM)] + [anywhere] * 4,
        out_specs=[anywhere] * 3,
        out_shape=[out(b_groups.shape, BF16)] * 2 + [out((pieces,) + own.shape, BF16)],
        scratch_shapes=[
            pltpu.VMEM((capacity, width), BF16),
            pltpu.VMEM((capacity, width), BF16),
            pltpu.VMEM((3, 2, hidden, width), BF16),
            pltpu.VMEM((2, hidden, width), F32),
            pltpu.SemaphoreType.DMA((2, 2 * count)),
            pltpu.SemaphoreType.DMA((3, pieces)),
            pltpu.SemaphoreType.DMA((2, 2 * count)),
            pltpu.SemaphoreType.DMA((3, pieces)),
        ],
        compiler_params=pltpu.CompilerParams(vmem_limit_bytes=VMEM_LIMIT),
        cost_estimate=pl.CostEstimate(
            flops=2 * 6 * count * ITEM_ROWS * width * hidden,
            bytes_accessed=45_000_000,
            transcendentals=count * ITEM_ROWS * hidden,
        ),
        name="experts",
    )(flags, own, more, b_groups, g_groups)


def rows_of_items(first):
    row = jnp.arange(ROWS, dtype=jnp.int32)
    item, inside = row // ITEM_ROWS, row % ITEM_ROWS
    caption = jnp.where(first, item, 1 - item)
    return jnp.where(
        inside < PATCHES,
        item * PATCHES + inside,
        jnp.where(
            inside < IMAGE_ROWS,
            -1,
            ITEMS * PATCHES + caption * CAPTION + inside - IMAGE_ROWS,
        ),
    )


def to_items(rows, first):
    images = ITEMS * PATCHES
    one, two = rows[images : images + CAPTION], rows[images + CAPTION :]
    gap = jnp.zeros((IMAGE_ROWS - PATCHES,) + rows.shape[1:], rows.dtype)
    return jnp.concatenate(
        [
            rows[:PATCHES],
            gap,
            jnp.where(first, one, two),
            rows[PATCHES:images],
            gap,
            jnp.where(first, two, one),
        ],
        axis=0,
    )


def from_items(rows, first):
    one, two = rows[IMAGE_ROWS:ITEM_ROWS], rows[ITEM_ROWS + IMAGE_ROWS :]
    return jnp.concatenate(
        [
            rows[:PATCHES],
            rows[ITEM_ROWS : ITEM_ROWS + PATCHES],
            jnp.where(first, one, two),
            jnp.where(first, two, one),
        ],
        axis=0,
    )


def kept_tokens(routing, priority, hosts, capacity):
    length = routing.shape[0]
    index = jnp.arange(length, dtype=jnp.int32)
    position = jnp.sum(
        jnp.where(priority[None, :] == index[:, None], index[None, :], 0), axis=1
    )
    ahead = (routing[None, :] == routing[:, None]) & (position[None, :] < position[:, None])
    rank = jnp.sum(ahead.astype(jnp.int32), axis=1)
    return rank < capacity * ((hosts - routing + 2) // 3)


class Links:
    def __init__(self):
        self.hosts = lax.axis_size("expert")
        self.dp = lax.axis_size("dp")
        self.direct = self.hosts == 4 and self.dp == 8
        self.me = lax.axis_index("expert")

    def flip(self, v, bit):
        return lax.ppermute(v, "expert", [(i, i ^ bit) for i in range(4)])

    def across_y(self, v):
        return lax.ppermute(v, "dp", [(i, i ^ 1) for i in range(8)])

    def along_z(self, v, shift):
        return lax.ppermute(v, "dp", [(i, (i + 2 * shift) % 8) for i in range(8)])

    def gather_tokens(self, v):
        if not self.direct:
            return list(lax.all_gather(v, "expert"))
        near, far = self.flip(v, 1), self.flip(v, 2)
        return [v, near, far, self.flip(far, 1)]

    def reduce_tokens(self, parts):
        if not self.direct:
            return [lax.psum_scatter(jnp.stack(parts), "expert", scatter_dimension=0)]
        far = (parts[2].astype(F32) + self.flip(parts[3], 1).astype(F32)).astype(BF16)
        return [parts[0], self.flip(parts[1], 1), self.flip(far, 2)]

    def reduce_weights(self, pieces):
        if not self.direct:
            return lax.psum_scatter(pieces[0], "dp", scatter_dimension=2, tiled=True)
        total = None
        for at, shift in enumerate((0, 1, 3, 2)):
            piece = pieces[2 * at].astype(F32) + self.across_y(pieces[2 * at + 1]).astype(F32)
            if shift:
                piece = self.along_z(piece.astype(BF16), -shift).astype(F32)
            total = piece if total is None else total + piece
        return total.astype(BF16)

    def join_hidden(self, v):
        if not self.direct:
            return lax.all_gather(v, "expert", axis=2, tiled=True)
        stacked = jnp.stack(self.gather_tokens(v))
        return jnp.concatenate(
            [
                lax.dynamic_index_in_dim(stacked, i ^ self.me, 0, keepdims=False)
                for i in range(4)
            ],
            axis=2,
        )


def shards(
    tokens,
    cotangent,
    item_group,
    routes,
    slot_order,
    attn_gain,
    ffn_gain,
    qkv_weight,
    out_weight,
    expert_in,
    expert_out,
):
    links = Links()
    hosts, me = links.hosts, links.me
    batches, length, width = tokens.shape
    capacity = 2 * length // hosts
    shard = expert_in.shape[2]
    part = shard // hosts
    gain1, gain2 = attn_gain[None, :], ffn_gain[None, :]

    own = jnp.stack(
        [
            jnp.swapaxes(lax.dynamic_slice_in_dim(expert_in, me * part, part, 2), 1, 2),
            lax.dynamic_slice_in_dim(expert_out, me * part, part, 1),
        ],
        axis=1,
    )
    first = item_group[:, ITEMS * PATCHES] == 0
    merged = (routes[:, 0 : ITEMS * PATCHES : PATCHES] == 2).astype(jnp.int32)
    flags = jnp.broadcast_to(
        jnp.pad(merged.reshape(1, -1), ((0, 0), (0, 128 - batches * ITEMS))), (8, 128)
    )
    kept = jnp.stack(
        [kept_tokens(routes[m], slot_order[m, 0], hosts, capacity) for m in range(batches)]
    )
    index = jnp.stack([rows_of_items(first[m]) for m in range(batches)])[:, :, None]
    w_all, gz_groups, flag_groups, b_groups, x_all, qkv_all, p_all, o_all, y_all = front(
        links.direct, own, tokens, cotangent, index, kept.astype(F32)[:, None, :], flags,
        gain1, gain2, qkv_weight, out_weight,
    )
    if not links.direct:
        own = lax.all_gather(own, "dp", axis=2, tiled=True)
        gz_groups, flag_groups, b_groups = [
            lax.all_gather(v[0], "expert") for v in (gz_groups, flag_groups, b_groups)
        ]
    z_parts, gb_parts, gw_pieces = experts(flag_groups, own, w_all, b_groups, gz_groups)
    if links.direct:
        result, token_grad, gall, wsum, gains, *_ = back(
            gb_parts, z_parts, gw_pieces, cotangent, index, kept.astype(F32)[:, None, :],
            x_all, o_all, y_all, qkv_all, p_all, gain1, gain2, qkv_weight, out_weight,
        )
        shape = (3, hosts * part, width)
        wsum = wsum.astype(F32)
        return (
            result,
            token_grad,
            gains[0],
            gains[1],
            gall[:, : 3 * width].astype(F32),
            gall[:, 3 * width :].astype(F32),
            jnp.transpose(wsum[:, :, 0], (1, 3, 0, 2)).reshape(3, width, hosts * part),
            jnp.transpose(wsum[:, :, 1], (1, 0, 2, 3)).reshape(shape),
        )
    cot_items = [to_items(cotangent[m], first[m]) for m in range(batches)]
    gb_terms = links.reduce_tokens(gb_parts)
    z_terms = links.reduce_tokens(z_parts)
    sums = links.join_hidden(links.reduce_weights(gw_pieces)).astype(F32)

    results, token_grads, carried = [], [], ()
    for m in range(batches):
        x, qkv, p, o, y = x_all[m], qkv_all[m], p_all[m], o_all[m], y_all[m]
        at = m
        tg, *carried = attention_backward(
            [t[at] for t in gb_terms],
            cot_items[m], x, y, qkv, p, o, gain1, gain2, qkv_weight, out_weight,
            tuple(carried),
        )
        token_grads.append(from_items(tg, first[m]))
        z = z_terms[0][at].astype(F32)
        for term in z_terms[1:]:
            z = z + term[at].astype(F32)
        branch = jnp.where(kept[m][:, None], from_items(z, first[m]), 0.0)
        results.append((from_items(y, first[m]) + branch).astype(BF16))
    gw_qkv, gw_out, gains = carried
    packed = jnp.concatenate(
        [
            jnp.concatenate([gw_qkv, gw_out], axis=1),
            jnp.pad(gains[:2].reshape(1, 2 * width), ((0, 7), (0, 2 * width))),
        ],
        axis=0,
    ).astype(BF16)
    packed = lax.psum(packed, ("dp", "expert")).astype(F32)
    return (
        jnp.stack(results),
        jnp.stack(token_grads),
        packed[width, :width],
        packed[width, width : 2 * width],
        packed[:width, : 3 * width],
        packed[:width, 3 * width :],
        jnp.swapaxes(sums[:, 0], 1, 2),
        sums[:, 1],
    )


def solution(mesh):
    in_specs = (
        P(None, ("dp", "expert"), None),
        P(None, ("dp", "expert"), None),
        P(None, ("dp", "expert")),
        P(None, ("dp", "expert")),
        P(None, ("dp", "expert"), None),
        P(),
        P(),
        P(),
        P(),
        P(None, None, "dp"),
        P(None, "dp", None),
    )
    out_specs = (
        P(None, ("dp", "expert"), None),
        P(None, ("dp", "expert"), None),
        P(),
        P(),
        P(),
        P(),
        P(None, None, "dp"),
        P(None, "dp", None),
    )
    return jax.shard_map(shards, mesh=mesh, in_specs=in_specs, out_specs=out_specs, check_vma=False)
```

```python
import functools

import jax
import jax.numpy as jnp
from jax import lax
from jax.experimental import pallas as pl
from jax.experimental.pallas import tpu as pltpu
from jax.sharding import PartitionSpec as P

HEADS = 12
EPSILON = 1e-05
PATCHES = 197
CAPTION = 64
ITEMS = 2
IMAGE_ROWS = 208
ITEM_ROWS = IMAGE_ROWS + CAPTION
ROWS = ITEMS * ITEM_ROWS
FLAG_ROWS = 16
TILE = 256
VMEM_LIMIT = 60 * 1024 * 1024
F32 = jnp.float32
BF16 = jnp.bfloat16


def dot(a, b, a_dim, b_dim):
    return lax.dot_general(
        a, b, (((a_dim,), (b_dim,)), ((), ())), preferred_element_type=F32
    )


def normalize_parts(v):
    centred = v - jnp.mean(v, axis=-1, keepdims=True)
    inverse = lax.rsqrt(jnp.mean(centred * centred, axis=-1, keepdims=True) + EPSILON)
    return centred * inverse, inverse


def normalize_back(grad_unit, unit_rows, inverse):
    return inverse * (
        grad_unit
        - jnp.mean(grad_unit, axis=-1, keepdims=True)
        - unit_rows * jnp.mean(grad_unit * unit_rows, axis=-1, keepdims=True)
    )


def gelu_and_slope(h):
    bell = jnp.exp(-0.5 * h * h)
    t = 1.0 / (1.0 + (0.3275911 * 0.7071067811865476) * jnp.abs(h))
    poly = t * (
        0.254829592
        + t * (-0.284496736 + t * (1.421413741 + t * (-1.453152027 + t * 1.061405429)))
    )
    below = 0.5 * poly * bell
    phi = jnp.where(h > 0, 1.0 - below, below)
    return h * phi, phi + h * (0.3989422804014327 * bell)


class Partners:
    def __init__(self):
        dp, expert = lax.axis_index("dp"), lax.axis_index("expert")
        self.core = (dp, expert + 1 - 2 * (expert % 2))
        self.x = (dp, (expert + 2) % 4)
        self.y = (dp + 1 - 2 * (dp % 2), expert)
        self.z = {shift: ((dp + 2 * shift) % 8, expert) for shift in (1, 2, 3)}
        self.z_pair = (dp + 2 - 4 * (dp // 2 % 2), expert)

    def greet(self):
        barrier = pltpu.get_barrier_semaphore()
        everyone = [self.core, self.x, self.y, self.z[1], self.z[2], self.z[3]]
        for other in everyone:
            pl.semaphore_signal(
                barrier, inc=1, device_id=other, device_id_type=pl.DeviceIdType.MESH
            )
        pl.semaphore_wait(barrier, len(everyone))


class Copies:
    def __init__(self, send_sem, recv_sem, local_sem):
        self.send_sem, self.recv_sem, self.local_sem = send_sem, recv_sem, local_sem
        self.sent, self.kept, self.locals = [], [], 0

    def send(self, src, dst, device):
        at = len(self.sent)
        copy = pltpu.make_async_remote_copy(
            src_ref=src,
            dst_ref=dst,
            send_sem=self.send_sem.at[at],
            recv_sem=self.recv_sem.at[at],
            device_id=device,
            device_id_type=pl.DeviceIdType.MESH,
        )
        copy.start()
        self.sent.append(copy)
        return copy

    def keep(self, src, dst):
        copy = self.load(src, dst)
        self.kept.append(copy)
        return copy

    def load(self, src, dst):
        copy = pltpu.make_async_copy(src, dst, self.local_sem.at[self.locals])
        self.locals += 1
        copy.start()
        return copy

    def finish(self):
        for copy in self.sent:
            copy.wait_send()
        for copy in self.kept:
            copy.wait()


def pick_rows(index_ref, m, length, rows=slice(0, ROWS)):
    token = lax.broadcasted_iota(jnp.int32, (rows.stop - rows.start, length), 1)
    return index_ref[m, rows] == token


def front_kernel(direct, batches, *refs):
    (own_ref, tokens_ref, cot_ref, index_ref, keep_ref, flags_ref, gain1_ref, gain2_ref) = refs[:8]
    wqkv_ref, wo_ref, w_all, gz_all, flags_all, b_all, x_out, qkv_out, p_out, o_out, y_out = refs[
        8:19
    ]
    gz_scr, b_scr, x_scr, qkv_scr, p_scr, o_scr, y_scr, send_sem, recv_sem, local_sem = refs[19:]
    length, width = tokens_ref.shape[1:]
    head_dim = width // HEADS
    pair = 2 * head_dim
    copies = Copies(send_sem, recv_sem, local_sem)

    def spread(src, slots):
        copies.keep(src, slots(0))
        if not direct:
            return None
        near = copies.send(src, slots(1), near_by.core)
        return near, copies.send(src, slots(2), near_by.x)

    def pass_on(pair_of, slots):
        near, far = pair_of
        far.wait_recv()
        return near, copies.send(slots(2), slots(3), near_by.core)

    if direct:
        near_by = Partners()
        near_by.greet()
        y0 = copies.send(own_ref, w_all.at[0], near_by.y)
        z1 = copies.send(own_ref, w_all.at[1], near_by.z[1])
    flags = spread(flags_ref, lambda i: flags_all.at[i])

    for m in range(batches):
        chosen = pick_rows(index_ref, m, length) & (keep_ref[m] > 0)
        gz_scr[m] = dot(chosen.astype(BF16), cot_ref[m], 1, 0).astype(BF16)
    gz = spread(gz_scr, lambda i: gz_all.at[i])

    left = lax.broadcasted_iota(jnp.int32, (ITEM_ROWS, pair), 1) < head_dim
    key = lax.broadcasted_iota(jnp.int32, (1, ITEM_ROWS), 1)
    bias = jnp.where((key >= PATCHES) & (key < IMAGE_ROWS), -1e30, 0.0).astype(F32)
    b_sent = []
    for m in range(batches):
        xb = dot(pick_rows(index_ref, m, length).astype(BF16), tokens_ref[m], 1, 0)
        x_scr[m] = xb.astype(BF16)
        unit, _ = normalize_parts(xb)
        a = (unit * gain1_ref[...]).astype(BF16)
        for part in range(3):
            cols = slice(part * width, (part + 1) * width)
            qkv_scr[m, :, cols] = dot(a, wqkv_ref[:, cols], 1, 0).astype(BF16)

        def heads(hp, carry, m=m):
            at_q = pl.ds(pl.multiple_of(hp * pair, pair), pair)
            at_k = pl.ds(pl.multiple_of(width + hp * pair, pair), pair)
            at_v = pl.ds(pl.multiple_of(2 * width + hp * pair, pair), pair)
            for item in range(ITEMS):
                rows = slice(item * ITEM_ROWS, (item + 1) * ITEM_ROWS)
                q, k, v = qkv_scr[m, rows, at_q], qkv_scr[m, rows, at_k], qkv_scr[m, rows, at_v]
                outs = []
                for half in range(2):
                    mine = left if half == 0 else ~left
                    s = dot(jnp.where(mine, q, 0), k, 1, 1) * (head_dim**-0.5) + bias
                    e = jnp.exp(s - jnp.max(s, axis=-1, keepdims=True))
                    p = (e * (1.0 / jnp.sum(e, axis=-1, keepdims=True))).astype(BF16)
                    p_scr[m, item, hp * 2 + half] = p
                    outs.append(dot(p, v, 1, 0))
                o_scr[m, rows, at_q] = jnp.where(left, outs[0], outs[1]).astype(BF16)
            return carry

        lax.fori_loop(0, HEADS // 2, heads, 0)
        y = x_scr[m].astype(F32) + dot(o_scr[m], wo_ref[...], 1, 0)
        y_scr[m] = y
        unit2, _ = normalize_parts(y)
        b_scr[m] = (unit2 * gain2_ref[...]).astype(BF16)
        b_sent.append(spread(b_scr.at[m], lambda i, m=m: b_all.at[i, m]))
        for scr, out in (
            (x_scr, x_out), (qkv_scr, qkv_out), (p_scr, p_out), (o_scr, o_out), (y_scr, y_out)
        ):
            copies.keep(scr.at[m], out.at[m])
        if direct and m == 0:
            z1.wait_recv()
            y1 = copies.send(w_all.at[1], w_all.at[2], near_by.y)
            z3 = copies.send(own_ref, w_all.at[3], near_by.z[3])
            flags = pass_on(flags, lambda i: flags_all.at[i])

    if direct:
        z3.wait_recv()
        y3 = copies.send(w_all.at[3], w_all.at[4], near_by.y)
        z2 = [copies.send(own_ref.at[:, i], w_all.at[5, :, i], near_by.z[2]) for i in range(2)]
        gz = pass_on(gz, lambda i: gz_all.at[i])
        b_sent[0] = pass_on(b_sent[0], lambda i: b_all.at[i, 0])
        y2 = []
        for i in range(2):
            z2[i].wait_recv()
            y2.append(copies.send(w_all.at[5, :, i], w_all.at[6, :, i], near_by.y))
        for m in range(1, batches):
            b_sent[m] = pass_on(b_sent[m], lambda i, m=m: b_all.at[i, m])
        for copy in [y0, y1, y3, *y2, *flags, *gz] + [c for pair_of in b_sent for c in pair_of]:
            copy.wait_recv()
    copies.finish()


def front(direct, own, tokens, cot, index, keep, flags, gain1, gain2, wqkv, wo):
    batches, length, width = tokens.shape
    groups = 4 if direct else 1
    out = jax.ShapeDtypeStruct
    vmem = pl.BlockSpec(memory_space=pltpu.VMEM)
    anywhere = pl.BlockSpec(memory_space=pl.ANY)
    kept = [
        ((batches, ROWS, width), BF16),
        ((batches, ROWS, 3 * width), BF16),
        ((batches, ITEMS, HEADS, ITEM_ROWS, ITEM_ROWS), BF16),
        ((batches, ROWS, width), BF16),
        ((batches, ROWS, width), F32),
    ]
    scratch = [pltpu.VMEM((batches, ROWS, width), BF16)] * 2
    return pl.pallas_call(
        functools.partial(front_kernel, direct, batches),
        in_specs=[anywhere] + [vmem] * 9,
        out_specs=[anywhere] * 9,
        out_shape=[
            out((7 if direct else 1,) + (own.shape if direct else (8, 128)), BF16),
            out((groups, batches, ROWS, width), BF16),
            out((groups,) + flags.shape, flags.dtype),
            out((groups, batches, ROWS, width), BF16),
        ]
        + [out(*k) for k in kept],
        scratch_shapes=scratch
        + [pltpu.VMEM(*k) for k in kept]
        + [
            pltpu.SemaphoreType.DMA((32,)),
            pltpu.SemaphoreType.DMA((32,)),
            pltpu.SemaphoreType.DMA((24,)),
        ],
        compiler_params=pltpu.CompilerParams(
            vmem_limit_bytes=VMEM_LIMIT,
            has_side_effects=direct,
            collective_id=0 if direct else None,
        ),
        cost_estimate=pl.CostEstimate(
            flops=batches
            * (2 * ROWS * width * width * 4 + 8 * HEADS * ITEMS * ITEM_ROWS**2 * 128),
            bytes_accessed=60_000_000,
            transcendentals=batches * HEADS * ITEMS * ITEM_ROWS**2,
        ),
        name="front",
    )(own, tokens, cot, index, keep, flags, gain1, gain2, wqkv, wo)


def head_gradients(qkv_at, go_at, p_of, gqkv_ref, row0, hp, width, left):
    head_dim = width // HEADS
    pair = 2 * head_dim
    scaling = head_dim**-0.5
    at_q = pl.ds(pl.multiple_of(hp * pair, pair), pair)
    at_k = pl.ds(pl.multiple_of(width + hp * pair, pair), pair)
    at_v = pl.ds(pl.multiple_of(2 * width + hp * pair, pair), pair)
    for item in range(ITEMS):
        rows = slice(item * ITEM_ROWS, (item + 1) * ITEM_ROWS)
        out_rows = slice(row0 + rows.start, row0 + rows.stop)
        q, k, v = qkv_at(rows, at_q), qkv_at(rows, at_k), qkv_at(rows, at_v)
        go = go_at(rows, at_q)
        gq, gk, gv = [], [], []
        for half in range(2):
            mine = left if half == 0 else ~left
            p = p_of(item, half)
            pf = p.astype(F32)
            gp = dot(jnp.where(mine, go, 0), v, 1, 1)
            gs = (pf * (gp - jnp.sum(pf * gp, axis=-1, keepdims=True))).astype(BF16)
            gv.append(dot(p, go, 0, 0))
            gq.append(dot(gs, k, 1, 0))
            gk.append(dot(gs, q, 0, 0))
        gqkv_ref[out_rows, at_q] = (jnp.where(left, gq[0], gq[1]) * scaling).astype(BF16)
        gqkv_ref[out_rows, at_k] = (jnp.where(left, gk[0], gk[1]) * scaling).astype(BF16)
        gqkv_ref[out_rows, at_v] = jnp.where(left, gv[0], gv[1]).astype(BF16)


def add(*terms):
    total = terms[0].astype(F32)
    for term in terms[1:]:
        total = total + term.astype(F32)
    return total.astype(BF16)


def rows_at(start, size):
    return pl.ds(pl.multiple_of(start, 32), size)


class BlockSum:
    def __init__(self, copies, near_by, place, grads, gall, first, size, buffers):
        self.copies, self.near_by, self.grads, self.gall = copies, near_by, grads, gall
        self.r_core, self.r_one, self.r_two, self.r_z, self.final = buffers
        self.first, self.size = first, size
        core, xi, yi, self.zi = place
        self.half = grads.shape[0] // 2
        self.quarter, self.eighth = self.half // 2, self.half // 4
        self.row = core * self.half
        self.parts = []
        for part, (one, two) in enumerate(((xi, yi), (yi, xi))):
            cols = pl.ds(first + part * size // 2, size // 2)
            ways = (near_by.x, near_by.y) if part == 0 else (near_by.y, near_by.x)
            row_one = self.row + one * self.quarter
            row_two = row_one + two * self.eighth
            away_one = self.row + (1 - one) * self.quarter
            away_two = row_one + (1 - two) * self.eighth
            self.parts.append((cols, ways, row_one, row_two, away_one, away_two))

    def z_cols(self, part, z):
        chunk = self.size // 8
        return pl.ds(
            pl.multiple_of(self.first + part * self.size // 2 + z * chunk, 128), chunk
        )

    def start(self):
        away = self.grads.at[
            rows_at(self.half - self.row, self.half), pl.ds(self.first, self.size)
        ]
        self.core = self.copies.send(away, self.r_core, self.near_by.core)

    def take(self, row, size, cols, term):
        at = rows_at(row, size)
        self.grads[at, cols] = add(self.grads[at, cols], term)

    def one(self):
        self.core.wait_recv()
        for part in range(4):
            step = self.size // 4
            self.take(
                self.row, self.half, pl.ds(self.first + part * step, step),
                self.r_core[:, part * step : (part + 1) * step],
            )
        self.ones = [
            self.copies.send(
                self.grads.at[rows_at(away, self.quarter), cols], self.r_one.at[i], ways[0]
            )
            for i, (cols, ways, _, _, away, _) in enumerate(self.parts)
        ]

    def two(self):
        self.twos = []
        for i, (cols, ways, row, _, _, away) in enumerate(self.parts):
            self.ones[i].wait_recv()
            self.take(row, self.quarter, cols, self.r_one[i])
            self.twos.append(
                self.copies.send(
                    self.grads.at[rows_at(away, self.eighth), cols], self.r_two.at[i], ways[1]
                )
            )

    def three(self):
        self.threes = []
        for i, (cols, _, _, row, _, _) in enumerate(self.parts):
            self.twos[i].wait_recv()
            self.take(row, self.eighth, cols, self.r_two[i])
            self.threes.append(
                [
                    self.copies.send(
                        self.grads.at[
                            rows_at(row, self.eighth), self.z_cols(i, (self.zi + shift) % 4)
                        ],
                        self.r_z.at[i, shift - 1], self.near_by.z[shift],
                    )
                    for shift in (1, 2, 3)
                ]
            )

    def back_three(self):
        self.threes_back = []
        for i, (_, _, _, row, _, _) in enumerate(self.parts):
            for copy in self.threes[i]:
                copy.wait_recv()
            at, mine = rows_at(row, self.eighth), self.z_cols(i, self.zi)
            self.final[i] = add(
                self.grads[at, mine], self.r_z[i, 0], self.r_z[i, 1], self.r_z[i, 2]
            )
            place = self.gall.at[at, mine]
            own = self.copies.load(self.final.at[i], place)
            self.threes_back.append(
                (
                    own,
                    [
                        self.copies.send(self.final.at[i], place, self.near_by.z[shift])
                        for shift in (1, 2, 3)
                    ],
                )
            )

    def give(self, row, size, cols, to):
        block = self.gall.at[rows_at(row, size), cols]
        return self.copies.send(block, block, to)

    def back_two(self):
        self.twos_back = []
        for i, (cols, ways, _, row, _, _) in enumerate(self.parts):
            own, others = self.threes_back[i]
            own.wait()
            for copy in others:
                copy.wait_recv()
            self.twos_back.append(self.give(row, self.eighth, cols, ways[1]))

    def back_one(self):
        self.ones_back = []
        for i, (cols, ways, row, _, _, _) in enumerate(self.parts):
            self.twos_back[i].wait_recv()
            self.ones_back.append(self.give(row, self.quarter, cols, ways[0]))

    def back_core(self):
        self.cores_back = []
        for i, (cols, *_) in enumerate(self.parts):
            self.ones_back[i].wait_recv()
            self.cores_back.append(self.give(self.row, self.half, cols, self.near_by.core))

    def finish(self):
        for copy in self.cores_back:
            copy.wait_recv()


PAIRS = HEADS // 2
FIRST_PAIRS = 4


def grad_columns(width):
    pair = width // PAIRS
    cut = FIRST_PAIRS * pair
    return [
        [slice(part * width + low, part * width + high) for part in range(4)]
        for low, high in ((0, cut), (cut, width))
    ]


def back_kernel(batches, *refs):
    gb_parts, z_parts, gw, cot_in, index_ref, keep_ref, x_in, o_in, y_in, qkv_in, p_in = refs[:11]
    gain1_ref, gain2_ref, wqkv_in, wo_in = refs[11:15]
    result_out, tg_out, gall, wsum, gains_out, z_core, z_far, rs_z = refs[15:23]
    (
        wqkv, wo, x, o, y, cot, qkv, p, gb_own, gb_far, gb_core, gb_cross, gb_x,
        gy, ga, go, gqkv, grads, *sum_buffers,
        held, r_y, gsum, gain_in, tok, send_sem, recv_sem, local_sem, p_sem,
    ) = refs[23:]
    width = x.shape[1]
    head_dim = width // HEADS
    pair = 2 * head_dim
    length = cot.shape[0]
    dp, expert = lax.axis_index("dp"), lax.axis_index("expert")
    core, xi, yi, zi = expert % 2, expert // 2, dp % 2, dp // 2
    copies = Copies(send_sem, recv_sem, local_sem)
    near_by = Partners()
    near_by.greet()
    load, send = copies.load, copies.send

    crossed, nearer = [], []
    for m in range(batches):
        crossed.append(send(gb_parts.at[3, m], gb_cross.at[m], near_by.core))
        nearer.append(send(gb_parts.at[1, m], gb_core.at[m], near_by.core))
    order = ((6, 2), (2, 3), (4, 1), (0, 0))
    pieces = [send(gw.at[order[0][0] + 1], r_y.at[0], near_by.y)]
    far_loads = [load(gb_parts.at[2, m], gb_far.at[m]) for m in range(batches)]
    own_loads = [load(gb_parts.at[0, m], gb_own.at[m]) for m in range(batches)]
    first_loads = [load(y_in.at[0], y), load(cot_in.at[0], cot)]
    held_loads = [load(gw.at[order[i][0]], held.at[i]) for i in range(4)]
    late_loads = [load(o_in, o), load(wo_in, wo), load(qkv_in.at[0], qkv)]
    last_loads = [load(x_in, x), load(wqkv_in, wqkv)]
    def far_sum(m):
        far_loads[m].wait()
        crossed[m].wait_recv()
        gb_far[m] = add(gb_far[m], gb_cross[m])

    far_sum(0)
    along = [send(gb_far.at[0], gb_x.at[0], near_by.x)]
    z_crossed = [send(z_parts.at[3, m], z_core.at[1, m], near_by.core) for m in range(batches)]
    z_nearer = [send(z_parts.at[1, m], z_core.at[0, m], near_by.core) for m in range(batches)]
    for m in range(1, batches):
        far_sum(m)

    sent_z = []

    def reduce_piece(i):
        pieces[i].wait_recv()
        if i < 3:
            pieces.append(send(gw.at[order[i + 1][0] + 1], r_y.at[i + 1], near_by.y))
        held_loads[i].wait()
        held[i] = add(held[i], r_y[i])
        if i < 3:
            sent_z.append(send(held.at[i], rs_z.at[i], near_by.z[order[i][1]]))

    z_along = []

    def z_load(m):
        z_crossed[m].wait_recv()
        return [load(z_parts.at[2, m], gb_own.at[m]), load(z_core.at[1, m], gb_core.at[m])]

    def z_send(m, loads):
        for copy in loads:
            copy.wait()
        gb_cross[m] = add(gb_own[m], gb_core[m])
        z_along.append(send(gb_cross.at[m], z_far.at[m], near_by.x))

    columns = grad_columns(width)
    sizes = [sum(cols.stop - cols.start for cols in group) for group in columns]
    firsts = [0, sizes[0]]
    sums = [
        BlockSum(
            copies, near_by, (core, xi, yi, zi), grads, gall, firsts[i], sizes[i],
            sum_buffers[i * 5 : i * 5 + 5],
        )
        for i in range(2)
    ]

    def weight_gradients(group, parts):
        at = firsts[group]
        for part, cols in enumerate(columns[group]):
            size = cols.stop - cols.start
            if part in parts:
                if part == 3:
                    inner = slice(cols.start - 3 * width, cols.stop - 3 * width)
                    product = dot(o[...], ga[:, inner], 0, 0)
                else:
                    product = dot(a[...], gqkv[:, cols], 0, 0)
                grads[:, at : at + size] = product.astype(BF16)
            at += size

    left = lax.broadcasted_iota(jnp.int32, (ITEM_ROWS, pair), 1) < head_dim
    reduce_piece(0)
    for copy in first_loads + late_loads:
        copy.wait()
    gain2_grad = jnp.zeros((1, width), F32)
    items = [slice(i * ITEM_ROWS, (i + 1) * ITEM_ROWS) for i in range(ITEMS)]
    a = ga
    for m in range(batches):
        row0 = m * ROWS

        def p_load(hp, m=m):
            return pltpu.make_async_copy(
                p_in.at[m, :, pl.ds(2 * hp, 2)], p.at[hp % 2], p_sem.at[hp % 2]
            )

        p_load(0).start()
        own_loads[m].wait()
        nearer[m].wait_recv()
        along[m].wait_recv()
        if m + 1 < batches:
            along.append(send(gb_far.at[m + 1], gb_x.at[m + 1], near_by.x))
        for rows in items:
            at = slice(row0 + rows.start, row0 + rows.stop)
            gb = (
                gb_own[m, rows].astype(F32)
                + gb_core[m, rows].astype(F32)
                + gb_x[m, rows].astype(F32)
            )
            unit2, inverse2 = normalize_parts(y[rows])
            gain2_grad = gain2_grad + jnp.sum(gb * unit2, axis=0, keepdims=True)
            g = dot(pick_rows(index_ref, m, length, rows).astype(BF16), cot[...], 1, 0)
            gy_rows = g + normalize_back(gb * gain2_ref[...], unit2, inverse2)
            gy[at] = gy_rows
            ga[at] = gy_rows.astype(BF16)
            go[rows] = dot(ga[at], wo[...], 1, 1).astype(BF16)
        if m + 1 < batches:
            first_loads = [load(y_in.at[m + 1], y), load(cot_in.at[m + 1], cot)]
        z_loads = z_load(m)

        def heads(hp, carry, row0=row0, p_load=p_load):
            @pl.when(hp + 1 < PAIRS)
            def _():
                p_load(hp + 1).start()

            p_load(hp).wait()
            slot = hp % 2
            head_gradients(
                lambda rows, cols: qkv[rows, cols],
                lambda rows, cols: go[rows, cols],
                lambda item, half: p[slot, item, half],
                gqkv, row0, hp, width, left,
            )
            return carry

        if m + 1 < batches:
            lax.fori_loop(0, PAIRS, heads, 0)
            first_loads.append(load(qkv_in.at[m + 1], qkv))
            reduce_piece(1 + m)
            z_send(m, z_loads)
            for copy in first_loads:
                copy.wait()
        else:
            z_send(m, z_loads)
            lax.fori_loop(0, FIRST_PAIRS, heads, 0)
            reduce_piece(2)
            for copy in last_loads:
                copy.wait()
            weight_gradients(0, (3,))
            weight_gradients(1, (3,))
            for micro in range(batches):
                at = slice(micro * ROWS, (micro + 1) * ROWS)
                unit, _ = normalize_parts(x[at].astype(F32))
                a[at] = (unit * gain1_ref[...]).astype(BF16)
            weight_gradients(0, (0, 1, 2))
            sums[0].start()
            lax.fori_loop(FIRST_PAIRS, PAIRS, heads, 0)
    sums[0].one()
    weight_gradients(1, (0, 1, 2))
    sums[1].start()

    gain1_grad = jnp.zeros((1, width), F32)
    token_stores = []
    between = [sums[0].two, sums[1].one, sums[0].three, sums[1].two]
    for m in range(batches):
        for rows in items:
            at = slice(m * ROWS + rows.start, m * ROWS + rows.stop)
            unit, inverse = normalize_parts(x[at].astype(F32))
            gnorm = dot(gqkv[at], wqkv[...], 1, 1)
            gain1_grad = gain1_grad + jnp.sum(gnorm * unit, axis=0, keepdims=True)
            go[rows] = (gy[at] + normalize_back(gnorm * gain1_ref[...], unit, inverse)).astype(BF16)
            if between:
                between.pop(0)()
        tok[m] = dot(pick_rows(index_ref, m, length).astype(BF16), go[...], 0, 0).astype(BF16)
        token_stores.append(load(tok.at[m], tg_out.at[m]))
    gsum[0] = jnp.concatenate([gain1_grad, gain2_grad, jnp.zeros((6, width), F32)], axis=0)
    gain_partners = [near_by.core, near_by.x, near_by.y, near_by.z_pair, near_by.z[2]]
    gain_sent = [send(gsum.at[0], gain_in.at[0], gain_partners[0])]

    def gain_step():
        at = len(gain_sent)
        gain_sent[-1].wait_recv()
        gsum[at] = gsum[at - 1] + gain_in[at - 1]
        if at < len(gain_partners):
            gain_sent.append(send(gsum.at[at], gain_in.at[at], gain_partners[at]))

    reduce_piece(3)
    sums[1].three()
    gain_step()

    for m in range(batches):
        z_nearer[m].wait_recv()
        z_along[m].wait_recv()
        loads = [
            load(z_parts.at[0, m], gb_own.at[m]),
            load(z_core.at[0, m], gb_core.at[m]),
            load(z_far.at[m], gb_x.at[m]),
            load(y_in.at[m], y),
        ]
        for copy in loads:
            copy.wait()
        for rows in items:
            chosen = pick_rows(index_ref, m, length, rows)
            keep = jnp.sum(jnp.where(chosen, keep_ref[m], 0.0), axis=1, keepdims=True)
            z = (
                gb_own[m, rows].astype(F32)
                + gb_core[m, rows].astype(F32)
                + gb_x[m, rows].astype(F32)
            )
            go[rows] = (y[rows] + jnp.where(keep > 0, z, 0.0)).astype(BF16)
        token_stores[m].wait()
        tok[m] = dot(pick_rows(index_ref, m, length).astype(BF16), go[...], 0, 0).astype(BF16)
        copies.keep(tok.at[m], result_out.at[m])
        if m == 0:
            sums[0].back_three()
        gain_step()
    sums[1].back_three()

    z_loads = []
    for i in range(3):
        sent_z[i].wait_recv()
        z_loads.append(load(rs_z.at[i], r_y.at[i]))
    for copy in z_loads:
        copy.wait()
    held[3] = add(held[3], r_y[0], r_y[1], r_y[2])
    copies.keep(held.at[3], wsum.at[expert])
    join_far = send(held.at[3], wsum.at[expert], near_by.x)
    join_near = send(held.at[3], wsum.at[expert], near_by.core)
    gain_step()
    for block_sum in sums:
        block_sum.back_two()
    gain_step()
    copies.keep(gsum.at[len(gain_partners)], gains_out)
    for block_sum in sums:
        block_sum.back_one()
    join_far.wait_recv()
    opposite = (expert + 2) % 4
    join_last = send(wsum.at[opposite], wsum.at[opposite], near_by.core)
    for block_sum in sums:
        block_sum.back_core()
    for block_sum in sums:
        block_sum.finish()
    for copy in (join_near, join_last):
        copy.wait_recv()
    copies.finish()


def back(gb_parts, z_parts, gw, cot, index, keep, x, o, y, qkv, p, gain1, gain2, wqkv, wo):
    batches, rows, width = x.shape
    length = cot.shape[1]
    out = jax.ShapeDtypeStruct
    vmem = pl.BlockSpec(memory_space=pltpu.VMEM)
    anywhere = pl.BlockSpec(memory_space=pl.ANY)
    piece = gw.shape[1:]
    both = batches * rows
    half = width // 2
    tokens_shape = (batches, rows, width)
    slots = [tokens_shape] * 5
    scratch = [
        ((width, 3 * width), BF16),
        ((width, width), BF16),
        ((both, width), BF16),
        ((both, width), BF16),
        ((rows, width), F32),
        ((length, width), BF16),
        ((rows, 3 * width), BF16),
        ((2, ITEMS, 2, ITEM_ROWS, ITEM_ROWS), BF16),
        *[(slot, BF16) for slot in slots],
        ((both, width), F32),
        ((both, width), BF16),
        ((rows, width), BF16),
        ((both, 3 * width), BF16),
        ((width, 4 * width), BF16),
        *[
            (shape, BF16)
            for size in (4 * FIRST_PAIRS * width // PAIRS, 4 * (PAIRS - FIRST_PAIRS) * width // PAIRS)
            for shape in (
                (half, size),
                (2, half // 2, size // 2),
                (2, half // 4, size // 2),
                (2, 3, half // 4, size // 8),
                (2, half // 4, size // 8),
            )
        ],
        ((4,) + piece, BF16),
        ((4,) + piece, BF16),
        ((6, 8, width), F32),
        ((5, 8, width), F32),
        ((batches, length, width), BF16),
    ]
    return pl.pallas_call(
        functools.partial(back_kernel, batches),
        in_specs=[anywhere] * 4 + [vmem] * 2 + [anywhere] * 5 + [vmem] * 2 + [anywhere] * 2,
        out_specs=[anywhere] * 8,
        out_shape=[
            out(cot.shape, BF16),
            out(cot.shape, BF16),
            out((width, 4 * width), BF16),
            out((4,) + piece, BF16),
            out((8, width), F32),
            out((2,) + tokens_shape, BF16),
            out(tokens_shape, BF16),
            out((3,) + piece, BF16),
        ],
        scratch_shapes=[pltpu.VMEM(*k) for k in scratch]
        + [
            pltpu.SemaphoreType.DMA((80,)),
            pltpu.SemaphoreType.DMA((80,)),
            pltpu.SemaphoreType.DMA((64,)),
            pltpu.SemaphoreType.DMA((2,)),
        ],
        compiler_params=pltpu.CompilerParams(
            vmem_limit_bytes=VMEM_LIMIT, has_side_effects=True, collective_id=1
        ),
        cost_estimate=pl.CostEstimate(
            flops=batches
            * (2 * rows * width * width * 8 + 16 * HEADS * ITEMS * ITEM_ROWS**2 * 128),
            bytes_accessed=80_000_000,
            transcendentals=0,
        ),
        name="back",
    )(
        gb_parts, z_parts, gw, cot, index, keep,
        x.reshape(both, width), o.reshape(both, width), y, qkv, p, gain1, gain2, wqkv, wo,
    )


def attention_backward_kernel(n_parts, n_carry, *refs):
    parts = refs[:n_parts]
    (cot_ref, x_ref, y_ref, qkv_ref, p_ref, o_ref, gain1_ref, gain2_ref, wqkv_ref, wo_ref) = refs[
        n_parts : n_parts + 10
    ]
    carried = refs[n_parts + 10 : n_parts + 10 + n_carry]
    tg_ref, gwqkv_ref, gwo_ref, ggain_ref, gmix_ref, gqkv_ref = refs[n_parts + 10 + n_carry :]
    width = x_ref.shape[1]
    head_dim = width // HEADS
    gb = parts[0][...].astype(F32)
    for part in parts[1:]:
        gb = gb + part[...].astype(F32)
    unit2, inverse2 = normalize_parts(y_ref[...])
    gain2_grad = jnp.sum(gb * unit2, axis=0, keepdims=True)
    gy = cot_ref[...].astype(F32) + normalize_back(gb * gain2_ref[...], unit2, inverse2)
    ga = gy.astype(BF16)
    gwo = dot(o_ref[...], ga, 0, 0)
    if n_carry:
        gwo = gwo + carried[1][...]
    gwo_ref[...] = gwo
    gmix_ref[...] = dot(ga, wo_ref[...], 1, 1).astype(BF16)
    pair = 2 * head_dim
    left = lax.broadcasted_iota(jnp.int32, (ITEM_ROWS, pair), 1) < head_dim

    def heads(hp, carry):
        head_gradients(
            lambda rows, cols: qkv_ref[rows, cols],
            lambda rows, cols: gmix_ref[rows, cols],
            lambda item, half: p_ref[item, hp * 2 + half],
            gqkv_ref, 0, hp, width, left,
        )
        return carry

    lax.fori_loop(0, HEADS // 2, heads, 0)
    unit, inverse = normalize_parts(x_ref[...].astype(F32))
    a = (unit * gain1_ref[...]).astype(BF16)
    for part in range(3):
        cols = slice(part * width, (part + 1) * width)
        gw = dot(a, gqkv_ref[:, cols], 0, 0)
        if n_carry:
            gw = gw + carried[0][:, cols]
        gwqkv_ref[:, cols] = gw
    gnorm = dot(gqkv_ref[...], wqkv_ref[...], 1, 1)
    gain1_grad = jnp.sum(gnorm * unit, axis=0, keepdims=True)
    gains = jnp.concatenate([gain1_grad, gain2_grad, jnp.zeros((6, width), F32)], axis=0)
    if n_carry:
        gains = gains + carried[2][...]
    ggain_ref[...] = gains
    tg_ref[...] = (gy + normalize_back(gnorm * gain1_ref[...], unit, inverse)).astype(BF16)


def attention_backward(parts, cot, x, y, qkv, p, o, gain1, gain2, wqkv, wo, carried):
    rows, width = x.shape
    out = jax.ShapeDtypeStruct
    return pl.pallas_call(
        functools.partial(attention_backward_kernel, len(parts), len(carried)),
        out_shape=(
            out((rows, width), BF16),
            out((width, 3 * width), F32),
            out((width, width), F32),
            out((8, width), F32),
        ),
        scratch_shapes=[pltpu.VMEM((rows, width), BF16), pltpu.VMEM((rows, 3 * width), BF16)],
        compiler_params=pltpu.CompilerParams(vmem_limit_bytes=VMEM_LIMIT),
        cost_estimate=pl.CostEstimate(
            flops=2 * rows * width * width * 8 + 16 * HEADS * ITEMS * ITEM_ROWS**2 * 128,
            bytes_accessed=30_000_000,
            transcendentals=0,
        ),
        name="attention_backward",
    )(*parts, cot, x, y, qkv, p, o, gain1, gain2, wqkv, wo, *carried)


def expert_kernel(groups, batches, pieces, *refs):
    flags, own_ref, more_ref, b_in, g_in, z_out, gb_out, gw_out = refs[:8]
    rows_b, rows_g, w, grads, in_sem, w_sem, out_sem, gw_sem = refs[8:]
    part = own_ref.shape[2]

    def rounded(rows):
        return (rows + TILE - 1) // TILE * TILE

    merged = [
        flags[g, 0, micro * ITEMS + item]
        for g in range(groups)
        for micro in range(batches)
        for item in range(ITEMS)
    ]
    n_merged = sum(merged)
    n_plain = len(merged) - n_merged
    sizes = [n_plain * IMAGE_ROWS, n_plain * CAPTION, n_merged * ITEM_ROWS]
    starts = [0, rounded(sizes[0]), rounded(sizes[0]) + rounded(sizes[1])]
    ends = [start + rounded(size) for start, size in zip(starts, sizes)]
    blocks = []
    plain, joined = 0, 0
    for flat, flag in enumerate(merged):
        g, micro, item = flat // (batches * ITEMS), flat // ITEMS % batches, flat % ITEMS
        base = item * ITEM_ROWS
        image = jnp.where(flag == 1, starts[2] + joined * ITEM_ROWS, plain * IMAGE_ROWS)
        caption = jnp.where(
            flag == 1, image + IMAGE_ROWS, starts[1] + plain * CAPTION
        )
        blocks.append((g, micro, base, IMAGE_ROWS, image, flag, 0))
        blocks.append((g, micro, base + IMAGE_ROWS, CAPTION, caption, flag, 1))
        plain, joined = plain + 1 - flag, joined + flag

    def copy_of(which, number, outward):
        g, micro, base, size, at, _, _ = blocks[number]
        held = (rows_b, rows_g)[which].at[pl.ds(pl.multiple_of(at, 16), size)]
        if outward:
            far = (gb_out, z_out)[which].at[g, micro, pl.ds(base, size)]
            return pltpu.make_async_copy(held, far, out_sem.at[which, number])
        far = (b_in, g_in)[which].at[g, micro, pl.ds(base, size)]
        return pltpu.make_async_copy(far, held, in_sem.at[which, number])

    def of_expert(expert, act):
        for number, (_, _, _, _, _, flag, kind) in enumerate(blocks):
            if expert == 2 or kind == expert:
                @pl.when(flag == (1 if expert == 2 else 0))
                def _(number=number):
                    for which in range(2):
                        act(which, number)

    def weight_copy(k, i):
        piece = own_ref if i == 0 else more_ref.at[i - 1]
        return pltpu.make_async_copy(
            piece.at[k], w.at[k, :, pl.ds(i * part, part), :], w_sem.at[k, i]
        )

    for k in range(3):
        tail = pl.multiple_of(jnp.maximum(ends[k] - TILE, 0), TILE)
        rows_b[pl.ds(tail, TILE), :] = jnp.zeros((TILE, rows_b.shape[1]), BF16)
        rows_g[pl.ds(tail, TILE), :] = jnp.zeros((TILE, rows_g.shape[1]), BF16)
    for k in range(3):
        of_expert(k, lambda which, number: copy_of(which, number, False).start())
        for i in range(pieces):
            weight_copy(k, i).start()

    for k in range(3):
        grads[...] = jnp.zeros(grads.shape, F32)
        of_expert(k, lambda which, number: copy_of(which, number, False).wait())
        for i in range(pieces):
            weight_copy(k, i).wait()

        def tile(t, carry, k=k):
            at = pl.ds(pl.multiple_of(t * TILE, TILE), TILE)
            b, gz = rows_b[at, :], rows_g[at, :]
            u, slope = gelu_and_slope(dot(b, w[k, 0], 1, 1))
            gh = (dot(gz, w[k, 1], 1, 1) * slope).astype(BF16)
            u = u.astype(BF16)
            z, gb = dot(u, w[k, 1], 1, 0), dot(gh, w[k, 0], 1, 0)
            grads[0] += dot(gh, b, 0, 0)
            grads[1] += dot(u, gz, 0, 0)
            rows_b[at, :] = gb.astype(BF16)
            rows_g[at, :] = z.astype(BF16)
            return carry

        lax.fori_loop(starts[k] // TILE, ends[k] // TILE, tile, 0)
        of_expert(k, lambda which, number: copy_of(which, number, True).start())
        w[k] = grads[...].astype(BF16)
        for i in range(pieces):
            pltpu.make_async_copy(
                w.at[k, :, pl.ds(i * part, part), :], gw_out.at[i, k], gw_sem.at[k, i]
            ).start()
    for number in range(len(blocks)):
        for which in range(2):
            copy_of(which, number, True).wait()
    for k in range(3):
        for i in range(pieces):
            pltpu.make_async_copy(
                w.at[k, :, pl.ds(i * part, part), :], gw_out.at[i, k], gw_sem.at[k, i]
            ).wait()


def experts(flags, own, more, b_groups, g_groups):
    groups, batches, rows, width = b_groups.shape
    part = own.shape[2]
    pieces = 1 + (more.shape[0] if more.ndim == 5 else 0)
    hidden = part * pieces
    count = groups * batches * ITEMS
    capacity = (count * ITEM_ROWS // TILE + 4) * TILE
    out = jax.ShapeDtypeStruct
    anywhere = pl.BlockSpec(memory_space=pl.ANY)
    return pl.pallas_call(
        functools.partial(expert_kernel, groups, batches, pieces),
        in_specs=[pl.BlockSpec(memory_space=pltpu.SMEM)] + [anywhere] * 4,
        out_specs=[anywhere] * 3,
        out_shape=[out(b_groups.shape, BF16)] * 2 + [out((pieces,) + own.shape, BF16)],
        scratch_shapes=[
            pltpu.VMEM((capacity, width), BF16),
            pltpu.VMEM((capacity, width), BF16),
            pltpu.VMEM((3, 2, hidden, width), BF16),
            pltpu.VMEM((2, hidden, width), F32),
            pltpu.SemaphoreType.DMA((2, 2 * count)),
            pltpu.SemaphoreType.DMA((3, pieces)),
            pltpu.SemaphoreType.DMA((2, 2 * count)),
            pltpu.SemaphoreType.DMA((3, pieces)),
        ],
        compiler_params=pltpu.CompilerParams(vmem_limit_bytes=VMEM_LIMIT),
        cost_estimate=pl.CostEstimate(
            flops=2 * 6 * count * ITEM_ROWS * width * hidden,
            bytes_accessed=45_000_000,
            transcendentals=count * ITEM_ROWS * hidden,
        ),
        name="experts",
    )(flags, own, more, b_groups, g_groups)


def rows_of_items(first):
    row = jnp.arange(ROWS, dtype=jnp.int32)
    item, inside = row // ITEM_ROWS, row % ITEM_ROWS
    caption = jnp.where(first, item, 1 - item)
    return jnp.where(
        inside < PATCHES,
        item * PATCHES + inside,
        jnp.where(
            inside < IMAGE_ROWS,
            -1,
            ITEMS * PATCHES + caption * CAPTION + inside - IMAGE_ROWS,
        ),
    )


def to_items(rows, first):
    images = ITEMS * PATCHES
    one, two = rows[images : images + CAPTION], rows[images + CAPTION :]
    gap = jnp.zeros((IMAGE_ROWS - PATCHES,) + rows.shape[1:], rows.dtype)
    return jnp.concatenate(
        [
            rows[:PATCHES],
            gap,
            jnp.where(first, one, two),
            rows[PATCHES:images],
            gap,
            jnp.where(first, two, one),
        ],
        axis=0,
    )


def from_items(rows, first):
    one, two = rows[IMAGE_ROWS:ITEM_ROWS], rows[ITEM_ROWS + IMAGE_ROWS :]
    return jnp.concatenate(
        [
            rows[:PATCHES],
            rows[ITEM_ROWS : ITEM_ROWS + PATCHES],
            jnp.where(first, one, two),
            jnp.where(first, two, one),
        ],
        axis=0,
    )


def kept_tokens(routing, priority, hosts, capacity):
    length = routing.shape[0]
    index = jnp.arange(length, dtype=jnp.int32)
    position = jnp.sum(
        jnp.where(priority[None, :] == index[:, None], index[None, :], 0), axis=1
    )
    ahead = (routing[None, :] == routing[:, None]) & (position[None, :] < position[:, None])
    rank = jnp.sum(ahead.astype(jnp.int32), axis=1)
    return rank < capacity * ((hosts - routing + 2) // 3)


class Links:
    def __init__(self):
        self.hosts = lax.axis_size("expert")
        self.dp = lax.axis_size("dp")
        self.direct = self.hosts == 4 and self.dp == 8
        self.me = lax.axis_index("expert")

    def flip(self, v, bit):
        return lax.ppermute(v, "expert", [(i, i ^ bit) for i in range(4)])

    def across_y(self, v):
        return lax.ppermute(v, "dp", [(i, i ^ 1) for i in range(8)])

    def along_z(self, v, shift):
        return lax.ppermute(v, "dp", [(i, (i + 2 * shift) % 8) for i in range(8)])

    def gather_tokens(self, v):
        if not self.direct:
            return list(lax.all_gather(v, "expert"))
        near, far = self.flip(v, 1), self.flip(v, 2)
        return [v, near, far, self.flip(far, 1)]

    def reduce_tokens(self, parts):
        if not self.direct:
            return [lax.psum_scatter(jnp.stack(parts), "expert", scatter_dimension=0)]
        far = (parts[2].astype(F32) + self.flip(parts[3], 1).astype(F32)).astype(BF16)
        return [parts[0], self.flip(parts[1], 1), self.flip(far, 2)]

    def reduce_weights(self, pieces):
        if not self.direct:
            return lax.psum_scatter(pieces[0], "dp", scatter_dimension=2, tiled=True)
        total = None
        for at, shift in enumerate((0, 1, 3, 2)):
            piece = pieces[2 * at].astype(F32) + self.across_y(pieces[2 * at + 1]).astype(F32)
            if shift:
                piece = self.along_z(piece.astype(BF16), -shift).astype(F32)
            total = piece if total is None else total + piece
        return total.astype(BF16)

    def join_hidden(self, v):
        if not self.direct:
            return lax.all_gather(v, "expert", axis=2, tiled=True)
        stacked = jnp.stack(self.gather_tokens(v))
        return jnp.concatenate(
            [
                lax.dynamic_index_in_dim(stacked, i ^ self.me, 0, keepdims=False)
                for i in range(4)
            ],
            axis=2,
        )


def shards(
    tokens,
    cotangent,
    item_group,
    routes,
    slot_order,
    attn_gain,
    ffn_gain,
    qkv_weight,
    out_weight,
    expert_in,
    expert_out,
):
    links = Links()
    hosts, me = links.hosts, links.me
    batches, length, width = tokens.shape
    capacity = 2 * length // hosts
    shard = expert_in.shape[2]
    part = shard // hosts
    gain1, gain2 = attn_gain[None, :], ffn_gain[None, :]

    own = jnp.stack(
        [
            jnp.swapaxes(lax.dynamic_slice_in_dim(expert_in, me * part, part, 2), 1, 2),
            lax.dynamic_slice_in_dim(expert_out, me * part, part, 1),
        ],
        axis=1,
    )
    first = item_group[:, ITEMS * PATCHES] == 0
    merged = (routes[:, 0 : ITEMS * PATCHES : PATCHES] == 2).astype(jnp.int32)
    flags = jnp.broadcast_to(
        jnp.pad(merged.reshape(1, -1), ((0, 0), (0, 128 - batches * ITEMS))), (8, 128)
    )
    kept = jnp.stack(
        [kept_tokens(routes[m], slot_order[m, 0], hosts, capacity) for m in range(batches)]
    )
    index = jnp.stack([rows_of_items(first[m]) for m in range(batches)])[:, :, None]
    w_all, gz_groups, flag_groups, b_groups, x_all, qkv_all, p_all, o_all, y_all = front(
        links.direct, own, tokens, cotangent, index, kept.astype(F32)[:, None, :], flags,
        gain1, gain2, qkv_weight, out_weight,
    )
    if not links.direct:
        own = lax.all_gather(own, "dp", axis=2, tiled=True)
        gz_groups, flag_groups, b_groups = [
            lax.all_gather(v[0], "expert") for v in (gz_groups, flag_groups, b_groups)
        ]
    z_parts, gb_parts, gw_pieces = experts(flag_groups, own, w_all, b_groups, gz_groups)
    if links.direct:
        result, token_grad, gall, wsum, gains, *_ = back(
            gb_parts, z_parts, gw_pieces, cotangent, index, kept.astype(F32)[:, None, :],
            x_all, o_all, y_all, qkv_all, p_all, gain1, gain2, qkv_weight, out_weight,
        )
        shape = (3, hosts * part, width)
        wsum = wsum.astype(F32)
        blocks = []
        for i in range(4):
            at = 0
            pieces = []
            for group in grad_columns(width):
                size = group[i].stop - group[i].start
                pieces.append(gall[:, at + i * size : at + (i + 1) * size].astype(F32))
                at += 4 * size
            blocks.append(jnp.concatenate(pieces, axis=1))
        return (
            result,
            token_grad,
            gains[0],
            gains[1],
            jnp.concatenate(blocks[:3], axis=1),
            blocks[3],
            jnp.transpose(wsum[:, :, 0], (1, 3, 0, 2)).reshape(3, width, hosts * part),
            jnp.transpose(wsum[:, :, 1], (1, 0, 2, 3)).reshape(shape),
        )
    cot_items = [to_items(cotangent[m], first[m]) for m in range(batches)]
    gb_terms = links.reduce_tokens(gb_parts)
    z_terms = links.reduce_tokens(z_parts)
    sums = links.join_hidden(links.reduce_weights(gw_pieces)).astype(F32)

    results, token_grads, carried = [], [], ()
    for m in range(batches):
        x, qkv, p, o, y = x_all[m], qkv_all[m], p_all[m], o_all[m], y_all[m]
        at = m
        tg, *carried = attention_backward(
            [t[at] for t in gb_terms],
            cot_items[m], x, y, qkv, p, o, gain1, gain2, qkv_weight, out_weight,
            tuple(carried),
        )
        token_grads.append(from_items(tg, first[m]))
        z = z_terms[0][at].astype(F32)
        for term in z_terms[1:]:
            z = z + term[at].astype(F32)
        branch = jnp.where(kept[m][:, None], from_items(z, first[m]), 0.0)
        results.append((from_items(y, first[m]) + branch).astype(BF16))
    gw_qkv, gw_out, gains = carried
    packed = jnp.concatenate(
        [
            jnp.concatenate([gw_qkv, gw_out], axis=1),
            jnp.pad(gains[:2].reshape(1, 2 * width), ((0, 7), (0, 2 * width))),
        ],
        axis=0,
    ).astype(BF16)
    packed = lax.psum(packed, ("dp", "expert")).astype(F32)
    return (
        jnp.stack(results),
        jnp.stack(token_grads),
        packed[width, :width],
        packed[width, width : 2 * width],
        packed[:width, : 3 * width],
        packed[:width, 3 * width :],
        jnp.swapaxes(sums[:, 0], 1, 2),
        sums[:, 1],
    )


def solution(mesh):
    in_specs = (
        P(None, ("dp", "expert"), None),
        P(None, ("dp", "expert"), None),
        P(None, ("dp", "expert")),
        P(None, ("dp", "expert")),
        P(None, ("dp", "expert"), None),
        P(),
        P(),
        P(),
        P(),
        P(None, None, "dp"),
        P(None, "dp", None),
    )
    out_specs = (
        P(None, ("dp", "expert"), None),
        P(None, ("dp", "expert"), None),
        P(),
        P(),
        P(),
        P(),
        P(None, None, "dp"),
        P(None, "dp", None),
    )
    return jax.shard_map(shards, mesh=mesh, in_specs=in_specs, out_specs=out_specs, check_vma=False)
```

```python
import functools

import jax
import jax.numpy as jnp
from jax import lax
from jax.experimental import pallas as pl
from jax.experimental.pallas import tpu as pltpu
from jax.sharding import PartitionSpec as P

HEADS = 12
EPSILON = 1e-05
PATCHES = 197
CAPTION = 64
ITEMS = 2
IMAGE_ROWS = 208
ITEM_ROWS = IMAGE_ROWS + CAPTION
ROWS = ITEMS * ITEM_ROWS
FLAG_ROWS = 16
TILE = 256
VMEM_LIMIT = 60 * 1024 * 1024
F32 = jnp.float32
BF16 = jnp.bfloat16


def dot(a, b, a_dim, b_dim):
    return lax.dot_general(
        a, b, (((a_dim,), (b_dim,)), ((), ())), preferred_element_type=F32
    )


def normalize_parts(v):
    centred = v - jnp.mean(v, axis=-1, keepdims=True)
    inverse = lax.rsqrt(jnp.mean(centred * centred, axis=-1, keepdims=True) + EPSILON)
    return centred * inverse, inverse


def normalize_back(grad_unit, unit_rows, inverse):
    return inverse * (
        grad_unit
        - jnp.mean(grad_unit, axis=-1, keepdims=True)
        - unit_rows * jnp.mean(grad_unit * unit_rows, axis=-1, keepdims=True)
    )


def gelu_and_slope(h):
    bell = jnp.exp(-0.5 * h * h)
    t = 1.0 / (1.0 + (0.3275911 * 0.7071067811865476) * jnp.abs(h))
    poly = t * (
        0.254829592
        + t * (-0.284496736 + t * (1.421413741 + t * (-1.453152027 + t * 1.061405429)))
    )
    below = 0.5 * poly * bell
    phi = jnp.where(h > 0, 1.0 - below, below)
    return h * phi, phi + h * (0.3989422804014327 * bell)


class Partners:
    def __init__(self):
        dp, expert = lax.axis_index("dp"), lax.axis_index("expert")
        self.core = (dp, expert + 1 - 2 * (expert % 2))
        self.x = (dp, (expert + 2) % 4)
        self.y = (dp + 1 - 2 * (dp % 2), expert)
        self.z = {shift: ((dp + 2 * shift) % 8, expert) for shift in (1, 2, 3)}
        self.z_pair = (dp + 2 - 4 * (dp // 2 % 2), expert)

    def greet(self):
        barrier = pltpu.get_barrier_semaphore()
        everyone = [self.core, self.x, self.y, self.z[1], self.z[2], self.z[3]]
        for other in everyone:
            pl.semaphore_signal(
                barrier, inc=1, device_id=other, device_id_type=pl.DeviceIdType.MESH
            )
        pl.semaphore_wait(barrier, len(everyone))


class Copies:
    def __init__(self, send_sem, recv_sem, local_sem):
        self.send_sem, self.recv_sem, self.local_sem = send_sem, recv_sem, local_sem
        self.sent, self.kept, self.sends, self.locals = [], [], 0, 0

    def send(self, src, dst, device):
        at = self.sends
        self.sends += 1
        copy = pltpu.make_async_remote_copy(
            src_ref=src,
            dst_ref=dst,
            send_sem=self.send_sem.at[at],
            recv_sem=self.recv_sem.at[at],
            device_id=device,
            device_id_type=pl.DeviceIdType.MESH,
        )
        copy.start()
        self.sent.append(copy)
        return copy

    def keep(self, src, dst):
        copy = self.load(src, dst)
        self.kept.append(copy)
        return copy

    def load(self, src, dst):
        copy = pltpu.make_async_copy(src, dst, self.local_sem.at[self.locals])
        self.locals += 1
        copy.start()
        return copy

    def settle(self, done):
        for copy in done:
            copy.wait_send()
        self.sent = [copy for copy in self.sent if all(copy is not other for other in done)]

    def finish(self):
        for copy in self.sent:
            copy.wait_send()
        for copy in self.kept:
            copy.wait()


def pick_rows(index_ref, m, length, rows=slice(0, ROWS)):
    token = lax.broadcasted_iota(jnp.int32, (rows.stop - rows.start, length), 1)
    return index_ref[m, rows] == token


def front_kernel(direct, batches, *refs):
    (own_ref, tokens_ref, cot_ref, index_ref, keep_ref, flags_ref, gain1_ref, gain2_ref) = refs[:8]
    wqkv_ref, wo_ref, w_all, gz_all, flags_all, b_all, x_out, qkv_out, p_out, o_out, y_out = refs[
        8:19
    ]
    gz_scr, b_scr, x_scr, qkv_scr, p_scr, o_scr, y_scr, send_sem, recv_sem, local_sem = refs[19:]
    length, width = tokens_ref.shape[1:]
    head_dim = width // HEADS
    pair = 2 * head_dim
    copies = Copies(send_sem, recv_sem, local_sem)

    def spread(src, slots):
        copies.keep(src, slots(0))
        if not direct:
            return None
        near = copies.send(src, slots(1), near_by.core)
        return near, copies.send(src, slots(2), near_by.x)

    def pass_on(pair_of, slots):
        near, far = pair_of
        far.wait_recv()
        return near, copies.send(slots(2), slots(3), near_by.core)

    if direct:
        near_by = Partners()
        near_by.greet()
        over_y = [copies.send(own_ref, w_all.at[0], near_by.y)]
        along = [[], [], []]

        def z_half(i):
            along[0].append(copies.send(own_ref.at[:, i], w_all.at[1, :, i], near_by.z_pair))
            along[1].append(copies.send(own_ref.at[:, i], w_all.at[3, :, i], near_by.z[2]))

        def z_pass(i):
            for k in (1, 0):
                along[k][i].wait_recv()
                if k == 1:
                    along[2].append(
                        copies.send(w_all.at[3, :, i], w_all.at[5, :, i], near_by.z_pair)
                    )
                at = 2 * k + 1
                over_y.append(copies.send(w_all.at[at, :, i], w_all.at[at + 1, :, i], near_by.y))

        def z_last(i):
            along[2][i].wait_recv()
            over_y.append(copies.send(w_all.at[5, :, i], w_all.at[6, :, i], near_by.y))

        z_half(0)
    flags = spread(flags_ref, lambda i: flags_all.at[i])

    for m in range(batches):
        chosen = pick_rows(index_ref, m, length) & (keep_ref[m] > 0)
        gz_scr[m] = dot(chosen.astype(BF16), cot_ref[m], 1, 0).astype(BF16)
    gz = spread(gz_scr, lambda i: gz_all.at[i])

    left = lax.broadcasted_iota(jnp.int32, (ITEM_ROWS, pair), 1) < head_dim
    key = lax.broadcasted_iota(jnp.int32, (1, ITEM_ROWS), 1)
    bias = jnp.where((key >= PATCHES) & (key < IMAGE_ROWS), -1e30, 0.0).astype(F32)
    b_sent = []
    for m in range(batches):
        xb = dot(pick_rows(index_ref, m, length).astype(BF16), tokens_ref[m], 1, 0)
        x_scr[m] = xb.astype(BF16)
        unit, _ = normalize_parts(xb)
        a = (unit * gain1_ref[...]).astype(BF16)
        for part in range(3):
            cols = slice(part * width, (part + 1) * width)
            qkv_scr[m, :, cols] = dot(a, wqkv_ref[:, cols], 1, 0).astype(BF16)

        def heads(hp, carry, m=m):
            at_q = pl.ds(pl.multiple_of(hp * pair, pair), pair)
            at_k = pl.ds(pl.multiple_of(width + hp * pair, pair), pair)
            at_v = pl.ds(pl.multiple_of(2 * width + hp * pair, pair), pair)
            for item in range(ITEMS):
                rows = slice(item * ITEM_ROWS, (item + 1) * ITEM_ROWS)
                q, k, v = qkv_scr[m, rows, at_q], qkv_scr[m, rows, at_k], qkv_scr[m, rows, at_v]
                outs = []
                for half in range(2):
                    mine = left if half == 0 else ~left
                    s = dot(jnp.where(mine, q, 0), k, 1, 1) * (head_dim**-0.5) + bias
                    e = jnp.exp(s - jnp.max(s, axis=-1, keepdims=True))
                    p = (e * (1.0 / jnp.sum(e, axis=-1, keepdims=True))).astype(BF16)
                    p_scr[m, item, hp * 2 + half] = p
                    outs.append(dot(p, v, 1, 0))
                o_scr[m, rows, at_q] = jnp.where(left, outs[0], outs[1]).astype(BF16)
            return carry

        lax.fori_loop(0, HEADS // 2, heads, 0)
        y = x_scr[m].astype(F32) + dot(o_scr[m], wo_ref[...], 1, 0)
        y_scr[m] = y
        unit2, _ = normalize_parts(y)
        b_scr[m] = (unit2 * gain2_ref[...]).astype(BF16)
        b_sent.append(spread(b_scr.at[m], lambda i, m=m: b_all.at[i, m]))
        for scr, out in (
            (x_scr, x_out), (qkv_scr, qkv_out), (p_scr, p_out), (o_scr, o_out), (y_scr, y_out)
        ):
            copies.keep(scr.at[m], out.at[m])
        if direct and m == 0:
            z_pass(0)
            z_half(1)
            flags = pass_on(flags, lambda i: flags_all.at[i])

    if direct:
        z_pass(1)
        z_last(0)
        gz = pass_on(gz, lambda i: gz_all.at[i])
        b_sent[0] = pass_on(b_sent[0], lambda i: b_all.at[i, 0])
        z_last(1)
        for m in range(1, batches):
            b_sent[m] = pass_on(b_sent[m], lambda i, m=m: b_all.at[i, m])
        for copy in [*over_y, *flags, *gz] + [c for pair_of in b_sent for c in pair_of]:
            copy.wait_recv()
    copies.finish()


def front(direct, own, tokens, cot, index, keep, flags, gain1, gain2, wqkv, wo):
    batches, length, width = tokens.shape
    groups = 4 if direct else 1
    out = jax.ShapeDtypeStruct
    vmem = pl.BlockSpec(memory_space=pltpu.VMEM)
    anywhere = pl.BlockSpec(memory_space=pl.ANY)
    kept = [
        ((batches, ROWS, width), BF16),
        ((batches, ROWS, 3 * width), BF16),
        ((batches, ITEMS, HEADS, ITEM_ROWS, ITEM_ROWS), BF16),
        ((batches, ROWS, width), BF16),
        ((batches, ROWS, width), F32),
    ]
    scratch = [pltpu.VMEM((batches, ROWS, width), BF16)] * 2
    return pl.pallas_call(
        functools.partial(front_kernel, direct, batches),
        in_specs=[anywhere] + [vmem] * 9,
        out_specs=[anywhere] * 9,
        out_shape=[
            out((7 if direct else 1,) + (own.shape if direct else (8, 128)), BF16),
            out((groups, batches, ROWS, width), BF16),
            out((groups,) + flags.shape, flags.dtype),
            out((groups, batches, ROWS, width), BF16),
        ]
        + [out(*k) for k in kept],
        scratch_shapes=scratch
        + [pltpu.VMEM(*k) for k in kept]
        + [
            pltpu.SemaphoreType.DMA((32,)),
            pltpu.SemaphoreType.DMA((32,)),
            pltpu.SemaphoreType.DMA((24,)),
        ],
        compiler_params=pltpu.CompilerParams(
            vmem_limit_bytes=VMEM_LIMIT,
            has_side_effects=direct,
            collective_id=0 if direct else None,
        ),
        cost_estimate=pl.CostEstimate(
            flops=batches
            * (2 * ROWS * width * width * 4 + 8 * HEADS * ITEMS * ITEM_ROWS**2 * 128),
            bytes_accessed=60_000_000,
            transcendentals=batches * HEADS * ITEMS * ITEM_ROWS**2,
        ),
        name="front",
    )(own, tokens, cot, index, keep, flags, gain1, gain2, wqkv, wo)


def head_gradients(qkv_at, go_at, p_of, gqkv_ref, row0, hp, width, left):
    head_dim = width // HEADS
    pair = 2 * head_dim
    scaling = head_dim**-0.5
    at_q = pl.ds(pl.multiple_of(hp * pair, pair), pair)
    at_k = pl.ds(pl.multiple_of(width + hp * pair, pair), pair)
    at_v = pl.ds(pl.multiple_of(2 * width + hp * pair, pair), pair)
    for item in range(ITEMS):
        rows = slice(item * ITEM_ROWS, (item + 1) * ITEM_ROWS)
        out_rows = slice(row0 + rows.start, row0 + rows.stop)
        q, k, v = qkv_at(rows, at_q), qkv_at(rows, at_k), qkv_at(rows, at_v)
        go = go_at(rows, at_q)
        gq, gk, gv = [], [], []
        for half in range(2):
            mine = left if half == 0 else ~left
            p = p_of(item, half)
            pf = p.astype(F32)
            gp = dot(jnp.where(mine, go, 0), v, 1, 1)
            gs = (pf * (gp - jnp.sum(pf * gp, axis=-1, keepdims=True))).astype(BF16)
            gv.append(dot(p, go, 0, 0))
            gq.append(dot(gs, k, 1, 0))
            gk.append(dot(gs, q, 0, 0))
        gqkv_ref[out_rows, at_q] = (jnp.where(left, gq[0], gq[1]) * scaling).astype(BF16)
        gqkv_ref[out_rows, at_k] = (jnp.where(left, gk[0], gk[1]) * scaling).astype(BF16)
        gqkv_ref[out_rows, at_v] = jnp.where(left, gv[0], gv[1]).astype(BF16)


def add(*terms):
    total = terms[0].astype(F32)
    for term in terms[1:]:
        total = total + term.astype(F32)
    return total.astype(BF16)


def rows_at(start, size):
    return pl.ds(pl.multiple_of(start, 32), size)


class BlockSum:
    def __init__(self, copies, near_by, place, grads, gall, first, size, buffers):
        self.copies, self.near_by, self.grads, self.gall = copies, near_by, grads, gall
        self.r_core, self.r_one, self.r_two, self.r_z, self.final = buffers
        self.first, self.size = first, size
        core, xi, yi, self.zi = place
        self.half = grads.shape[0] // 2
        self.quarter, self.eighth = self.half // 2, self.half // 4
        self.row = core * self.half
        self.parts = []
        for part, (one, two) in enumerate(((xi, yi), (yi, xi))):
            cols = pl.ds(first + part * size // 2, size // 2)
            ways = (near_by.x, near_by.y) if part == 0 else (near_by.y, near_by.x)
            row_one = self.row + one * self.quarter
            row_two = row_one + two * self.eighth
            away_one = self.row + (1 - one) * self.quarter
            away_two = row_one + (1 - two) * self.eighth
            self.parts.append((cols, ways, row_one, row_two, away_one, away_two))

    def z_cols(self, part, z):
        chunk = self.size // 8
        return pl.ds(
            pl.multiple_of(self.first + part * self.size // 2 + z * chunk, 128), chunk
        )

    def start(self):
        away = self.grads.at[
            rows_at(self.half - self.row, self.half), pl.ds(self.first, self.size)
        ]
        self.core = self.copies.send(away, self.r_core, self.near_by.core)

    def take(self, row, size, cols, term):
        at = rows_at(row, size)
        self.grads[at, cols] = add(self.grads[at, cols], term)

    def one(self):
        self.core.wait_recv()
        for part in range(4):
            step = self.size // 4
            self.take(
                self.row, self.half, pl.ds(self.first + part * step, step),
                self.r_core[:, part * step : (part + 1) * step],
            )
        self.ones = [
            self.copies.send(
                self.grads.at[rows_at(away, self.quarter), cols], self.r_one.at[i], ways[0]
            )
            for i, (cols, ways, _, _, away, _) in enumerate(self.parts)
        ]

    def two(self):
        self.twos = []
        for i, (cols, ways, row, _, _, away) in enumerate(self.parts):
            self.ones[i].wait_recv()
            self.take(row, self.quarter, cols, self.r_one[i])
            self.twos.append(
                self.copies.send(
                    self.grads.at[rows_at(away, self.eighth), cols], self.r_two.at[i], ways[1]
                )
            )

    def three(self):
        self.threes = []
        for i, (cols, _, _, row, _, _) in enumerate(self.parts):
            self.twos[i].wait_recv()
            self.take(row, self.eighth, cols, self.r_two[i])
            self.threes.append(
                [
                    self.copies.send(
                        self.grads.at[
                            rows_at(row, self.eighth), self.z_cols(i, (self.zi + shift) % 4)
                        ],
                        self.r_z.at[i, shift - 1], self.near_by.z[shift],
                    )
                    for shift in (1, 2, 3)
                ]
            )

    def back_three(self):
        self.threes_back = []
        for i, (_, _, _, row, _, _) in enumerate(self.parts):
            for copy in self.threes[i]:
                copy.wait_recv()
            at, mine = rows_at(row, self.eighth), self.z_cols(i, self.zi)
            self.final[i] = add(
                self.grads[at, mine], self.r_z[i, 0], self.r_z[i, 1], self.r_z[i, 2]
            )
            place = self.gall.at[at, mine]
            own = self.copies.load(self.final.at[i], place)
            self.threes_back.append(
                (
                    own,
                    [
                        self.copies.send(self.final.at[i], place, self.near_by.z[shift])
                        for shift in (1, 2, 3)
                    ],
                )
            )

    def give(self, row, size, cols, to):
        block = self.gall.at[rows_at(row, size), cols]
        return self.copies.send(block, block, to)

    def back_two(self):
        self.twos_back = []
        for i, (cols, ways, _, row, _, _) in enumerate(self.parts):
            own, others = self.threes_back[i]
            own.wait()
            for copy in others:
                copy.wait_recv()
            self.twos_back.append(self.give(row, self.eighth, cols, ways[1]))

    def back_one(self):
        self.ones_back = []
        for i, (cols, ways, row, _, _, _) in enumerate(self.parts):
            self.twos_back[i].wait_recv()
            self.ones_back.append(self.give(row, self.quarter, cols, ways[0]))

    def back_core(self):
        self.cores_back = []
        for i, (cols, *_) in enumerate(self.parts):
            self.ones_back[i].wait_recv()
            self.cores_back.append(self.give(self.row, self.half, cols, self.near_by.core))

    def finish(self):
        for copy in self.cores_back:
            copy.wait_recv()

    def settle(self):
        sent = [self.core, *self.ones, *self.twos, *self.threes[0], *self.threes[1]]
        self.copies.settle(sent)


PAIRS = HEADS // 2
FIRST_PAIRS = 4


def grad_columns(width):
    pair = width // PAIRS
    cut = FIRST_PAIRS * pair
    return [
        [slice(part * width + low, part * width + high) for part in range(4)]
        for low, high in ((0, cut), (cut, width))
    ]


def back_kernel(batches, *refs):
    gb_parts, z_parts, gw, cot_in, index_ref, keep_ref, x_in, o_in, y_in, qkv_in, p_in = refs[:11]
    gain1_ref, gain2_ref, wqkv_in, wo_in = refs[11:15]
    result_out, tg_out, gall, ein_out, eout, gains_out, z_core, z_far, rs_z = refs[15:24]
    (
        wqkv, wo, x, o, y, cot, qkv, p, gb_own, gb_far, gb_core, gb_cross, gb_x,
        gy, ga, go, gqkv, grads, *sum_buffers,
        held, r_y, ein, gsum, gain_in, tok, send_sem, recv_sem, local_sem, p_sem,
    ) = refs[24:]
    width = x.shape[1]
    head_dim = width // HEADS
    pair = 2 * head_dim
    length = cot.shape[0]
    dp, expert = lax.axis_index("dp"), lax.axis_index("expert")
    core, xi, yi, zi = expert % 2, expert // 2, dp % 2, dp // 2
    copies = Copies(send_sem, recv_sem, local_sem)
    near_by = Partners()
    near_by.greet()
    load, send = copies.load, copies.send

    crossed, nearer = [], []
    for m in range(batches):
        crossed.append(send(gb_parts.at[3, m], gb_cross.at[m], near_by.core))
        nearer.append(send(gb_parts.at[1, m], gb_core.at[m], near_by.core))
    order = (6, 4, 2, 0)
    pieces = [send(gw.at[order[0] + 1], r_y.at[0], near_by.y)]
    far_loads = [load(gb_parts.at[2, m], gb_far.at[m]) for m in range(batches)]
    own_loads = [load(gb_parts.at[0, m], gb_own.at[m]) for m in range(batches)]
    first_loads = [load(y_in.at[0], y), load(cot_in.at[0], cot)]
    held_loads = [load(gw.at[order[i]], held.at[i]) for i in range(4)]
    late_loads = [load(o_in, o), load(wo_in, wo), load(qkv_in.at[0], qkv)]
    last_loads = [load(x_in, x), load(wqkv_in, wqkv)]
    def far_sum(m):
        far_loads[m].wait()
        crossed[m].wait_recv()
        gb_far[m] = add(gb_far[m], gb_cross[m])

    far_sum(0)
    along = [send(gb_far.at[0], gb_x.at[0], near_by.x)]
    z_crossed = [send(z_parts.at[3, m], z_core.at[1, m], near_by.core) for m in range(batches)]
    z_nearer = [send(z_parts.at[1, m], z_core.at[0, m], near_by.core) for m in range(batches)]
    for m in range(1, batches):
        far_sum(m)

    sent_z = []
    z_ways = (near_by.z_pair, near_by.z[2], near_by.z_pair)

    def reduce_piece(i):
        pieces[i].wait_recv()
        if i < 3:
            pieces.append(send(gw.at[order[i + 1] + 1], r_y.at[i + 1], near_by.y))
        held_loads[i].wait()
        come = {0: (), 1: (0,), 2: (), 3: (1, 2)}[i]
        for j in come:
            sent_z[j].wait_recv()
        loads = [load(rs_z.at[j], r_y.at[at]) for at, j in enumerate(come)]
        for copy in loads:
            copy.wait()
        held[i] = add(held[i], r_y[i], *[r_y[at] for at in range(len(come))])
        if i < 3:
            sent_z.append(send(held.at[i], rs_z.at[i], z_ways[i]))

    z_along = []

    def z_load(m):
        z_crossed[m].wait_recv()
        return [load(z_parts.at[2, m], gb_own.at[m]), load(z_core.at[1, m], gb_core.at[m])]

    def z_send(m, loads):
        for copy in loads:
            copy.wait()
        gb_cross[m] = add(gb_own[m], gb_core[m])
        z_along.append(send(gb_cross.at[m], z_far.at[m], near_by.x))

    columns = grad_columns(width)
    sizes = [sum(cols.stop - cols.start for cols in group) for group in columns]
    firsts = [0, sizes[0]]
    sums = [
        BlockSum(
            copies, near_by, (core, xi, yi, zi), grads, gall, firsts[i], sizes[i],
            sum_buffers[i * 5 : i * 5 + 5],
        )
        for i in range(2)
    ]

    def weight_gradients(group, parts):
        at = firsts[group]
        for part, cols in enumerate(columns[group]):
            size = cols.stop - cols.start
            if part in parts:
                if part == 3:
                    inner = slice(cols.start - 3 * width, cols.stop - 3 * width)
                    product = dot(o[...], ga[:, inner], 0, 0)
                else:
                    product = dot(a[...], gqkv[:, cols], 0, 0)
                grads[:, at : at + size] = product.astype(BF16)
            at += size

    left = lax.broadcasted_iota(jnp.int32, (ITEM_ROWS, pair), 1) < head_dim
    reduce_piece(0)
    for copy in first_loads + late_loads:
        copy.wait()
    gain2_grad = jnp.zeros((1, width), F32)
    items = [slice(i * ITEM_ROWS, (i + 1) * ITEM_ROWS) for i in range(ITEMS)]
    a = ga
    for m in range(batches):
        row0 = m * ROWS

        def p_load(hp, m=m):
            return pltpu.make_async_copy(
                p_in.at[m, :, pl.ds(2 * hp, 2)], p.at[hp % 2], p_sem.at[hp % 2]
            )

        p_load(0).start()
        own_loads[m].wait()
        nearer[m].wait_recv()
        along[m].wait_recv()
        if m + 1 < batches:
            along.append(send(gb_far.at[m + 1], gb_x.at[m + 1], near_by.x))
        for rows in items:
            at = slice(row0 + rows.start, row0 + rows.stop)
            gb = (
                gb_own[m, rows].astype(F32)
                + gb_core[m, rows].astype(F32)
                + gb_x[m, rows].astype(F32)
            )
            unit2, inverse2 = normalize_parts(y[rows])
            gain2_grad = gain2_grad + jnp.sum(gb * unit2, axis=0, keepdims=True)
            g = dot(pick_rows(index_ref, m, length, rows).astype(BF16), cot[...], 1, 0)
            gy_rows = g + normalize_back(gb * gain2_ref[...], unit2, inverse2)
            gy[at] = gy_rows
            ga[at] = gy_rows.astype(BF16)
            go[rows] = dot(ga[at], wo[...], 1, 1).astype(BF16)
        if m + 1 < batches:
            first_loads = [load(y_in.at[m + 1], y), load(cot_in.at[m + 1], cot)]
        z_loads = z_load(m)

        def heads(hp, carry, row0=row0, p_load=p_load):
            @pl.when(hp + 1 < PAIRS)
            def _():
                p_load(hp + 1).start()

            p_load(hp).wait()
            slot = hp % 2
            head_gradients(
                lambda rows, cols: qkv[rows, cols],
                lambda rows, cols: go[rows, cols],
                lambda item, half: p[slot, item, half],
                gqkv, row0, hp, width, left,
            )
            return carry

        if m + 1 < batches:
            lax.fori_loop(0, PAIRS, heads, 0)
            first_loads.append(load(qkv_in.at[m + 1], qkv))
            reduce_piece(1 + m)
            z_send(m, z_loads)
            for copy in first_loads:
                copy.wait()
        else:
            z_send(m, z_loads)
            lax.fori_loop(0, FIRST_PAIRS, heads, 0)
            reduce_piece(2)
            for copy in last_loads:
                copy.wait()
            weight_gradients(0, (3,))
            weight_gradients(1, (3,))
            for micro in range(batches):
                at = slice(micro * ROWS, (micro + 1) * ROWS)
                unit, _ = normalize_parts(x[at].astype(F32))
                a[at] = (unit * gain1_ref[...]).astype(BF16)
            weight_gradients(0, (0, 1, 2))
            sums[0].start()
            lax.fori_loop(FIRST_PAIRS, PAIRS, heads, 0)
    sums[0].one()
    weight_gradients(1, (0, 1, 2))
    sums[1].start()

    gain1_grad = jnp.zeros((1, width), F32)
    token_stores = []
    between = [sums[0].two, sums[1].one, sums[0].three, sums[1].two]
    for m in range(batches):
        for rows in items:
            at = slice(m * ROWS + rows.start, m * ROWS + rows.stop)
            unit, inverse = normalize_parts(x[at].astype(F32))
            gnorm = dot(gqkv[at], wqkv[...], 1, 1)
            gain1_grad = gain1_grad + jnp.sum(gnorm * unit, axis=0, keepdims=True)
            go[rows] = (gy[at] + normalize_back(gnorm * gain1_ref[...], unit, inverse)).astype(BF16)
            if between:
                between.pop(0)()
        tok[m] = dot(pick_rows(index_ref, m, length).astype(BF16), go[...], 0, 0).astype(BF16)
        token_stores.append(load(tok.at[m], tg_out.at[m]))
    gsum[0] = jnp.concatenate([gain1_grad, gain2_grad, jnp.zeros((6, width), F32)], axis=0)
    gain_partners = [near_by.core, near_by.x, near_by.y, near_by.z_pair, near_by.z[2]]
    gain_sent = [send(gsum.at[0], gain_in.at[0], gain_partners[0])]

    def gain_step():
        at = len(gain_sent)
        gain_sent[-1].wait_recv()
        gsum[at] = gsum[at - 1] + gain_in[at - 1]
        if at < len(gain_partners):
            gain_sent.append(send(gsum.at[at], gain_in.at[at], gain_partners[at]))

    sums[1].three()
    reduce_piece(3)

    def join(to, own):
        at = rows_at(expert * part_rows, part_rows)
        return [own(held.at[3, :, 1], eout.at[:, at], *to), own(held.at[3, :, 0], ein.at[:, at], *to)]

    part_rows = held.shape[3]
    joined = join((near_by.x,), send)
    join_near = join((near_by.core,), send)
    join_own = join((), load)
    gain_step()

    for m in range(batches):
        z_nearer[m].wait_recv()
        z_along[m].wait_recv()
        loads = [
            load(z_parts.at[0, m], gb_own.at[m]),
            load(z_core.at[0, m], gb_core.at[m]),
            load(z_far.at[m], gb_x.at[m]),
            load(y_in.at[m], y),
        ]
        for copy in loads:
            copy.wait()
        for rows in items:
            chosen = pick_rows(index_ref, m, length, rows)
            keep = jnp.sum(jnp.where(chosen, keep_ref[m], 0.0), axis=1, keepdims=True)
            z = (
                gb_own[m, rows].astype(F32)
                + gb_core[m, rows].astype(F32)
                + gb_x[m, rows].astype(F32)
            )
            go[rows] = (y[rows] + jnp.where(keep > 0, z, 0.0)).astype(BF16)
        token_stores[m].wait()
        tok[m] = dot(pick_rows(index_ref, m, length).astype(BF16), go[...], 0, 0).astype(BF16)
        copies.keep(tok.at[m], result_out.at[m])
        if m == 0:
            sums[0].back_three()
        gain_step()
    sums[1].back_three()

    gain_step()
    for block_sum in sums:
        block_sum.back_two()
    gain_step()
    copies.keep(gsum.at[len(gain_partners)], gains_out)
    for block_sum in sums:
        block_sum.back_one()
    for block_sum in sums:
        block_sum.back_core()
    opposite = rows_at((expert + 2) % 4 * part_rows, part_rows)
    for copy in joined:
        copy.wait_recv()
    join_near += [
        send(ref.at[:, opposite], ref.at[:, opposite], near_by.core) for ref in (eout, ein)
    ]
    for block_sum in sums:
        block_sum.settle()
    for copy in join_own:
        copy.wait()
    for copy in join_near:
        copy.wait_recv()
    hidden = ein.shape[1]
    for k in range(3):
        cols = pl.ds(k * hidden, hidden)
        grads[:, cols] = ein[k].astype(F32).T.astype(BF16)
        copies.keep(grads.at[:, cols], ein_out.at[k])
    for block_sum in sums:
        block_sum.finish()
    copies.finish()


def back(gb_parts, z_parts, gw, cot, index, keep, x, o, y, qkv, p, gain1, gain2, wqkv, wo):
    batches, rows, width = x.shape
    length = cot.shape[1]
    out = jax.ShapeDtypeStruct
    vmem = pl.BlockSpec(memory_space=pltpu.VMEM)
    anywhere = pl.BlockSpec(memory_space=pl.ANY)
    piece = gw.shape[1:]
    both = batches * rows
    half = width // 2
    tokens_shape = (batches, rows, width)
    slots = [tokens_shape] * 5
    scratch = [
        ((width, 3 * width), BF16),
        ((width, width), BF16),
        ((both, width), BF16),
        ((both, width), BF16),
        ((rows, width), F32),
        ((length, width), BF16),
        ((rows, 3 * width), BF16),
        ((2, ITEMS, 2, ITEM_ROWS, ITEM_ROWS), BF16),
        *[(slot, BF16) for slot in slots],
        ((both, width), F32),
        ((both, width), BF16),
        ((rows, width), BF16),
        ((both, 3 * width), BF16),
        ((width, 4 * width), BF16),
        *[
            (shape, BF16)
            for size in (4 * FIRST_PAIRS * width // PAIRS, 4 * (PAIRS - FIRST_PAIRS) * width // PAIRS)
            for shape in (
                (half, size),
                (2, half // 2, size // 2),
                (2, half // 4, size // 2),
                (2, 3, half // 4, size // 8),
                (2, half // 4, size // 8),
            )
        ],
        ((4,) + piece, BF16),
        ((4,) + piece, BF16),
        ((3, 4 * piece[2], width), BF16),
        ((6, 8, width), F32),
        ((5, 8, width), F32),
        ((batches, length, width), BF16),
    ]
    return pl.pallas_call(
        functools.partial(back_kernel, batches),
        in_specs=[anywhere] * 4 + [vmem] * 2 + [anywhere] * 5 + [vmem] * 2 + [anywhere] * 2,
        out_specs=[anywhere] * 9,
        out_shape=[
            out(cot.shape, BF16),
            out(cot.shape, BF16),
            out((width, 4 * width), BF16),
            out((3, width, 4 * piece[2]), BF16),
            out((3, 4 * piece[2], width), BF16),
            out((8, width), F32),
            out((2,) + tokens_shape, BF16),
            out(tokens_shape, BF16),
            out((3,) + piece, BF16),
        ],
        scratch_shapes=[pltpu.VMEM(*k) for k in scratch]
        + [
            pltpu.SemaphoreType.DMA((80,)),
            pltpu.SemaphoreType.DMA((80,)),
            pltpu.SemaphoreType.DMA((64,)),
            pltpu.SemaphoreType.DMA((2,)),
        ],
        compiler_params=pltpu.CompilerParams(
            vmem_limit_bytes=VMEM_LIMIT, has_side_effects=True, collective_id=1
        ),
        cost_estimate=pl.CostEstimate(
            flops=batches
            * (2 * rows * width * width * 8 + 16 * HEADS * ITEMS * ITEM_ROWS**2 * 128),
            bytes_accessed=80_000_000,
            transcendentals=0,
        ),
        name="back",
    )(
        gb_parts, z_parts, gw, cot, index, keep,
        x.reshape(both, width), o.reshape(both, width), y, qkv, p, gain1, gain2, wqkv, wo,
    )


def attention_backward_kernel(n_parts, n_carry, *refs):
    parts = refs[:n_parts]
    (cot_ref, x_ref, y_ref, qkv_ref, p_ref, o_ref, gain1_ref, gain2_ref, wqkv_ref, wo_ref) = refs[
        n_parts : n_parts + 10
    ]
    carried = refs[n_parts + 10 : n_parts + 10 + n_carry]
    tg_ref, gwqkv_ref, gwo_ref, ggain_ref, gmix_ref, gqkv_ref = refs[n_parts + 10 + n_carry :]
    width = x_ref.shape[1]
    head_dim = width // HEADS
    gb = parts[0][...].astype(F32)
    for part in parts[1:]:
        gb = gb + part[...].astype(F32)
    unit2, inverse2 = normalize_parts(y_ref[...])
    gain2_grad = jnp.sum(gb * unit2, axis=0, keepdims=True)
    gy = cot_ref[...].astype(F32) + normalize_back(gb * gain2_ref[...], unit2, inverse2)
    ga = gy.astype(BF16)
    gwo = dot(o_ref[...], ga, 0, 0)
    if n_carry:
        gwo = gwo + carried[1][...]
    gwo_ref[...] = gwo
    gmix_ref[...] = dot(ga, wo_ref[...], 1, 1).astype(BF16)
    pair = 2 * head_dim
    left = lax.broadcasted_iota(jnp.int32, (ITEM_ROWS, pair), 1) < head_dim

    def heads(hp, carry):
        head_gradients(
            lambda rows, cols: qkv_ref[rows, cols],
            lambda rows, cols: gmix_ref[rows, cols],
            lambda item, half: p_ref[item, hp * 2 + half],
            gqkv_ref, 0, hp, width, left,
        )
        return carry

    lax.fori_loop(0, HEADS // 2, heads, 0)
    unit, inverse = normalize_parts(x_ref[...].astype(F32))
    a = (unit * gain1_ref[...]).astype(BF16)
    for part in range(3):
        cols = slice(part * width, (part + 1) * width)
        gw = dot(a, gqkv_ref[:, cols], 0, 0)
        if n_carry:
            gw = gw + carried[0][:, cols]
        gwqkv_ref[:, cols] = gw
    gnorm = dot(gqkv_ref[...], wqkv_ref[...], 1, 1)
    gain1_grad = jnp.sum(gnorm * unit, axis=0, keepdims=True)
    gains = jnp.concatenate([gain1_grad, gain2_grad, jnp.zeros((6, width), F32)], axis=0)
    if n_carry:
        gains = gains + carried[2][...]
    ggain_ref[...] = gains
    tg_ref[...] = (gy + normalize_back(gnorm * gain1_ref[...], unit, inverse)).astype(BF16)


def attention_backward(parts, cot, x, y, qkv, p, o, gain1, gain2, wqkv, wo, carried):
    rows, width = x.shape
    out = jax.ShapeDtypeStruct
    return pl.pallas_call(
        functools.partial(attention_backward_kernel, len(parts), len(carried)),
        out_shape=(
            out((rows, width), BF16),
            out((width, 3 * width), F32),
            out((width, width), F32),
            out((8, width), F32),
        ),
        scratch_shapes=[pltpu.VMEM((rows, width), BF16), pltpu.VMEM((rows, 3 * width), BF16)],
        compiler_params=pltpu.CompilerParams(vmem_limit_bytes=VMEM_LIMIT),
        cost_estimate=pl.CostEstimate(
            flops=2 * rows * width * width * 8 + 16 * HEADS * ITEMS * ITEM_ROWS**2 * 128,
            bytes_accessed=30_000_000,
            transcendentals=0,
        ),
        name="attention_backward",
    )(*parts, cot, x, y, qkv, p, o, gain1, gain2, wqkv, wo, *carried)


def expert_kernel(groups, batches, pieces, *refs):
    flags, own_ref, more_ref, b_in, g_in, z_out, gb_out, gw_out = refs[:8]
    rows_b, rows_g, w, grads, in_sem, w_sem, out_sem, gw_sem = refs[8:]
    part = own_ref.shape[2]

    def rounded(rows):
        return (rows + TILE - 1) // TILE * TILE

    merged = [
        flags[g, 0, micro * ITEMS + item]
        for g in range(groups)
        for micro in range(batches)
        for item in range(ITEMS)
    ]
    n_merged = sum(merged)
    n_plain = len(merged) - n_merged
    sizes = [n_plain * IMAGE_ROWS, n_plain * CAPTION, n_merged * ITEM_ROWS]
    starts = [0, rounded(sizes[0]), rounded(sizes[0]) + rounded(sizes[1])]
    ends = [start + rounded(size) for start, size in zip(starts, sizes)]
    blocks = []
    plain, joined = 0, 0
    for flat, flag in enumerate(merged):
        g, micro, item = flat // (batches * ITEMS), flat // ITEMS % batches, flat % ITEMS
        base = item * ITEM_ROWS
        image = jnp.where(flag == 1, starts[2] + joined * ITEM_ROWS, plain * IMAGE_ROWS)
        caption = jnp.where(
            flag == 1, image + IMAGE_ROWS, starts[1] + plain * CAPTION
        )
        blocks.append((g, micro, base, IMAGE_ROWS, image, flag, 0))
        blocks.append((g, micro, base + IMAGE_ROWS, CAPTION, caption, flag, 1))
        plain, joined = plain + 1 - flag, joined + flag

    def copy_of(which, number, outward):
        g, micro, base, size, at, _, _ = blocks[number]
        held = (rows_b, rows_g)[which].at[pl.ds(pl.multiple_of(at, 16), size)]
        if outward:
            far = (gb_out, z_out)[which].at[g, micro, pl.ds(base, size)]
            return pltpu.make_async_copy(held, far, out_sem.at[which, number])
        far = (b_in, g_in)[which].at[g, micro, pl.ds(base, size)]
        return pltpu.make_async_copy(far, held, in_sem.at[which, number])

    def of_expert(expert, act):
        for number, (_, _, _, _, _, flag, kind) in enumerate(blocks):
            if expert == 2 or kind == expert:
                @pl.when(flag == (1 if expert == 2 else 0))
                def _(number=number):
                    for which in range(2):
                        act(which, number)

    def weight_copy(k, i):
        piece = own_ref if i == 0 else more_ref.at[i - 1]
        return pltpu.make_async_copy(
            piece.at[k], w.at[k, :, pl.ds(i * part, part), :], w_sem.at[k, i]
        )

    for k in range(3):
        tail = pl.multiple_of(jnp.maximum(ends[k] - TILE, 0), TILE)
        rows_b[pl.ds(tail, TILE), :] = jnp.zeros((TILE, rows_b.shape[1]), BF16)
        rows_g[pl.ds(tail, TILE), :] = jnp.zeros((TILE, rows_g.shape[1]), BF16)
    for k in range(3):
        of_expert(k, lambda which, number: copy_of(which, number, False).start())
        for i in range(pieces):
            weight_copy(k, i).start()

    for k in range(3):
        grads[...] = jnp.zeros(grads.shape, F32)
        of_expert(k, lambda which, number: copy_of(which, number, False).wait())
        for i in range(pieces):
            weight_copy(k, i).wait()

        def tile(t, carry, k=k):
            at = pl.ds(pl.multiple_of(t * TILE, TILE), TILE)
            b, gz = rows_b[at, :], rows_g[at, :]
            u, slope = gelu_and_slope(dot(b, w[k, 0], 1, 1))
            gh = (dot(gz, w[k, 1], 1, 1) * slope).astype(BF16)
            u = u.astype(BF16)
            z, gb = dot(u, w[k, 1], 1, 0), dot(gh, w[k, 0], 1, 0)
            grads[0] += dot(gh, b, 0, 0)
            grads[1] += dot(u, gz, 0, 0)
            rows_b[at, :] = gb.astype(BF16)
            rows_g[at, :] = z.astype(BF16)
            return carry

        lax.fori_loop(starts[k] // TILE, ends[k] // TILE, tile, 0)
        of_expert(k, lambda which, number: copy_of(which, number, True).start())
        w[k] = grads[...].astype(BF16)
        for i in range(pieces):
            pltpu.make_async_copy(
                w.at[k, :, pl.ds(i * part, part), :], gw_out.at[i, k], gw_sem.at[k, i]
            ).start()
    for number in range(len(blocks)):
        for which in range(2):
            copy_of(which, number, True).wait()
    for k in range(3):
        for i in range(pieces):
            pltpu.make_async_copy(
                w.at[k, :, pl.ds(i * part, part), :], gw_out.at[i, k], gw_sem.at[k, i]
            ).wait()


def experts(flags, own, more, b_groups, g_groups):
    groups, batches, rows, width = b_groups.shape
    part = own.shape[2]
    pieces = 1 + (more.shape[0] if more.ndim == 5 else 0)
    hidden = part * pieces
    count = groups * batches * ITEMS
    capacity = (count * ITEM_ROWS // TILE + 4) * TILE
    out = jax.ShapeDtypeStruct
    anywhere = pl.BlockSpec(memory_space=pl.ANY)
    return pl.pallas_call(
        functools.partial(expert_kernel, groups, batches, pieces),
        in_specs=[pl.BlockSpec(memory_space=pltpu.SMEM)] + [anywhere] * 4,
        out_specs=[anywhere] * 3,
        out_shape=[out(b_groups.shape, BF16)] * 2 + [out((pieces,) + own.shape, BF16)],
        scratch_shapes=[
            pltpu.VMEM((capacity, width), BF16),
            pltpu.VMEM((capacity, width), BF16),
            pltpu.VMEM((3, 2, hidden, width), BF16),
            pltpu.VMEM((2, hidden, width), F32),
            pltpu.SemaphoreType.DMA((2, 2 * count)),
            pltpu.SemaphoreType.DMA((3, pieces)),
            pltpu.SemaphoreType.DMA((2, 2 * count)),
            pltpu.SemaphoreType.DMA((3, pieces)),
        ],
        compiler_params=pltpu.CompilerParams(vmem_limit_bytes=VMEM_LIMIT),
        cost_estimate=pl.CostEstimate(
            flops=2 * 6 * count * ITEM_ROWS * width * hidden,
            bytes_accessed=45_000_000,
            transcendentals=count * ITEM_ROWS * hidden,
        ),
        name="experts",
    )(flags, own, more, b_groups, g_groups)


def rows_of_items(first):
    row = jnp.arange(ROWS, dtype=jnp.int32)
    item, inside = row // ITEM_ROWS, row % ITEM_ROWS
    caption = jnp.where(first, item, 1 - item)
    return jnp.where(
        inside < PATCHES,
        item * PATCHES + inside,
        jnp.where(
            inside < IMAGE_ROWS,
            -1,
            ITEMS * PATCHES + caption * CAPTION + inside - IMAGE_ROWS,
        ),
    )


def to_items(rows, first):
    images = ITEMS * PATCHES
    one, two = rows[images : images + CAPTION], rows[images + CAPTION :]
    gap = jnp.zeros((IMAGE_ROWS - PATCHES,) + rows.shape[1:], rows.dtype)
    return jnp.concatenate(
        [
            rows[:PATCHES],
            gap,
            jnp.where(first, one, two),
            rows[PATCHES:images],
            gap,
            jnp.where(first, two, one),
        ],
        axis=0,
    )


def from_items(rows, first):
    one, two = rows[IMAGE_ROWS:ITEM_ROWS], rows[ITEM_ROWS + IMAGE_ROWS :]
    return jnp.concatenate(
        [
            rows[:PATCHES],
            rows[ITEM_ROWS : ITEM_ROWS + PATCHES],
            jnp.where(first, one, two),
            jnp.where(first, two, one),
        ],
        axis=0,
    )


def kept_tokens(routing, priority, hosts, capacity):
    length = routing.shape[0]
    index = jnp.arange(length, dtype=jnp.int32)
    position = jnp.sum(
        jnp.where(priority[None, :] == index[:, None], index[None, :], 0), axis=1
    )
    ahead = (routing[None, :] == routing[:, None]) & (position[None, :] < position[:, None])
    rank = jnp.sum(ahead.astype(jnp.int32), axis=1)
    return rank < capacity * ((hosts - routing + 2) // 3)


class Links:
    def __init__(self):
        self.hosts = lax.axis_size("expert")
        self.dp = lax.axis_size("dp")
        self.direct = self.hosts == 4 and self.dp == 8
        self.me = lax.axis_index("expert")

    def flip(self, v, bit):
        return lax.ppermute(v, "expert", [(i, i ^ bit) for i in range(4)])

    def across_y(self, v):
        return lax.ppermute(v, "dp", [(i, i ^ 1) for i in range(8)])

    def along_z(self, v, shift):
        return lax.ppermute(v, "dp", [(i, (i + 2 * shift) % 8) for i in range(8)])

    def gather_tokens(self, v):
        if not self.direct:
            return list(lax.all_gather(v, "expert"))
        near, far = self.flip(v, 1), self.flip(v, 2)
        return [v, near, far, self.flip(far, 1)]

    def reduce_tokens(self, parts):
        if not self.direct:
            return [lax.psum_scatter(jnp.stack(parts), "expert", scatter_dimension=0)]
        far = (parts[2].astype(F32) + self.flip(parts[3], 1).astype(F32)).astype(BF16)
        return [parts[0], self.flip(parts[1], 1), self.flip(far, 2)]

    def reduce_weights(self, pieces):
        if not self.direct:
            return lax.psum_scatter(pieces[0], "dp", scatter_dimension=2, tiled=True)
        total = None
        for at, shift in enumerate((0, 1, 3, 2)):
            piece = pieces[2 * at].astype(F32) + self.across_y(pieces[2 * at + 1]).astype(F32)
            if shift:
                piece = self.along_z(piece.astype(BF16), -shift).astype(F32)
            total = piece if total is None else total + piece
        return total.astype(BF16)

    def join_hidden(self, v):
        if not self.direct:
            return lax.all_gather(v, "expert", axis=2, tiled=True)
        stacked = jnp.stack(self.gather_tokens(v))
        return jnp.concatenate(
            [
                lax.dynamic_index_in_dim(stacked, i ^ self.me, 0, keepdims=False)
                for i in range(4)
            ],
            axis=2,
        )


def shards(
    tokens,
    cotangent,
    item_group,
    routes,
    slot_order,
    attn_gain,
    ffn_gain,
    qkv_weight,
    out_weight,
    expert_in,
    expert_out,
):
    links = Links()
    hosts, me = links.hosts, links.me
    batches, length, width = tokens.shape
    capacity = 2 * length // hosts
    shard = expert_in.shape[2]
    part = shard // hosts
    gain1, gain2 = attn_gain[None, :], ffn_gain[None, :]

    own = jnp.stack(
        [
            jnp.swapaxes(lax.dynamic_slice_in_dim(expert_in, me * part, part, 2), 1, 2),
            lax.dynamic_slice_in_dim(expert_out, me * part, part, 1),
        ],
        axis=1,
    )
    first = item_group[:, ITEMS * PATCHES] == 0
    merged = (routes[:, 0 : ITEMS * PATCHES : PATCHES] == 2).astype(jnp.int32)
    flags = jnp.broadcast_to(
        jnp.pad(merged.reshape(1, -1), ((0, 0), (0, 128 - batches * ITEMS))), (8, 128)
    )
    kept = jnp.stack(
        [kept_tokens(routes[m], slot_order[m, 0], hosts, capacity) for m in range(batches)]
    )
    index = jnp.stack([rows_of_items(first[m]) for m in range(batches)])[:, :, None]
    w_all, gz_groups, flag_groups, b_groups, x_all, qkv_all, p_all, o_all, y_all = front(
        links.direct, own, tokens, cotangent, index, kept.astype(F32)[:, None, :], flags,
        gain1, gain2, qkv_weight, out_weight,
    )
    if not links.direct:
        own = lax.all_gather(own, "dp", axis=2, tiled=True)
        gz_groups, flag_groups, b_groups = [
            lax.all_gather(v[0], "expert") for v in (gz_groups, flag_groups, b_groups)
        ]
    z_parts, gb_parts, gw_pieces = experts(flag_groups, own, w_all, b_groups, gz_groups)
    if links.direct:
        result, token_grad, gall, ein_sum, eout_sum, gains, *_ = back(
            gb_parts, z_parts, gw_pieces, cotangent, index, kept.astype(F32)[:, None, :],
            x_all, o_all, y_all, qkv_all, p_all, gain1, gain2, qkv_weight, out_weight,
        )
        blocks = []
        for i in range(4):
            at = 0
            pieces = []
            for group in grad_columns(width):
                size = group[i].stop - group[i].start
                pieces.append(gall[:, at + i * size : at + (i + 1) * size].astype(F32))
                at += 4 * size
            blocks.append(jnp.concatenate(pieces, axis=1))
        return (
            result,
            token_grad,
            gains[0],
            gains[1],
            jnp.concatenate(blocks[:3], axis=1),
            blocks[3],
            ein_sum.astype(F32),
            eout_sum.astype(F32),
        )
    cot_items = [to_items(cotangent[m], first[m]) for m in range(batches)]
    gb_terms = links.reduce_tokens(gb_parts)
    z_terms = links.reduce_tokens(z_parts)
    sums = links.join_hidden(links.reduce_weights(gw_pieces)).astype(F32)

    results, token_grads, carried = [], [], ()
    for m in range(batches):
        x, qkv, p, o, y = x_all[m], qkv_all[m], p_all[m], o_all[m], y_all[m]
        at = m
        tg, *carried = attention_backward(
            [t[at] for t in gb_terms],
            cot_items[m], x, y, qkv, p, o, gain1, gain2, qkv_weight, out_weight,
            tuple(carried),
        )
        token_grads.append(from_items(tg, first[m]))
        z = z_terms[0][at].astype(F32)
        for term in z_terms[1:]:
            z = z + term[at].astype(F32)
        branch = jnp.where(kept[m][:, None], from_items(z, first[m]), 0.0)
        results.append((from_items(y, first[m]) + branch).astype(BF16))
    gw_qkv, gw_out, gains = carried
    packed = jnp.concatenate(
        [
            jnp.concatenate([gw_qkv, gw_out], axis=1),
            jnp.pad(gains[:2].reshape(1, 2 * width), ((0, 7), (0, 2 * width))),
        ],
        axis=0,
    ).astype(BF16)
    packed = lax.psum(packed, ("dp", "expert")).astype(F32)
    return (
        jnp.stack(results),
        jnp.stack(token_grads),
        packed[width, :width],
        packed[width, width : 2 * width],
        packed[:width, : 3 * width],
        packed[:width, 3 * width :],
        jnp.swapaxes(sums[:, 0], 1, 2),
        sums[:, 1],
    )


def solution(mesh):
    in_specs = (
        P(None, ("dp", "expert"), None),
        P(None, ("dp", "expert"), None),
        P(None, ("dp", "expert")),
        P(None, ("dp", "expert")),
        P(None, ("dp", "expert"), None),
        P(),
        P(),
        P(),
        P(),
        P(None, None, "dp"),
        P(None, "dp", None),
    )
    out_specs = (
        P(None, ("dp", "expert"), None),
        P(None, ("dp", "expert"), None),
        P(),
        P(),
        P(),
        P(),
        P(None, None, "dp"),
        P(None, "dp", None),
    )
    return jax.shard_map(shards, mesh=mesh, in_specs=in_specs, out_specs=out_specs, check_vma=False)
```

```python
import functools

import jax
import jax.numpy as jnp
from jax import lax
from jax.experimental import pallas as pl
from jax.experimental.pallas import tpu as pltpu
from jax.sharding import PartitionSpec as P

HEADS = 12
EPSILON = 1e-05
PATCHES = 197
CAPTION = 64
ITEMS = 2
IMAGE_ROWS = 208
ITEM_ROWS = IMAGE_ROWS + CAPTION
ROWS = ITEMS * ITEM_ROWS
TILE = 256
VMEM_LIMIT = 60 * 1024 * 1024
F32 = jnp.float32
BF16 = jnp.bfloat16


def dot(a, b, a_dim, b_dim):
    return lax.dot_general(
        a, b, (((a_dim,), (b_dim,)), ((), ())), preferred_element_type=F32
    )


def normalize_parts(v):
    centred = v - jnp.mean(v, axis=-1, keepdims=True)
    inverse = lax.rsqrt(jnp.mean(centred * centred, axis=-1, keepdims=True) + EPSILON)
    return centred * inverse, inverse


def normalize_back(grad_unit, unit_rows, inverse):
    return inverse * (
        grad_unit
        - jnp.mean(grad_unit, axis=-1, keepdims=True)
        - unit_rows * jnp.mean(grad_unit * unit_rows, axis=-1, keepdims=True)
    )


def gelu_and_slope(h):
    bell = jnp.exp(-0.5 * h * h)
    t = 1.0 / (1.0 + (0.3275911 * 0.7071067811865476) * jnp.abs(h))
    poly = t * (
        0.254829592
        + t * (-0.284496736 + t * (1.421413741 + t * (-1.453152027 + t * 1.061405429)))
    )
    below = 0.5 * poly * bell
    phi = jnp.where(h > 0, 1.0 - below, below)
    return h * phi, phi + h * (0.3989422804014327 * bell)


class Partners:
    def __init__(self):
        dp, expert = lax.axis_index("dp"), lax.axis_index("expert")
        self.core = (dp, expert + 1 - 2 * (expert % 2))
        self.x = (dp, (expert + 2) % 4)
        self.y = (dp + 1 - 2 * (dp % 2), expert)
        self.z = {shift: ((dp + 2 * shift) % 8, expert) for shift in (1, 2, 3)}
        self.z_pair = (dp + 2 - 4 * (dp // 2 % 2), expert)

    def greet(self):
        barrier = pltpu.get_barrier_semaphore()
        everyone = [self.core, self.x, self.y, self.z[1], self.z[2], self.z[3]]
        for other in everyone:
            pl.semaphore_signal(
                barrier, inc=1, device_id=other, device_id_type=pl.DeviceIdType.MESH
            )
        pl.semaphore_wait(barrier, len(everyone))


class Copies:
    def __init__(self, send_sem, recv_sem, local_sem):
        self.send_sem, self.recv_sem, self.local_sem = send_sem, recv_sem, local_sem
        self.sent, self.kept, self.sends, self.locals = [], [], 0, 0

    def send(self, src, dst, device):
        at = self.sends
        self.sends += 1
        copy = pltpu.make_async_remote_copy(
            src_ref=src,
            dst_ref=dst,
            send_sem=self.send_sem.at[at],
            recv_sem=self.recv_sem.at[at],
            device_id=device,
            device_id_type=pl.DeviceIdType.MESH,
        )
        copy.start()
        self.sent.append(copy)
        return copy

    def keep(self, src, dst):
        copy = self.load(src, dst)
        self.kept.append(copy)
        return copy

    def load(self, src, dst):
        copy = pltpu.make_async_copy(src, dst, self.local_sem.at[self.locals])
        self.locals += 1
        copy.start()
        return copy

    def settle(self, done):
        for copy in done:
            copy.wait_send()
        self.sent = [copy for copy in self.sent if all(copy is not other for other in done)]

    def finish(self):
        for copy in self.sent:
            copy.wait_send()
        for copy in self.kept:
            copy.wait()


def pick_rows(group_ref, m, length, rows=slice(0, ROWS)):
    count = rows.stop - rows.start
    row = lax.broadcasted_iota(jnp.int32, (count, 1), 0) + rows.start
    item = (row >= ITEM_ROWS).astype(jnp.int32)
    inside = row - item * ITEM_ROWS
    images = ITEMS * PATCHES
    swapped = (group_ref[m : m + 1, images : images + 1] != 0).astype(jnp.int32)
    caption = item + swapped - 2 * item * swapped
    token = jnp.where(
        inside < PATCHES,
        item * PATCHES + inside,
        jnp.where(inside < IMAGE_ROWS, -1, images + caption * CAPTION + inside - IMAGE_ROWS),
    )
    return lax.broadcasted_iota(jnp.int32, (count, length), 1) == token


def kept_tokens(routing, priority, hosts, capacity):
    length = routing.shape[1]
    across = lax.broadcasted_iota(jnp.int32, (length, length), 1)
    down = lax.broadcasted_iota(jnp.int32, (length, length), 0)

    def upright(row):
        return jnp.sum(jnp.where(across == down, row, 0.0), axis=1, keepdims=True)

    order = upright(priority.astype(F32))
    position = jnp.sum(
        jnp.where(order == across.astype(F32), down.astype(F32), 0.0), axis=0, keepdims=True
    )
    route = routing.astype(F32)
    ahead = (upright(route) == route) & (upright(position) < position)
    rank = jnp.sum(jnp.where(ahead, 1.0, 0.0), axis=0, keepdims=True)
    slots = jnp.zeros_like(rank)
    for kind in range(3):
        slots = jnp.where(routing == kind, float(capacity * ((hosts - kind + 2) // 3)), slots)
    return jnp.where(rank < slots, 1.0, 0.0)


def front_kernel(direct, hosts, batches, *refs):
    (own_ref, tokens_ref, cot_ref, group_ref, routes_ref, order_ref, gain1_ref, gain2_ref) = refs[:8]
    wqkv_ref, wo_ref, w_all, gz_all, flags_all, b_all = refs[8:14]
    x_out, qkv_out, p_out, o_out, y_out, cot_out = refs[14:20]
    (
        keep_ref, gz_scr, b_scr, x_scr, qkv_scr, p_scr, o_scr, y_scr, cot_scr, flags_scr,
        send_sem, recv_sem, local_sem,
    ) = refs[20:]
    length, _, width = tokens_ref.shape
    head_dim = width // HEADS
    pair = 2 * head_dim
    copies = Copies(send_sem, recv_sem, local_sem)

    def spread(src, slots):
        copies.keep(src, slots(0))
        if not direct:
            return None
        near = copies.send(src, slots(1), near_by.core)
        return near, copies.send(src, slots(2), near_by.x)

    def pass_on(pair_of, slots):
        near, far = pair_of
        far.wait_recv()
        return near, copies.send(slots(2), slots(3), near_by.core)

    if direct:
        near_by = Partners()
        near_by.greet()
        over_y = [copies.send(own_ref, w_all.at[0], near_by.y)]
        along = [[], [], []]

        def z_half(i):
            along[0].append(copies.send(own_ref.at[:, i], w_all.at[1, :, i], near_by.z_pair))
            along[1].append(copies.send(own_ref.at[:, i], w_all.at[3, :, i], near_by.z[2]))

        def z_pass(i):
            for k in (1, 0):
                along[k][i].wait_recv()
                if k == 1:
                    along[2].append(
                        copies.send(w_all.at[3, :, i], w_all.at[5, :, i], near_by.z_pair)
                    )
                at = 2 * k + 1
                over_y.append(copies.send(w_all.at[at, :, i], w_all.at[at + 1, :, i], near_by.y))

        def z_last(i):
            along[2][i].wait_recv()
            over_y.append(copies.send(w_all.at[5, :, i], w_all.at[6, :, i], near_by.y))

        z_half(0)
    lane = lax.broadcasted_iota(jnp.int32, flags_scr.shape, 1)
    merged = jnp.zeros(flags_scr.shape, jnp.int32)
    for m in range(batches):
        for item in range(ITEMS):
            route = routes_ref[m : m + 1, item * PATCHES : item * PATCHES + 1]
            here = lane == m * ITEMS + item
            merged = jnp.where(here & (route == 2), 1, merged)
    flags_scr[...] = merged
    flags = spread(flags_scr, lambda i: flags_all.at[i])

    for m in range(batches):
        keep_ref[m] = kept_tokens(
            routes_ref[m : m + 1], order_ref[m], hosts, 2 * length // hosts
        )
        chosen = pick_rows(group_ref, m, length) & (keep_ref[m] > 0)
        gz_scr[m] = dot(chosen.astype(BF16), cot_ref[:, m], 1, 0).astype(BF16)
    gz = spread(gz_scr, lambda i: gz_all.at[i])

    left = lax.broadcasted_iota(jnp.int32, (ITEM_ROWS, pair), 1) < head_dim
    key = lax.broadcasted_iota(jnp.int32, (1, ITEM_ROWS), 1)
    bias = jnp.where((key >= PATCHES) & (key < IMAGE_ROWS), -1e30, 0.0).astype(F32)
    b_sent = []
    for m in range(batches):
        xb = dot(pick_rows(group_ref, m, length).astype(BF16), tokens_ref[:, m], 1, 0)
        x_scr[m] = xb.astype(BF16)
        unit, _ = normalize_parts(xb)
        a = (unit * gain1_ref[...]).astype(BF16)
        for part in range(3):
            cols = slice(part * width, (part + 1) * width)
            qkv_scr[m, :, cols] = dot(a, wqkv_ref[:, cols], 1, 0).astype(BF16)

        def heads(hp, carry, m=m):
            at_q = pl.ds(pl.multiple_of(hp * pair, pair), pair)
            at_k = pl.ds(pl.multiple_of(width + hp * pair, pair), pair)
            at_v = pl.ds(pl.multiple_of(2 * width + hp * pair, pair), pair)
            for item in range(ITEMS):
                rows = slice(item * ITEM_ROWS, (item + 1) * ITEM_ROWS)
                q, k, v = qkv_scr[m, rows, at_q], qkv_scr[m, rows, at_k], qkv_scr[m, rows, at_v]
                outs = []
                for half in range(2):
                    mine = left if half == 0 else ~left
                    s = dot(jnp.where(mine, q, 0), k, 1, 1) * (head_dim**-0.5) + bias
                    e = jnp.exp(s - jnp.max(s, axis=-1, keepdims=True))
                    p = (e * (1.0 / jnp.sum(e, axis=-1, keepdims=True))).astype(BF16)
                    p_scr[m, item, hp * 2 + half] = p
                    outs.append(dot(p, v, 1, 0))
                o_scr[m, rows, at_q] = jnp.where(left, outs[0], outs[1]).astype(BF16)
            return carry

        lax.fori_loop(0, HEADS // 2, heads, 0)
        y = x_scr[m].astype(F32) + dot(o_scr[m], wo_ref[...], 1, 0)
        y_scr[m] = y
        cot_scr[m] = dot(pick_rows(group_ref, m, length).astype(BF16), cot_ref[:, m], 1, 0).astype(
            BF16
        )
        unit2, _ = normalize_parts(y)
        b_scr[m] = (unit2 * gain2_ref[...]).astype(BF16)
        b_sent.append(spread(b_scr.at[m], lambda i, m=m: b_all.at[i, m]))
        for scr, out in (
            (x_scr, x_out), (qkv_scr, qkv_out), (p_scr, p_out), (o_scr, o_out), (y_scr, y_out),
            (cot_scr, cot_out),
        ):
            copies.keep(scr.at[m], out.at[m])
        if direct and m == 0:
            z_pass(0)
            z_half(1)
            flags = pass_on(flags, lambda i: flags_all.at[i])

    if direct:
        z_pass(1)
        z_last(0)
        gz = pass_on(gz, lambda i: gz_all.at[i])
        b_sent[0] = pass_on(b_sent[0], lambda i: b_all.at[i, 0])
        z_last(1)
        for m in range(1, batches):
            b_sent[m] = pass_on(b_sent[m], lambda i, m=m: b_all.at[i, m])
        for copy in [*over_y, *flags, *gz] + [c for pair_of in b_sent for c in pair_of]:
            copy.wait_recv()
    copies.finish()


def front(direct, hosts, own, tokens, cot, group, routes, order, gain1, gain2, wqkv, wo):
    length, batches, width = tokens.shape
    groups = 4 if direct else 1
    out = jax.ShapeDtypeStruct
    vmem = pl.BlockSpec(memory_space=pltpu.VMEM)
    anywhere = pl.BlockSpec(memory_space=pl.ANY)
    kept = [
        ((batches, ROWS, width), BF16),
        ((batches, ROWS, 3 * width), BF16),
        ((batches, ITEMS, HEADS, ITEM_ROWS, ITEM_ROWS), BF16),
        ((batches, ROWS, width), BF16),
        ((batches, ROWS, width), F32),
        ((batches, ROWS, width), BF16),
    ]
    scratch = [pltpu.VMEM((batches, ROWS, width), BF16)] * 2
    return pl.pallas_call(
        functools.partial(front_kernel, direct, hosts, batches),
        in_specs=[anywhere] + [vmem] * 9,
        out_specs=[anywhere] * 10 + [vmem],
        out_shape=[
            out((7 if direct else 1,) + (own.shape if direct else (8, 128)), BF16),
            out((groups, batches, ROWS, width), BF16),
            out((groups, 8, 128), jnp.int32),
            out((groups, batches, ROWS, width), BF16),
        ]
        + [out(*k) for k in kept]
        + [out((batches, 1, length), F32)],
        scratch_shapes=scratch
        + [pltpu.VMEM(*k) for k in kept]
        + [
            pltpu.VMEM((8, 128), jnp.int32),
            pltpu.SemaphoreType.DMA((32,)),
            pltpu.SemaphoreType.DMA((32,)),
            pltpu.SemaphoreType.DMA((24,)),
        ],
        compiler_params=pltpu.CompilerParams(
            vmem_limit_bytes=VMEM_LIMIT,
            has_side_effects=direct,
            collective_id=0 if direct else None,
        ),
        cost_estimate=pl.CostEstimate(
            flops=batches
            * (2 * ROWS * width * width * 4 + 8 * HEADS * ITEMS * ITEM_ROWS**2 * 128),
            bytes_accessed=60_000_000,
            transcendentals=batches * HEADS * ITEMS * ITEM_ROWS**2,
        ),
        name="front",
    )(own, tokens, cot, group, routes, order, gain1, gain2, wqkv, wo)


def head_gradients(qkv_at, go_at, p_of, gqkv_ref, row0, hp, width, left):
    head_dim = width // HEADS
    pair = 2 * head_dim
    scaling = head_dim**-0.5
    at_q = pl.ds(pl.multiple_of(hp * pair, pair), pair)
    at_k = pl.ds(pl.multiple_of(width + hp * pair, pair), pair)
    at_v = pl.ds(pl.multiple_of(2 * width + hp * pair, pair), pair)
    for item in range(ITEMS):
        rows = slice(item * ITEM_ROWS, (item + 1) * ITEM_ROWS)
        out_rows = slice(row0 + rows.start, row0 + rows.stop)
        q, k, v = qkv_at(rows, at_q), qkv_at(rows, at_k), qkv_at(rows, at_v)
        go = go_at(rows, at_q)
        gq, gk, gv = [], [], []
        for half in range(2):
            mine = left if half == 0 else ~left
            p = p_of(item, half)
            pf = p.astype(F32)
            gp = dot(jnp.where(mine, go, 0), v, 1, 1)
            gs = (pf * (gp - jnp.sum(pf * gp, axis=-1, keepdims=True))).astype(BF16)
            gv.append(dot(p, go, 0, 0))
            gq.append(dot(gs, k, 1, 0))
            gk.append(dot(gs, q, 0, 0))
        gqkv_ref[out_rows, at_q] = (jnp.where(left, gq[0], gq[1]) * scaling).astype(BF16)
        gqkv_ref[out_rows, at_k] = (jnp.where(left, gk[0], gk[1]) * scaling).astype(BF16)
        gqkv_ref[out_rows, at_v] = jnp.where(left, gv[0], gv[1]).astype(BF16)


def add(*terms):
    total = terms[0].astype(F32)
    for term in terms[1:]:
        total = total + term.astype(F32)
    return total.astype(BF16)


def rows_at(start, size):
    return pl.ds(pl.multiple_of(start, 32), size)


class BlockSum:
    def __init__(self, copies, near_by, place, grads, gall, low, high, buffers):
        self.copies, self.near_by, self.grads, self.gall = copies, near_by, grads, gall
        self.r_core, self.r_one, self.r_two, self.r_z, self.final = buffers
        self.low, self.size = low, high - low
        self.cols = pl.ds(low, high - low)
        core, xi, yi, self.zi = place
        self.half = grads.shape[1] // 2
        self.quarter, self.eighth = self.half // 2, self.half // 4
        self.row = core * self.half
        self.parts = []
        for part, (one, two) in enumerate(((xi, yi), (yi, xi))):
            pair = pl.ds(2 * part, 2)
            ways = (near_by.x, near_by.y) if part == 0 else (near_by.y, near_by.x)
            row_one = self.row + one * self.quarter
            row_two = row_one + two * self.eighth
            away_one = self.row + (1 - one) * self.quarter
            away_two = row_one + (1 - two) * self.eighth
            self.parts.append((pair, ways, row_one, row_two, away_one, away_two))

    def z_block(self, ref, part, row, z):
        chunk = self.size // 2
        cols = pl.ds(pl.multiple_of(self.low + z % 2 * chunk, 128), chunk)
        return ref.at[2 * part + z // 2, rows_at(row, self.eighth), cols]

    def start(self):
        away = self.grads.at[:, rows_at(self.half - self.row, self.half), self.cols]
        self.core = self.copies.send(away, self.r_core, self.near_by.core)

    def take(self, row, size, first, terms):
        at = rows_at(row, size)
        for i in range(terms.shape[0]):
            self.grads[first + i, at, self.cols] = add(
                self.grads[first + i, at, self.cols], terms[i]
            )

    def one(self):
        self.core.wait_recv()
        self.take(self.row, self.half, 0, self.r_core)
        self.ones = [
            self.copies.send(
                self.grads.at[pair, rows_at(away, self.quarter), self.cols],
                self.r_one.at[i], ways[0],
            )
            for i, (pair, ways, _, _, away, _) in enumerate(self.parts)
        ]

    def two(self):
        self.twos = []
        for i, (pair, ways, row, _, _, away) in enumerate(self.parts):
            self.ones[i].wait_recv()
            self.take(row, self.quarter, 2 * i, self.r_one.at[i])
            self.twos.append(
                self.copies.send(
                    self.grads.at[pair, rows_at(away, self.eighth), self.cols],
                    self.r_two.at[i], ways[1],
                )
            )

    def three(self):
        self.threes = []
        for i, (_, _, _, row, _, _) in enumerate(self.parts):
            self.twos[i].wait_recv()
            self.take(row, self.eighth, 2 * i, self.r_two.at[i])
            self.threes.append(
                [
                    self.copies.send(
                        self.z_block(self.grads, i, row, (self.zi + shift) % 4),
                        self.r_z.at[i, shift - 1], self.near_by.z[shift],
                    )
                    for shift in (1, 2, 3)
                ]
            )

    def back_three(self):
        self.threes_back = []
        for i, (_, _, _, row, _, _) in enumerate(self.parts):
            for copy in self.threes[i]:
                copy.wait_recv()
            mine = self.z_block(self.grads, i, row, self.zi)
            self.final[i] = add(mine[...], self.r_z[i, 0], self.r_z[i, 1], self.r_z[i, 2])
            place = self.z_block(self.gall, i, row, self.zi)
            own = self.copies.load(self.final.at[i], place)
            self.threes_back.append(
                (
                    own,
                    [
                        self.copies.send(self.final.at[i], place, self.near_by.z[shift])
                        for shift in (1, 2, 3)
                    ],
                )
            )

    def give(self, row, size, pair, to):
        block = self.gall.at[pair, rows_at(row, size), self.cols]
        return self.copies.send(block, block, to)

    def back_two(self):
        self.twos_back = []
        for i, (pair, ways, _, row, _, _) in enumerate(self.parts):
            own, others = self.threes_back[i]
            own.wait()
            for copy in others:
                copy.wait_recv()
            self.twos_back.append(self.give(row, self.eighth, pair, ways[1]))

    def back_one(self):
        self.ones_back = []
        for i, (pair, ways, row, _, _, _) in enumerate(self.parts):
            self.twos_back[i].wait_recv()
            self.ones_back.append(self.give(row, self.quarter, pair, ways[0]))

    def back_core(self):
        self.cores_back = []
        for i, (pair, *_) in enumerate(self.parts):
            self.ones_back[i].wait_recv()
            self.cores_back.append(self.give(self.row, self.half, pair, self.near_by.core))

    def finish(self):
        for copy in self.cores_back:
            copy.wait_recv()

    def settle(self):
        sent = [self.core, *self.ones, *self.twos, *self.threes[0], *self.threes[1]]
        self.copies.settle(sent)


PAIRS = HEADS // 2
FIRST_PAIRS = 4


def grad_columns(width):
    cut = FIRST_PAIRS * (width // PAIRS)
    return ((0, cut), (cut, width))


def back_kernel(batches, *refs):
    gb_parts, z_parts, gw, cot_in, group_ref, keep_ref, x_in, o_in, y_in, qkv_in, p_in = refs[:11]
    gain1_ref, gain2_ref, wqkv_in, wo_in = refs[11:15]
    result_out, tg_out, gall, ein_out, eout, gains_out, z_core, z_far, rs_z = refs[15:24]
    (
        wqkv, wo, x, o, y, cot, qkv, p, gb_own, gb_far, gb_core, gb_cross, gb_x,
        gy, ga, go, gqkv, grads, *sum_buffers,
        held, r_y, ein, gsum, gain_in, tok, send_sem, recv_sem, local_sem, p_sem,
    ) = refs[24:]
    width = x.shape[1]
    head_dim = width // HEADS
    pair = 2 * head_dim
    length = tok.shape[0]
    dp, expert = lax.axis_index("dp"), lax.axis_index("expert")
    core, xi, yi, zi = expert % 2, expert // 2, dp % 2, dp // 2
    copies = Copies(send_sem, recv_sem, local_sem)
    near_by = Partners()
    near_by.greet()
    load, send = copies.load, copies.send

    crossed, nearer = [], []
    for m in range(batches):
        crossed.append(send(gb_parts.at[3, m], gb_cross.at[m], near_by.core))
        nearer.append(send(gb_parts.at[1, m], gb_core.at[m], near_by.core))
    order = (6, 4, 2, 0)
    pieces = [send(gw.at[order[0] + 1], r_y.at[0], near_by.y)]
    far_loads = [load(gb_parts.at[2, m], gb_far.at[m]) for m in range(batches)]
    own_loads = [load(gb_parts.at[0, m], gb_own.at[m]) for m in range(batches)]
    first_loads = [load(y_in.at[0], y), load(cot_in.at[0], cot)]
    held_loads = [load(gw.at[order[i]], held.at[i]) for i in range(4)]
    late_loads = [load(o_in, o), load(wo_in, wo), load(qkv_in.at[0], qkv)]
    last_loads = [load(x_in, x), load(wqkv_in, wqkv)]
    def far_sum(m):
        far_loads[m].wait()
        crossed[m].wait_recv()
        gb_far[m] = add(gb_far[m], gb_cross[m])

    far_sum(0)
    along = [send(gb_far.at[0], gb_x.at[0], near_by.x)]
    z_crossed = [send(z_parts.at[3, m], z_core.at[1, m], near_by.core) for m in range(batches)]
    z_nearer = [send(z_parts.at[1, m], z_core.at[0, m], near_by.core) for m in range(batches)]
    for m in range(1, batches):
        far_sum(m)

    sent_z = []
    z_ways = (near_by.z_pair, near_by.z[2], near_by.z_pair)

    def reduce_piece(i):
        pieces[i].wait_recv()
        if i < 3:
            pieces.append(send(gw.at[order[i + 1] + 1], r_y.at[i + 1], near_by.y))
        held_loads[i].wait()
        come = {0: (), 1: (0,), 2: (), 3: (1, 2)}[i]
        for j in come:
            sent_z[j].wait_recv()
        loads = [load(rs_z.at[j], r_y.at[at]) for at, j in enumerate(come)]
        for copy in loads:
            copy.wait()
        held[i] = add(held[i], r_y[i], *[r_y[at] for at in range(len(come))])
        if i < 3:
            sent_z.append(send(held.at[i], rs_z.at[i], z_ways[i]))

    z_along = []

    def z_load(m):
        z_crossed[m].wait_recv()
        return [load(z_parts.at[2, m], gb_own.at[m]), load(z_core.at[1, m], gb_core.at[m])]

    def z_send(m, loads):
        for copy in loads:
            copy.wait()
        gb_cross[m] = add(gb_own[m], gb_core[m])
        z_along.append(send(gb_cross.at[m], z_far.at[m], near_by.x))

    sums = [
        BlockSum(
            copies, near_by, (core, xi, yi, zi), grads, gall, low, high,
            sum_buffers[i * 5 : i * 5 + 5],
        )
        for i, (low, high) in enumerate(grad_columns(width))
    ]

    def weight_gradients(group, parts):
        low, high = grad_columns(width)[group]
        for part in parts:
            if part == 3:
                product = dot(o[...], ga[:, low:high], 0, 0)
            else:
                product = dot(a[...], gqkv[:, part * width + low : part * width + high], 0, 0)
            grads[part, :, low:high] = product.astype(BF16)

    left = lax.broadcasted_iota(jnp.int32, (ITEM_ROWS, pair), 1) < head_dim
    reduce_piece(0)
    for copy in first_loads + late_loads:
        copy.wait()
    gain2_grad = jnp.zeros((1, width), F32)
    items = [slice(i * ITEM_ROWS, (i + 1) * ITEM_ROWS) for i in range(ITEMS)]
    a = ga
    for m in range(batches):
        row0 = m * ROWS

        def p_load(hp, m=m):
            return pltpu.make_async_copy(
                p_in.at[m, :, pl.ds(2 * hp, 2)], p.at[hp % 2], p_sem.at[hp % 2]
            )

        p_load(0).start()
        own_loads[m].wait()
        nearer[m].wait_recv()
        along[m].wait_recv()
        if m + 1 < batches:
            along.append(send(gb_far.at[m + 1], gb_x.at[m + 1], near_by.x))
        for rows in items:
            at = slice(row0 + rows.start, row0 + rows.stop)
            gb = (
                gb_own[m, rows].astype(F32)
                + gb_core[m, rows].astype(F32)
                + gb_x[m, rows].astype(F32)
            )
            unit2, inverse2 = normalize_parts(y[rows])
            gain2_grad = gain2_grad + jnp.sum(gb * unit2, axis=0, keepdims=True)
            gy_rows = cot[rows].astype(F32) + normalize_back(gb * gain2_ref[...], unit2, inverse2)
            gy[at] = gy_rows
            ga[at] = gy_rows.astype(BF16)
            go[rows] = dot(ga[at], wo[...], 1, 1).astype(BF16)
        if m + 1 < batches:
            first_loads = [load(y_in.at[m + 1], y), load(cot_in.at[m + 1], cot)]
        z_loads = z_load(m)

        def heads(hp, carry, row0=row0, p_load=p_load):
            @pl.when(hp + 1 < PAIRS)
            def _():
                p_load(hp + 1).start()

            p_load(hp).wait()
            slot = hp % 2
            head_gradients(
                lambda rows, cols: qkv[rows, cols],
                lambda rows, cols: go[rows, cols],
                lambda item, half: p[slot, item, half],
                gqkv, row0, hp, width, left,
            )
            return carry

        if m + 1 < batches:
            lax.fori_loop(0, PAIRS, heads, 0)
            first_loads.append(load(qkv_in.at[m + 1], qkv))
            reduce_piece(1 + m)
            z_send(m, z_loads)
            for copy in first_loads:
                copy.wait()
        else:
            z_send(m, z_loads)
            lax.fori_loop(0, FIRST_PAIRS, heads, 0)
            for copy in last_loads:
                copy.wait()
            weight_gradients(0, (3,))
            weight_gradients(1, (3,))
            for micro in range(batches):
                at = slice(micro * ROWS, (micro + 1) * ROWS)
                unit, _ = normalize_parts(x[at].astype(F32))
                a[at] = (unit * gain1_ref[...]).astype(BF16)
            weight_gradients(0, (0, 1, 2))
            sums[0].start()
            reduce_piece(2)
            lax.fori_loop(FIRST_PAIRS, PAIRS, heads, 0)
    sums[0].one()
    weight_gradients(1, (0, 1, 2))
    sums[1].start()

    gain1_grad = jnp.zeros((1, width), F32)
    between = [sums[0].two, sums[1].one, sums[0].three, sums[1].two]
    for m in range(batches):
        for rows in items:
            at = slice(m * ROWS + rows.start, m * ROWS + rows.stop)
            unit, inverse = normalize_parts(x[at].astype(F32))
            gnorm = dot(gqkv[at], wqkv[...], 1, 1)
            gain1_grad = gain1_grad + jnp.sum(gnorm * unit, axis=0, keepdims=True)
            go[rows] = (gy[at] + normalize_back(gnorm * gain1_ref[...], unit, inverse)).astype(BF16)
            if between:
                between.pop(0)()
        tok[:, m] = dot(pick_rows(group_ref, m, length).astype(BF16), go[...], 0, 0).astype(BF16)
    token_store = load(tok, tg_out)
    gsum[0] = jnp.concatenate([gain1_grad, gain2_grad, jnp.zeros((6, width), F32)], axis=0)
    gain_partners = [near_by.core, near_by.x, near_by.y, near_by.z_pair, near_by.z[2]]
    gain_sent = [send(gsum.at[0], gain_in.at[0], gain_partners[0])]

    def gain_step():
        at = len(gain_sent)
        gain_sent[-1].wait_recv()
        gsum[at] = gsum[at - 1] + gain_in[at - 1]
        if at < len(gain_partners):
            gain_sent.append(send(gsum.at[at], gain_in.at[at], gain_partners[at]))

    sums[1].three()
    reduce_piece(3)

    def join(to, own):
        at = rows_at(expert * part_rows, part_rows)
        return [own(held.at[3, :, 1], eout.at[:, at], *to), own(held.at[3, :, 0], ein.at[:, at], *to)]

    part_rows = held.shape[3]
    joined = join((near_by.x,), send)
    join_near = join((near_by.core,), send)
    join_own = join((), load)
    gain_step()

    for m in range(batches):
        z_nearer[m].wait_recv()
        z_along[m].wait_recv()
        loads = [
            load(z_parts.at[0, m], gb_own.at[m]),
            load(z_core.at[0, m], gb_core.at[m]),
            load(z_far.at[m], gb_x.at[m]),
            load(y_in.at[m], y),
        ]
        for copy in loads:
            copy.wait()
        for rows in items:
            chosen = pick_rows(group_ref, m, length, rows)
            keep = jnp.sum(jnp.where(chosen, keep_ref[m], 0.0), axis=1, keepdims=True)
            z = (
                gb_own[m, rows].astype(F32)
                + gb_core[m, rows].astype(F32)
                + gb_x[m, rows].astype(F32)
            )
            go[rows] = (y[rows] + jnp.where(keep > 0, z, 0.0)).astype(BF16)
        if m == 0:
            token_store.wait()
        tok[:, m] = dot(pick_rows(group_ref, m, length).astype(BF16), go[...], 0, 0).astype(BF16)
        if m == 0:
            sums[0].back_three()
        gain_step()
    copies.keep(tok, result_out)
    sums[1].back_three()

    gain_step()
    for block_sum in sums:
        block_sum.back_two()
    gain_step()
    copies.keep(gsum.at[len(gain_partners)], gains_out)
    for block_sum in sums:
        block_sum.back_one()
    for block_sum in sums:
        block_sum.back_core()
    opposite = rows_at((expert + 2) % 4 * part_rows, part_rows)
    for copy in joined:
        copy.wait_recv()
    join_near += [
        send(ref.at[:, opposite], ref.at[:, opposite], near_by.core) for ref in (eout, ein)
    ]
    for block_sum in sums:
        block_sum.settle()
    for copy in join_own:
        copy.wait()
    for copy in join_near:
        copy.wait_recv()
    hidden = ein.shape[1]
    for k in range(3):
        cols = pl.ds(0, hidden)
        grads[k, :, cols] = ein[k].astype(F32).T.astype(BF16)
        copies.keep(grads.at[k, :, cols], ein_out.at[k])
    for block_sum in sums:
        block_sum.finish()
    copies.finish()


def back(gb_parts, z_parts, gw, cot, group, keep, x, o, y, qkv, p, gain1, gain2, wqkv, wo):
    batches, rows, width = x.shape
    length = keep.shape[2]
    out = jax.ShapeDtypeStruct
    vmem = pl.BlockSpec(memory_space=pltpu.VMEM)
    anywhere = pl.BlockSpec(memory_space=pl.ANY)
    piece = gw.shape[1:]
    both = batches * rows
    half = width // 2
    tokens_shape = (batches, rows, width)
    slots = [tokens_shape] * 5
    scratch = [
        ((width, 3 * width), BF16),
        ((width, width), BF16),
        ((both, width), BF16),
        ((both, width), BF16),
        ((rows, width), F32),
        ((rows, width), BF16),
        ((rows, 3 * width), BF16),
        ((2, ITEMS, 2, ITEM_ROWS, ITEM_ROWS), BF16),
        *[(slot, BF16) for slot in slots],
        ((both, width), F32),
        ((both, width), BF16),
        ((rows, width), BF16),
        ((both, 3 * width), BF16),
        ((4, width, width), BF16),
        *[
            (shape, BF16)
            for low, high in grad_columns(width)
            for shape in (
                (4, half, high - low),
                (2, 2, half // 2, high - low),
                (2, 2, half // 4, high - low),
                (2, 3, half // 4, (high - low) // 2),
                (2, half // 4, (high - low) // 2),
            )
        ],
        ((4,) + piece, BF16),
        ((4,) + piece, BF16),
        ((3, 4 * piece[2], width), BF16),
        ((6, 8, width), F32),
        ((5, 8, width), F32),
        ((length, batches, width), BF16),
    ]
    return pl.pallas_call(
        functools.partial(back_kernel, batches),
        in_specs=[anywhere] * 4 + [vmem] * 2 + [anywhere] * 5 + [vmem] * 2 + [anywhere] * 2,
        out_specs=[anywhere] * 9,
        out_shape=[
            out((length, batches, width), BF16),
            out((length, batches, width), BF16),
            out((4, width, width), BF16),
            out((3, width, 4 * piece[2]), BF16),
            out((3, 4 * piece[2], width), BF16),
            out((8, width), F32),
            out((2,) + tokens_shape, BF16),
            out(tokens_shape, BF16),
            out((3,) + piece, BF16),
        ],
        scratch_shapes=[pltpu.VMEM(*k) for k in scratch]
        + [
            pltpu.SemaphoreType.DMA((80,)),
            pltpu.SemaphoreType.DMA((80,)),
            pltpu.SemaphoreType.DMA((64,)),
            pltpu.SemaphoreType.DMA((2,)),
        ],
        compiler_params=pltpu.CompilerParams(
            vmem_limit_bytes=VMEM_LIMIT, has_side_effects=True, collective_id=1
        ),
        cost_estimate=pl.CostEstimate(
            flops=batches
            * (2 * rows * width * width * 8 + 16 * HEADS * ITEMS * ITEM_ROWS**2 * 128),
            bytes_accessed=80_000_000,
            transcendentals=0,
        ),
        name="back",
    )(
        gb_parts, z_parts, gw, cot, group, keep,
        x.reshape(both, width), o.reshape(both, width), y, qkv, p, gain1, gain2, wqkv, wo,
    )


def attention_backward_kernel(n_parts, n_carry, *refs):
    parts = refs[:n_parts]
    (cot_ref, x_ref, y_ref, qkv_ref, p_ref, o_ref, gain1_ref, gain2_ref, wqkv_ref, wo_ref) = refs[
        n_parts : n_parts + 10
    ]
    carried = refs[n_parts + 10 : n_parts + 10 + n_carry]
    tg_ref, gwqkv_ref, gwo_ref, ggain_ref, gmix_ref, gqkv_ref = refs[n_parts + 10 + n_carry :]
    width = x_ref.shape[1]
    head_dim = width // HEADS
    gb = parts[0][...].astype(F32)
    for part in parts[1:]:
        gb = gb + part[...].astype(F32)
    unit2, inverse2 = normalize_parts(y_ref[...])
    gain2_grad = jnp.sum(gb * unit2, axis=0, keepdims=True)
    gy = cot_ref[...].astype(F32) + normalize_back(gb * gain2_ref[...], unit2, inverse2)
    ga = gy.astype(BF16)
    gwo = dot(o_ref[...], ga, 0, 0)
    if n_carry:
        gwo = gwo + carried[1][...]
    gwo_ref[...] = gwo
    gmix_ref[...] = dot(ga, wo_ref[...], 1, 1).astype(BF16)
    pair = 2 * head_dim
    left = lax.broadcasted_iota(jnp.int32, (ITEM_ROWS, pair), 1) < head_dim

    def heads(hp, carry):
        head_gradients(
            lambda rows, cols: qkv_ref[rows, cols],
            lambda rows, cols: gmix_ref[rows, cols],
            lambda item, half: p_ref[item, hp * 2 + half],
            gqkv_ref, 0, hp, width, left,
        )
        return carry

    lax.fori_loop(0, HEADS // 2, heads, 0)
    unit, inverse = normalize_parts(x_ref[...].astype(F32))
    a = (unit * gain1_ref[...]).astype(BF16)
    for part in range(3):
        cols = slice(part * width, (part + 1) * width)
        gw = dot(a, gqkv_ref[:, cols], 0, 0)
        if n_carry:
            gw = gw + carried[0][:, cols]
        gwqkv_ref[:, cols] = gw
    gnorm = dot(gqkv_ref[...], wqkv_ref[...], 1, 1)
    gain1_grad = jnp.sum(gnorm * unit, axis=0, keepdims=True)
    gains = jnp.concatenate([gain1_grad, gain2_grad, jnp.zeros((6, width), F32)], axis=0)
    if n_carry:
        gains = gains + carried[2][...]
    ggain_ref[...] = gains
    tg_ref[...] = (gy + normalize_back(gnorm * gain1_ref[...], unit, inverse)).astype(BF16)


def attention_backward(parts, cot, x, y, qkv, p, o, gain1, gain2, wqkv, wo, carried):
    rows, width = x.shape
    out = jax.ShapeDtypeStruct
    return pl.pallas_call(
        functools.partial(attention_backward_kernel, len(parts), len(carried)),
        out_shape=(
            out((rows, width), BF16),
            out((width, 3 * width), F32),
            out((width, width), F32),
            out((8, width), F32),
        ),
        scratch_shapes=[pltpu.VMEM((rows, width), BF16), pltpu.VMEM((rows, 3 * width), BF16)],
        compiler_params=pltpu.CompilerParams(vmem_limit_bytes=VMEM_LIMIT),
        cost_estimate=pl.CostEstimate(
            flops=2 * rows * width * width * 8 + 16 * HEADS * ITEMS * ITEM_ROWS**2 * 128,
            bytes_accessed=30_000_000,
            transcendentals=0,
        ),
        name="attention_backward",
    )(*parts, cot, x, y, qkv, p, o, gain1, gain2, wqkv, wo, *carried)


def expert_kernel(groups, batches, pieces, *refs):
    flags, own_ref, more_ref, b_in, g_in, z_out, gb_out, gw_out = refs[:8]
    rows_b, rows_g, w, grads, in_sem, w_sem, out_sem, gw_sem = refs[8:]
    part = own_ref.shape[2]

    def rounded(rows):
        return (rows + TILE - 1) // TILE * TILE

    merged = [
        flags[g, 0, micro * ITEMS + item]
        for g in range(groups)
        for micro in range(batches)
        for item in range(ITEMS)
    ]
    n_merged = sum(merged)
    n_plain = len(merged) - n_merged
    sizes = [n_plain * IMAGE_ROWS, n_plain * CAPTION, n_merged * ITEM_ROWS]
    starts = [0, rounded(sizes[0]), rounded(sizes[0]) + rounded(sizes[1])]
    ends = [start + rounded(size) for start, size in zip(starts, sizes)]
    blocks = []
    plain, joined = 0, 0
    for flat, flag in enumerate(merged):
        g, micro, item = flat // (batches * ITEMS), flat // ITEMS % batches, flat % ITEMS
        base = item * ITEM_ROWS
        image = jnp.where(flag == 1, starts[2] + joined * ITEM_ROWS, plain * IMAGE_ROWS)
        caption = jnp.where(
            flag == 1, image + IMAGE_ROWS, starts[1] + plain * CAPTION
        )
        blocks.append((g, micro, base, IMAGE_ROWS, image, flag, 0))
        blocks.append((g, micro, base + IMAGE_ROWS, CAPTION, caption, flag, 1))
        plain, joined = plain + 1 - flag, joined + flag

    def copy_of(which, number, outward):
        g, micro, base, size, at, _, _ = blocks[number]
        held = (rows_b, rows_g)[which].at[pl.ds(pl.multiple_of(at, 16), size)]
        if outward:
            far = (gb_out, z_out)[which].at[g, micro, pl.ds(base, size)]
            return pltpu.make_async_copy(held, far, out_sem.at[which, number])
        far = (b_in, g_in)[which].at[g, micro, pl.ds(base, size)]
        return pltpu.make_async_copy(far, held, in_sem.at[which, number])

    def of_expert(expert, act):
        for number, (_, _, _, _, _, flag, kind) in enumerate(blocks):
            if expert == 2 or kind == expert:
                @pl.when(flag == (1 if expert == 2 else 0))
                def _(number=number):
                    for which in range(2):
                        act(which, number)

    def weight_copy(k, i):
        piece = own_ref if i == 0 else more_ref.at[i - 1]
        return pltpu.make_async_copy(
            piece.at[k], w.at[k, :, pl.ds(i * part, part), :], w_sem.at[k, i]
        )

    for k in range(3):
        tail = pl.multiple_of(jnp.maximum(ends[k] - TILE, 0), TILE)
        rows_b[pl.ds(tail, TILE), :] = jnp.zeros((TILE, rows_b.shape[1]), BF16)
        rows_g[pl.ds(tail, TILE), :] = jnp.zeros((TILE, rows_g.shape[1]), BF16)
    for k in range(3):
        of_expert(k, lambda which, number: copy_of(which, number, False).start())
        for i in range(pieces):
            weight_copy(k, i).start()

    for k in range(3):
        grads[...] = jnp.zeros(grads.shape, F32)
        of_expert(k, lambda which, number: copy_of(which, number, False).wait())
        for i in range(pieces):
            weight_copy(k, i).wait()

        def tile(t, carry, k=k):
            at = pl.ds(pl.multiple_of(t * TILE, TILE), TILE)
            b, gz = rows_b[at, :], rows_g[at, :]
            u, slope = gelu_and_slope(dot(b, w[k, 0], 1, 1))
            gh = (dot(gz, w[k, 1], 1, 1) * slope).astype(BF16)
            u = u.astype(BF16)
            z, gb = dot(u, w[k, 1], 1, 0), dot(gh, w[k, 0], 1, 0)
            grads[0] += dot(gh, b, 0, 0)
            grads[1] += dot(u, gz, 0, 0)
            rows_b[at, :] = gb.astype(BF16)
            rows_g[at, :] = z.astype(BF16)
            return carry

        lax.fori_loop(starts[k] // TILE, ends[k] // TILE, tile, 0)
        of_expert(k, lambda which, number: copy_of(which, number, True).start())
        w[k] = grads[...].astype(BF16)
        for i in range(pieces):
            pltpu.make_async_copy(
                w.at[k, :, pl.ds(i * part, part), :], gw_out.at[i, k], gw_sem.at[k, i]
            ).start()
    for number in range(len(blocks)):
        for which in range(2):
            copy_of(which, number, True).wait()
    for k in range(3):
        for i in range(pieces):
            pltpu.make_async_copy(
                w.at[k, :, pl.ds(i * part, part), :], gw_out.at[i, k], gw_sem.at[k, i]
            ).wait()


def experts(flags, own, more, b_groups, g_groups):
    groups, batches, rows, width = b_groups.shape
    part = own.shape[2]
    pieces = 1 + (more.shape[0] if more.ndim == 5 else 0)
    hidden = part * pieces
    count = groups * batches * ITEMS
    capacity = (count * ITEM_ROWS // TILE + 4) * TILE
    out = jax.ShapeDtypeStruct
    anywhere = pl.BlockSpec(memory_space=pl.ANY)
    return pl.pallas_call(
        functools.partial(expert_kernel, groups, batches, pieces),
        in_specs=[pl.BlockSpec(memory_space=pltpu.SMEM)] + [anywhere] * 4,
        out_specs=[anywhere] * 3,
        out_shape=[out(b_groups.shape, BF16)] * 2 + [out((pieces,) + own.shape, BF16)],
        scratch_shapes=[
            pltpu.VMEM((capacity, width), BF16),
            pltpu.VMEM((capacity, width), BF16),
            pltpu.VMEM((3, 2, hidden, width), BF16),
            pltpu.VMEM((2, hidden, width), F32),
            pltpu.SemaphoreType.DMA((2, 2 * count)),
            pltpu.SemaphoreType.DMA((3, pieces)),
            pltpu.SemaphoreType.DMA((2, 2 * count)),
            pltpu.SemaphoreType.DMA((3, pieces)),
        ],
        compiler_params=pltpu.CompilerParams(vmem_limit_bytes=VMEM_LIMIT),
        cost_estimate=pl.CostEstimate(
            flops=2 * 6 * count * ITEM_ROWS * width * hidden,
            bytes_accessed=45_000_000,
            transcendentals=count * ITEM_ROWS * hidden,
        ),
        name="experts",
    )(flags, own, more, b_groups, g_groups)


def from_items(rows, first):
    one, two = rows[IMAGE_ROWS:ITEM_ROWS], rows[ITEM_ROWS + IMAGE_ROWS :]
    return jnp.concatenate(
        [
            rows[:PATCHES],
            rows[ITEM_ROWS : ITEM_ROWS + PATCHES],
            jnp.where(first, one, two),
            jnp.where(first, two, one),
        ],
        axis=0,
    )


class Links:
    def __init__(self):
        self.hosts = lax.axis_size("expert")
        self.dp = lax.axis_size("dp")
        self.direct = self.hosts == 4 and self.dp == 8
        self.me = lax.axis_index("expert")

    def flip(self, v, bit):
        return lax.ppermute(v, "expert", [(i, i ^ bit) for i in range(4)])

    def across_y(self, v):
        return lax.ppermute(v, "dp", [(i, i ^ 1) for i in range(8)])

    def along_z(self, v, shift):
        return lax.ppermute(v, "dp", [(i, (i + 2 * shift) % 8) for i in range(8)])

    def gather_tokens(self, v):
        if not self.direct:
            return list(lax.all_gather(v, "expert"))
        near, far = self.flip(v, 1), self.flip(v, 2)
        return [v, near, far, self.flip(far, 1)]

    def reduce_tokens(self, parts):
        if not self.direct:
            return [lax.psum_scatter(jnp.stack(parts), "expert", scatter_dimension=0)]
        far = (parts[2].astype(F32) + self.flip(parts[3], 1).astype(F32)).astype(BF16)
        return [parts[0], self.flip(parts[1], 1), self.flip(far, 2)]

    def reduce_weights(self, pieces):
        if not self.direct:
            return lax.psum_scatter(pieces[0], "dp", scatter_dimension=2, tiled=True)
        total = None
        for at, shift in enumerate((0, 1, 3, 2)):
            piece = pieces[2 * at].astype(F32) + self.across_y(pieces[2 * at + 1]).astype(F32)
            if shift:
                piece = self.along_z(piece.astype(BF16), -shift).astype(F32)
            total = piece if total is None else total + piece
        return total.astype(BF16)

    def join_hidden(self, v):
        if not self.direct:
            return lax.all_gather(v, "expert", axis=2, tiled=True)
        stacked = jnp.stack(self.gather_tokens(v))
        return jnp.concatenate(
            [
                lax.dynamic_index_in_dim(stacked, i ^ self.me, 0, keepdims=False)
                for i in range(4)
            ],
            axis=2,
        )


def shards(
    tokens,
    cotangent,
    item_group,
    routes,
    slot_order,
    attn_gain,
    ffn_gain,
    qkv_weight,
    out_weight,
    expert_in,
    expert_out,
):
    links = Links()
    hosts, me = links.hosts, links.me
    batches, length, width = tokens.shape
    shard = expert_in.shape[2]
    part = shard // hosts
    gain1, gain2 = attn_gain[None, :], ffn_gain[None, :]

    own = jnp.stack(
        [
            jnp.swapaxes(lax.dynamic_slice_in_dim(expert_in, me * part, part, 2), 1, 2),
            lax.dynamic_slice_in_dim(expert_out, me * part, part, 1),
        ],
        axis=1,
    )
    first = item_group[:, ITEMS * PATCHES] == 0
    (
        w_all, gz_groups, flag_groups, b_groups, x_all, qkv_all, p_all, o_all, y_all, cot_all, kept
    ) = front(
        links.direct, hosts, own, jnp.swapaxes(tokens, 0, 1), jnp.swapaxes(cotangent, 0, 1),
        item_group, routes, slot_order, gain1, gain2, qkv_weight, out_weight,
    )
    if not links.direct:
        own = lax.all_gather(own, "dp", axis=2, tiled=True)
        gz_groups, flag_groups, b_groups = [
            lax.all_gather(v[0], "expert") for v in (gz_groups, flag_groups, b_groups)
        ]
    z_parts, gb_parts, gw_pieces = experts(flag_groups, own, w_all, b_groups, gz_groups)
    if links.direct:
        result, token_grad, gall, ein_sum, eout_sum, gains, *_ = back(
            gb_parts, z_parts, gw_pieces, cot_all, item_group, kept,
            x_all, o_all, y_all, qkv_all, p_all, gain1, gain2, qkv_weight, out_weight,
        )
        return (
            jnp.swapaxes(result, 0, 1),
            jnp.swapaxes(token_grad, 0, 1),
            gains[0],
            gains[1],
            jnp.concatenate([gall[i].astype(F32) for i in range(3)], axis=1),
            gall[3].astype(F32),
            ein_sum.astype(F32),
            eout_sum.astype(F32),
        )
    gb_terms = links.reduce_tokens(gb_parts)
    z_terms = links.reduce_tokens(z_parts)
    sums = links.join_hidden(links.reduce_weights(gw_pieces)).astype(F32)

    results, token_grads, carried = [], [], ()
    for m in range(batches):
        x, qkv, p, o, y = x_all[m], qkv_all[m], p_all[m], o_all[m], y_all[m]
        at = m
        tg, *carried = attention_backward(
            [t[at] for t in gb_terms],
            cot_all[m], x, y, qkv, p, o, gain1, gain2, qkv_weight, out_weight,
            tuple(carried),
        )
        token_grads.append(from_items(tg, first[m]))
        z = z_terms[0][at].astype(F32)
        for term in z_terms[1:]:
            z = z + term[at].astype(F32)
        branch = jnp.where(kept[m, 0][:, None] > 0, from_items(z, first[m]), 0.0)
        results.append((from_items(y, first[m]) + branch).astype(BF16))
    gw_qkv, gw_out, gains = carried
    packed = jnp.concatenate(
        [
            jnp.concatenate([gw_qkv, gw_out], axis=1),
            jnp.pad(gains[:2].reshape(1, 2 * width), ((0, 7), (0, 2 * width))),
        ],
        axis=0,
    ).astype(BF16)
    packed = lax.psum(packed, ("dp", "expert")).astype(F32)
    return (
        jnp.stack(results),
        jnp.stack(token_grads),
        packed[width, :width],
        packed[width, width : 2 * width],
        packed[:width, : 3 * width],
        packed[:width, 3 * width :],
        jnp.swapaxes(sums[:, 0], 1, 2),
        sums[:, 1],
    )


def solution(mesh):
    in_specs = (
        P(None, ("dp", "expert"), None),
        P(None, ("dp", "expert"), None),
        P(None, ("dp", "expert")),
        P(None, ("dp", "expert")),
        P(None, ("dp", "expert"), None),
        P(),
        P(),
        P(),
        P(),
        P(None, None, "dp"),
        P(None, "dp", None),
    )
    out_specs = (
        P(None, ("dp", "expert"), None),
        P(None, ("dp", "expert"), None),
        P(),
        P(),
        P(),
        P(),
        P(None, None, "dp"),
        P(None, "dp", None),
    )
    return jax.shard_map(shards, mesh=mesh, in_specs=in_specs, out_specs=out_specs, check_vma=False)
```

```python
import functools

import jax
import jax.numpy as jnp
from jax import lax
from jax.experimental import pallas as pl
from jax.experimental.pallas import tpu as pltpu
from jax.sharding import PartitionSpec as P

HEADS = 12
EPSILON = 1e-05
PATCHES = 197
CAPTION = 64
ITEMS = 2
IMAGE_ROWS = 208
ITEM_ROWS = IMAGE_ROWS + CAPTION
ROWS = ITEMS * ITEM_ROWS
TILE = 256
VMEM_LIMIT = 60 * 1024 * 1024
F32 = jnp.float32
BF16 = jnp.bfloat16


def dot(a, b, a_dim, b_dim):
    return lax.dot_general(
        a, b, (((a_dim,), (b_dim,)), ((), ())), preferred_element_type=F32
    )


def normalize_parts(v):
    centred = v - jnp.mean(v, axis=-1, keepdims=True)
    inverse = lax.rsqrt(jnp.mean(centred * centred, axis=-1, keepdims=True) + EPSILON)
    return centred * inverse, inverse


def normalize_back(grad_unit, unit_rows, inverse):
    return inverse * (
        grad_unit
        - jnp.mean(grad_unit, axis=-1, keepdims=True)
        - unit_rows * jnp.mean(grad_unit * unit_rows, axis=-1, keepdims=True)
    )


def gelu_and_slope(h):
    bell = jnp.exp2(h * h * (-0.5 * 1.4426950408889634))
    t = pl.reciprocal(1.0 + (0.3275911 * 0.7071067811865476) * jnp.abs(h))
    half_poly = t * (
        0.127414796
        + t * (-0.142248368 + t * (0.7107068705 + t * (-0.7265760135 + t * 0.5307027145)))
    )
    below = half_poly * bell
    phi = jnp.where(h > 0, 1.0 - below, below)
    return h * phi, phi + (h * bell) * 0.3989422804014327


class Partners:
    def __init__(self):
        dp, expert = lax.axis_index("dp"), lax.axis_index("expert")
        self.core = (dp, expert + 1 - 2 * (expert % 2))
        self.x = (dp, (expert + 2) % 4)
        self.y = (dp + 1 - 2 * (dp % 2), expert)
        self.z = {shift: ((dp + 2 * shift) % 8, expert) for shift in (1, 2, 3)}
        self.z_pair = (dp + 2 - 4 * (dp // 2 % 2), expert)

    def greet(self):
        barrier = pltpu.get_barrier_semaphore()
        everyone = [self.core, self.x, self.y, self.z[1], self.z[2], self.z[3]]
        for other in everyone:
            pl.semaphore_signal(
                barrier, inc=1, device_id=other, device_id_type=pl.DeviceIdType.MESH
            )
        pl.semaphore_wait(barrier, len(everyone))


class Copies:
    def __init__(self, send_sem, recv_sem, local_sem):
        self.send_sem, self.recv_sem, self.local_sem = send_sem, recv_sem, local_sem
        self.sent, self.kept, self.sends, self.locals = [], [], 0, 0

    def send(self, src, dst, device):
        at = self.sends
        self.sends += 1
        copy = pltpu.make_async_remote_copy(
            src_ref=src,
            dst_ref=dst,
            send_sem=self.send_sem.at[at],
            recv_sem=self.recv_sem.at[at],
            device_id=device,
            device_id_type=pl.DeviceIdType.MESH,
        )
        copy.start()
        self.sent.append(copy)
        return copy

    def keep(self, src, dst):
        copy = self.load(src, dst)
        self.kept.append(copy)
        return copy

    def load(self, src, dst):
        copy = pltpu.make_async_copy(src, dst, self.local_sem.at[self.locals])
        self.locals += 1
        copy.start()
        return copy

    def settle(self, done):
        for copy in done:
            copy.wait_send()
        self.sent = [copy for copy in self.sent if all(copy is not other for other in done)]

    def finish(self):
        for copy in self.sent:
            copy.wait_send()
        for copy in self.kept:
            copy.wait()


def pick_rows(group_ref, m, length, rows=slice(0, ROWS)):
    count = rows.stop - rows.start
    row = lax.broadcasted_iota(jnp.int32, (count, 1), 0) + rows.start
    item = (row >= ITEM_ROWS).astype(jnp.int32)
    inside = row - item * ITEM_ROWS
    images = ITEMS * PATCHES
    swapped = (group_ref[m : m + 1, images : images + 1] != 0).astype(jnp.int32)
    caption = item + swapped - 2 * item * swapped
    token = jnp.where(
        inside < PATCHES,
        item * PATCHES + inside,
        jnp.where(inside < IMAGE_ROWS, -1, images + caption * CAPTION + inside - IMAGE_ROWS),
    )
    return lax.broadcasted_iota(jnp.int32, (count, length), 1) == token


def kept_tokens(routing, priority, hosts, capacity):
    length = routing.shape[1]
    across = lax.broadcasted_iota(jnp.int32, (length, length), 1)
    down = lax.broadcasted_iota(jnp.int32, (length, length), 0)

    def upright(row):
        return jnp.sum(jnp.where(across == down, row, 0.0), axis=1, keepdims=True)

    order = upright(priority.astype(F32))
    position = jnp.sum(
        jnp.where(order == across.astype(F32), down.astype(F32), 0.0), axis=0, keepdims=True
    )
    route = routing.astype(F32)
    ahead = (upright(route) == route) & (upright(position) < position)
    rank = jnp.sum(jnp.where(ahead, 1.0, 0.0), axis=0, keepdims=True)
    slots = jnp.zeros_like(rank)
    for kind in range(3):
        slots = jnp.where(routing == kind, float(capacity * ((hosts - kind + 2) // 3)), slots)
    return jnp.where(rank < slots, 1.0, 0.0)


def front_kernel(direct, hosts, batches, *refs):
    (own_ref, tokens_ref, cot_ref, group_ref, routes_ref, order_ref, gain1_ref, gain2_ref) = refs[:8]
    wqkv_ref, wo_ref, w_all, gz_all, flags_all, b_all = refs[8:14]
    x_out, qkv_out, p_out, o_out, y_out, cot_out = refs[14:20]
    (
        keep_ref, gz_scr, b_scr, x_scr, qkv_scr, p_scr, o_scr, y_scr, cot_scr, flags_scr,
        send_sem, recv_sem, local_sem,
    ) = refs[20:]
    length, _, width = tokens_ref.shape
    head_dim = width // HEADS
    pair = 2 * head_dim
    copies = Copies(send_sem, recv_sem, local_sem)

    def spread(src, slots):
        copies.keep(src, slots(0))
        if not direct:
            return None
        near = copies.send(src, slots(1), near_by.core)
        return near, copies.send(src, slots(2), near_by.x)

    def pass_on(pair_of, slots):
        near, far = pair_of
        far.wait_recv()
        return near, copies.send(slots(2), slots(3), near_by.core)

    if direct:
        near_by = Partners()
        near_by.greet()
        over_y = [copies.send(own_ref, w_all.at[0], near_by.y)]
        along = [[], [], []]

        def z_half(i):
            along[0].append(copies.send(own_ref.at[:, i], w_all.at[1, :, i], near_by.z_pair))
            along[1].append(copies.send(own_ref.at[:, i], w_all.at[3, :, i], near_by.z[2]))

        def z_pass(i):
            for k in (1, 0):
                along[k][i].wait_recv()
                if k == 1:
                    along[2].append(
                        copies.send(w_all.at[3, :, i], w_all.at[5, :, i], near_by.z_pair)
                    )
                at = 2 * k + 1
                over_y.append(copies.send(w_all.at[at, :, i], w_all.at[at + 1, :, i], near_by.y))

        def z_last(i):
            along[2][i].wait_recv()
            over_y.append(copies.send(w_all.at[5, :, i], w_all.at[6, :, i], near_by.y))

        z_half(0)
    lane = lax.broadcasted_iota(jnp.int32, flags_scr.shape, 1)
    merged = jnp.zeros(flags_scr.shape, jnp.int32)
    for m in range(batches):
        for item in range(ITEMS):
            route = routes_ref[m : m + 1, item * PATCHES : item * PATCHES + 1]
            here = lane == m * ITEMS + item
            merged = jnp.where(here & (route == 2), 1, merged)
    flags_scr[...] = merged
    flags = spread(flags_scr, lambda i: flags_all.at[i])

    for m in range(batches):
        keep_ref[m] = kept_tokens(
            routes_ref[m : m + 1], order_ref[m], hosts, 2 * length // hosts
        )
        chosen = pick_rows(group_ref, m, length) & (keep_ref[m] > 0)
        gz_scr[m] = dot(chosen.astype(BF16), cot_ref[:, m], 1, 0).astype(BF16)
    gz = spread(gz_scr, lambda i: gz_all.at[i])

    left = lax.broadcasted_iota(jnp.int32, (ITEM_ROWS, pair), 1) < head_dim
    key = lax.broadcasted_iota(jnp.int32, (1, ITEM_ROWS), 1)
    bias = jnp.where((key >= PATCHES) & (key < IMAGE_ROWS), -1e30, 0.0).astype(F32)
    b_sent = []
    for m in range(batches):
        xb = dot(pick_rows(group_ref, m, length).astype(BF16), tokens_ref[:, m], 1, 0)
        x_scr[m] = xb.astype(BF16)
        unit, _ = normalize_parts(xb)
        a = (unit * gain1_ref[...]).astype(BF16)
        for part in range(3):
            cols = slice(part * width, (part + 1) * width)
            qkv_scr[m, :, cols] = dot(a, wqkv_ref[:, cols], 1, 0).astype(BF16)

        def heads(hp, carry, m=m):
            at_q = pl.ds(pl.multiple_of(hp * pair, pair), pair)
            at_k = pl.ds(pl.multiple_of(width + hp * pair, pair), pair)
            at_v = pl.ds(pl.multiple_of(2 * width + hp * pair, pair), pair)
            for item in range(ITEMS):
                rows = slice(item * ITEM_ROWS, (item + 1) * ITEM_ROWS)
                q, k, v = qkv_scr[m, rows, at_q], qkv_scr[m, rows, at_k], qkv_scr[m, rows, at_v]
                outs = []
                for half in range(2):
                    mine = left if half == 0 else ~left
                    s = dot(jnp.where(mine, q, 0), k, 1, 1) * (head_dim**-0.5) + bias
                    e = jnp.exp(s - jnp.max(s, axis=-1, keepdims=True))
                    p = (e * (1.0 / jnp.sum(e, axis=-1, keepdims=True))).astype(BF16)
                    p_scr[m, item, hp * 2 + half] = p
                    outs.append(dot(p, v, 1, 0))
                o_scr[m, rows, at_q] = jnp.where(left, outs[0], outs[1]).astype(BF16)
            return carry

        lax.fori_loop(0, HEADS // 2, heads, 0)
        y = x_scr[m].astype(F32) + dot(o_scr[m], wo_ref[...], 1, 0)
        y_scr[m] = y
        cot_scr[m] = dot(pick_rows(group_ref, m, length).astype(BF16), cot_ref[:, m], 1, 0).astype(
            BF16
        )
        unit2, _ = normalize_parts(y)
        b_scr[m] = (unit2 * gain2_ref[...]).astype(BF16)
        b_sent.append(spread(b_scr.at[m], lambda i, m=m: b_all.at[i, m]))
        for scr, out in (
            (x_scr, x_out), (qkv_scr, qkv_out), (p_scr, p_out), (o_scr, o_out), (y_scr, y_out),
            (cot_scr, cot_out),
        ):
            copies.keep(scr.at[m], out.at[m])
        if direct and m == 0:
            z_pass(0)
            z_half(1)
            flags = pass_on(flags, lambda i: flags_all.at[i])

    if direct:
        z_pass(1)
        z_last(0)
        gz = pass_on(gz, lambda i: gz_all.at[i])
        b_sent[0] = pass_on(b_sent[0], lambda i: b_all.at[i, 0])
        z_last(1)
        for m in range(1, batches):
            b_sent[m] = pass_on(b_sent[m], lambda i, m=m: b_all.at[i, m])
        for copy in [*over_y, *flags, *gz] + [c for pair_of in b_sent for c in pair_of]:
            copy.wait_recv()
    copies.finish()


def front(direct, hosts, own, tokens, cot, group, routes, order, gain1, gain2, wqkv, wo):
    length, batches, width = tokens.shape
    groups = 4 if direct else 1
    out = jax.ShapeDtypeStruct
    vmem = pl.BlockSpec(memory_space=pltpu.VMEM)
    anywhere = pl.BlockSpec(memory_space=pl.ANY)
    kept = [
        ((batches, ROWS, width), BF16),
        ((batches, ROWS, 3 * width), BF16),
        ((batches, ITEMS, HEADS, ITEM_ROWS, ITEM_ROWS), BF16),
        ((batches, ROWS, width), BF16),
        ((batches, ROWS, width), F32),
        ((batches, ROWS, width), BF16),
    ]
    scratch = [pltpu.VMEM((batches, ROWS, width), BF16)] * 2
    return pl.pallas_call(
        functools.partial(front_kernel, direct, hosts, batches),
        in_specs=[anywhere] + [vmem] * 9,
        out_specs=[anywhere] * 10 + [vmem],
        out_shape=[
            out((7 if direct else 1,) + (own.shape if direct else (8, 128)), BF16),
            out((groups, batches, ROWS, width), BF16),
            out((groups, 8, 128), jnp.int32),
            out((groups, batches, ROWS, width), BF16),
        ]
        + [out(*k) for k in kept]
        + [out((batches, 1, length), F32)],
        scratch_shapes=scratch
        + [pltpu.VMEM(*k) for k in kept]
        + [
            pltpu.VMEM((8, 128), jnp.int32),
            pltpu.SemaphoreType.DMA((32,)),
            pltpu.SemaphoreType.DMA((32,)),
            pltpu.SemaphoreType.DMA((24,)),
        ],
        compiler_params=pltpu.CompilerParams(
            vmem_limit_bytes=VMEM_LIMIT,
            has_side_effects=direct,
            collective_id=0 if direct else None,
        ),
        cost_estimate=pl.CostEstimate(
            flops=batches
            * (2 * ROWS * width * width * 4 + 8 * HEADS * ITEMS * ITEM_ROWS**2 * 128),
            bytes_accessed=60_000_000,
            transcendentals=batches * HEADS * ITEMS * ITEM_ROWS**2,
        ),
        name="front",
    )(own, tokens, cot, group, routes, order, gain1, gain2, wqkv, wo)


def head_gradients(qkv_at, go_at, p_of, gqkv_ref, row0, hp, width, left):
    head_dim = width // HEADS
    pair = 2 * head_dim
    scaling = head_dim**-0.5
    at_q = pl.ds(pl.multiple_of(hp * pair, pair), pair)
    at_k = pl.ds(pl.multiple_of(width + hp * pair, pair), pair)
    at_v = pl.ds(pl.multiple_of(2 * width + hp * pair, pair), pair)
    for item in range(ITEMS):
        rows = slice(item * ITEM_ROWS, (item + 1) * ITEM_ROWS)
        out_rows = slice(row0 + rows.start, row0 + rows.stop)
        q, k, v = qkv_at(rows, at_q), qkv_at(rows, at_k), qkv_at(rows, at_v)
        go = go_at(rows, at_q)
        gq, gk, gv = [], [], []
        for half in range(2):
            mine = left if half == 0 else ~left
            p = p_of(item, half)
            pf = p.astype(F32)
            gp = dot(jnp.where(mine, go, 0), v, 1, 1)
            gs = (pf * (gp - jnp.sum(pf * gp, axis=-1, keepdims=True))).astype(BF16)
            gv.append(dot(p, go, 0, 0))
            gq.append(dot(gs, k, 1, 0))
            gk.append(dot(gs, q, 0, 0))
        gqkv_ref[out_rows, at_q] = (jnp.where(left, gq[0], gq[1]) * scaling).astype(BF16)
        gqkv_ref[out_rows, at_k] = (jnp.where(left, gk[0], gk[1]) * scaling).astype(BF16)
        gqkv_ref[out_rows, at_v] = jnp.where(left, gv[0], gv[1]).astype(BF16)


def add(*terms):
    total = terms[0].astype(F32)
    for term in terms[1:]:
        total = total + term.astype(F32)
    return total.astype(BF16)


def rows_at(start, size):
    return pl.ds(pl.multiple_of(start, 32), size)


class BlockSum:
    def __init__(self, copies, near_by, place, grads, gall, low, high, buffers):
        self.copies, self.near_by, self.grads, self.gall = copies, near_by, grads, gall
        self.r_core, self.r_one, self.r_two, self.r_z, self.final = buffers
        self.low, self.size = low, high - low
        self.cols = pl.ds(low, high - low)
        core, xi, yi, self.zi = place
        self.half = grads.shape[1] // 2
        self.quarter, self.eighth = self.half // 2, self.half // 4
        self.row = core * self.half
        self.parts = []
        for part, (one, two) in enumerate(((xi, yi), (yi, xi))):
            pair = pl.ds(2 * part, 2)
            ways = (near_by.x, near_by.y) if part == 0 else (near_by.y, near_by.x)
            row_one = self.row + one * self.quarter
            row_two = row_one + two * self.eighth
            away_one = self.row + (1 - one) * self.quarter
            away_two = row_one + (1 - two) * self.eighth
            self.parts.append((pair, ways, row_one, row_two, away_one, away_two))

    def z_block(self, ref, part, row, z):
        chunk = self.size // 2
        cols = pl.ds(pl.multiple_of(self.low + z % 2 * chunk, 128), chunk)
        return ref.at[2 * part + z // 2, rows_at(row, self.eighth), cols]

    def start(self):
        away = self.grads.at[:, rows_at(self.half - self.row, self.half), self.cols]
        self.core = self.copies.send(away, self.r_core, self.near_by.core)

    def take(self, row, size, first, terms):
        at = rows_at(row, size)
        for i in range(terms.shape[0]):
            self.grads[first + i, at, self.cols] = add(
                self.grads[first + i, at, self.cols], terms[i]
            )

    def one(self):
        self.core.wait_recv()
        self.take(self.row, self.half, 0, self.r_core)
        self.ones = [
            self.copies.send(
                self.grads.at[pair, rows_at(away, self.quarter), self.cols],
                self.r_one.at[i], ways[0],
            )
            for i, (pair, ways, _, _, away, _) in enumerate(self.parts)
        ]

    def two(self):
        self.twos = []
        for i, (pair, ways, row, _, _, away) in enumerate(self.parts):
            self.ones[i].wait_recv()
            self.take(row, self.quarter, 2 * i, self.r_one.at[i])
            self.twos.append(
                self.copies.send(
                    self.grads.at[pair, rows_at(away, self.eighth), self.cols],
                    self.r_two.at[i], ways[1],
                )
            )

    def three(self):
        self.threes = []
        for i, (_, _, _, row, _, _) in enumerate(self.parts):
            self.twos[i].wait_recv()
            self.take(row, self.eighth, 2 * i, self.r_two.at[i])
            self.threes.append(
                [
                    self.copies.send(
                        self.z_block(self.grads, i, row, (self.zi + shift) % 4),
                        self.r_z.at[i, shift - 1], self.near_by.z[shift],
                    )
                    for shift in (1, 2, 3)
                ]
            )

    def back_three(self):
        self.threes_back = []
        for i, (_, _, _, row, _, _) in enumerate(self.parts):
            for copy in self.threes[i]:
                copy.wait_recv()
            mine = self.z_block(self.grads, i, row, self.zi)
            self.final[i] = add(mine[...], self.r_z[i, 0], self.r_z[i, 1], self.r_z[i, 2])
            place = self.z_block(self.gall, i, row, self.zi)
            own = self.copies.load(self.final.at[i], place)
            self.threes_back.append(
                (
                    own,
                    [
                        self.copies.send(self.final.at[i], place, self.near_by.z[shift])
                        for shift in (1, 2, 3)
                    ],
                )
            )

    def give(self, row, size, pair, to):
        block = self.gall.at[pair, rows_at(row, size), self.cols]
        return self.copies.send(block, block, to)

    def back_two(self):
        self.twos_back = []
        for i, (pair, ways, _, row, _, _) in enumerate(self.parts):
            own, others = self.threes_back[i]
            own.wait()
            for copy in others:
                copy.wait_recv()
            self.twos_back.append(self.give(row, self.eighth, pair, ways[1]))

    def back_one(self):
        self.ones_back = []
        for i, (pair, ways, row, _, _, _) in enumerate(self.parts):
            self.twos_back[i].wait_recv()
            self.ones_back.append(self.give(row, self.quarter, pair, ways[0]))

    def back_core(self):
        self.cores_back = []
        for i, (pair, *_) in enumerate(self.parts):
            self.ones_back[i].wait_recv()
            self.cores_back.append(self.give(self.row, self.half, pair, self.near_by.core))

    def finish(self):
        for copy in self.cores_back:
            copy.wait_recv()

    def settle(self):
        sent = [self.core, *self.ones, *self.twos, *self.threes[0], *self.threes[1]]
        self.copies.settle(sent)


PAIRS = HEADS // 2
FIRST_PAIRS = 4


def grad_columns(width):
    cut = FIRST_PAIRS * (width // PAIRS)
    return ((0, cut), (cut, width))


def back_kernel(batches, *refs):
    gb_parts, z_parts, gw, cot_in, group_ref, keep_ref, x_in, o_in, y_in, qkv_in, p_in = refs[:11]
    gain1_ref, gain2_ref, wqkv_in, wo_in = refs[11:15]
    result_out, tg_out, gall, ein_out, eout, gains_out, z_core, z_far, rs_z = refs[15:24]
    (
        wqkv, wo, x, o, y, cot, qkv, p, gb_own, gb_far, gb_core, gb_cross, gb_x,
        gy, ga, go, gqkv, grads, *sum_buffers,
        held, r_y, ein, gsum, gain_in, tok, send_sem, recv_sem, local_sem, p_sem,
    ) = refs[24:]
    width = x.shape[1]
    head_dim = width // HEADS
    pair = 2 * head_dim
    length = tok.shape[0]
    dp, expert = lax.axis_index("dp"), lax.axis_index("expert")
    core, xi, yi, zi = expert % 2, expert // 2, dp % 2, dp // 2
    copies = Copies(send_sem, recv_sem, local_sem)
    near_by = Partners()
    near_by.greet()
    load, send = copies.load, copies.send

    crossed, nearer = [], []
    for m in range(batches):
        crossed.append(send(gb_parts.at[3, m], gb_cross.at[m], near_by.core))
        nearer.append(send(gb_parts.at[1, m], gb_core.at[m], near_by.core))
    order = (6, 4, 2, 0)
    pieces = [send(gw.at[order[0] + 1], r_y.at[0], near_by.y)]
    far_loads = [load(gb_parts.at[2, m], gb_far.at[m]) for m in range(batches)]
    own_loads = [load(gb_parts.at[0, m], gb_own.at[m]) for m in range(batches)]
    first_loads = [load(y_in.at[0], y), load(cot_in.at[0], cot)]
    held_loads = [load(gw.at[order[i]], held.at[i]) for i in range(4)]
    late_loads = [load(o_in, o), load(wo_in, wo), load(qkv_in.at[0], qkv)]
    last_loads = [load(x_in, x), load(wqkv_in, wqkv)]
    def far_sum(m):
        far_loads[m].wait()
        crossed[m].wait_recv()
        gb_far[m] = add(gb_far[m], gb_cross[m])

    far_sum(0)
    along = [send(gb_far.at[0], gb_x.at[0], near_by.x)]
    z_crossed = [send(z_parts.at[3, m], z_core.at[1, m], near_by.core) for m in range(batches)]
    z_nearer = [send(z_parts.at[1, m], z_core.at[0, m], near_by.core) for m in range(batches)]
    for m in range(1, batches):
        far_sum(m)

    sent_z = []
    z_ways = (near_by.z_pair, near_by.z[2], near_by.z_pair)

    def reduce_piece(i):
        pieces[i].wait_recv()
        if i < 3:
            pieces.append(send(gw.at[order[i + 1] + 1], r_y.at[i + 1], near_by.y))
        held_loads[i].wait()
        come = {0: (), 1: (0,), 2: (), 3: (1, 2)}[i]
        for j in come:
            sent_z[j].wait_recv()
        loads = [load(rs_z.at[j], r_y.at[at]) for at, j in enumerate(come)]
        for copy in loads:
            copy.wait()
        held[i] = add(held[i], r_y[i], *[r_y[at] for at in range(len(come))])
        if i < 3:
            sent_z.append(send(held.at[i], rs_z.at[i], z_ways[i]))

    z_along = []

    def z_load(m):
        z_crossed[m].wait_recv()
        return [load(z_parts.at[2, m], gb_own.at[m]), load(z_core.at[1, m], gb_core.at[m])]

    def z_send(m, loads):
        for copy in loads:
            copy.wait()
        gb_cross[m] = add(gb_own[m], gb_core[m])
        z_along.append(send(gb_cross.at[m], z_far.at[m], near_by.x))

    sums = [
        BlockSum(
            copies, near_by, (core, xi, yi, zi), grads, gall, low, high,
            sum_buffers[i * 5 : i * 5 + 5],
        )
        for i, (low, high) in enumerate(grad_columns(width))
    ]

    def weight_gradients(group, parts):
        low, high = grad_columns(width)[group]
        for part in parts:
            if part == 3:
                product = dot(o[...], ga[:, low:high], 0, 0)
            else:
                product = dot(a[...], gqkv[:, part * width + low : part * width + high], 0, 0)
            grads[part, :, low:high] = product.astype(BF16)

    left = lax.broadcasted_iota(jnp.int32, (ITEM_ROWS, pair), 1) < head_dim
    reduce_piece(0)
    for copy in first_loads + late_loads:
        copy.wait()
    gain2_grad = jnp.zeros((1, width), F32)
    items = [slice(i * ITEM_ROWS, (i + 1) * ITEM_ROWS) for i in range(ITEMS)]
    a = ga
    for m in range(batches):
        row0 = m * ROWS

        def p_load(hp, m=m):
            return pltpu.make_async_copy(
                p_in.at[m, :, pl.ds(2 * hp, 2)], p.at[hp % 2], p_sem.at[hp % 2]
            )

        p_load(0).start()
        own_loads[m].wait()
        nearer[m].wait_recv()
        along[m].wait_recv()
        if m + 1 < batches:
            along.append(send(gb_far.at[m + 1], gb_x.at[m + 1], near_by.x))
        for rows in items:
            at = slice(row0 + rows.start, row0 + rows.stop)
            gb = (
                gb_own[m, rows].astype(F32)
                + gb_core[m, rows].astype(F32)
                + gb_x[m, rows].astype(F32)
            )
            unit2, inverse2 = normalize_parts(y[rows])
            gain2_grad = gain2_grad + jnp.sum(gb * unit2, axis=0, keepdims=True)
            gy_rows = cot[rows].astype(F32) + normalize_back(gb * gain2_ref[...], unit2, inverse2)
            gy[at] = gy_rows
            ga[at] = gy_rows.astype(BF16)
            go[rows] = dot(ga[at], wo[...], 1, 1).astype(BF16)
        if m + 1 < batches:
            first_loads = [load(y_in.at[m + 1], y), load(cot_in.at[m + 1], cot)]
        z_loads = z_load(m)

        def heads(hp, carry, row0=row0, p_load=p_load):
            @pl.when(hp + 1 < PAIRS)
            def _():
                p_load(hp + 1).start()

            p_load(hp).wait()
            slot = hp % 2
            head_gradients(
                lambda rows, cols: qkv[rows, cols],
                lambda rows, cols: go[rows, cols],
                lambda item, half: p[slot, item, half],
                gqkv, row0, hp, width, left,
            )
            return carry

        if m + 1 < batches:
            lax.fori_loop(0, PAIRS, heads, 0)
            first_loads.append(load(qkv_in.at[m + 1], qkv))
            reduce_piece(1 + m)
            z_send(m, z_loads)
            for copy in first_loads:
                copy.wait()
        else:
            z_send(m, z_loads)
            lax.fori_loop(0, FIRST_PAIRS, heads, 0)
            for copy in last_loads:
                copy.wait()
            weight_gradients(0, (3,))
            weight_gradients(1, (3,))
            for micro in range(batches):
                at = slice(micro * ROWS, (micro + 1) * ROWS)
                unit, _ = normalize_parts(x[at].astype(F32))
                a[at] = (unit * gain1_ref[...]).astype(BF16)
            weight_gradients(0, (0, 1, 2))
            sums[0].start()
            reduce_piece(2)
            lax.fori_loop(FIRST_PAIRS, PAIRS, heads, 0)
    sums[0].one()
    weight_gradients(1, (0, 1, 2))
    sums[1].start()

    gain1_grad = jnp.zeros((1, width), F32)
    between = [sums[0].two, sums[1].one, sums[0].three, sums[1].two]
    for m in range(batches):
        for rows in items:
            at = slice(m * ROWS + rows.start, m * ROWS + rows.stop)
            unit, inverse = normalize_parts(x[at].astype(F32))
            gnorm = dot(gqkv[at], wqkv[...], 1, 1)
            gain1_grad = gain1_grad + jnp.sum(gnorm * unit, axis=0, keepdims=True)
            go[rows] = (gy[at] + normalize_back(gnorm * gain1_ref[...], unit, inverse)).astype(BF16)
            if between:
                between.pop(0)()
        tok[:, m] = dot(pick_rows(group_ref, m, length).astype(BF16), go[...], 0, 0).astype(BF16)
    token_store = load(tok, tg_out)
    gsum[0] = jnp.concatenate([gain1_grad, gain2_grad, jnp.zeros((6, width), F32)], axis=0)
    gain_partners = [near_by.core, near_by.x, near_by.y, near_by.z_pair, near_by.z[2]]
    gain_sent = [send(gsum.at[0], gain_in.at[0], gain_partners[0])]

    def gain_step():
        at = len(gain_sent)
        gain_sent[-1].wait_recv()
        gsum[at] = gsum[at - 1] + gain_in[at - 1]
        if at < len(gain_partners):
            gain_sent.append(send(gsum.at[at], gain_in.at[at], gain_partners[at]))

    sums[1].three()
    reduce_piece(3)

    def join(to, own):
        at = rows_at(expert * part_rows, part_rows)
        return [own(held.at[3, :, 1], eout.at[:, at], *to), own(held.at[3, :, 0], ein.at[:, at], *to)]

    part_rows = held.shape[3]
    joined = join((near_by.x,), send)
    join_near = join((near_by.core,), send)
    join_own = join((), load)
    gain_step()

    for m in range(batches):
        z_nearer[m].wait_recv()
        z_along[m].wait_recv()
        loads = [
            load(z_parts.at[0, m], gb_own.at[m]),
            load(z_core.at[0, m], gb_core.at[m]),
            load(z_far.at[m], gb_x.at[m]),
            load(y_in.at[m], y),
        ]
        for copy in loads:
            copy.wait()
        for rows in items:
            chosen = pick_rows(group_ref, m, length, rows)
            keep = jnp.sum(jnp.where(chosen, keep_ref[m], 0.0), axis=1, keepdims=True)
            z = (
                gb_own[m, rows].astype(F32)
                + gb_core[m, rows].astype(F32)
                + gb_x[m, rows].astype(F32)
            )
            go[rows] = (y[rows] + jnp.where(keep > 0, z, 0.0)).astype(BF16)
        if m == 0:
            token_store.wait()
        tok[:, m] = dot(pick_rows(group_ref, m, length).astype(BF16), go[...], 0, 0).astype(BF16)
        if m == 0:
            sums[0].back_three()
        gain_step()
    copies.keep(tok, result_out)
    sums[1].back_three()

    gain_step()
    for block_sum in sums:
        block_sum.back_two()
    gain_step()
    copies.keep(gsum.at[len(gain_partners)], gains_out)
    for block_sum in sums:
        block_sum.back_one()
    for block_sum in sums:
        block_sum.back_core()
    opposite = rows_at((expert + 2) % 4 * part_rows, part_rows)
    for copy in joined:
        copy.wait_recv()
    join_near += [
        send(ref.at[:, opposite], ref.at[:, opposite], near_by.core) for ref in (eout, ein)
    ]
    for block_sum in sums:
        block_sum.settle()
    for copy in join_own:
        copy.wait()
    for copy in join_near:
        copy.wait_recv()
    hidden = ein.shape[1]
    for k in range(3):
        cols = pl.ds(0, hidden)
        grads[k, :, cols] = ein[k].astype(F32).T.astype(BF16)
        copies.keep(grads.at[k, :, cols], ein_out.at[k])
    for block_sum in sums:
        block_sum.finish()
    copies.finish()


def back(gb_parts, z_parts, gw, cot, group, keep, x, o, y, qkv, p, gain1, gain2, wqkv, wo):
    batches, rows, width = x.shape
    length = keep.shape[2]
    out = jax.ShapeDtypeStruct
    vmem = pl.BlockSpec(memory_space=pltpu.VMEM)
    anywhere = pl.BlockSpec(memory_space=pl.ANY)
    piece = gw.shape[1:]
    both = batches * rows
    half = width // 2
    tokens_shape = (batches, rows, width)
    slots = [tokens_shape] * 5
    scratch = [
        ((width, 3 * width), BF16),
        ((width, width), BF16),
        ((both, width), BF16),
        ((both, width), BF16),
        ((rows, width), F32),
        ((rows, width), BF16),
        ((rows, 3 * width), BF16),
        ((2, ITEMS, 2, ITEM_ROWS, ITEM_ROWS), BF16),
        *[(slot, BF16) for slot in slots],
        ((both, width), F32),
        ((both, width), BF16),
        ((rows, width), BF16),
        ((both, 3 * width), BF16),
        ((4, width, width), BF16),
        *[
            (shape, BF16)
            for low, high in grad_columns(width)
            for shape in (
                (4, half, high - low),
                (2, 2, half // 2, high - low),
                (2, 2, half // 4, high - low),
                (2, 3, half // 4, (high - low) // 2),
                (2, half // 4, (high - low) // 2),
            )
        ],
        ((4,) + piece, BF16),
        ((4,) + piece, BF16),
        ((3, 4 * piece[2], width), BF16),
        ((6, 8, width), F32),
        ((5, 8, width), F32),
        ((length, batches, width), BF16),
    ]
    return pl.pallas_call(
        functools.partial(back_kernel, batches),
        in_specs=[anywhere] * 4 + [vmem] * 2 + [anywhere] * 5 + [vmem] * 2 + [anywhere] * 2,
        out_specs=[anywhere] * 9,
        out_shape=[
            out((length, batches, width), BF16),
            out((length, batches, width), BF16),
            out((4, width, width), BF16),
            out((3, width, 4 * piece[2]), BF16),
            out((3, 4 * piece[2], width), BF16),
            out((8, width), F32),
            out((2,) + tokens_shape, BF16),
            out(tokens_shape, BF16),
            out((3,) + piece, BF16),
        ],
        scratch_shapes=[pltpu.VMEM(*k) for k in scratch]
        + [
            pltpu.SemaphoreType.DMA((80,)),
            pltpu.SemaphoreType.DMA((80,)),
            pltpu.SemaphoreType.DMA((64,)),
            pltpu.SemaphoreType.DMA((2,)),
        ],
        compiler_params=pltpu.CompilerParams(
            vmem_limit_bytes=VMEM_LIMIT, has_side_effects=True, collective_id=1
        ),
        cost_estimate=pl.CostEstimate(
            flops=batches
            * (2 * rows * width * width * 8 + 16 * HEADS * ITEMS * ITEM_ROWS**2 * 128),
            bytes_accessed=80_000_000,
            transcendentals=0,
        ),
        name="back",
    )(
        gb_parts, z_parts, gw, cot, group, keep,
        x.reshape(both, width), o.reshape(both, width), y, qkv, p, gain1, gain2, wqkv, wo,
    )


def attention_backward_kernel(n_parts, n_carry, *refs):
    parts = refs[:n_parts]
    (cot_ref, x_ref, y_ref, qkv_ref, p_ref, o_ref, gain1_ref, gain2_ref, wqkv_ref, wo_ref) = refs[
        n_parts : n_parts + 10
    ]
    carried = refs[n_parts + 10 : n_parts + 10 + n_carry]
    tg_ref, gwqkv_ref, gwo_ref, ggain_ref, gmix_ref, gqkv_ref = refs[n_parts + 10 + n_carry :]
    width = x_ref.shape[1]
    head_dim = width // HEADS
    gb = parts[0][...].astype(F32)
    for part in parts[1:]:
        gb = gb + part[...].astype(F32)
    unit2, inverse2 = normalize_parts(y_ref[...])
    gain2_grad = jnp.sum(gb * unit2, axis=0, keepdims=True)
    gy = cot_ref[...].astype(F32) + normalize_back(gb * gain2_ref[...], unit2, inverse2)
    ga = gy.astype(BF16)
    gwo = dot(o_ref[...], ga, 0, 0)
    if n_carry:
        gwo = gwo + carried[1][...]
    gwo_ref[...] = gwo
    gmix_ref[...] = dot(ga, wo_ref[...], 1, 1).astype(BF16)
    pair = 2 * head_dim
    left = lax.broadcasted_iota(jnp.int32, (ITEM_ROWS, pair), 1) < head_dim

    def heads(hp, carry):
        head_gradients(
            lambda rows, cols: qkv_ref[rows, cols],
            lambda rows, cols: gmix_ref[rows, cols],
            lambda item, half: p_ref[item, hp * 2 + half],
            gqkv_ref, 0, hp, width, left,
        )
        return carry

    lax.fori_loop(0, HEADS // 2, heads, 0)
    unit, inverse = normalize_parts(x_ref[...].astype(F32))
    a = (unit * gain1_ref[...]).astype(BF16)
    for part in range(3):
        cols = slice(part * width, (part + 1) * width)
        gw = dot(a, gqkv_ref[:, cols], 0, 0)
        if n_carry:
            gw = gw + carried[0][:, cols]
        gwqkv_ref[:, cols] = gw
    gnorm = dot(gqkv_ref[...], wqkv_ref[...], 1, 1)
    gain1_grad = jnp.sum(gnorm * unit, axis=0, keepdims=True)
    gains = jnp.concatenate([gain1_grad, gain2_grad, jnp.zeros((6, width), F32)], axis=0)
    if n_carry:
        gains = gains + carried[2][...]
    ggain_ref[...] = gains
    tg_ref[...] = (gy + normalize_back(gnorm * gain1_ref[...], unit, inverse)).astype(BF16)


def attention_backward(parts, cot, x, y, qkv, p, o, gain1, gain2, wqkv, wo, carried):
    rows, width = x.shape
    out = jax.ShapeDtypeStruct
    return pl.pallas_call(
        functools.partial(attention_backward_kernel, len(parts), len(carried)),
        out_shape=(
            out((rows, width), BF16),
            out((width, 3 * width), F32),
            out((width, width), F32),
            out((8, width), F32),
        ),
        scratch_shapes=[pltpu.VMEM((rows, width), BF16), pltpu.VMEM((rows, 3 * width), BF16)],
        compiler_params=pltpu.CompilerParams(vmem_limit_bytes=VMEM_LIMIT),
        cost_estimate=pl.CostEstimate(
            flops=2 * rows * width * width * 8 + 16 * HEADS * ITEMS * ITEM_ROWS**2 * 128,
            bytes_accessed=30_000_000,
            transcendentals=0,
        ),
        name="attention_backward",
    )(*parts, cot, x, y, qkv, p, o, gain1, gain2, wqkv, wo, *carried)


def expert_kernel(groups, batches, pieces, *refs):
    flags, own_ref, more_ref, b_in, g_in, z_out, gb_out, gw_out = refs[:8]
    rows_b, rows_g, w, grads, in_sem, w_sem, out_sem, gw_sem = refs[8:]
    part = own_ref.shape[2]

    def rounded(rows):
        return (rows + TILE - 1) // TILE * TILE

    merged = [
        flags[g, 0, micro * ITEMS + item]
        for g in range(groups)
        for micro in range(batches)
        for item in range(ITEMS)
    ]
    n_merged = sum(merged)
    n_plain = len(merged) - n_merged
    sizes = [n_plain * IMAGE_ROWS, n_plain * CAPTION, n_merged * ITEM_ROWS]
    starts = [0, rounded(sizes[0]), rounded(sizes[0]) + rounded(sizes[1])]
    ends = [start + rounded(size) for start, size in zip(starts, sizes)]
    blocks = []
    plain, joined = 0, 0
    for flat, flag in enumerate(merged):
        g, micro, item = flat // (batches * ITEMS), flat // ITEMS % batches, flat % ITEMS
        base = item * ITEM_ROWS
        image = jnp.where(flag == 1, starts[2] + joined * ITEM_ROWS, plain * IMAGE_ROWS)
        caption = jnp.where(
            flag == 1, image + IMAGE_ROWS, starts[1] + plain * CAPTION
        )
        blocks.append((g, micro, base, IMAGE_ROWS, image, flag, 0))
        blocks.append((g, micro, base + IMAGE_ROWS, CAPTION, caption, flag, 1))
        plain, joined = plain + 1 - flag, joined + flag

    def copy_of(which, number, outward):
        g, micro, base, size, at, _, _ = blocks[number]
        held = (rows_b, rows_g)[which].at[pl.ds(pl.multiple_of(at, 16), size)]
        if outward:
            far = (gb_out, z_out)[which].at[g, micro, pl.ds(base, size)]
            return pltpu.make_async_copy(held, far, out_sem.at[which, number])
        far = (b_in, g_in)[which].at[g, micro, pl.ds(base, size)]
        return pltpu.make_async_copy(far, held, in_sem.at[which, number])

    def of_expert(expert, act, numbers=None):
        for number, (_, _, _, _, _, flag, kind) in enumerate(blocks):
            if numbers is not None and number not in numbers:
                continue
            if expert == 2 or kind == expert:
                @pl.when(flag == (1 if expert == 2 else 0))
                def _(number=number):
                    for which in range(2):
                        act(which, number)

    def weight_copy(k, i):
        piece = own_ref if i == 0 else more_ref.at[i - 1]
        return pltpu.make_async_copy(
            piece.at[k], w.at[k, :, pl.ds(i * part, part), :], w_sem.at[k, i]
        )

    for k in range(3):
        tail = pl.multiple_of(jnp.maximum(ends[k] - TILE, 0), TILE)
        rows_b[pl.ds(tail, TILE), :] = jnp.zeros((TILE, rows_b.shape[1]), BF16)
        rows_g[pl.ds(tail, TILE), :] = jnp.zeros((TILE, rows_g.shape[1]), BF16)
    def start_rows(k, numbers):
        of_expert(k, lambda which, number: copy_of(which, number, False).start(), numbers)

    early = range(len(blocks) // 2)
    late = range(len(blocks) // 2, len(blocks))
    early_plain = sum(1 - flag for flag in merged[: len(merged) // 2])
    middle = early_plain * IMAGE_ROWS // (2 * TILE)

    def wait_rows(k, numbers):
        of_expert(k, lambda which, number: copy_of(which, number, False).wait(), numbers)

    for i in range(pieces):
        weight_copy(0, i).start()
    start_rows(0, early)
    start_rows(0, late)
    for k in range(3):
        grads[...] = jnp.zeros(grads.shape, F32)
        for i in range(pieces):
            weight_copy(k, i).wait()
        wait_rows(k, early)
        if k == 0:
            for other in (1, 2):
                for i in range(pieces):
                    weight_copy(other, i).start()
                start_rows(other, early)
                start_rows(other, late)
        if k > 0:
            wait_rows(k, late)

        def tile(start, size, k=k):
            at = pl.ds(pl.multiple_of(start, TILE), size)
            b, gz = rows_b[at, :], rows_g[at, :]
            u, slope = gelu_and_slope(dot(b, w[k, 0], 1, 1))
            gh = (dot(gz, w[k, 1], 1, 1) * slope).astype(BF16)
            u = u.astype(BF16)
            z, gb = dot(u, w[k, 1], 1, 0), dot(gh, w[k, 0], 1, 0)
            grads[0] += dot(gh, b, 0, 0)
            grads[1] += dot(u, gz, 0, 0)
            rows_b[at, :] = gb.astype(BF16)
            rows_g[at, :] = z.astype(BF16)

        doubles = (ends[k] - starts[k]) // (2 * TILE)

        def double(t, carry, k=k):
            if k == 0:
                @pl.when(t == middle)
                def _():
                    wait_rows(0, late)

            tile(starts[k] + t * 2 * TILE, 2 * TILE)
            return carry

        lax.fori_loop(0, doubles, double, 0)
        if k == 0:
            @pl.when(middle >= doubles)
            def _():
                wait_rows(0, late)

        @pl.when((ends[k] - starts[k]) // TILE > 2 * doubles)
        def _(k=k):
            tile(ends[k] - TILE, TILE)

        of_expert(k, lambda which, number: copy_of(which, number, True).start())
        w[k] = grads[...].astype(BF16)
        for i in range(pieces):
            pltpu.make_async_copy(
                w.at[k, :, pl.ds(i * part, part), :], gw_out.at[i, k], gw_sem.at[k, i]
            ).start()
    for number in range(len(blocks)):
        for which in range(2):
            copy_of(which, number, True).wait()
    for k in range(3):
        for i in range(pieces):
            pltpu.make_async_copy(
                w.at[k, :, pl.ds(i * part, part), :], gw_out.at[i, k], gw_sem.at[k, i]
            ).wait()


def experts(flags, own, more, b_groups, g_groups):
    groups, batches, rows, width = b_groups.shape
    part = own.shape[2]
    pieces = 1 + (more.shape[0] if more.ndim == 5 else 0)
    hidden = part * pieces
    count = groups * batches * ITEMS
    capacity = (count * ITEM_ROWS // TILE + 4) * TILE
    out = jax.ShapeDtypeStruct
    anywhere = pl.BlockSpec(memory_space=pl.ANY)
    return pl.pallas_call(
        functools.partial(expert_kernel, groups, batches, pieces),
        in_specs=[pl.BlockSpec(memory_space=pltpu.SMEM)] + [anywhere] * 4,
        out_specs=[anywhere] * 3,
        out_shape=[out(b_groups.shape, BF16)] * 2 + [out((pieces,) + own.shape, BF16)],
        scratch_shapes=[
            pltpu.VMEM((capacity, width), BF16),
            pltpu.VMEM((capacity, width), BF16),
            pltpu.VMEM((3, 2, hidden, width), BF16),
            pltpu.VMEM((2, hidden, width), F32),
            pltpu.SemaphoreType.DMA((2, 2 * count)),
            pltpu.SemaphoreType.DMA((3, pieces)),
            pltpu.SemaphoreType.DMA((2, 2 * count)),
            pltpu.SemaphoreType.DMA((3, pieces)),
        ],
        compiler_params=pltpu.CompilerParams(vmem_limit_bytes=VMEM_LIMIT),
        cost_estimate=pl.CostEstimate(
            flops=2 * 6 * count * ITEM_ROWS * width * hidden,
            bytes_accessed=45_000_000,
            transcendentals=count * ITEM_ROWS * hidden,
        ),
        name="experts",
    )(flags, own, more, b_groups, g_groups)


def from_items(rows, first):
    one, two = rows[IMAGE_ROWS:ITEM_ROWS], rows[ITEM_ROWS + IMAGE_ROWS :]
    return jnp.concatenate(
        [
            rows[:PATCHES],
            rows[ITEM_ROWS : ITEM_ROWS + PATCHES],
            jnp.where(first, one, two),
            jnp.where(first, two, one),
        ],
        axis=0,
    )


class Links:
    def __init__(self):
        self.hosts = lax.axis_size("expert")
        self.dp = lax.axis_size("dp")
        self.direct = self.hosts == 4 and self.dp == 8
        self.me = lax.axis_index("expert")

    def flip(self, v, bit):
        return lax.ppermute(v, "expert", [(i, i ^ bit) for i in range(4)])

    def across_y(self, v):
        return lax.ppermute(v, "dp", [(i, i ^ 1) for i in range(8)])

    def along_z(self, v, shift):
        return lax.ppermute(v, "dp", [(i, (i + 2 * shift) % 8) for i in range(8)])

    def gather_tokens(self, v):
        if not self.direct:
            return list(lax.all_gather(v, "expert"))
        near, far = self.flip(v, 1), self.flip(v, 2)
        return [v, near, far, self.flip(far, 1)]

    def reduce_tokens(self, parts):
        if not self.direct:
            return [lax.psum_scatter(jnp.stack(parts), "expert", scatter_dimension=0)]
        far = (parts[2].astype(F32) + self.flip(parts[3], 1).astype(F32)).astype(BF16)
        return [parts[0], self.flip(parts[1], 1), self.flip(far, 2)]

    def reduce_weights(self, pieces):
        if not self.direct:
            return lax.psum_scatter(pieces[0], "dp", scatter_dimension=2, tiled=True)
        total = None
        for at, shift in enumerate((0, 1, 3, 2)):
            piece = pieces[2 * at].astype(F32) + self.across_y(pieces[2 * at + 1]).astype(F32)
            if shift:
                piece = self.along_z(piece.astype(BF16), -shift).astype(F32)
            total = piece if total is None else total + piece
        return total.astype(BF16)

    def join_hidden(self, v):
        if not self.direct:
            return lax.all_gather(v, "expert", axis=2, tiled=True)
        stacked = jnp.stack(self.gather_tokens(v))
        return jnp.concatenate(
            [
                lax.dynamic_index_in_dim(stacked, i ^ self.me, 0, keepdims=False)
                for i in range(4)
            ],
            axis=2,
        )


def shards(
    tokens,
    cotangent,
    item_group,
    routes,
    slot_order,
    attn_gain,
    ffn_gain,
    qkv_weight,
    out_weight,
    expert_in,
    expert_out,
):
    links = Links()
    hosts, me = links.hosts, links.me
    batches, length, width = tokens.shape
    shard = expert_in.shape[2]
    part = shard // hosts
    gain1, gain2 = attn_gain, ffn_gain

    own = jnp.stack(
        [
            jnp.swapaxes(lax.dynamic_slice_in_dim(expert_in, me * part, part, 2), 1, 2),
            lax.dynamic_slice_in_dim(expert_out, me * part, part, 1),
        ],
        axis=1,
    )
    first = item_group[:, ITEMS * PATCHES] == 0
    (
        w_all, gz_groups, flag_groups, b_groups, x_all, qkv_all, p_all, o_all, y_all, cot_all, kept
    ) = front(
        links.direct, hosts, own, jnp.swapaxes(tokens, 0, 1), jnp.swapaxes(cotangent, 0, 1),
        item_group, routes, slot_order, gain1, gain2, qkv_weight, out_weight,
    )
    if not links.direct:
        own = lax.all_gather(own, "dp", axis=2, tiled=True)
        gz_groups, flag_groups, b_groups = [
            lax.all_gather(v[0], "expert") for v in (gz_groups, flag_groups, b_groups)
        ]
    z_parts, gb_parts, gw_pieces = experts(flag_groups, own, w_all, b_groups, gz_groups)
    if links.direct:
        result, token_grad, gall, ein_sum, eout_sum, gains, *_ = back(
            gb_parts, z_parts, gw_pieces, cot_all, item_group, kept,
            x_all, o_all, y_all, qkv_all, p_all, gain1, gain2, qkv_weight, out_weight,
        )
        return (
            jnp.swapaxes(result, 0, 1),
            jnp.swapaxes(token_grad, 0, 1),
            gains[0],
            gains[1],
            jnp.concatenate([gall[i].astype(F32) for i in range(3)], axis=1),
            gall[3].astype(F32),
            ein_sum.astype(F32),
            eout_sum.astype(F32),
        )
    gb_terms = links.reduce_tokens(gb_parts)
    z_terms = links.reduce_tokens(z_parts)
    sums = links.join_hidden(links.reduce_weights(gw_pieces)).astype(F32)

    results, token_grads, carried = [], [], ()
    for m in range(batches):
        x, qkv, p, o, y = x_all[m], qkv_all[m], p_all[m], o_all[m], y_all[m]
        at = m
        tg, *carried = attention_backward(
            [t[at] for t in gb_terms],
            cot_all[m], x, y, qkv, p, o, gain1, gain2, qkv_weight, out_weight,
            tuple(carried),
        )
        token_grads.append(from_items(tg, first[m]))
        z = z_terms[0][at].astype(F32)
        for term in z_terms[1:]:
            z = z + term[at].astype(F32)
        branch = jnp.where(kept[m, 0][:, None] > 0, from_items(z, first[m]), 0.0)
        results.append((from_items(y, first[m]) + branch).astype(BF16))
    gw_qkv, gw_out, gains = carried
    packed = jnp.concatenate(
        [
            jnp.concatenate([gw_qkv, gw_out], axis=1),
            jnp.pad(gains[:2].reshape(1, 2 * width), ((0, 7), (0, 2 * width))),
        ],
        axis=0,
    ).astype(BF16)
    packed = lax.psum(packed, ("dp", "expert")).astype(F32)
    return (
        jnp.stack(results),
        jnp.stack(token_grads),
        packed[width, :width],
        packed[width, width : 2 * width],
        packed[:width, : 3 * width],
        packed[:width, 3 * width :],
        jnp.swapaxes(sums[:, 0], 1, 2),
        sums[:, 1],
    )


def solution(mesh):
    in_specs = (
        P(None, ("dp", "expert"), None),
        P(None, ("dp", "expert"), None),
        P(None, ("dp", "expert")),
        P(None, ("dp", "expert")),
        P(None, ("dp", "expert"), None),
        P(),
        P(),
        P(),
        P(),
        P(None, None, "dp"),
        P(None, "dp", None),
    )
    out_specs = (
        P(None, ("dp", "expert"), None),
        P(None, ("dp", "expert"), None),
        P(),
        P(),
        P(),
        P(),
        P(None, None, "dp"),
        P(None, "dp", None),
    )
    return jax.shard_map(shards, mesh=mesh, in_specs=in_specs, out_specs=out_specs, check_vma=False)
```

```python
import functools

import jax
import jax.numpy as jnp
from jax import lax
from jax.experimental import pallas as pl
from jax.experimental.pallas import tpu as pltpu
from jax.sharding import PartitionSpec as P

HEADS = 12
EPSILON = 1e-05
PATCHES = 197
CAPTION = 64
ITEMS = 2
IMAGE_ROWS = 208
ITEM_ROWS = IMAGE_ROWS + CAPTION
ROWS = ITEMS * ITEM_ROWS
TILE = 256
VMEM_LIMIT = 60 * 1024 * 1024
F32 = jnp.float32
BF16 = jnp.bfloat16


def dot(a, b, a_dim, b_dim):
    return lax.dot_general(
        a, b, (((a_dim,), (b_dim,)), ((), ())), preferred_element_type=F32
    )


def normalize_parts(v):
    centred = v - jnp.mean(v, axis=-1, keepdims=True)
    inverse = lax.rsqrt(jnp.mean(centred * centred, axis=-1, keepdims=True) + EPSILON)
    return centred * inverse, inverse


def normalize_back(grad_unit, unit_rows, inverse):
    return inverse * (
        grad_unit
        - jnp.mean(grad_unit, axis=-1, keepdims=True)
        - unit_rows * jnp.mean(grad_unit * unit_rows, axis=-1, keepdims=True)
    )


def gelu_and_slope(h):
    bell = jnp.exp2(h * h * (-0.5 * 1.4426950408889634))
    t = pl.reciprocal(1.0 + (0.3275911 * 0.7071067811865476) * jnp.abs(h))
    half_poly = t * (
        0.127414796
        + t * (-0.142248368 + t * (0.7107068705 + t * (-0.7265760135 + t * 0.5307027145)))
    )
    below = half_poly * bell
    phi = jnp.where(h > 0, 1.0 - below, below)
    return h * phi, phi + (h * bell) * 0.3989422804014327


class Partners:
    def __init__(self):
        dp, expert = lax.axis_index("dp"), lax.axis_index("expert")
        self.core = (dp, expert + 1 - 2 * (expert % 2))
        self.x = (dp, (expert + 2) % 4)
        self.y = (dp + 1 - 2 * (dp % 2), expert)
        self.z = {shift: ((dp + 2 * shift) % 8, expert) for shift in (1, 2, 3)}
        self.z_pair = (dp + 2 - 4 * (dp // 2 % 2), expert)

    def greet(self):
        barrier = pltpu.get_barrier_semaphore()
        everyone = [self.core, self.x, self.y, self.z[1], self.z[2], self.z[3]]
        for other in everyone:
            pl.semaphore_signal(
                barrier, inc=1, device_id=other, device_id_type=pl.DeviceIdType.MESH
            )
        pl.semaphore_wait(barrier, len(everyone))


class Copies:
    def __init__(self, send_sem, recv_sem, local_sem):
        self.send_sem, self.recv_sem, self.local_sem = send_sem, recv_sem, local_sem
        self.sent, self.kept, self.sends, self.locals = [], [], 0, 0

    def send(self, src, dst, device):
        at = self.sends
        self.sends += 1
        copy = pltpu.make_async_remote_copy(
            src_ref=src,
            dst_ref=dst,
            send_sem=self.send_sem.at[at],
            recv_sem=self.recv_sem.at[at],
            device_id=device,
            device_id_type=pl.DeviceIdType.MESH,
        )
        copy.start()
        self.sent.append(copy)
        return copy

    def keep(self, src, dst):
        copy = self.load(src, dst)
        self.kept.append(copy)
        return copy

    def load(self, src, dst):
        copy = pltpu.make_async_copy(src, dst, self.local_sem.at[self.locals])
        self.locals += 1
        copy.start()
        return copy

    def settle(self, done):
        for copy in done:
            copy.wait_send()
        self.sent = [copy for copy in self.sent if all(copy is not other for other in done)]

    def finish(self):
        for copy in self.sent:
            copy.wait_send()
        for copy in self.kept:
            copy.wait()


def pick_rows(group_ref, m, length, rows=slice(0, ROWS)):
    count = rows.stop - rows.start
    row = lax.broadcasted_iota(jnp.int32, (count, 1), 0) + rows.start
    item = (row >= ITEM_ROWS).astype(jnp.int32)
    inside = row - item * ITEM_ROWS
    images = ITEMS * PATCHES
    swapped = (group_ref[m : m + 1, images : images + 1] != 0).astype(jnp.int32)
    caption = item + swapped - 2 * item * swapped
    token = jnp.where(
        inside < PATCHES,
        item * PATCHES + inside,
        jnp.where(inside < IMAGE_ROWS, -1, images + caption * CAPTION + inside - IMAGE_ROWS),
    )
    return lax.broadcasted_iota(jnp.int32, (count, length), 1) == token


def kept_tokens(routing, priority, hosts, capacity):
    length = routing.shape[1]
    across = lax.broadcasted_iota(jnp.int32, (length, length), 1)
    down = lax.broadcasted_iota(jnp.int32, (length, length), 0)

    def upright(row):
        return jnp.sum(jnp.where(across == down, row, 0.0), axis=1, keepdims=True)

    order = upright(priority.astype(F32))
    position = jnp.sum(
        jnp.where(order == across.astype(F32), down.astype(F32), 0.0), axis=0, keepdims=True
    )
    route = routing.astype(F32)
    ahead = (upright(route) == route) & (upright(position) < position)
    rank = jnp.sum(jnp.where(ahead, 1.0, 0.0), axis=0, keepdims=True)
    slots = jnp.zeros_like(rank)
    for kind in range(3):
        slots = jnp.where(routing == kind, float(capacity * ((hosts - kind + 2) // 3)), slots)
    return jnp.where(rank < slots, 1.0, 0.0)


def front_kernel(direct, hosts, batches, *refs):
    (own_ref, tokens_ref, cot_ref, group_ref, routes_ref, order_ref, gain1_ref, gain2_ref) = refs[:8]
    wqkv_ref, wo_ref, w_all, gz_all, flags_all, b_all = refs[8:14]
    x_out, qkv_out, p_out, o_out, y_out, cot_out = refs[14:20]
    (
        keep_ref, gz_scr, b_scr, x_scr, qkv_scr, p_scr, o_scr, y_scr, cot_scr, flags_scr,
        send_sem, recv_sem, local_sem,
    ) = refs[20:]
    length, _, width = tokens_ref.shape
    head_dim = width // HEADS
    pair = 2 * head_dim
    copies = Copies(send_sem, recv_sem, local_sem)

    def spread(src, slots):
        copies.keep(src, slots(0))
        if not direct:
            return None
        near = copies.send(src, slots(1), near_by.core)
        return near, copies.send(src, slots(2), near_by.x)

    def pass_on(pair_of, slots):
        near, far = pair_of
        far.wait_recv()
        return near, copies.send(slots(2), slots(3), near_by.core)

    if direct:
        near_by = Partners()
        near_by.greet()
        over_y = [copies.send(own_ref, w_all.at[0], near_by.y)]
        along = [[], [], []]

        def z_half(i):
            along[0].append(copies.send(own_ref.at[:, i], w_all.at[1, :, i], near_by.z_pair))
            along[1].append(copies.send(own_ref.at[:, i], w_all.at[3, :, i], near_by.z[2]))

        def z_pass(i):
            for k in (1, 0):
                along[k][i].wait_recv()
            if i == 1:
                for half in range(2):
                    along[2].append(
                        copies.send(w_all.at[3, :, half], w_all.at[5, :, half], near_by.z_pair)
                    )
            for at in (3, 1):
                over_y.append(copies.send(w_all.at[at, :, i], w_all.at[at + 1, :, i], near_by.y))

        def z_last(i):
            along[2][i].wait_recv()
            over_y.append(copies.send(w_all.at[5, :, i], w_all.at[6, :, i], near_by.y))

        z_half(0)
    lane = lax.broadcasted_iota(jnp.int32, flags_scr.shape, 1)
    merged = jnp.zeros(flags_scr.shape, jnp.int32)
    for m in range(batches):
        for item in range(ITEMS):
            route = routes_ref[m : m + 1, item * PATCHES : item * PATCHES + 1]
            here = lane == m * ITEMS + item
            merged = jnp.where(here & (route == 2), 1, merged)
    flags_scr[...] = merged
    flags = spread(flags_scr, lambda i: flags_all.at[i])

    gz = []
    for m in range(batches):
        keep_ref[m] = kept_tokens(
            routes_ref[m : m + 1], order_ref[m], hosts, 2 * length // hosts
        )
        chosen = pick_rows(group_ref, m, length)
        cot = dot(chosen.astype(BF16), cot_ref[:, m], 1, 0)
        keep = jnp.sum(jnp.where(chosen, keep_ref[m], 0.0), axis=1, keepdims=True)
        cot_scr[m] = cot.astype(BF16)
        gz_scr[m] = jnp.where(keep > 0, cot, 0.0).astype(BF16)
        gz.append(spread(gz_scr.at[m], lambda i, m=m: gz_all.at[i, m]))

    left = lax.broadcasted_iota(jnp.int32, (ITEM_ROWS, pair), 1) < head_dim
    key = lax.broadcasted_iota(jnp.int32, (1, ITEM_ROWS), 1)
    bias = jnp.where((key >= PATCHES) & (key < IMAGE_ROWS), -1e30, 0.0).astype(F32)
    b_sent = []
    for m in range(batches):
        xb = dot(pick_rows(group_ref, m, length).astype(BF16), tokens_ref[:, m], 1, 0)
        x_scr[m] = xb.astype(BF16)
        unit, _ = normalize_parts(xb)
        a = (unit * gain1_ref[...]).astype(BF16)
        for part in range(3):
            cols = slice(part * width, (part + 1) * width)
            qkv_scr[m, :, cols] = dot(a, wqkv_ref[:, cols], 1, 0).astype(BF16)

        def heads(hp, carry, m=m):
            at_q = pl.ds(pl.multiple_of(hp * pair, pair), pair)
            at_k = pl.ds(pl.multiple_of(width + hp * pair, pair), pair)
            at_v = pl.ds(pl.multiple_of(2 * width + hp * pair, pair), pair)
            for item in range(ITEMS):
                rows = slice(item * ITEM_ROWS, (item + 1) * ITEM_ROWS)
                q, k, v = qkv_scr[m, rows, at_q], qkv_scr[m, rows, at_k], qkv_scr[m, rows, at_v]
                outs = []
                for half in range(2):
                    mine = left if half == 0 else ~left
                    s = dot(jnp.where(mine, q, 0), k, 1, 1) * (head_dim**-0.5) + bias
                    e = jnp.exp(s - jnp.max(s, axis=-1, keepdims=True))
                    p = (e * (1.0 / jnp.sum(e, axis=-1, keepdims=True))).astype(BF16)
                    p_scr[m, item, hp * 2 + half] = p
                    outs.append(dot(p, v, 1, 0))
                o_scr[m, rows, at_q] = jnp.where(left, outs[0], outs[1]).astype(BF16)
            return carry

        lax.fori_loop(0, HEADS // 2, heads, 0)
        if direct and m == 0:
            z_pass(0)
            z_half(1)
        y = x_scr[m].astype(F32) + dot(o_scr[m], wo_ref[...], 1, 0)
        y_scr[m] = y
        unit2, _ = normalize_parts(y)
        b_scr[m] = (unit2 * gain2_ref[...]).astype(BF16)
        b_sent.append(spread(b_scr.at[m], lambda i, m=m: b_all.at[i, m]))
        for scr, out in (
            (x_scr, x_out), (qkv_scr, qkv_out), (p_scr, p_out), (o_scr, o_out), (y_scr, y_out),
            (cot_scr, cot_out),
        ):
            copies.keep(scr.at[m], out.at[m])
        if direct and m == 0:
            flags = pass_on(flags, lambda i: flags_all.at[i])

    if direct:
        z_pass(1)
        z_last(0)
        gz = [
            pass_on(sent, lambda i, m=m: gz_all.at[i, m]) for m, sent in enumerate(gz)
        ]
        b_sent[0] = pass_on(b_sent[0], lambda i: b_all.at[i, 0])
        z_last(1)
        for m in range(1, batches):
            b_sent[m] = pass_on(b_sent[m], lambda i, m=m: b_all.at[i, m])
        for copy in [*over_y, *flags] + [c for pair_of in gz + b_sent for c in pair_of]:
            copy.wait_recv()
    copies.finish()


def front(direct, hosts, own, tokens, cot, group, routes, order, gain1, gain2, wqkv, wo):
    length, batches, width = tokens.shape
    groups = 4 if direct else 1
    out = jax.ShapeDtypeStruct
    vmem = pl.BlockSpec(memory_space=pltpu.VMEM)
    anywhere = pl.BlockSpec(memory_space=pl.ANY)
    kept = [
        ((batches, ROWS, width), BF16),
        ((batches, ROWS, 3 * width), BF16),
        ((batches, ITEMS, HEADS, ITEM_ROWS, ITEM_ROWS), BF16),
        ((batches, ROWS, width), BF16),
        ((batches, ROWS, width), F32),
        ((batches, ROWS, width), BF16),
    ]
    scratch = [pltpu.VMEM((batches, ROWS, width), BF16)] * 2
    return pl.pallas_call(
        functools.partial(front_kernel, direct, hosts, batches),
        in_specs=[anywhere] + [vmem] * 9,
        out_specs=[anywhere] * 10 + [vmem],
        out_shape=[
            out((7 if direct else 1,) + (own.shape if direct else (8, 128)), BF16),
            out((groups, batches, ROWS, width), BF16),
            out((groups, 8, 128), jnp.int32),
            out((groups, batches, ROWS, width), BF16),
        ]
        + [out(*k) for k in kept]
        + [out((batches, 1, length), F32)],
        scratch_shapes=scratch
        + [pltpu.VMEM(*k) for k in kept]
        + [
            pltpu.VMEM((8, 128), jnp.int32),
            pltpu.SemaphoreType.DMA((32,)),
            pltpu.SemaphoreType.DMA((32,)),
            pltpu.SemaphoreType.DMA((24,)),
        ],
        compiler_params=pltpu.CompilerParams(
            vmem_limit_bytes=VMEM_LIMIT,
            has_side_effects=direct,
            collective_id=0 if direct else None,
        ),
        cost_estimate=pl.CostEstimate(
            flops=batches
            * (2 * ROWS * width * width * 4 + 8 * HEADS * ITEMS * ITEM_ROWS**2 * 128),
            bytes_accessed=60_000_000,
            transcendentals=batches * HEADS * ITEMS * ITEM_ROWS**2,
        ),
        name="front",
    )(own, tokens, cot, group, routes, order, gain1, gain2, wqkv, wo)


def head_gradients(qkv_at, go_at, p_of, gqkv_ref, row0, hp, width, left):
    head_dim = width // HEADS
    pair = 2 * head_dim
    scaling = head_dim**-0.5
    at_q = pl.ds(pl.multiple_of(hp * pair, pair), pair)
    at_k = pl.ds(pl.multiple_of(width + hp * pair, pair), pair)
    at_v = pl.ds(pl.multiple_of(2 * width + hp * pair, pair), pair)
    for item in range(ITEMS):
        rows = slice(item * ITEM_ROWS, (item + 1) * ITEM_ROWS)
        out_rows = slice(row0 + rows.start, row0 + rows.stop)
        q, k, v = qkv_at(rows, at_q), qkv_at(rows, at_k), qkv_at(rows, at_v)
        go = go_at(rows, at_q)
        gq, gk, gv = [], [], []
        for half in range(2):
            mine = left if half == 0 else ~left
            p = p_of(item, half)
            pf = p.astype(F32)
            gp = dot(jnp.where(mine, go, 0), v, 1, 1)
            gs = (pf * (gp - jnp.sum(pf * gp, axis=-1, keepdims=True))).astype(BF16)
            gv.append(dot(p, go, 0, 0))
            gq.append(dot(gs, k, 1, 0))
            gk.append(dot(gs, q, 0, 0))
        gqkv_ref[out_rows, at_q] = (jnp.where(left, gq[0], gq[1]) * scaling).astype(BF16)
        gqkv_ref[out_rows, at_k] = (jnp.where(left, gk[0], gk[1]) * scaling).astype(BF16)
        gqkv_ref[out_rows, at_v] = jnp.where(left, gv[0], gv[1]).astype(BF16)


def add(*terms):
    total = terms[0].astype(F32)
    for term in terms[1:]:
        total = total + term.astype(F32)
    return total.astype(BF16)


def rows_at(start, size):
    return pl.ds(pl.multiple_of(start, 32), size)


class BlockSum:
    def __init__(self, copies, near_by, place, grads, gall, low, high, buffers):
        self.copies, self.near_by, self.grads, self.gall = copies, near_by, grads, gall
        self.r_core, self.r_one, self.r_two, self.r_z, self.final = buffers
        self.low, self.size = low, high - low
        self.cols = pl.ds(low, high - low)
        core, xi, yi, self.zi = place
        self.half = grads.shape[1] // 2
        self.quarter, self.eighth = self.half // 2, self.half // 4
        self.row = core * self.half
        self.parts = []
        for part, (one, two) in enumerate(((xi, yi), (yi, xi))):
            pair = pl.ds(2 * part, 2)
            ways = (near_by.x, near_by.y) if part == 0 else (near_by.y, near_by.x)
            row_one = self.row + one * self.quarter
            row_two = row_one + two * self.eighth
            away_one = self.row + (1 - one) * self.quarter
            away_two = row_one + (1 - two) * self.eighth
            self.parts.append((pair, ways, row_one, row_two, away_one, away_two))

    def z_block(self, ref, part, row, z):
        chunk = self.size // 2
        cols = pl.ds(pl.multiple_of(self.low + z % 2 * chunk, 128), chunk)
        return ref.at[2 * part + z // 2, rows_at(row, self.eighth), cols]

    def start(self):
        away = self.grads.at[:, rows_at(self.half - self.row, self.half), self.cols]
        self.core = self.copies.send(away, self.r_core, self.near_by.core)

    def take(self, row, size, first, terms):
        at = rows_at(row, size)
        for i in range(terms.shape[0]):
            self.grads[first + i, at, self.cols] = add(
                self.grads[first + i, at, self.cols], terms[i]
            )

    def one(self):
        self.core.wait_recv()
        self.take(self.row, self.half, 0, self.r_core)
        self.ones = [
            self.copies.send(
                self.grads.at[pair, rows_at(away, self.quarter), self.cols],
                self.r_one.at[i], ways[0],
            )
            for i, (pair, ways, _, _, away, _) in enumerate(self.parts)
        ]

    def two(self):
        self.twos = []
        for i, (pair, ways, row, _, _, away) in enumerate(self.parts):
            self.ones[i].wait_recv()
            self.take(row, self.quarter, 2 * i, self.r_one.at[i])
            self.twos.append(
                self.copies.send(
                    self.grads.at[pair, rows_at(away, self.eighth), self.cols],
                    self.r_two.at[i], ways[1],
                )
            )

    def three(self):
        self.threes = []
        for i, (_, _, _, row, _, _) in enumerate(self.parts):
            self.twos[i].wait_recv()
            self.take(row, self.eighth, 2 * i, self.r_two.at[i])
            self.threes.append(
                [
                    self.copies.send(
                        self.z_block(self.grads, i, row, (self.zi + shift) % 4),
                        self.r_z.at[i, shift - 1], self.near_by.z[shift],
                    )
                    for shift in (1, 2, 3)
                ]
            )

    def back_three(self):
        self.threes_back = []
        for i, (_, _, _, row, _, _) in enumerate(self.parts):
            for copy in self.threes[i]:
                copy.wait_recv()
            mine = self.z_block(self.grads, i, row, self.zi)
            self.final[i] = add(mine[...], self.r_z[i, 0], self.r_z[i, 1], self.r_z[i, 2])
            place = self.z_block(self.gall, i, row, self.zi)
            own = self.copies.load(self.final.at[i], place)
            self.threes_back.append(
                (
                    own,
                    [
                        self.copies.send(self.final.at[i], place, self.near_by.z[shift])
                        for shift in (1, 2, 3)
                    ],
                )
            )

    def give(self, row, size, pair, to):
        block = self.gall.at[pair, rows_at(row, size), self.cols]
        return self.copies.send(block, block, to)

    def back_two(self):
        self.twos_back = []
        for i, (pair, ways, _, row, _, _) in enumerate(self.parts):
            own, others = self.threes_back[i]
            own.wait()
            for copy in others:
                copy.wait_recv()
            self.twos_back.append(self.give(row, self.eighth, pair, ways[1]))

    def back_one(self):
        self.ones_back = []
        for i, (pair, ways, row, _, _, _) in enumerate(self.parts):
            self.twos_back[i].wait_recv()
            self.ones_back.append(self.give(row, self.quarter, pair, ways[0]))

    def back_core(self):
        self.cores_back = []
        for i, (pair, *_) in enumerate(self.parts):
            self.ones_back[i].wait_recv()
            self.cores_back.append(self.give(self.row, self.half, pair, self.near_by.core))

    def finish(self):
        for copy in self.cores_back:
            copy.wait_recv()

    def settle(self):
        sent = [self.core, *self.ones, *self.twos, *self.threes[0], *self.threes[1]]
        self.copies.settle(sent)


PAIRS = HEADS // 2
FIRST_PAIRS = 4


def grad_columns(width):
    cut = FIRST_PAIRS * (width // PAIRS)
    return ((0, cut), (cut, width))


def back_kernel(batches, *refs):
    gb_parts, z_parts, gw, cot_in, group_ref, keep_ref, x_in, o_in, y_in, qkv_in, p_in = refs[:11]
    gain1_ref, gain2_ref, wqkv_in, wo_in = refs[11:15]
    result_out, tg_out, gall, ein_out, eout, gains_out, z_core, z_far, rs_z = refs[15:24]
    (
        wqkv, wo, x, o, y, cot, qkv, p, gb_own, gb_far, gb_core, gb_cross, gb_x,
        gy, ga, go, gqkv, grads, *sum_buffers,
        held, r_y, ein, gsum, gain_in, tok, send_sem, recv_sem, local_sem, p_sem,
    ) = refs[24:]
    width = x.shape[1]
    head_dim = width // HEADS
    pair = 2 * head_dim
    length = tok.shape[0]
    dp, expert = lax.axis_index("dp"), lax.axis_index("expert")
    core, xi, yi, zi = expert % 2, expert // 2, dp % 2, dp // 2
    copies = Copies(send_sem, recv_sem, local_sem)
    near_by = Partners()
    near_by.greet()
    load, send = copies.load, copies.send

    crossed, nearer = [], []
    for m in range(batches):
        crossed.append(send(gb_parts.at[3, m], gb_cross.at[m], near_by.core))
        nearer.append(send(gb_parts.at[1, m], gb_core.at[m], near_by.core))
    order = (6, 4, 2, 0)
    pieces = [send(gw.at[order[0] + 1], r_y.at[0], near_by.y)]
    far_loads = [load(gb_parts.at[2, m], gb_far.at[m]) for m in range(batches)]
    own_loads = [load(gb_parts.at[0, m], gb_own.at[m]) for m in range(batches)]
    first_loads = [load(y_in.at[0], y), load(cot_in.at[0], cot)]
    held_loads = [load(gw.at[order[i]], held.at[i]) for i in range(4)]
    late_loads = [load(o_in, o), load(wo_in, wo), load(qkv_in.at[0], qkv)]
    last_loads = [load(x_in, x), load(wqkv_in, wqkv)]
    def far_sum(m):
        far_loads[m].wait()
        crossed[m].wait_recv()
        gb_far[m] = add(gb_far[m], gb_cross[m])

    far_sum(0)
    along = [send(gb_far.at[0], gb_x.at[0], near_by.x)]
    z_crossed = [send(z_parts.at[3, m], z_core.at[1, m], near_by.core) for m in range(batches)]
    z_nearer = [send(z_parts.at[1, m], z_core.at[0, m], near_by.core) for m in range(batches)]
    for m in range(1, batches):
        far_sum(m)

    sent_z = []
    z_ways = (near_by.z_pair, near_by.z[2], near_by.z_pair)

    def reduce_piece(i):
        pieces[i].wait_recv()
        if i < 3:
            pieces.append(send(gw.at[order[i + 1] + 1], r_y.at[i + 1], near_by.y))
        held_loads[i].wait()
        come = {0: (), 1: (0,), 2: (), 3: (1, 2)}[i]
        for j in come:
            sent_z[j].wait_recv()
        loads = [load(rs_z.at[j], r_y.at[at]) for at, j in enumerate(come)]
        for copy in loads:
            copy.wait()
        held[i] = add(held[i], r_y[i], *[r_y[at] for at in range(len(come))])
        if i < 3:
            sent_z.append(send(held.at[i], rs_z.at[i], z_ways[i]))

    z_along = []

    def z_load(m):
        z_crossed[m].wait_recv()
        return [load(z_parts.at[2, m], gb_own.at[m]), load(z_core.at[1, m], gb_core.at[m])]

    def z_send(m, loads):
        for copy in loads:
            copy.wait()
        gb_cross[m] = add(gb_own[m], gb_core[m])
        z_along.append(send(gb_cross.at[m], z_far.at[m], near_by.x))

    sums = [
        BlockSum(
            copies, near_by, (core, xi, yi, zi), grads, gall, low, high,
            sum_buffers[i * 5 : i * 5 + 5],
        )
        for i, (low, high) in enumerate(grad_columns(width))
    ]

    def weight_gradients(group, parts):
        low, high = grad_columns(width)[group]
        for part in parts:
            if part == 3:
                product = dot(o[...], ga[:, low:high], 0, 0)
            else:
                product = dot(a[...], gqkv[:, part * width + low : part * width + high], 0, 0)
            grads[part, :, low:high] = product.astype(BF16)

    left = lax.broadcasted_iota(jnp.int32, (ITEM_ROWS, pair), 1) < head_dim
    reduce_piece(0)
    for copy in first_loads + late_loads:
        copy.wait()
    gain2_grad = jnp.zeros((1, width), F32)
    items = [slice(i * ITEM_ROWS, (i + 1) * ITEM_ROWS) for i in range(ITEMS)]
    a = ga
    for m in range(batches):
        row0 = m * ROWS

        def p_load(hp, m=m):
            return pltpu.make_async_copy(
                p_in.at[m, :, pl.ds(2 * hp, 2)], p.at[hp % 2], p_sem.at[hp % 2]
            )

        p_load(0).start()
        own_loads[m].wait()
        nearer[m].wait_recv()
        along[m].wait_recv()
        if m + 1 < batches:
            along.append(send(gb_far.at[m + 1], gb_x.at[m + 1], near_by.x))
        for rows in items:
            at = slice(row0 + rows.start, row0 + rows.stop)
            gb = (
                gb_own[m, rows].astype(F32)
                + gb_core[m, rows].astype(F32)
                + gb_x[m, rows].astype(F32)
            )
            unit2, inverse2 = normalize_parts(y[rows])
            gain2_grad = gain2_grad + jnp.sum(gb * unit2, axis=0, keepdims=True)
            gy_rows = cot[rows].astype(F32) + normalize_back(gb * gain2_ref[...], unit2, inverse2)
            gy[at] = gy_rows
            ga[at] = gy_rows.astype(BF16)
            go[rows] = dot(ga[at], wo[...], 1, 1).astype(BF16)
        if m + 1 < batches:
            first_loads = [load(y_in.at[m + 1], y), load(cot_in.at[m + 1], cot)]
        z_loads = z_load(m)

        def heads(hp, carry, row0=row0, p_load=p_load):
            @pl.when(hp + 1 < PAIRS)
            def _():
                p_load(hp + 1).start()

            p_load(hp).wait()
            slot = hp % 2
            head_gradients(
                lambda rows, cols: qkv[rows, cols],
                lambda rows, cols: go[rows, cols],
                lambda item, half: p[slot, item, half],
                gqkv, row0, hp, width, left,
            )
            return carry

        if m + 1 < batches:
            lax.fori_loop(0, PAIRS, heads, 0)
            first_loads.append(load(qkv_in.at[m + 1], qkv))
            reduce_piece(1 + m)
            z_send(m, z_loads)
            for copy in first_loads:
                copy.wait()
        else:
            z_send(m, z_loads)
            lax.fori_loop(0, FIRST_PAIRS, heads, 0)
            for copy in last_loads:
                copy.wait()
            weight_gradients(0, (3,))
            weight_gradients(1, (3,))
            for micro in range(batches):
                at = slice(micro * ROWS, (micro + 1) * ROWS)
                unit, _ = normalize_parts(x[at].astype(F32))
                a[at] = (unit * gain1_ref[...]).astype(BF16)
            weight_gradients(0, (0, 1, 2))
            sums[0].start()
            reduce_piece(2)
            lax.fori_loop(FIRST_PAIRS, PAIRS, heads, 0)
    sums[0].one()
    weight_gradients(1, (0, 1, 2))
    sums[1].start()

    gain1_grad = jnp.zeros((1, width), F32)
    between = [sums[0].two, sums[1].one, sums[0].three, sums[1].two]
    for m in range(batches):
        for rows in items:
            at = slice(m * ROWS + rows.start, m * ROWS + rows.stop)
            unit, inverse = normalize_parts(x[at].astype(F32))
            gnorm = dot(gqkv[at], wqkv[...], 1, 1)
            gain1_grad = gain1_grad + jnp.sum(gnorm * unit, axis=0, keepdims=True)
            go[rows] = (gy[at] + normalize_back(gnorm * gain1_ref[...], unit, inverse)).astype(BF16)
            if between:
                between.pop(0)()
        tok[:, m] = dot(pick_rows(group_ref, m, length).astype(BF16), go[...], 0, 0).astype(BF16)
    token_store = load(tok, tg_out)
    gsum[0] = jnp.concatenate([gain1_grad, gain2_grad, jnp.zeros((6, width), F32)], axis=0)
    gain_partners = [near_by.core, near_by.x, near_by.y, near_by.z_pair, near_by.z[2]]
    gain_sent = [send(gsum.at[0], gain_in.at[0], gain_partners[0])]

    def gain_step():
        at = len(gain_sent)
        gain_sent[-1].wait_recv()
        gsum[at] = gsum[at - 1] + gain_in[at - 1]
        if at < len(gain_partners):
            gain_sent.append(send(gsum.at[at], gain_in.at[at], gain_partners[at]))

    sums[1].three()
    reduce_piece(3)

    def join(to, own):
        at = rows_at(expert * part_rows, part_rows)
        return [own(held.at[3, :, 1], eout.at[:, at], *to), own(held.at[3, :, 0], ein.at[:, at], *to)]

    part_rows = held.shape[3]
    joined = join((near_by.x,), send)
    join_near = join((near_by.core,), send)
    join_own = join((), load)
    gain_step()

    for m in range(batches):
        z_nearer[m].wait_recv()
        z_along[m].wait_recv()
        loads = [
            load(z_parts.at[0, m], gb_own.at[m]),
            load(z_core.at[0, m], gb_core.at[m]),
            load(z_far.at[m], gb_x.at[m]),
            load(y_in.at[m], y),
        ]
        for copy in loads:
            copy.wait()
        for rows in items:
            chosen = pick_rows(group_ref, m, length, rows)
            keep = jnp.sum(jnp.where(chosen, keep_ref[m], 0.0), axis=1, keepdims=True)
            z = (
                gb_own[m, rows].astype(F32)
                + gb_core[m, rows].astype(F32)
                + gb_x[m, rows].astype(F32)
            )
            go[rows] = (y[rows] + jnp.where(keep > 0, z, 0.0)).astype(BF16)
        if m == 0:
            token_store.wait()
        tok[:, m] = dot(pick_rows(group_ref, m, length).astype(BF16), go[...], 0, 0).astype(BF16)
        if m == 0:
            sums[0].back_three()
        gain_step()
    copies.keep(tok, result_out)
    sums[1].back_three()

    gain_step()
    for block_sum in sums:
        block_sum.back_two()
    gain_step()
    copies.keep(gsum.at[len(gain_partners)], gains_out)
    opposite = rows_at((expert + 2) % 4 * part_rows, part_rows)
    for copy in joined:
        copy.wait_recv()
    join_near += [
        send(ref.at[:, opposite], ref.at[:, opposite], near_by.core) for ref in (eout, ein)
    ]
    for block_sum in sums:
        block_sum.back_one()
    for block_sum in sums:
        block_sum.settle()
    for copy in join_own:
        copy.wait()
    for copy in join_near:
        copy.wait_recv()
    hidden = ein.shape[1]
    for k in range(3):
        cols = pl.ds(0, hidden)
        grads[k, :, cols] = ein[k].astype(F32).T.astype(BF16)
        copies.keep(grads.at[k, :, cols], ein_out.at[k])
    for block_sum in sums:
        block_sum.back_core()
    for block_sum in sums:
        block_sum.finish()
    copies.finish()


def back(gb_parts, z_parts, gw, cot, group, keep, x, o, y, qkv, p, gain1, gain2, wqkv, wo):
    batches, rows, width = x.shape
    length = keep.shape[2]
    out = jax.ShapeDtypeStruct
    vmem = pl.BlockSpec(memory_space=pltpu.VMEM)
    anywhere = pl.BlockSpec(memory_space=pl.ANY)
    piece = gw.shape[1:]
    both = batches * rows
    half = width // 2
    tokens_shape = (batches, rows, width)
    slots = [tokens_shape] * 5
    scratch = [
        ((width, 3 * width), BF16),
        ((width, width), BF16),
        ((both, width), BF16),
        ((both, width), BF16),
        ((rows, width), F32),
        ((rows, width), BF16),
        ((rows, 3 * width), BF16),
        ((2, ITEMS, 2, ITEM_ROWS, ITEM_ROWS), BF16),
        *[(slot, BF16) for slot in slots],
        ((both, width), F32),
        ((both, width), BF16),
        ((rows, width), BF16),
        ((both, 3 * width), BF16),
        ((4, width, width), BF16),
        *[
            (shape, BF16)
            for low, high in grad_columns(width)
            for shape in (
                (4, half, high - low),
                (2, 2, half // 2, high - low),
                (2, 2, half // 4, high - low),
                (2, 3, half // 4, (high - low) // 2),
                (2, half // 4, (high - low) // 2),
            )
        ],
        ((4,) + piece, BF16),
        ((4,) + piece, BF16),
        ((3, 4 * piece[2], width), BF16),
        ((6, 8, width), F32),
        ((5, 8, width), F32),
        ((length, batches, width), BF16),
    ]
    return pl.pallas_call(
        functools.partial(back_kernel, batches),
        in_specs=[anywhere] * 4 + [vmem] * 2 + [anywhere] * 5 + [vmem] * 2 + [anywhere] * 2,
        out_specs=[anywhere] * 9,
        out_shape=[
            out((length, batches, width), BF16),
            out((length, batches, width), BF16),
            out((4, width, width), BF16),
            out((3, width, 4 * piece[2]), BF16),
            out((3, 4 * piece[2], width), BF16),
            out((8, width), F32),
            out((2,) + tokens_shape, BF16),
            out(tokens_shape, BF16),
            out((3,) + piece, BF16),
        ],
        scratch_shapes=[pltpu.VMEM(*k) for k in scratch]
        + [
            pltpu.SemaphoreType.DMA((80,)),
            pltpu.SemaphoreType.DMA((80,)),
            pltpu.SemaphoreType.DMA((64,)),
            pltpu.SemaphoreType.DMA((2,)),
        ],
        compiler_params=pltpu.CompilerParams(
            vmem_limit_bytes=VMEM_LIMIT, has_side_effects=True, collective_id=1
        ),
        cost_estimate=pl.CostEstimate(
            flops=batches
            * (2 * rows * width * width * 8 + 16 * HEADS * ITEMS * ITEM_ROWS**2 * 128),
            bytes_accessed=80_000_000,
            transcendentals=0,
        ),
        name="back",
    )(
        gb_parts, z_parts, gw, cot, group, keep,
        x.reshape(both, width), o.reshape(both, width), y, qkv, p, gain1, gain2, wqkv, wo,
    )


def attention_backward_kernel(n_parts, n_carry, *refs):
    parts = refs[:n_parts]
    (cot_ref, x_ref, y_ref, qkv_ref, p_ref, o_ref, gain1_ref, gain2_ref, wqkv_ref, wo_ref) = refs[
        n_parts : n_parts + 10
    ]
    carried = refs[n_parts + 10 : n_parts + 10 + n_carry]
    tg_ref, gwqkv_ref, gwo_ref, ggain_ref, gmix_ref, gqkv_ref = refs[n_parts + 10 + n_carry :]
    width = x_ref.shape[1]
    head_dim = width // HEADS
    gb = parts[0][...].astype(F32)
    for part in parts[1:]:
        gb = gb + part[...].astype(F32)
    unit2, inverse2 = normalize_parts(y_ref[...])
    gain2_grad = jnp.sum(gb * unit2, axis=0, keepdims=True)
    gy = cot_ref[...].astype(F32) + normalize_back(gb * gain2_ref[...], unit2, inverse2)
    ga = gy.astype(BF16)
    gwo = dot(o_ref[...], ga, 0, 0)
    if n_carry:
        gwo = gwo + carried[1][...]
    gwo_ref[...] = gwo
    gmix_ref[...] = dot(ga, wo_ref[...], 1, 1).astype(BF16)
    pair = 2 * head_dim
    left = lax.broadcasted_iota(jnp.int32, (ITEM_ROWS, pair), 1) < head_dim

    def heads(hp, carry):
        head_gradients(
            lambda rows, cols: qkv_ref[rows, cols],
            lambda rows, cols: gmix_ref[rows, cols],
            lambda item, half: p_ref[item, hp * 2 + half],
            gqkv_ref, 0, hp, width, left,
        )
        return carry

    lax.fori_loop(0, HEADS // 2, heads, 0)
    unit, inverse = normalize_parts(x_ref[...].astype(F32))
    a = (unit * gain1_ref[...]).astype(BF16)
    for part in range(3):
        cols = slice(part * width, (part + 1) * width)
        gw = dot(a, gqkv_ref[:, cols], 0, 0)
        if n_carry:
            gw = gw + carried[0][:, cols]
        gwqkv_ref[:, cols] = gw
    gnorm = dot(gqkv_ref[...], wqkv_ref[...], 1, 1)
    gain1_grad = jnp.sum(gnorm * unit, axis=0, keepdims=True)
    gains = jnp.concatenate([gain1_grad, gain2_grad, jnp.zeros((6, width), F32)], axis=0)
    if n_carry:
        gains = gains + carried[2][...]
    ggain_ref[...] = gains
    tg_ref[...] = (gy + normalize_back(gnorm * gain1_ref[...], unit, inverse)).astype(BF16)


def attention_backward(parts, cot, x, y, qkv, p, o, gain1, gain2, wqkv, wo, carried):
    rows, width = x.shape
    out = jax.ShapeDtypeStruct
    return pl.pallas_call(
        functools.partial(attention_backward_kernel, len(parts), len(carried)),
        out_shape=(
            out((rows, width), BF16),
            out((width, 3 * width), F32),
            out((width, width), F32),
            out((8, width), F32),
        ),
        scratch_shapes=[pltpu.VMEM((rows, width), BF16), pltpu.VMEM((rows, 3 * width), BF16)],
        compiler_params=pltpu.CompilerParams(vmem_limit_bytes=VMEM_LIMIT),
        cost_estimate=pl.CostEstimate(
            flops=2 * rows * width * width * 8 + 16 * HEADS * ITEMS * ITEM_ROWS**2 * 128,
            bytes_accessed=30_000_000,
            transcendentals=0,
        ),
        name="attention_backward",
    )(*parts, cot, x, y, qkv, p, o, gain1, gain2, wqkv, wo, *carried)


def expert_kernel(groups, batches, pieces, *refs):
    flags, own_ref, more_ref, b_in, g_in, z_out, gb_out, gw_out = refs[:8]
    rows_b, rows_g, w, grads, in_sem, w_sem, out_sem, gw_sem = refs[8:]
    part = own_ref.shape[2]

    def rounded(rows):
        return (rows + TILE - 1) // TILE * TILE

    merged = [
        flags[g, 0, micro * ITEMS + item]
        for g in range(groups)
        for micro in range(batches)
        for item in range(ITEMS)
    ]
    n_merged = sum(merged)
    n_plain = len(merged) - n_merged
    sizes = [n_plain * IMAGE_ROWS, n_plain * CAPTION, n_merged * ITEM_ROWS]
    starts = [0, rounded(sizes[0]), rounded(sizes[0]) + rounded(sizes[1])]
    ends = [start + rounded(size) for start, size in zip(starts, sizes)]
    blocks = []
    plain, joined = 0, 0
    for flat, flag in enumerate(merged):
        g, micro, item = flat // (batches * ITEMS), flat // ITEMS % batches, flat % ITEMS
        base = item * ITEM_ROWS
        image = jnp.where(flag == 1, starts[2] + joined * ITEM_ROWS, plain * IMAGE_ROWS)
        caption = jnp.where(
            flag == 1, image + IMAGE_ROWS, starts[1] + plain * CAPTION
        )
        blocks.append((g, micro, base, IMAGE_ROWS, image, flag, 0))
        blocks.append((g, micro, base + IMAGE_ROWS, CAPTION, caption, flag, 1))
        plain, joined = plain + 1 - flag, joined + flag

    def copy_of(which, number, outward):
        g, micro, base, size, at, _, _ = blocks[number]
        held = (rows_b, rows_g)[which].at[pl.ds(pl.multiple_of(at, 16), size)]
        if outward:
            far = (gb_out, z_out)[which].at[g, micro, pl.ds(base, size)]
            return pltpu.make_async_copy(held, far, out_sem.at[which, number])
        far = (b_in, g_in)[which].at[g, micro, pl.ds(base, size)]
        return pltpu.make_async_copy(far, held, in_sem.at[which, number])

    def of_expert(expert, act, numbers=None):
        for number, (_, _, _, _, _, flag, kind) in enumerate(blocks):
            if numbers is not None and number not in numbers:
                continue
            if expert == 2 or kind == expert:
                @pl.when(flag == (1 if expert == 2 else 0))
                def _(number=number):
                    for which in range(2):
                        act(which, number)

    def weight_copy(k, i):
        piece = own_ref if i == 0 else more_ref.at[i - 1]
        return pltpu.make_async_copy(
            piece.at[k], w.at[k, :, pl.ds(i * part, part), :], w_sem.at[k, i]
        )

    for k in range(3):
        tail = pl.multiple_of(jnp.maximum(ends[k] - TILE, 0), TILE)
        rows_b[pl.ds(tail, TILE), :] = jnp.zeros((TILE, rows_b.shape[1]), BF16)
        rows_g[pl.ds(tail, TILE), :] = jnp.zeros((TILE, rows_g.shape[1]), BF16)
    def start_rows(k, numbers):
        of_expert(k, lambda which, number: copy_of(which, number, False).start(), numbers)

    early = range(len(blocks) // 2)
    late = range(len(blocks) // 2, len(blocks))
    early_plain = sum(1 - flag for flag in merged[: len(merged) // 2])
    middle = early_plain * IMAGE_ROWS // (2 * TILE)

    def wait_rows(k, numbers):
        of_expert(k, lambda which, number: copy_of(which, number, False).wait(), numbers)

    for i in range(pieces):
        weight_copy(0, i).start()
    start_rows(0, early)
    start_rows(0, late)
    for k in range(3):
        grads[...] = jnp.zeros(grads.shape, F32)
        for i in range(pieces):
            weight_copy(k, i).wait()
        wait_rows(k, early)
        if k == 0:
            for other in (1, 2):
                for i in range(pieces):
                    weight_copy(other, i).start()
                start_rows(other, early)
                start_rows(other, late)
        if k > 0:
            wait_rows(k, late)

        def tile(start, size, k=k):
            at = pl.ds(pl.multiple_of(start, TILE), size)
            b, gz = rows_b[at, :], rows_g[at, :]
            u, slope = gelu_and_slope(dot(b, w[k, 0], 1, 1))
            gh = (dot(gz, w[k, 1], 1, 1) * slope).astype(BF16)
            u = u.astype(BF16)
            z, gb = dot(u, w[k, 1], 1, 0), dot(gh, w[k, 0], 1, 0)
            grads[0] += dot(gh, b, 0, 0)
            grads[1] += dot(u, gz, 0, 0)
            rows_b[at, :] = gb.astype(BF16)
            rows_g[at, :] = z.astype(BF16)

        doubles = (ends[k] - starts[k]) // (2 * TILE)

        def double(t, carry, k=k):
            if k == 0:
                @pl.when(t == middle)
                def _():
                    wait_rows(0, late)

            tile(starts[k] + t * 2 * TILE, 2 * TILE)
            return carry

        lax.fori_loop(0, doubles, double, 0)
        if k == 0:
            @pl.when(middle >= doubles)
            def _():
                wait_rows(0, late)

        @pl.when((ends[k] - starts[k]) // TILE > 2 * doubles)
        def _(k=k):
            tile(ends[k] - TILE, TILE)

        of_expert(k, lambda which, number: copy_of(which, number, True).start())
        w[k] = grads[...].astype(BF16)
        for i in range(pieces):
            pltpu.make_async_copy(
                w.at[k, :, pl.ds(i * part, part), :], gw_out.at[i, k], gw_sem.at[k, i]
            ).start()
    for number in range(len(blocks)):
        for which in range(2):
            copy_of(which, number, True).wait()
    for k in range(3):
        for i in range(pieces):
            pltpu.make_async_copy(
                w.at[k, :, pl.ds(i * part, part), :], gw_out.at[i, k], gw_sem.at[k, i]
            ).wait()


def experts(flags, own, more, b_groups, g_groups):
    groups, batches, rows, width = b_groups.shape
    part = own.shape[2]
    pieces = 1 + (more.shape[0] if more.ndim == 5 else 0)
    hidden = part * pieces
    count = groups * batches * ITEMS
    capacity = (count * ITEM_ROWS // TILE + 4) * TILE
    out = jax.ShapeDtypeStruct
    anywhere = pl.BlockSpec(memory_space=pl.ANY)
    return pl.pallas_call(
        functools.partial(expert_kernel, groups, batches, pieces),
        in_specs=[pl.BlockSpec(memory_space=pltpu.SMEM)] + [anywhere] * 4,
        out_specs=[anywhere] * 3,
        out_shape=[out(b_groups.shape, BF16)] * 2 + [out((pieces,) + own.shape, BF16)],
        scratch_shapes=[
            pltpu.VMEM((capacity, width), BF16),
            pltpu.VMEM((capacity, width), BF16),
            pltpu.VMEM((3, 2, hidden, width), BF16),
            pltpu.VMEM((2, hidden, width), F32),
            pltpu.SemaphoreType.DMA((2, 2 * count)),
            pltpu.SemaphoreType.DMA((3, pieces)),
            pltpu.SemaphoreType.DMA((2, 2 * count)),
            pltpu.SemaphoreType.DMA((3, pieces)),
        ],
        compiler_params=pltpu.CompilerParams(vmem_limit_bytes=VMEM_LIMIT),
        cost_estimate=pl.CostEstimate(
            flops=2 * 6 * count * ITEM_ROWS * width * hidden,
            bytes_accessed=45_000_000,
            transcendentals=count * ITEM_ROWS * hidden,
        ),
        name="experts",
    )(flags, own, more, b_groups, g_groups)


def from_items(rows, first):
    one, two = rows[IMAGE_ROWS:ITEM_ROWS], rows[ITEM_ROWS + IMAGE_ROWS :]
    return jnp.concatenate(
        [
            rows[:PATCHES],
            rows[ITEM_ROWS : ITEM_ROWS + PATCHES],
            jnp.where(first, one, two),
            jnp.where(first, two, one),
        ],
        axis=0,
    )


class Links:
    def __init__(self):
        self.hosts = lax.axis_size("expert")
        self.dp = lax.axis_size("dp")
        self.direct = self.hosts == 4 and self.dp == 8
        self.me = lax.axis_index("expert")

    def flip(self, v, bit):
        return lax.ppermute(v, "expert", [(i, i ^ bit) for i in range(4)])

    def across_y(self, v):
        return lax.ppermute(v, "dp", [(i, i ^ 1) for i in range(8)])

    def along_z(self, v, shift):
        return lax.ppermute(v, "dp", [(i, (i + 2 * shift) % 8) for i in range(8)])

    def gather_tokens(self, v):
        if not self.direct:
            return list(lax.all_gather(v, "expert"))
        near, far = self.flip(v, 1), self.flip(v, 2)
        return [v, near, far, self.flip(far, 1)]

    def reduce_tokens(self, parts):
        if not self.direct:
            return [lax.psum_scatter(jnp.stack(parts), "expert", scatter_dimension=0)]
        far = (parts[2].astype(F32) + self.flip(parts[3], 1).astype(F32)).astype(BF16)
        return [parts[0], self.flip(parts[1], 1), self.flip(far, 2)]

    def reduce_weights(self, pieces):
        if not self.direct:
            return lax.psum_scatter(pieces[0], "dp", scatter_dimension=2, tiled=True)
        total = None
        for at, shift in enumerate((0, 1, 3, 2)):
            piece = pieces[2 * at].astype(F32) + self.across_y(pieces[2 * at + 1]).astype(F32)
            if shift:
                piece = self.along_z(piece.astype(BF16), -shift).astype(F32)
            total = piece if total is None else total + piece
        return total.astype(BF16)

    def join_hidden(self, v):
        if not self.direct:
            return lax.all_gather(v, "expert", axis=2, tiled=True)
        stacked = jnp.stack(self.gather_tokens(v))
        return jnp.concatenate(
            [
                lax.dynamic_index_in_dim(stacked, i ^ self.me, 0, keepdims=False)
                for i in range(4)
            ],
            axis=2,
        )


def shards(
    tokens,
    cotangent,
    item_group,
    routes,
    slot_order,
    attn_gain,
    ffn_gain,
    qkv_weight,
    out_weight,
    expert_in,
    expert_out,
):
    links = Links()
    hosts, me = links.hosts, links.me
    batches, length, width = tokens.shape
    shard = expert_in.shape[2]
    part = shard // hosts
    gain1, gain2 = attn_gain, ffn_gain

    own = jnp.stack(
        [
            jnp.swapaxes(lax.dynamic_slice_in_dim(expert_in, me * part, part, 2), 1, 2),
            lax.dynamic_slice_in_dim(expert_out, me * part, part, 1),
        ],
        axis=1,
    )
    first = item_group[:, ITEMS * PATCHES] == 0
    (
        w_all, gz_groups, flag_groups, b_groups, x_all, qkv_all, p_all, o_all, y_all, cot_all, kept
    ) = front(
        links.direct, hosts, own, jnp.swapaxes(tokens, 0, 1), jnp.swapaxes(cotangent, 0, 1),
        item_group, routes, slot_order, gain1, gain2, qkv_weight, out_weight,
    )
    if not links.direct:
        own = lax.all_gather(own, "dp", axis=2, tiled=True)
        gz_groups, flag_groups, b_groups = [
            lax.all_gather(v[0], "expert") for v in (gz_groups, flag_groups, b_groups)
        ]
    z_parts, gb_parts, gw_pieces = experts(flag_groups, own, w_all, b_groups, gz_groups)
    if links.direct:
        result, token_grad, gall, ein_sum, eout_sum, gains, *_ = back(
            gb_parts, z_parts, gw_pieces, cot_all, item_group, kept,
            x_all, o_all, y_all, qkv_all, p_all, gain1, gain2, qkv_weight, out_weight,
        )
        return (
            jnp.swapaxes(result, 0, 1),
            jnp.swapaxes(token_grad, 0, 1),
            gains[0],
            gains[1],
            jnp.concatenate([gall[i].astype(F32) for i in range(3)], axis=1),
            gall[3].astype(F32),
            ein_sum.astype(F32),
            eout_sum.astype(F32),
        )
    gb_terms = links.reduce_tokens(gb_parts)
    z_terms = links.reduce_tokens(z_parts)
    sums = links.join_hidden(links.reduce_weights(gw_pieces)).astype(F32)

    results, token_grads, carried = [], [], ()
    for m in range(batches):
        x, qkv, p, o, y = x_all[m], qkv_all[m], p_all[m], o_all[m], y_all[m]
        at = m
        tg, *carried = attention_backward(
            [t[at] for t in gb_terms],
            cot_all[m], x, y, qkv, p, o, gain1, gain2, qkv_weight, out_weight,
            tuple(carried),
        )
        token_grads.append(from_items(tg, first[m]))
        z = z_terms[0][at].astype(F32)
        for term in z_terms[1:]:
            z = z + term[at].astype(F32)
        branch = jnp.where(kept[m, 0][:, None] > 0, from_items(z, first[m]), 0.0)
        results.append((from_items(y, first[m]) + branch).astype(BF16))
    gw_qkv, gw_out, gains = carried
    packed = jnp.concatenate(
        [
            jnp.concatenate([gw_qkv, gw_out], axis=1),
            jnp.pad(gains[:2].reshape(1, 2 * width), ((0, 7), (0, 2 * width))),
        ],
        axis=0,
    ).astype(BF16)
    packed = lax.psum(packed, ("dp", "expert")).astype(F32)
    return (
        jnp.stack(results),
        jnp.stack(token_grads),
        packed[width, :width],
        packed[width, width : 2 * width],
        packed[:width, : 3 * width],
        packed[:width, 3 * width :],
        jnp.swapaxes(sums[:, 0], 1, 2),
        sums[:, 1],
    )


def solution(mesh):
    in_specs = (
        P(None, ("dp", "expert"), None),
        P(None, ("dp", "expert"), None),
        P(None, ("dp", "expert")),
        P(None, ("dp", "expert")),
        P(None, ("dp", "expert"), None),
        P(),
        P(),
        P(),
        P(),
        P(None, None, "dp"),
        P(None, "dp", None),
    )
    out_specs = (
        P(None, ("dp", "expert"), None),
        P(None, ("dp", "expert"), None),
        P(),
        P(),
        P(),
        P(),
        P(None, None, "dp"),
        P(None, "dp", None),
    )
    return jax.shard_map(shards, mesh=mesh, in_specs=in_specs, out_specs=out_specs, check_vma=False)
```

```python
import functools

import jax
import jax.numpy as jnp
from jax import lax
from jax.experimental import pallas as pl
from jax.experimental.pallas import tpu as pltpu
from jax.sharding import PartitionSpec as P

HEADS = 12
EPSILON = 1e-05
PATCHES = 197
CAPTION = 64
ITEMS = 2
IMAGE_ROWS = 208
ITEM_ROWS = IMAGE_ROWS + CAPTION
ROWS = ITEMS * ITEM_ROWS
TILE = 256
VMEM_LIMIT = 60 * 1024 * 1024
F32 = jnp.float32
BF16 = jnp.bfloat16


def dot(a, b, a_dim, b_dim):
    return lax.dot_general(
        a, b, (((a_dim,), (b_dim,)), ((), ())), preferred_element_type=F32
    )


def normalize_parts(v):
    centred = v - jnp.mean(v, axis=-1, keepdims=True)
    inverse = lax.rsqrt(jnp.mean(centred * centred, axis=-1, keepdims=True) + EPSILON)
    return centred * inverse, inverse


def normalize_back(grad_unit, unit_rows, inverse):
    return inverse * (
        grad_unit
        - jnp.mean(grad_unit, axis=-1, keepdims=True)
        - unit_rows * jnp.mean(grad_unit * unit_rows, axis=-1, keepdims=True)
    )


def gelu_and_slope(h):
    bell = jnp.exp2(h * h * (-0.5 * 1.4426950408889634))
    t = pl.reciprocal(1.0 + (0.3275911 * 0.7071067811865476) * jnp.abs(h))
    half_poly = t * (
        0.127414796
        + t * (-0.142248368 + t * (0.7107068705 + t * (-0.7265760135 + t * 0.5307027145)))
    )
    below = half_poly * bell
    phi = jnp.where(h > 0, 1.0 - below, below)
    return h * phi, phi + (h * bell) * 0.3989422804014327


class Partners:
    def __init__(self):
        dp, expert = lax.axis_index("dp"), lax.axis_index("expert")
        self.core = (dp, expert + 1 - 2 * (expert % 2))
        self.x = (dp, (expert + 2) % 4)
        self.y = (dp + 1 - 2 * (dp % 2), expert)
        self.z = {shift: ((dp + 2 * shift) % 8, expert) for shift in (1, 2, 3)}
        self.z_pair = (dp + 2 - 4 * (dp // 2 % 2), expert)

    def greet(self):
        barrier = pltpu.get_barrier_semaphore()
        everyone = [self.core, self.x, self.y, self.z[1], self.z[2], self.z[3]]
        for other in everyone:
            pl.semaphore_signal(
                barrier, inc=1, device_id=other, device_id_type=pl.DeviceIdType.MESH
            )
        pl.semaphore_wait(barrier, len(everyone))


class Copies:
    def __init__(self, send_sem, recv_sem, local_sem):
        self.send_sem, self.recv_sem, self.local_sem = send_sem, recv_sem, local_sem
        self.sent, self.kept, self.sends, self.locals = [], [], 0, 0

    def send(self, src, dst, device):
        at = self.sends
        self.sends += 1
        copy = pltpu.make_async_remote_copy(
            src_ref=src,
            dst_ref=dst,
            send_sem=self.send_sem.at[at],
            recv_sem=self.recv_sem.at[at],
            device_id=device,
            device_id_type=pl.DeviceIdType.MESH,
        )
        copy.start()
        self.sent.append(copy)
        return copy

    def keep(self, src, dst):
        copy = self.load(src, dst)
        self.kept.append(copy)
        return copy

    def load(self, src, dst):
        copy = pltpu.make_async_copy(src, dst, self.local_sem.at[self.locals])
        self.locals += 1
        copy.start()
        return copy

    def settle(self, done):
        for copy in done:
            copy.wait_send()
        self.sent = [copy for copy in self.sent if all(copy is not other for other in done)]

    def finish(self):
        for copy in self.sent:
            copy.wait_send()
        for copy in self.kept:
            copy.wait()


def pick_rows(group_ref, m, length, rows=slice(0, ROWS)):
    count = rows.stop - rows.start
    row = lax.broadcasted_iota(jnp.int32, (count, 1), 0) + rows.start
    item = (row >= ITEM_ROWS).astype(jnp.int32)
    inside = row - item * ITEM_ROWS
    images = ITEMS * PATCHES
    swapped = (group_ref[m : m + 1, images : images + 1] != 0).astype(jnp.int32)
    caption = item + swapped - 2 * item * swapped
    token = jnp.where(
        inside < PATCHES,
        item * PATCHES + inside,
        jnp.where(inside < IMAGE_ROWS, -1, images + caption * CAPTION + inside - IMAGE_ROWS),
    )
    return lax.broadcasted_iota(jnp.int32, (count, length), 1) == token


def kept_tokens(routing, priority, hosts, capacity):
    length = routing.shape[1]
    across = lax.broadcasted_iota(jnp.int32, (length, length), 1)
    down = lax.broadcasted_iota(jnp.int32, (length, length), 0)

    def upright(row):
        return jnp.sum(jnp.where(across == down, row, 0.0), axis=1, keepdims=True)

    order = upright(priority.astype(F32))
    position = jnp.sum(
        jnp.where(order == across.astype(F32), down.astype(F32), 0.0), axis=0, keepdims=True
    )
    route = routing.astype(F32)
    ahead = (upright(route) == route) & (upright(position) < position)
    rank = jnp.sum(jnp.where(ahead, 1.0, 0.0), axis=0, keepdims=True)
    slots = jnp.zeros_like(rank)
    for kind in range(3):
        slots = jnp.where(routing == kind, float(capacity * ((hosts - kind + 2) // 3)), slots)
    return jnp.where(rank < slots, 1.0, 0.0)


def front_kernel(direct, hosts, batches, *refs):
    (own_ref, tokens_ref, cot_ref, group_ref, routes_ref, order_ref, gain1_ref, gain2_ref) = refs[:8]
    wqkv_ref, wo_ref, w_all, gz_all, flags_all, b_all = refs[8:14]
    x_out, qkv_out, p_out, o_out, y_out, cot_out = refs[14:20]
    (
        keep_ref, gz_scr, b_scr, x_scr, qkv_scr, p_scr, o_scr, y_scr, cot_scr, flags_scr,
        send_sem, recv_sem, local_sem,
    ) = refs[20:]
    length, _, width = tokens_ref.shape
    head_dim = width // HEADS
    pair = 2 * head_dim
    copies = Copies(send_sem, recv_sem, local_sem)

    def spread(src, slots):
        copies.keep(src, slots(0))
        if not direct:
            return None
        near = copies.send(src, slots(1), near_by.core)
        return near, copies.send(src, slots(2), near_by.x)

    def pass_on(pair_of, slots):
        near, far = pair_of
        far.wait_recv()
        return near, copies.send(slots(2), slots(3), near_by.core)

    if direct:
        near_by = Partners()
        near_by.greet()
        over_y = [copies.send(own_ref, w_all.at[0], near_by.y)]
        along = [[], [], []]

        def z_half(i):
            along[0].append(copies.send(own_ref.at[:, i], w_all.at[1, :, i], near_by.z_pair))
            along[1].append(copies.send(own_ref.at[:, i], w_all.at[3, :, i], near_by.z[2]))

        def z_pass(i):
            for k in (1, 0):
                along[k][i].wait_recv()
            if i == 1:
                for half in range(2):
                    along[2].append(
                        copies.send(w_all.at[3, :, half], w_all.at[5, :, half], near_by.z_pair)
                    )
            for at in (3, 1):
                over_y.append(copies.send(w_all.at[at, :, i], w_all.at[at + 1, :, i], near_by.y))

        def z_last(i):
            along[2][i].wait_recv()
            over_y.append(copies.send(w_all.at[5, :, i], w_all.at[6, :, i], near_by.y))

        z_half(0)
    lane = lax.broadcasted_iota(jnp.int32, flags_scr.shape, 1)
    merged = jnp.zeros(flags_scr.shape, jnp.int32)
    for m in range(batches):
        for item in range(ITEMS):
            route = routes_ref[m : m + 1, item * PATCHES : item * PATCHES + 1]
            here = lane == m * ITEMS + item
            merged = jnp.where(here & (route == 2), 1, merged)
    flags_scr[...] = merged
    flags = spread(flags_scr, lambda i: flags_all.at[i])

    gz = []
    for m in range(batches):
        keep_ref[m] = kept_tokens(
            routes_ref[m : m + 1], order_ref[m], hosts, 2 * length // hosts
        )
        chosen = pick_rows(group_ref, m, length)
        cot = dot(chosen.astype(BF16), cot_ref[:, m], 1, 0)
        keep = jnp.sum(jnp.where(chosen, keep_ref[m], 0.0), axis=1, keepdims=True)
        cot_scr[m] = cot.astype(BF16)
        gz_scr[m] = jnp.where(keep > 0, cot, 0.0).astype(BF16)
        gz.append(spread(gz_scr.at[m], lambda i, m=m: gz_all.at[i, m]))

    left = lax.broadcasted_iota(jnp.int32, (ITEM_ROWS, pair), 1) < head_dim
    key = lax.broadcasted_iota(jnp.int32, (1, ITEM_ROWS), 1)
    bias = jnp.where((key >= PATCHES) & (key < IMAGE_ROWS), -1e30, 0.0).astype(F32)
    b_sent = []
    for m in range(batches):
        xb = dot(pick_rows(group_ref, m, length).astype(BF16), tokens_ref[:, m], 1, 0)
        x_scr[m] = xb.astype(BF16)
        unit, _ = normalize_parts(xb)
        a = (unit * gain1_ref[...]).astype(BF16)
        for part in range(3):
            cols = slice(part * width, (part + 1) * width)
            qkv_scr[m, :, cols] = dot(a, wqkv_ref[:, cols], 1, 0).astype(BF16)

        def heads(hp, carry, m=m):
            at_q = pl.ds(pl.multiple_of(hp * pair, pair), pair)
            at_k = pl.ds(pl.multiple_of(width + hp * pair, pair), pair)
            at_v = pl.ds(pl.multiple_of(2 * width + hp * pair, pair), pair)
            for item in range(ITEMS):
                rows = slice(item * ITEM_ROWS, (item + 1) * ITEM_ROWS)
                q, k, v = qkv_scr[m, rows, at_q], qkv_scr[m, rows, at_k], qkv_scr[m, rows, at_v]
                outs = []
                for half in range(2):
                    mine = left if half == 0 else ~left
                    s = dot(jnp.where(mine, q, 0), k, 1, 1) * (head_dim**-0.5) + bias
                    e = jnp.exp(s - jnp.max(s, axis=-1, keepdims=True))
                    p = (e * (1.0 / jnp.sum(e, axis=-1, keepdims=True))).astype(BF16)
                    p_scr[m, item, hp * 2 + half] = p
                    outs.append(dot(p, v, 1, 0))
                o_scr[m, rows, at_q] = jnp.where(left, outs[0], outs[1]).astype(BF16)
            return carry

        lax.fori_loop(0, HEADS // 2, heads, 0)
        if direct and m == 0:
            z_pass(0)
            z_half(1)
        y = x_scr[m].astype(F32) + dot(o_scr[m], wo_ref[...], 1, 0)
        y_scr[m] = y
        unit2, _ = normalize_parts(y)
        b_scr[m] = (unit2 * gain2_ref[...]).astype(BF16)
        b_sent.append(spread(b_scr.at[m], lambda i, m=m: b_all.at[i, m]))
        for scr, out in (
            (x_scr, x_out), (qkv_scr, qkv_out), (p_scr, p_out), (o_scr, o_out), (y_scr, y_out),
            (cot_scr, cot_out),
        ):
            copies.keep(scr.at[m], out.at[m])
        if direct and m == 0:
            flags = pass_on(flags, lambda i: flags_all.at[i])

    if direct:
        z_pass(1)
        z_last(0)
        gz = [
            pass_on(sent, lambda i, m=m: gz_all.at[i, m]) for m, sent in enumerate(gz)
        ]
        b_sent[0] = pass_on(b_sent[0], lambda i: b_all.at[i, 0])
        z_last(1)
        for m in range(1, batches):
            b_sent[m] = pass_on(b_sent[m], lambda i, m=m: b_all.at[i, m])
        for copy in [*over_y, *flags] + [c for pair_of in gz + b_sent for c in pair_of]:
            copy.wait_recv()
    copies.finish()


def front(direct, hosts, own, tokens, cot, group, routes, order, gain1, gain2, wqkv, wo):
    length, batches, width = tokens.shape
    groups = 4 if direct else 1
    out = jax.ShapeDtypeStruct
    vmem = pl.BlockSpec(memory_space=pltpu.VMEM)
    anywhere = pl.BlockSpec(memory_space=pl.ANY)
    kept = [
        ((batches, ROWS, width), BF16),
        ((batches, ROWS, 3 * width), BF16),
        ((batches, ITEMS, HEADS, ITEM_ROWS, ITEM_ROWS), BF16),
        ((batches, ROWS, width), BF16),
        ((batches, ROWS, width), F32),
        ((batches, ROWS, width), BF16),
    ]
    scratch = [pltpu.VMEM((batches, ROWS, width), BF16)] * 2
    return pl.pallas_call(
        functools.partial(front_kernel, direct, hosts, batches),
        in_specs=[anywhere] + [vmem] * 9,
        out_specs=[anywhere] * 10 + [vmem],
        out_shape=[
            out((7 if direct else 1,) + (own.shape if direct else (8, 128)), BF16),
            out((groups, batches, ROWS, width), BF16),
            out((groups, 8, 128), jnp.int32),
            out((groups, batches, ROWS, width), BF16),
        ]
        + [out(*k) for k in kept]
        + [out((batches, 1, length), F32)],
        scratch_shapes=scratch
        + [pltpu.VMEM(*k) for k in kept]
        + [
            pltpu.VMEM((8, 128), jnp.int32),
            pltpu.SemaphoreType.DMA((32,)),
            pltpu.SemaphoreType.DMA((32,)),
            pltpu.SemaphoreType.DMA((24,)),
        ],
        compiler_params=pltpu.CompilerParams(
            vmem_limit_bytes=VMEM_LIMIT,
            has_side_effects=direct,
            collective_id=0 if direct else None,
        ),
        cost_estimate=pl.CostEstimate(
            flops=batches
            * (2 * ROWS * width * width * 4 + 8 * HEADS * ITEMS * ITEM_ROWS**2 * 128),
            bytes_accessed=60_000_000,
            transcendentals=batches * HEADS * ITEMS * ITEM_ROWS**2,
        ),
        name="front",
    )(own, tokens, cot, group, routes, order, gain1, gain2, wqkv, wo)


def head_gradients(qkv_at, go_at, p_of, gqkv_ref, row0, hp, width, left):
    head_dim = width // HEADS
    pair = 2 * head_dim
    scaling = head_dim**-0.5
    at_q = pl.ds(pl.multiple_of(hp * pair, pair), pair)
    at_k = pl.ds(pl.multiple_of(width + hp * pair, pair), pair)
    at_v = pl.ds(pl.multiple_of(2 * width + hp * pair, pair), pair)
    for item in range(ITEMS):
        rows = slice(item * ITEM_ROWS, (item + 1) * ITEM_ROWS)
        out_rows = slice(row0 + rows.start, row0 + rows.stop)
        q, k, v = qkv_at(rows, at_q), qkv_at(rows, at_k), qkv_at(rows, at_v)
        go = go_at(rows, at_q)
        gq, gk, gv = [], [], []
        for half in range(2):
            mine = left if half == 0 else ~left
            p = p_of(item, half)
            pf = p.astype(F32)
            gp = dot(jnp.where(mine, go, 0), v, 1, 1)
            gs = (pf * (gp - jnp.sum(pf * gp, axis=-1, keepdims=True))).astype(BF16)
            gv.append(dot(p, go, 0, 0))
            gq.append(dot(gs, k, 1, 0))
            gk.append(dot(gs, q, 0, 0))
        gqkv_ref[out_rows, at_q] = (jnp.where(left, gq[0], gq[1]) * scaling).astype(BF16)
        gqkv_ref[out_rows, at_k] = (jnp.where(left, gk[0], gk[1]) * scaling).astype(BF16)
        gqkv_ref[out_rows, at_v] = jnp.where(left, gv[0], gv[1]).astype(BF16)


def add(*terms):
    total = terms[0].astype(F32)
    for term in terms[1:]:
        total = total + term.astype(F32)
    return total.astype(BF16)


def rows_at(start, size):
    return pl.ds(pl.multiple_of(start, 32), size)


class BlockSum:
    def __init__(self, copies, near_by, place, grads, gall, low, high, buffers):
        self.copies, self.near_by, self.grads, self.gall = copies, near_by, grads, gall
        self.r_core, self.r_one, self.r_two, self.r_z, self.final = buffers
        self.low, self.size = low, high - low
        self.cols = pl.ds(low, high - low)
        core, xi, yi, self.zi = place
        self.half = grads.shape[1] // 2
        self.quarter, self.eighth = self.half // 2, self.half // 4
        self.row = core * self.half
        self.parts = []
        for part, (one, two) in enumerate(((xi, yi), (yi, xi))):
            pair = pl.ds(2 * part, 2)
            ways = (near_by.x, near_by.y) if part == 0 else (near_by.y, near_by.x)
            row_one = self.row + one * self.quarter
            row_two = row_one + two * self.eighth
            away_one = self.row + (1 - one) * self.quarter
            away_two = row_one + (1 - two) * self.eighth
            self.parts.append((pair, ways, row_one, row_two, away_one, away_two))

    def z_block(self, ref, part, row, z):
        chunk = self.size // 2
        cols = pl.ds(pl.multiple_of(self.low + z % 2 * chunk, 128), chunk)
        return ref.at[2 * part + z // 2, rows_at(row, self.eighth), cols]

    def start(self):
        away = self.grads.at[:, rows_at(self.half - self.row, self.half), self.cols]
        self.core = self.copies.send(away, self.r_core, self.near_by.core)

    def take(self, row, size, first, terms):
        at = rows_at(row, size)
        for i in range(terms.shape[0]):
            self.grads[first + i, at, self.cols] = add(
                self.grads[first + i, at, self.cols], terms[i]
            )

    def one(self):
        self.core.wait_recv()
        self.take(self.row, self.half, 0, self.r_core)
        self.ones = [
            self.copies.send(
                self.grads.at[pair, rows_at(away, self.quarter), self.cols],
                self.r_one.at[i], ways[0],
            )
            for i, (pair, ways, _, _, away, _) in enumerate(self.parts)
        ]

    def two(self):
        self.twos = []
        for i, (pair, ways, row, _, _, away) in enumerate(self.parts):
            self.ones[i].wait_recv()
            self.take(row, self.quarter, 2 * i, self.r_one.at[i])
            self.twos.append(
                self.copies.send(
                    self.grads.at[pair, rows_at(away, self.eighth), self.cols],
                    self.r_two.at[i], ways[1],
                )
            )

    def three(self):
        self.threes = []
        for i, (_, _, _, row, _, _) in enumerate(self.parts):
            self.twos[i].wait_recv()
            self.take(row, self.eighth, 2 * i, self.r_two.at[i])
            self.threes.append(
                [
                    self.copies.send(
                        self.z_block(self.grads, i, row, (self.zi + shift) % 4),
                        self.r_z.at[i, shift - 1], self.near_by.z[shift],
                    )
                    for shift in (1, 2, 3)
                ]
            )

    def back_three(self):
        self.threes_back = []
        for i, (_, _, _, row, _, _) in enumerate(self.parts):
            for copy in self.threes[i]:
                copy.wait_recv()
            mine = self.z_block(self.grads, i, row, self.zi)
            self.final[i] = add(mine[...], self.r_z[i, 0], self.r_z[i, 1], self.r_z[i, 2])
            place = self.z_block(self.gall, i, row, self.zi)
            own = self.copies.load(self.final.at[i], place)
            self.threes_back.append(
                (
                    own,
                    [
                        self.copies.send(self.final.at[i], place, self.near_by.z[shift])
                        for shift in (1, 2, 3)
                    ],
                )
            )

    def give(self, row, size, pair, to):
        block = self.gall.at[pair, rows_at(row, size), self.cols]
        return self.copies.send(block, block, to)

    def back_two(self):
        self.twos_back = []
        for i, (pair, ways, _, row, _, _) in enumerate(self.parts):
            own, others = self.threes_back[i]
            own.wait()
            for copy in others:
                copy.wait_recv()
            self.twos_back.append(self.give(row, self.eighth, pair, ways[1]))

    def back_one(self):
        self.ones_back = []
        for i, (pair, ways, row, _, _, _) in enumerate(self.parts):
            self.twos_back[i].wait_recv()
            self.ones_back.append(self.give(row, self.quarter, pair, ways[0]))

    def back_core(self):
        self.cores_back = []
        for i, (pair, *_) in enumerate(self.parts):
            self.ones_back[i].wait_recv()
            self.cores_back.append(self.give(self.row, self.half, pair, self.near_by.core))

    def finish(self):
        for copy in self.cores_back:
            copy.wait_recv()

    def settle(self):
        sent = [self.core, *self.ones, *self.twos, *self.threes[0], *self.threes[1]]
        self.copies.settle(sent)


PAIRS = HEADS // 2
FIRST_PAIRS = 4


def grad_columns(width):
    cut = FIRST_PAIRS * (width // PAIRS)
    return ((0, cut), (cut, width))


def back_kernel(batches, *refs):
    gb_parts, z_parts, gw, cot_in, group_ref, keep_ref, x_in, o_in, y_in, qkv_in, p_in = refs[:11]
    gain1_ref, gain2_ref, wqkv_in, wo_in = refs[11:15]
    result_out, tg_out, gall, ein_out, eout, gains_out, z_core, z_far, rs_z = refs[15:24]
    (
        wqkv, wo, x, o, y, cot, qkv, p, gb_own, gb_far, gb_core, gb_cross, gb_x,
        gy, ga, go, gqkv, grads, *sum_buffers,
        held, r_y, ein, gsum, gain_in, tok, send_sem, recv_sem, local_sem, p_sem,
    ) = refs[24:]
    width = x.shape[1]
    head_dim = width // HEADS
    pair = 2 * head_dim
    length = tok.shape[0]
    dp, expert = lax.axis_index("dp"), lax.axis_index("expert")
    core, xi, yi, zi = expert % 2, expert // 2, dp % 2, dp // 2
    copies = Copies(send_sem, recv_sem, local_sem)
    near_by = Partners()
    near_by.greet()
    load, send = copies.load, copies.send

    crossed, nearer = [], []
    for m in range(batches):
        crossed.append(send(gb_parts.at[3, m], gb_cross.at[m], near_by.core))
        nearer.append(send(gb_parts.at[1, m], gb_core.at[m], near_by.core))
    order = (6, 4, 2, 0)
    pieces = [send(gw.at[order[0] + 1], r_y.at[0], near_by.y)]
    far_loads = [load(gb_parts.at[2, m], gb_far.at[m]) for m in range(batches)]
    own_loads = [load(gb_parts.at[0, m], gb_own.at[m]) for m in range(batches)]
    first_loads = [load(y_in.at[0], y), load(cot_in.at[0], cot)]
    held_loads = [load(gw.at[order[i]], held.at[i]) for i in range(4)]
    late_loads = [load(o_in, o), load(wo_in, wo), load(qkv_in.at[0], qkv)]
    last_loads = [load(x_in, x), load(wqkv_in, wqkv)]
    def far_sum(m):
        far_loads[m].wait()
        crossed[m].wait_recv()
        gb_far[m] = add(gb_far[m], gb_cross[m])

    far_sum(0)
    along = [send(gb_far.at[0], gb_x.at[0], near_by.x)]
    z_crossed = [send(z_parts.at[3, m], z_core.at[1, m], near_by.core) for m in range(batches)]
    z_nearer = [send(z_parts.at[1, m], z_core.at[0, m], near_by.core) for m in range(batches)]
    for m in range(1, batches):
        far_sum(m)

    sent_z = []
    z_ways = (near_by.z_pair, near_by.z[2], near_by.z_pair)

    def reduce_piece(i):
        pieces[i].wait_recv()
        if i < 3:
            pieces.append(send(gw.at[order[i + 1] + 1], r_y.at[i + 1], near_by.y))
        held_loads[i].wait()
        come = {0: (), 1: (0,), 2: (), 3: (1, 2)}[i]
        for j in come:
            sent_z[j].wait_recv()
        loads = [load(rs_z.at[j], r_y.at[at]) for at, j in enumerate(come)]
        for copy in loads:
            copy.wait()
        held[i] = add(held[i], r_y[i], *[r_y[at] for at in range(len(come))])
        if i < 3:
            sent_z.append(send(held.at[i], rs_z.at[i], z_ways[i]))

    z_along = []

    def z_load(m):
        z_crossed[m].wait_recv()
        return [load(z_parts.at[2, m], gb_own.at[m]), load(z_core.at[1, m], gb_core.at[m])]

    def z_send(m, loads):
        for copy in loads:
            copy.wait()
        gb_cross[m] = add(gb_own[m], gb_core[m])
        z_along.append(send(gb_cross.at[m], z_far.at[m], near_by.x))

    sums = [
        BlockSum(
            copies, near_by, (core, xi, yi, zi), grads, gall, low, high,
            sum_buffers[i * 5 : i * 5 + 5],
        )
        for i, (low, high) in enumerate(grad_columns(width))
    ]

    def weight_gradients(group, parts):
        low, high = grad_columns(width)[group]
        for part in parts:
            if part == 3:
                product = dot(o[...], ga[:, low:high], 0, 0)
            else:
                product = dot(a[...], gqkv[:, part * width + low : part * width + high], 0, 0)
            grads[part, :, low:high] = product.astype(BF16)

    left = lax.broadcasted_iota(jnp.int32, (ITEM_ROWS, pair), 1) < head_dim
    reduce_piece(0)
    for copy in first_loads + late_loads:
        copy.wait()
    gain2_grad = jnp.zeros((1, width), F32)
    items = [slice(i * ITEM_ROWS, (i + 1) * ITEM_ROWS) for i in range(ITEMS)]
    a = ga
    for m in range(batches):
        row0 = m * ROWS

        def p_load(hp, m=m):
            return pltpu.make_async_copy(
                p_in.at[m, :, pl.ds(2 * hp, 2)], p.at[hp % 2], p_sem.at[hp % 2]
            )

        p_load(0).start()
        own_loads[m].wait()
        nearer[m].wait_recv()
        along[m].wait_recv()
        if m + 1 < batches:
            along.append(send(gb_far.at[m + 1], gb_x.at[m + 1], near_by.x))
        for rows in items:
            at = slice(row0 + rows.start, row0 + rows.stop)
            gb = (
                gb_own[m, rows].astype(F32)
                + gb_core[m, rows].astype(F32)
                + gb_x[m, rows].astype(F32)
            )
            unit2, inverse2 = normalize_parts(y[rows])
            gain2_grad = gain2_grad + jnp.sum(gb * unit2, axis=0, keepdims=True)
            gy_rows = cot[rows].astype(F32) + normalize_back(gb * gain2_ref[...], unit2, inverse2)
            gy[at] = gy_rows
            ga[at] = gy_rows.astype(BF16)
            go[rows] = dot(ga[at], wo[...], 1, 1).astype(BF16)
        if m + 1 < batches:
            first_loads = [load(y_in.at[m + 1], y), load(cot_in.at[m + 1], cot)]
        z_loads = z_load(m)

        def heads(hp, carry, row0=row0, p_load=p_load):
            @pl.when(hp + 1 < PAIRS)
            def _():
                p_load(hp + 1).start()

            p_load(hp).wait()
            slot = hp % 2
            head_gradients(
                lambda rows, cols: qkv[rows, cols],
                lambda rows, cols: go[rows, cols],
                lambda item, half: p[slot, item, half],
                gqkv, row0, hp, width, left,
            )
            return carry

        if m + 1 < batches:
            lax.fori_loop(0, PAIRS, heads, 0)
            first_loads.append(load(qkv_in.at[m + 1], qkv))
            reduce_piece(1 + m)
            z_send(m, z_loads)
            for copy in first_loads:
                copy.wait()
        else:
            z_send(m, z_loads)
            lax.fori_loop(0, FIRST_PAIRS, heads, 0)
            for copy in last_loads:
                copy.wait()
            weight_gradients(0, (3,))
            weight_gradients(1, (3,))
            for micro in range(batches):
                at = slice(micro * ROWS, (micro + 1) * ROWS)
                unit, _ = normalize_parts(x[at].astype(F32))
                a[at] = (unit * gain1_ref[...]).astype(BF16)
            weight_gradients(0, (0, 1, 2))
            sums[0].start()
            reduce_piece(2)
            lax.fori_loop(FIRST_PAIRS, PAIRS, heads, 0)
    sums[0].one()
    weight_gradients(1, (0, 1, 2))
    sums[1].start()

    gain1_grad = jnp.zeros((1, width), F32)
    between = [sums[0].two, sums[1].one, sums[0].three, sums[1].two]
    for m in range(batches):
        for rows in items:
            at = slice(m * ROWS + rows.start, m * ROWS + rows.stop)
            unit, inverse = normalize_parts(x[at].astype(F32))
            gnorm = dot(gqkv[at], wqkv[...], 1, 1)
            gain1_grad = gain1_grad + jnp.sum(gnorm * unit, axis=0, keepdims=True)
            go[rows] = (gy[at] + normalize_back(gnorm * gain1_ref[...], unit, inverse)).astype(BF16)
            if between:
                between.pop(0)()
        tok[:, m] = dot(pick_rows(group_ref, m, length).astype(BF16), go[...], 0, 0).astype(BF16)
    token_store = load(tok, tg_out)
    gsum[0] = jnp.concatenate([gain1_grad, gain2_grad, jnp.zeros((6, width), F32)], axis=0)
    gain_partners = [near_by.x, near_by.y, near_by.z_pair, near_by.z[2], near_by.core]
    gain_sent = [send(gsum.at[0], gain_in.at[0], gain_partners[0])]

    def gain_step():
        at = len(gain_sent)
        gain_sent[-1].wait_recv()
        gsum[at] = gsum[at - 1] + gain_in[at - 1]
        if at < len(gain_partners):
            gain_sent.append(send(gsum.at[at], gain_in.at[at], gain_partners[at]))

    sums[1].three()
    reduce_piece(3)

    def join(to, own):
        at = rows_at(expert * part_rows, part_rows)
        return [own(held.at[3, :, 1], eout.at[:, at], *to), own(held.at[3, :, 0], ein.at[:, at], *to)]

    part_rows = held.shape[3]
    joined = join((near_by.x,), send)
    join_near = join((near_by.core,), send)
    join_own = join((), load)
    gain_step()

    for m in range(batches):
        z_nearer[m].wait_recv()
        z_along[m].wait_recv()
        loads = [
            load(z_parts.at[0, m], gb_own.at[m]),
            load(z_core.at[0, m], gb_core.at[m]),
            load(z_far.at[m], gb_x.at[m]),
            load(y_in.at[m], y),
        ]
        for copy in loads:
            copy.wait()
        for rows in items:
            chosen = pick_rows(group_ref, m, length, rows)
            keep = jnp.sum(jnp.where(chosen, keep_ref[m], 0.0), axis=1, keepdims=True)
            z = (
                gb_own[m, rows].astype(F32)
                + gb_core[m, rows].astype(F32)
                + gb_x[m, rows].astype(F32)
            )
            go[rows] = (y[rows] + jnp.where(keep > 0, z, 0.0)).astype(BF16)
        if m == 0:
            token_store.wait()
        tok[:, m] = dot(pick_rows(group_ref, m, length).astype(BF16), go[...], 0, 0).astype(BF16)
        if m == 0:
            sums[0].back_three()
        gain_step()
    copies.keep(tok, result_out)
    sums[1].back_three()

    gain_step()
    for block_sum in sums:
        block_sum.back_two()
    gain_step()
    copies.keep(gsum.at[len(gain_partners)], gains_out)
    opposite = rows_at((expert + 2) % 4 * part_rows, part_rows)
    for copy in joined:
        copy.wait_recv()
    join_near += [
        send(ref.at[:, opposite], ref.at[:, opposite], near_by.core) for ref in (eout, ein)
    ]
    for block_sum in sums:
        block_sum.back_one()
    for block_sum in sums:
        block_sum.settle()
    for copy in join_own:
        copy.wait()
    for copy in join_near:
        copy.wait_recv()
    hidden = ein.shape[1]
    for k in range(3):
        cols = pl.ds(0, hidden)
        grads[k, :, cols] = ein[k].astype(F32).T.astype(BF16)
        copies.keep(grads.at[k, :, cols], ein_out.at[k])
    for block_sum in sums:
        block_sum.back_core()
    for block_sum in sums:
        block_sum.finish()
    copies.finish()


def back(gb_parts, z_parts, gw, cot, group, keep, x, o, y, qkv, p, gain1, gain2, wqkv, wo):
    batches, rows, width = x.shape
    length = keep.shape[2]
    out = jax.ShapeDtypeStruct
    vmem = pl.BlockSpec(memory_space=pltpu.VMEM)
    anywhere = pl.BlockSpec(memory_space=pl.ANY)
    piece = gw.shape[1:]
    both = batches * rows
    half = width // 2
    tokens_shape = (batches, rows, width)
    slots = [tokens_shape] * 5
    scratch = [
        ((width, 3 * width), BF16),
        ((width, width), BF16),
        ((both, width), BF16),
        ((both, width), BF16),
        ((rows, width), F32),
        ((rows, width), BF16),
        ((rows, 3 * width), BF16),
        ((2, ITEMS, 2, ITEM_ROWS, ITEM_ROWS), BF16),
        *[(slot, BF16) for slot in slots],
        ((both, width), F32),
        ((both, width), BF16),
        ((rows, width), BF16),
        ((both, 3 * width), BF16),
        ((4, width, width), BF16),
        *[
            (shape, BF16)
            for low, high in grad_columns(width)
            for shape in (
                (4, half, high - low),
                (2, 2, half // 2, high - low),
                (2, 2, half // 4, high - low),
                (2, 3, half // 4, (high - low) // 2),
                (2, half // 4, (high - low) // 2),
            )
        ],
        ((4,) + piece, BF16),
        ((4,) + piece, BF16),
        ((3, 4 * piece[2], width), BF16),
        ((6, 8, width), F32),
        ((5, 8, width), F32),
        ((length, batches, width), BF16),
    ]
    return pl.pallas_call(
        functools.partial(back_kernel, batches),
        in_specs=[anywhere] * 4 + [vmem] * 2 + [anywhere] * 5 + [vmem] * 2 + [anywhere] * 2,
        out_specs=[anywhere] * 9,
        out_shape=[
            out((length, batches, width), BF16),
            out((length, batches, width), BF16),
            out((4, width, width), BF16),
            out((3, width, 4 * piece[2]), BF16),
            out((3, 4 * piece[2], width), BF16),
            out((8, width), F32),
            out((2,) + tokens_shape, BF16),
            out(tokens_shape, BF16),
            out((3,) + piece, BF16),
        ],
        scratch_shapes=[pltpu.VMEM(*k) for k in scratch]
        + [
            pltpu.SemaphoreType.DMA((80,)),
            pltpu.SemaphoreType.DMA((80,)),
            pltpu.SemaphoreType.DMA((64,)),
            pltpu.SemaphoreType.DMA((2,)),
        ],
        compiler_params=pltpu.CompilerParams(
            vmem_limit_bytes=VMEM_LIMIT, has_side_effects=True, collective_id=1
        ),
        cost_estimate=pl.CostEstimate(
            flops=batches
            * (2 * rows * width * width * 8 + 16 * HEADS * ITEMS * ITEM_ROWS**2 * 128),
            bytes_accessed=80_000_000,
            transcendentals=0,
        ),
        name="back",
    )(
        gb_parts, z_parts, gw, cot, group, keep,
        x.reshape(both, width), o.reshape(both, width), y, qkv, p, gain1, gain2, wqkv, wo,
    )


def attention_backward_kernel(n_parts, n_carry, *refs):
    parts = refs[:n_parts]
    (cot_ref, x_ref, y_ref, qkv_ref, p_ref, o_ref, gain1_ref, gain2_ref, wqkv_ref, wo_ref) = refs[
        n_parts : n_parts + 10
    ]
    carried = refs[n_parts + 10 : n_parts + 10 + n_carry]
    tg_ref, gwqkv_ref, gwo_ref, ggain_ref, gmix_ref, gqkv_ref = refs[n_parts + 10 + n_carry :]
    width = x_ref.shape[1]
    head_dim = width // HEADS
    gb = parts[0][...].astype(F32)
    for part in parts[1:]:
        gb = gb + part[...].astype(F32)
    unit2, inverse2 = normalize_parts(y_ref[...])
    gain2_grad = jnp.sum(gb * unit2, axis=0, keepdims=True)
    gy = cot_ref[...].astype(F32) + normalize_back(gb * gain2_ref[...], unit2, inverse2)
    ga = gy.astype(BF16)
    gwo = dot(o_ref[...], ga, 0, 0)
    if n_carry:
        gwo = gwo + carried[1][...]
    gwo_ref[...] = gwo
    gmix_ref[...] = dot(ga, wo_ref[...], 1, 1).astype(BF16)
    pair = 2 * head_dim
    left = lax.broadcasted_iota(jnp.int32, (ITEM_ROWS, pair), 1) < head_dim

    def heads(hp, carry):
        head_gradients(
            lambda rows, cols: qkv_ref[rows, cols],
            lambda rows, cols: gmix_ref[rows, cols],
            lambda item, half: p_ref[item, hp * 2 + half],
            gqkv_ref, 0, hp, width, left,
        )
        return carry

    lax.fori_loop(0, HEADS // 2, heads, 0)
    unit, inverse = normalize_parts(x_ref[...].astype(F32))
    a = (unit * gain1_ref[...]).astype(BF16)
    for part in range(3):
        cols = slice(part * width, (part + 1) * width)
        gw = dot(a, gqkv_ref[:, cols], 0, 0)
        if n_carry:
            gw = gw + carried[0][:, cols]
        gwqkv_ref[:, cols] = gw
    gnorm = dot(gqkv_ref[...], wqkv_ref[...], 1, 1)
    gain1_grad = jnp.sum(gnorm * unit, axis=0, keepdims=True)
    gains = jnp.concatenate([gain1_grad, gain2_grad, jnp.zeros((6, width), F32)], axis=0)
    if n_carry:
        gains = gains + carried[2][...]
    ggain_ref[...] = gains
    tg_ref[...] = (gy + normalize_back(gnorm * gain1_ref[...], unit, inverse)).astype(BF16)


def attention_backward(parts, cot, x, y, qkv, p, o, gain1, gain2, wqkv, wo, carried):
    rows, width = x.shape
    out = jax.ShapeDtypeStruct
    return pl.pallas_call(
        functools.partial(attention_backward_kernel, len(parts), len(carried)),
        out_shape=(
            out((rows, width), BF16),
            out((width, 3 * width), F32),
            out((width, width), F32),
            out((8, width), F32),
        ),
        scratch_shapes=[pltpu.VMEM((rows, width), BF16), pltpu.VMEM((rows, 3 * width), BF16)],
        compiler_params=pltpu.CompilerParams(vmem_limit_bytes=VMEM_LIMIT),
        cost_estimate=pl.CostEstimate(
            flops=2 * rows * width * width * 8 + 16 * HEADS * ITEMS * ITEM_ROWS**2 * 128,
            bytes_accessed=30_000_000,
            transcendentals=0,
        ),
        name="attention_backward",
    )(*parts, cot, x, y, qkv, p, o, gain1, gain2, wqkv, wo, *carried)


def expert_kernel(groups, batches, pieces, *refs):
    flags, own_ref, more_ref, b_in, g_in, z_out, gb_out, gw_out = refs[:8]
    rows_b, rows_g, w, grads, in_sem, w_sem, out_sem, gw_sem = refs[8:]
    part = own_ref.shape[2]

    def rounded(rows):
        return (rows + TILE - 1) // TILE * TILE

    merged = [
        flags[g, 0, micro * ITEMS + item]
        for g in range(groups)
        for micro in range(batches)
        for item in range(ITEMS)
    ]
    n_merged = sum(merged)
    n_plain = len(merged) - n_merged
    sizes = [n_plain * IMAGE_ROWS, n_plain * CAPTION, n_merged * ITEM_ROWS]
    starts = [0, rounded(sizes[0]), rounded(sizes[0]) + rounded(sizes[1])]
    ends = [start + rounded(size) for start, size in zip(starts, sizes)]
    blocks = []
    plain, joined = 0, 0
    for flat, flag in enumerate(merged):
        g, micro, item = flat // (batches * ITEMS), flat // ITEMS % batches, flat % ITEMS
        base = item * ITEM_ROWS
        image = jnp.where(flag == 1, starts[2] + joined * ITEM_ROWS, plain * IMAGE_ROWS)
        caption = jnp.where(
            flag == 1, image + IMAGE_ROWS, starts[1] + plain * CAPTION
        )
        blocks.append((g, micro, base, IMAGE_ROWS, image, flag, 0))
        blocks.append((g, micro, base + IMAGE_ROWS, CAPTION, caption, flag, 1))
        plain, joined = plain + 1 - flag, joined + flag

    def copy_of(which, number, outward):
        g, micro, base, size, at, _, _ = blocks[number]
        held = (rows_b, rows_g)[which].at[pl.ds(pl.multiple_of(at, 16), size)]
        if outward:
            far = (gb_out, z_out)[which].at[g, micro, pl.ds(base, size)]
            return pltpu.make_async_copy(held, far, out_sem.at[which, number])
        far = (b_in, g_in)[which].at[g, micro, pl.ds(base, size)]
        return pltpu.make_async_copy(far, held, in_sem.at[which, number])

    def of_expert(expert, act, numbers=None):
        for number, (_, _, _, _, _, flag, kind) in enumerate(blocks):
            if numbers is not None and number not in numbers:
                continue
            if expert == 2 or kind == expert:
                @pl.when(flag == (1 if expert == 2 else 0))
                def _(number=number):
                    for which in range(2):
                        act(which, number)

    def weight_copy(k, i):
        piece = own_ref if i == 0 else more_ref.at[i - 1]
        return pltpu.make_async_copy(
            piece.at[k], w.at[k, :, pl.ds(i * part, part), :], w_sem.at[k, i]
        )

    for k in range(3):
        tail = pl.multiple_of(jnp.maximum(ends[k] - TILE, 0), TILE)
        rows_b[pl.ds(tail, TILE), :] = jnp.zeros((TILE, rows_b.shape[1]), BF16)
        rows_g[pl.ds(tail, TILE), :] = jnp.zeros((TILE, rows_g.shape[1]), BF16)
    def start_rows(k, numbers):
        of_expert(k, lambda which, number: copy_of(which, number, False).start(), numbers)

    early = range(len(blocks) // 2)
    late = range(len(blocks) // 2, len(blocks))
    early_plain = sum(1 - flag for flag in merged[: len(merged) // 2])
    middle = early_plain * IMAGE_ROWS // (2 * TILE)

    def wait_rows(k, numbers):
        of_expert(k, lambda which, number: copy_of(which, number, False).wait(), numbers)

    for i in range(pieces):
        weight_copy(0, i).start()
    start_rows(0, early)
    start_rows(0, late)
    for k in range(3):
        grads[...] = jnp.zeros(grads.shape, F32)
        for i in range(pieces):
            weight_copy(k, i).wait()
        wait_rows(k, early)
        if k == 0:
            for other in (1, 2):
                for i in range(pieces):
                    weight_copy(other, i).start()
                start_rows(other, early)
                start_rows(other, late)
        if k > 0:
            wait_rows(k, late)

        def tile(start, size, k=k):
            at = pl.ds(pl.multiple_of(start, TILE), size)
            b, gz = rows_b[at, :], rows_g[at, :]
            u, slope = gelu_and_slope(dot(b, w[k, 0], 1, 1))
            gh = (dot(gz, w[k, 1], 1, 1) * slope).astype(BF16)
            u = u.astype(BF16)
            z, gb = dot(u, w[k, 1], 1, 0), dot(gh, w[k, 0], 1, 0)
            grads[0] += dot(gh, b, 0, 0)
            grads[1] += dot(u, gz, 0, 0)
            rows_b[at, :] = gb.astype(BF16)
            rows_g[at, :] = z.astype(BF16)

        doubles = (ends[k] - starts[k]) // (2 * TILE)

        def double(t, carry, k=k):
            if k == 0:
                @pl.when(t == middle)
                def _():
                    wait_rows(0, late)

            tile(starts[k] + t * 2 * TILE, 2 * TILE)
            return carry

        lax.fori_loop(0, doubles, double, 0)
        if k == 0:
            @pl.when(middle >= doubles)
            def _():
                wait_rows(0, late)

        @pl.when((ends[k] - starts[k]) // TILE > 2 * doubles)
        def _(k=k):
            tile(ends[k] - TILE, TILE)

        of_expert(k, lambda which, number: copy_of(which, number, True).start())
        w[k] = grads[...].astype(BF16)
        for i in range(pieces):
            pltpu.make_async_copy(
                w.at[k, :, pl.ds(i * part, part), :], gw_out.at[i, k], gw_sem.at[k, i]
            ).start()
    for number in range(len(blocks)):
        for which in range(2):
            copy_of(which, number, True).wait()
    for k in range(3):
        for i in range(pieces):
            pltpu.make_async_copy(
                w.at[k, :, pl.ds(i * part, part), :], gw_out.at[i, k], gw_sem.at[k, i]
            ).wait()


def experts(flags, own, more, b_groups, g_groups):
    groups, batches, rows, width = b_groups.shape
    part = own.shape[2]
    pieces = 1 + (more.shape[0] if more.ndim == 5 else 0)
    hidden = part * pieces
    count = groups * batches * ITEMS
    capacity = (count * ITEM_ROWS // TILE + 4) * TILE
    out = jax.ShapeDtypeStruct
    anywhere = pl.BlockSpec(memory_space=pl.ANY)
    return pl.pallas_call(
        functools.partial(expert_kernel, groups, batches, pieces),
        in_specs=[pl.BlockSpec(memory_space=pltpu.SMEM)] + [anywhere] * 4,
        out_specs=[anywhere] * 3,
        out_shape=[out(b_groups.shape, BF16)] * 2 + [out((pieces,) + own.shape, BF16)],
        scratch_shapes=[
            pltpu.VMEM((capacity, width), BF16),
            pltpu.VMEM((capacity, width), BF16),
            pltpu.VMEM((3, 2, hidden, width), BF16),
            pltpu.VMEM((2, hidden, width), F32),
            pltpu.SemaphoreType.DMA((2, 2 * count)),
            pltpu.SemaphoreType.DMA((3, pieces)),
            pltpu.SemaphoreType.DMA((2, 2 * count)),
            pltpu.SemaphoreType.DMA((3, pieces)),
        ],
        compiler_params=pltpu.CompilerParams(vmem_limit_bytes=VMEM_LIMIT),
        cost_estimate=pl.CostEstimate(
            flops=2 * 6 * count * ITEM_ROWS * width * hidden,
            bytes_accessed=45_000_000,
            transcendentals=count * ITEM_ROWS * hidden,
        ),
        name="experts",
    )(flags, own, more, b_groups, g_groups)


def from_items(rows, first):
    one, two = rows[IMAGE_ROWS:ITEM_ROWS], rows[ITEM_ROWS + IMAGE_ROWS :]
    return jnp.concatenate(
        [
            rows[:PATCHES],
            rows[ITEM_ROWS : ITEM_ROWS + PATCHES],
            jnp.where(first, one, two),
            jnp.where(first, two, one),
        ],
        axis=0,
    )


class Links:
    def __init__(self):
        self.hosts = lax.axis_size("expert")
        self.dp = lax.axis_size("dp")
        self.direct = self.hosts == 4 and self.dp == 8
        self.me = lax.axis_index("expert")

    def flip(self, v, bit):
        return lax.ppermute(v, "expert", [(i, i ^ bit) for i in range(4)])

    def across_y(self, v):
        return lax.ppermute(v, "dp", [(i, i ^ 1) for i in range(8)])

    def along_z(self, v, shift):
        return lax.ppermute(v, "dp", [(i, (i + 2 * shift) % 8) for i in range(8)])

    def gather_tokens(self, v):
        if not self.direct:
            return list(lax.all_gather(v, "expert"))
        near, far = self.flip(v, 1), self.flip(v, 2)
        return [v, near, far, self.flip(far, 1)]

    def reduce_tokens(self, parts):
        if not self.direct:
            return [lax.psum_scatter(jnp.stack(parts), "expert", scatter_dimension=0)]
        far = (parts[2].astype(F32) + self.flip(parts[3], 1).astype(F32)).astype(BF16)
        return [parts[0], self.flip(parts[1], 1), self.flip(far, 2)]

    def reduce_weights(self, pieces):
        if not self.direct:
            return lax.psum_scatter(pieces[0], "dp", scatter_dimension=2, tiled=True)
        total = None
        for at, shift in enumerate((0, 1, 3, 2)):
            piece = pieces[2 * at].astype(F32) + self.across_y(pieces[2 * at + 1]).astype(F32)
            if shift:
                piece = self.along_z(piece.astype(BF16), -shift).astype(F32)
            total = piece if total is None else total + piece
        return total.astype(BF16)

    def join_hidden(self, v):
        if not self.direct:
            return lax.all_gather(v, "expert", axis=2, tiled=True)
        stacked = jnp.stack(self.gather_tokens(v))
        return jnp.concatenate(
            [
                lax.dynamic_index_in_dim(stacked, i ^ self.me, 0, keepdims=False)
                for i in range(4)
            ],
            axis=2,
        )


def shards(
    tokens,
    cotangent,
    item_group,
    routes,
    slot_order,
    attn_gain,
    ffn_gain,
    qkv_weight,
    out_weight,
    expert_in,
    expert_out,
):
    links = Links()
    hosts, me = links.hosts, links.me
    batches, length, width = tokens.shape
    shard = expert_in.shape[2]
    part = shard // hosts
    gain1, gain2 = attn_gain, ffn_gain

    own = jnp.stack(
        [
            jnp.swapaxes(lax.dynamic_slice_in_dim(expert_in, me * part, part, 2), 1, 2),
            lax.dynamic_slice_in_dim(expert_out, me * part, part, 1),
        ],
        axis=1,
    )
    first = item_group[:, ITEMS * PATCHES] == 0
    (
        w_all, gz_groups, flag_groups, b_groups, x_all, qkv_all, p_all, o_all, y_all, cot_all, kept
    ) = front(
        links.direct, hosts, own, jnp.swapaxes(tokens, 0, 1), jnp.swapaxes(cotangent, 0, 1),
        item_group, routes, slot_order, gain1, gain2, qkv_weight, out_weight,
    )
    if not links.direct:
        own = lax.all_gather(own, "dp", axis=2, tiled=True)
        gz_groups, flag_groups, b_groups = [
            lax.all_gather(v[0], "expert") for v in (gz_groups, flag_groups, b_groups)
        ]
    z_parts, gb_parts, gw_pieces = experts(flag_groups, own, w_all, b_groups, gz_groups)
    if links.direct:
        result, token_grad, gall, ein_sum, eout_sum, gains, *_ = back(
            gb_parts, z_parts, gw_pieces, cot_all, item_group, kept,
            x_all, o_all, y_all, qkv_all, p_all, gain1, gain2, qkv_weight, out_weight,
        )
        return (
            jnp.swapaxes(result, 0, 1),
            jnp.swapaxes(token_grad, 0, 1),
            gains[0],
            gains[1],
            jnp.concatenate([gall[i].astype(F32) for i in range(3)], axis=1),
            gall[3].astype(F32),
            ein_sum.astype(F32),
            eout_sum.astype(F32),
        )
    gb_terms = links.reduce_tokens(gb_parts)
    z_terms = links.reduce_tokens(z_parts)
    sums = links.join_hidden(links.reduce_weights(gw_pieces)).astype(F32)

    results, token_grads, carried = [], [], ()
    for m in range(batches):
        x, qkv, p, o, y = x_all[m], qkv_all[m], p_all[m], o_all[m], y_all[m]
        at = m
        tg, *carried = attention_backward(
            [t[at] for t in gb_terms],
            cot_all[m], x, y, qkv, p, o, gain1, gain2, qkv_weight, out_weight,
            tuple(carried),
        )
        token_grads.append(from_items(tg, first[m]))
        z = z_terms[0][at].astype(F32)
        for term in z_terms[1:]:
            z = z + term[at].astype(F32)
        branch = jnp.where(kept[m, 0][:, None] > 0, from_items(z, first[m]), 0.0)
        results.append((from_items(y, first[m]) + branch).astype(BF16))
    gw_qkv, gw_out, gains = carried
    packed = jnp.concatenate(
        [
            jnp.concatenate([gw_qkv, gw_out], axis=1),
            jnp.pad(gains[:2].reshape(1, 2 * width), ((0, 7), (0, 2 * width))),
        ],
        axis=0,
    ).astype(BF16)
    packed = lax.psum(packed, ("dp", "expert")).astype(F32)
    return (
        jnp.stack(results),
        jnp.stack(token_grads),
        packed[width, :width],
        packed[width, width : 2 * width],
        packed[:width, : 3 * width],
        packed[:width, 3 * width :],
        jnp.swapaxes(sums[:, 0], 1, 2),
        sums[:, 1],
    )


def solution(mesh):
    in_specs = (
        P(None, ("dp", "expert"), None),
        P(None, ("dp", "expert"), None),
        P(None, ("dp", "expert")),
        P(None, ("dp", "expert")),
        P(None, ("dp", "expert"), None),
        P(),
        P(),
        P(),
        P(),
        P(None, None, "dp"),
        P(None, "dp", None),
    )
    out_specs = (
        P(None, ("dp", "expert"), None),
        P(None, ("dp", "expert"), None),
        P(),
        P(),
        P(),
        P(),
        P(None, None, "dp"),
        P(None, "dp", None),
    )
    return jax.shard_map(shards, mesh=mesh, in_specs=in_specs, out_specs=out_specs, check_vma=False)
```

```python
import functools

import jax
import jax.numpy as jnp
from jax import lax
from jax.experimental import pallas as pl
from jax.experimental.pallas import tpu as pltpu
from jax.sharding import PartitionSpec as P

HEADS = 12
EPSILON = 1e-05
PATCHES = 197
CAPTION = 64
ITEMS = 2
IMAGE_ROWS = 208
ITEM_ROWS = IMAGE_ROWS + CAPTION
ROWS = ITEMS * ITEM_ROWS
TILE = 256
VMEM_LIMIT = 60 * 1024 * 1024
F32 = jnp.float32
BF16 = jnp.bfloat16


def dot(a, b, a_dim, b_dim):
    return lax.dot_general(
        a, b, (((a_dim,), (b_dim,)), ((), ())), preferred_element_type=F32
    )


def normalize_parts(v):
    centred = v - jnp.mean(v, axis=-1, keepdims=True)
    inverse = lax.rsqrt(jnp.mean(centred * centred, axis=-1, keepdims=True) + EPSILON)
    return centred * inverse, inverse


def normalize_back(grad_unit, unit_rows, inverse):
    return inverse * (
        grad_unit
        - jnp.mean(grad_unit, axis=-1, keepdims=True)
        - unit_rows * jnp.mean(grad_unit * unit_rows, axis=-1, keepdims=True)
    )


def gelu_and_slope(h):
    bell = jnp.exp2(h * h * (-0.5 * 1.4426950408889634))
    t = pl.reciprocal(1.0 + (0.3275911 * 0.7071067811865476) * jnp.abs(h))
    half_poly = t * (
        0.127414796
        + t * (-0.142248368 + t * (0.7107068705 + t * (-0.7265760135 + t * 0.5307027145)))
    )
    below = half_poly * bell
    phi = jnp.where(h > 0, 1.0 - below, below)
    return h * phi, phi + (h * bell) * 0.3989422804014327


class Partners:
    def __init__(self):
        dp, expert = lax.axis_index("dp"), lax.axis_index("expert")
        self.core = (dp, expert + 1 - 2 * (expert % 2))
        self.x = (dp, (expert + 2) % 4)
        self.y = (dp + 1 - 2 * (dp % 2), expert)
        self.z = {shift: ((dp + 2 * shift) % 8, expert) for shift in (1, 2, 3)}
        self.z_pair = (dp + 2 - 4 * (dp // 2 % 2), expert)

    def greet(self):
        barrier = pltpu.get_barrier_semaphore()
        everyone = [self.core, self.x, self.y, self.z[1], self.z[2], self.z[3]]
        for other in everyone:
            pl.semaphore_signal(
                barrier, inc=1, device_id=other, device_id_type=pl.DeviceIdType.MESH
            )
        pl.semaphore_wait(barrier, len(everyone))


class Copies:
    def __init__(self, send_sem, recv_sem, local_sem):
        self.send_sem, self.recv_sem, self.local_sem = send_sem, recv_sem, local_sem
        self.sent, self.kept, self.sends, self.locals = [], [], 0, 0

    def send(self, src, dst, device):
        at = self.sends
        self.sends += 1
        copy = pltpu.make_async_remote_copy(
            src_ref=src,
            dst_ref=dst,
            send_sem=self.send_sem.at[at],
            recv_sem=self.recv_sem.at[at],
            device_id=device,
            device_id_type=pl.DeviceIdType.MESH,
        )
        copy.start()
        self.sent.append(copy)
        return copy

    def keep(self, src, dst):
        copy = self.load(src, dst)
        self.kept.append(copy)
        return copy

    def load(self, src, dst):
        copy = pltpu.make_async_copy(src, dst, self.local_sem.at[self.locals])
        self.locals += 1
        copy.start()
        return copy

    def settle(self, done):
        for copy in done:
            copy.wait_send()
        self.sent = [copy for copy in self.sent if all(copy is not other for other in done)]

    def finish(self):
        for copy in self.sent:
            copy.wait_send()
        for copy in self.kept:
            copy.wait()


def pick_rows(group_ref, m, length, rows=slice(0, ROWS)):
    count = rows.stop - rows.start
    row = lax.broadcasted_iota(jnp.int32, (count, 1), 0) + rows.start
    item = (row >= ITEM_ROWS).astype(jnp.int32)
    inside = row - item * ITEM_ROWS
    images = ITEMS * PATCHES
    swapped = (group_ref[m : m + 1, images : images + 1] != 0).astype(jnp.int32)
    caption = item + swapped - 2 * item * swapped
    token = jnp.where(
        inside < PATCHES,
        item * PATCHES + inside,
        jnp.where(inside < IMAGE_ROWS, -1, images + caption * CAPTION + inside - IMAGE_ROWS),
    )
    return lax.broadcasted_iota(jnp.int32, (count, length), 1) == token


def kept_tokens(routing, priority, hosts, capacity):
    length = routing.shape[1]
    across = lax.broadcasted_iota(jnp.int32, (length, length), 1)
    down = lax.broadcasted_iota(jnp.int32, (length, length), 0)

    def upright(row):
        return jnp.sum(jnp.where(across == down, row, 0.0), axis=1, keepdims=True)

    order = upright(priority.astype(F32))
    position = jnp.sum(
        jnp.where(order == across.astype(F32), down.astype(F32), 0.0), axis=0, keepdims=True
    )
    route = routing.astype(F32)
    ahead = (upright(route) == route) & (upright(position) < position)
    rank = jnp.sum(jnp.where(ahead, 1.0, 0.0), axis=0, keepdims=True)
    slots = jnp.zeros_like(rank)
    for kind in range(3):
        slots = jnp.where(routing == kind, float(capacity * ((hosts - kind + 2) // 3)), slots)
    return jnp.where(rank < slots, 1.0, 0.0)


def front_kernel(direct, hosts, batches, *refs):
    (own_ref, tokens_ref, cot_ref, group_ref, routes_ref, order_ref, gain1_ref, gain2_ref) = refs[:8]
    wqkv_ref, wo_ref, w_all, gz_all, flags_all, b_all = refs[8:14]
    x_out, qkv_out, p_out, o_out, y_out, cot_out = refs[14:20]
    (
        keep_ref, gz_scr, b_scr, x_scr, qkv_scr, p_scr, o_scr, y_scr, cot_scr, flags_scr,
        send_sem, recv_sem, local_sem,
    ) = refs[20:]
    length, _, width = tokens_ref.shape
    head_dim = width // HEADS
    pair = 2 * head_dim
    copies = Copies(send_sem, recv_sem, local_sem)

    def spread(src, slots):
        copies.keep(src, slots(0))
        if not direct:
            return None
        near = copies.send(src, slots(1), near_by.core)
        return near, copies.send(src, slots(2), near_by.x)

    def pass_on(pair_of, slots):
        near, far = pair_of
        far.wait_recv()
        return near, copies.send(slots(2), slots(3), near_by.core)

    if direct:
        near_by = Partners()
        near_by.greet()
        over_y = [copies.send(own_ref, w_all.at[0], near_by.y)]
        along = [[], [], []]

        def z_half(i):
            along[0].append(copies.send(own_ref.at[:, i], w_all.at[1, :, i], near_by.z_pair))
            along[1].append(copies.send(own_ref.at[:, i], w_all.at[3, :, i], near_by.z[2]))

        def z_pass(i):
            for k in (1, 0):
                along[k][i].wait_recv()
            if i == 1:
                for half in range(2):
                    along[2].append(
                        copies.send(w_all.at[3, :, half], w_all.at[5, :, half], near_by.z_pair)
                    )
            for at in (3, 1):
                over_y.append(copies.send(w_all.at[at, :, i], w_all.at[at + 1, :, i], near_by.y))

        def z_last(i):
            along[2][i].wait_recv()
            over_y.append(copies.send(w_all.at[5, :, i], w_all.at[6, :, i], near_by.y))

        z_half(0)
    lane = lax.broadcasted_iota(jnp.int32, flags_scr.shape, 1)
    merged = jnp.zeros(flags_scr.shape, jnp.int32)
    for m in range(batches):
        for item in range(ITEMS):
            route = routes_ref[m : m + 1, item * PATCHES : item * PATCHES + 1]
            here = lane == m * ITEMS + item
            merged = jnp.where(here & (route == 2), 1, merged)
    flags_scr[...] = merged
    flags = spread(flags_scr, lambda i: flags_all.at[i])

    gz = []
    for m in range(batches):
        keep_ref[m] = kept_tokens(
            routes_ref[m : m + 1], order_ref[m], hosts, 2 * length // hosts
        )
        chosen = pick_rows(group_ref, m, length)
        cot = dot(chosen.astype(BF16), cot_ref[:, m], 1, 0)
        keep = jnp.sum(jnp.where(chosen, keep_ref[m], 0.0), axis=1, keepdims=True)
        cot_scr[m] = cot.astype(BF16)
        gz_scr[m] = jnp.where(keep > 0, cot, 0.0).astype(BF16)
        gz.append(spread(gz_scr.at[m], lambda i, m=m: gz_all.at[i, m]))

    left = lax.broadcasted_iota(jnp.int32, (ITEM_ROWS, pair), 1) < head_dim
    key = lax.broadcasted_iota(jnp.int32, (1, ITEM_ROWS), 1)
    bias = jnp.where((key >= PATCHES) & (key < IMAGE_ROWS), -1e30, 0.0).astype(F32)
    b_sent = []
    for m in range(batches):
        xb = dot(pick_rows(group_ref, m, length).astype(BF16), tokens_ref[:, m], 1, 0)
        x_scr[m] = xb.astype(BF16)
        unit, _ = normalize_parts(xb)
        a = (unit * gain1_ref[...]).astype(BF16)
        for part in range(3):
            cols = slice(part * width, (part + 1) * width)
            qkv_scr[m, :, cols] = dot(a, wqkv_ref[:, cols], 1, 0).astype(BF16)

        def heads(hp, carry, m=m):
            at_q = pl.ds(pl.multiple_of(hp * pair, pair), pair)
            at_k = pl.ds(pl.multiple_of(width + hp * pair, pair), pair)
            at_v = pl.ds(pl.multiple_of(2 * width + hp * pair, pair), pair)
            for item in range(ITEMS):
                rows = slice(item * ITEM_ROWS, (item + 1) * ITEM_ROWS)
                q, k, v = qkv_scr[m, rows, at_q], qkv_scr[m, rows, at_k], qkv_scr[m, rows, at_v]
                outs = []
                for half in range(2):
                    mine = left if half == 0 else ~left
                    s = dot(jnp.where(mine, q, 0), k, 1, 1) * (head_dim**-0.5) + bias
                    e = jnp.exp(s - jnp.max(s, axis=-1, keepdims=True))
                    p = (e * (1.0 / jnp.sum(e, axis=-1, keepdims=True))).astype(BF16)
                    p_scr[m, item, hp * 2 + half] = p
                    outs.append(dot(p, v, 1, 0))
                o_scr[m, rows, at_q] = jnp.where(left, outs[0], outs[1]).astype(BF16)
            return carry

        lax.fori_loop(0, HEADS // 2, heads, 0)
        if direct and m == 0:
            z_pass(0)
            z_half(1)
        y = x_scr[m].astype(F32) + dot(o_scr[m], wo_ref[...], 1, 0)
        y_scr[m] = y
        unit2, _ = normalize_parts(y)
        b_scr[m] = (unit2 * gain2_ref[...]).astype(BF16)
        b_sent.append(spread(b_scr.at[m], lambda i, m=m: b_all.at[i, m]))
        for scr, out in (
            (x_scr, x_out), (qkv_scr, qkv_out), (p_scr, p_out), (o_scr, o_out), (y_scr, y_out),
            (cot_scr, cot_out),
        ):
            copies.keep(scr.at[m], out.at[m])
        if direct and m == 0:
            flags = pass_on(flags, lambda i: flags_all.at[i])

    if direct:
        z_pass(1)
        z_last(0)
        gz = [
            pass_on(sent, lambda i, m=m: gz_all.at[i, m]) for m, sent in enumerate(gz)
        ]
        b_sent[0] = pass_on(b_sent[0], lambda i: b_all.at[i, 0])
        z_last(1)
        for m in range(1, batches):
            b_sent[m] = pass_on(b_sent[m], lambda i, m=m: b_all.at[i, m])
        for copy in [*over_y, *flags] + [c for pair_of in gz + b_sent for c in pair_of]:
            copy.wait_recv()
    copies.finish()


def front(direct, hosts, own, tokens, cot, group, routes, order, gain1, gain2, wqkv, wo):
    length, batches, width = tokens.shape
    groups = 4 if direct else 1
    out = jax.ShapeDtypeStruct
    vmem = pl.BlockSpec(memory_space=pltpu.VMEM)
    anywhere = pl.BlockSpec(memory_space=pl.ANY)
    kept = [
        ((batches, ROWS, width), BF16),
        ((batches, ROWS, 3 * width), BF16),
        ((batches, ITEMS, HEADS, ITEM_ROWS, ITEM_ROWS), BF16),
        ((batches, ROWS, width), BF16),
        ((batches, ROWS, width), F32),
        ((batches, ROWS, width), BF16),
    ]
    scratch = [pltpu.VMEM((batches, ROWS, width), BF16)] * 2
    return pl.pallas_call(
        functools.partial(front_kernel, direct, hosts, batches),
        in_specs=[anywhere] + [vmem] * 9,
        out_specs=[anywhere] * 10 + [vmem],
        out_shape=[
            out((7 if direct else 1,) + (own.shape if direct else (8, 128)), BF16),
            out((groups, batches, ROWS, width), BF16),
            out((groups, 8, 128), jnp.int32),
            out((groups, batches, ROWS, width), BF16),
        ]
        + [out(*k) for k in kept]
        + [out((batches, 1, length), F32)],
        scratch_shapes=scratch
        + [pltpu.VMEM(*k) for k in kept]
        + [
            pltpu.VMEM((8, 128), jnp.int32),
            pltpu.SemaphoreType.DMA((32,)),
            pltpu.SemaphoreType.DMA((32,)),
            pltpu.SemaphoreType.DMA((24,)),
        ],
        compiler_params=pltpu.CompilerParams(
            vmem_limit_bytes=VMEM_LIMIT,
            has_side_effects=direct,
            collective_id=0 if direct else None,
        ),
        cost_estimate=pl.CostEstimate(
            flops=batches
            * (2 * ROWS * width * width * 4 + 8 * HEADS * ITEMS * ITEM_ROWS**2 * 128),
            bytes_accessed=60_000_000,
            transcendentals=batches * HEADS * ITEMS * ITEM_ROWS**2,
        ),
        name="front",
    )(own, tokens, cot, group, routes, order, gain1, gain2, wqkv, wo)


def head_gradients(qkv_at, go_at, p_of, gqkv_ref, row0, hp, width, left):
    head_dim = width // HEADS
    pair = 2 * head_dim
    scaling = head_dim**-0.5
    at_q = pl.ds(pl.multiple_of(hp * pair, pair), pair)
    at_k = pl.ds(pl.multiple_of(width + hp * pair, pair), pair)
    at_v = pl.ds(pl.multiple_of(2 * width + hp * pair, pair), pair)
    for item in range(ITEMS):
        rows = slice(item * ITEM_ROWS, (item + 1) * ITEM_ROWS)
        out_rows = slice(row0 + rows.start, row0 + rows.stop)
        q, k, v = qkv_at(rows, at_q), qkv_at(rows, at_k), qkv_at(rows, at_v)
        go = go_at(rows, at_q)
        gq, gk, gv = [], [], []
        for half in range(2):
            mine = left if half == 0 else ~left
            p = p_of(item, half)
            pf = p.astype(F32)
            gp = dot(jnp.where(mine, go, 0), v, 1, 1)
            gs = (pf * (gp - jnp.sum(pf * gp, axis=-1, keepdims=True))).astype(BF16)
            gv.append(dot(p, go, 0, 0))
            gq.append(dot(gs, k, 1, 0))
            gk.append(dot(gs, q, 0, 0))
        gqkv_ref[out_rows, at_q] = (jnp.where(left, gq[0], gq[1]) * scaling).astype(BF16)
        gqkv_ref[out_rows, at_k] = (jnp.where(left, gk[0], gk[1]) * scaling).astype(BF16)
        gqkv_ref[out_rows, at_v] = jnp.where(left, gv[0], gv[1]).astype(BF16)


def add(*terms):
    total = terms[0].astype(F32)
    for term in terms[1:]:
        total = total + term.astype(F32)
    return total.astype(BF16)


def rows_at(start, size):
    return pl.ds(pl.multiple_of(start, 32), size)


class BlockSum:
    def __init__(self, copies, near_by, place, grads, gall, low, high, buffers):
        self.copies, self.near_by, self.grads, self.gall = copies, near_by, grads, gall
        self.r_core, self.r_one, self.r_two, self.r_z, self.final = buffers
        self.low, self.size = low, high - low
        self.cols = pl.ds(low, high - low)
        core, xi, yi, self.zi = place
        self.half = grads.shape[1] // 2
        self.quarter, self.eighth = self.half // 2, self.half // 4
        self.row = core * self.half
        self.parts = []
        for part, (one, two) in enumerate(((xi, yi), (yi, xi))):
            pair = pl.ds(2 * part, 2)
            ways = (near_by.x, near_by.y) if part == 0 else (near_by.y, near_by.x)
            row_one = self.row + one * self.quarter
            row_two = row_one + two * self.eighth
            away_one = self.row + (1 - one) * self.quarter
            away_two = row_one + (1 - two) * self.eighth
            self.parts.append((pair, ways, row_one, row_two, away_one, away_two))

    def z_block(self, ref, part, row, z):
        chunk = self.size // 2
        cols = pl.ds(pl.multiple_of(self.low + z % 2 * chunk, 128), chunk)
        return ref.at[2 * part + z // 2, rows_at(row, self.eighth), cols]

    def start(self):
        away = self.grads.at[:, rows_at(self.half - self.row, self.half), self.cols]
        self.core = self.copies.send(away, self.r_core, self.near_by.core)

    def take(self, row, size, first, terms):
        at = rows_at(row, size)
        for i in range(terms.shape[0]):
            self.grads[first + i, at, self.cols] = add(
                self.grads[first + i, at, self.cols], terms[i]
            )

    def one(self):
        self.core.wait_recv()
        self.take(self.row, self.half, 0, self.r_core)
        self.ones = [
            self.copies.send(
                self.grads.at[pair, rows_at(away, self.quarter), self.cols],
                self.r_one.at[i], ways[0],
            )
            for i, (pair, ways, _, _, away, _) in enumerate(self.parts)
        ]

    def two(self):
        self.twos = []
        for i, (pair, ways, row, _, _, away) in enumerate(self.parts):
            self.ones[i].wait_recv()
            self.take(row, self.quarter, 2 * i, self.r_one.at[i])
            self.twos.append(
                self.copies.send(
                    self.grads.at[pair, rows_at(away, self.eighth), self.cols],
                    self.r_two.at[i], ways[1],
                )
            )

    def three(self):
        self.threes = []
        for i, (_, _, _, row, _, _) in enumerate(self.parts):
            self.twos[i].wait_recv()
            self.take(row, self.eighth, 2 * i, self.r_two.at[i])
            self.threes.append(
                [
                    self.copies.send(
                        self.z_block(self.grads, i, row, (self.zi + shift) % 4),
                        self.r_z.at[i, shift - 1], self.near_by.z[shift],
                    )
                    for shift in (1, 2, 3)
                ]
            )

    def back_three(self):
        self.threes_back = []
        for i, (_, _, _, row, _, _) in enumerate(self.parts):
            for copy in self.threes[i]:
                copy.wait_recv()
            mine = self.z_block(self.grads, i, row, self.zi)
            self.final[i] = add(mine[...], self.r_z[i, 0], self.r_z[i, 1], self.r_z[i, 2])
            place = self.z_block(self.gall, i, row, self.zi)
            own = self.copies.load(self.final.at[i], place)
            self.threes_back.append(
                (
                    own,
                    [
                        self.copies.send(self.final.at[i], place, self.near_by.z[shift])
                        for shift in (1, 2, 3)
                    ],
                )
            )

    def give(self, row, size, pair, to):
        block = self.gall.at[pair, rows_at(row, size), self.cols]
        return self.copies.send(block, block, to)

    def back_two(self):
        self.twos_back = []
        for i, (pair, ways, _, row, _, _) in enumerate(self.parts):
            own, others = self.threes_back[i]
            own.wait()
            for copy in others:
                copy.wait_recv()
            self.twos_back.append(self.give(row, self.eighth, pair, ways[1]))

    def back_one(self):
        self.ones_back = []
        for i, (pair, ways, row, _, _, _) in enumerate(self.parts):
            self.twos_back[i].wait_recv()
            self.ones_back.append(self.give(row, self.quarter, pair, ways[0]))

    def back_core(self):
        self.cores_back = []
        for i, (pair, *_) in enumerate(self.parts):
            self.ones_back[i].wait_recv()
            self.cores_back.append(self.give(self.row, self.half, pair, self.near_by.core))

    def finish(self):
        for copy in self.cores_back:
            copy.wait_recv()

    def settle(self):
        sent = [self.core, *self.ones, *self.twos, *self.threes[0], *self.threes[1]]
        self.copies.settle(sent)


PAIRS = HEADS // 2
FIRST_PAIRS = 4


def grad_columns(width):
    cut = FIRST_PAIRS * (width // PAIRS)
    return ((0, cut), (cut, width))


def back_kernel(batches, *refs):
    gb_parts, z_parts, gw, cot_in, group_ref, keep_ref, x_in, o_in, y_in, qkv_in, p_in = refs[:11]
    gain1_ref, gain2_ref, wqkv_in, wo_in = refs[11:15]
    result_out, tg_out, gall, ein_out, eout, gains_out, z_core, z_far, rs_z = refs[15:24]
    (
        wqkv, wo, x, o, y, cot, qkv, p, gb_own, gb_far, gb_core, gb_cross, gb_x,
        gy, ga, go, gqkv, grads, *sum_buffers,
        held, r_y, ein, gsum, gain_in, tok, send_sem, recv_sem, local_sem, p_sem,
    ) = refs[24:]
    width = x.shape[1]
    head_dim = width // HEADS
    pair = 2 * head_dim
    length = tok.shape[0]
    dp, expert = lax.axis_index("dp"), lax.axis_index("expert")
    core, xi, yi, zi = expert % 2, expert // 2, dp % 2, dp // 2
    copies = Copies(send_sem, recv_sem, local_sem)
    near_by = Partners()
    near_by.greet()
    load, send = copies.load, copies.send

    crossed, nearer = [], []
    for m in range(batches):
        crossed.append(send(gb_parts.at[3, m], gb_cross.at[m], near_by.core))
        nearer.append(send(gb_parts.at[1, m], gb_core.at[m], near_by.core))
    order = (6, 4, 2, 0)
    pieces = [send(gw.at[order[0] + 1], r_y.at[0], near_by.y)]
    far_loads = [load(gb_parts.at[2, m], gb_far.at[m]) for m in range(batches)]
    own_loads = [load(gb_parts.at[0, m], gb_own.at[m]) for m in range(batches)]
    first_loads = [load(y_in.at[0], y), load(cot_in.at[0], cot)]
    held_loads = [load(gw.at[order[i]], held.at[i]) for i in range(4)]
    late_loads = [load(o_in, o), load(wo_in, wo), load(qkv_in.at[0], qkv)]
    last_loads = [load(x_in, x), load(wqkv_in, wqkv)]
    def far_sum(m):
        far_loads[m].wait()
        crossed[m].wait_recv()
        gb_far[m] = add(gb_far[m], gb_cross[m])

    far_sum(0)
    along = [send(gb_far.at[0], gb_x.at[0], near_by.x)]
    z_crossed = [send(z_parts.at[3, m], z_core.at[1, m], near_by.core) for m in range(batches)]
    z_nearer = [send(z_parts.at[1, m], z_core.at[0, m], near_by.core) for m in range(batches)]
    for m in range(1, batches):
        far_sum(m)

    sent_z = []
    z_ways = (near_by.z_pair, near_by.z[2], near_by.z_pair)

    def reduce_piece(i):
        pieces[i].wait_recv()
        if i < 3:
            pieces.append(send(gw.at[order[i + 1] + 1], r_y.at[i + 1], near_by.y))
        held_loads[i].wait()
        come = {0: (), 1: (0,), 2: (), 3: (1, 2)}[i]
        for j in come:
            sent_z[j].wait_recv()
        loads = [load(rs_z.at[j], r_y.at[at]) for at, j in enumerate(come)]
        for copy in loads:
            copy.wait()
        held[i] = add(held[i], r_y[i], *[r_y[at] for at in range(len(come))])
        if i < 3:
            sent_z.append(send(held.at[i], rs_z.at[i], z_ways[i]))

    z_along = []

    def z_load(m):
        z_crossed[m].wait_recv()
        return [load(z_parts.at[2, m], gb_own.at[m]), load(z_core.at[1, m], gb_core.at[m])]

    def z_send(m, loads):
        for copy in loads:
            copy.wait()
        gb_cross[m] = add(gb_own[m], gb_core[m])
        z_along.append(send(gb_cross.at[m], z_far.at[m], near_by.x))

    sums = [
        BlockSum(
            copies, near_by, (core, xi, yi, zi), grads, gall, low, high,
            sum_buffers[i * 5 : i * 5 + 5],
        )
        for i, (low, high) in enumerate(grad_columns(width))
    ]

    def weight_gradients(group, parts):
        low, high = grad_columns(width)[group]
        for part in parts:
            if part == 3:
                product = dot(o[...], ga[:, low:high], 0, 0)
            else:
                product = dot(a[...], gqkv[:, part * width + low : part * width + high], 0, 0)
            grads[part, :, low:high] = product.astype(BF16)

    left = lax.broadcasted_iota(jnp.int32, (ITEM_ROWS, pair), 1) < head_dim
    reduce_piece(0)
    for copy in first_loads + late_loads:
        copy.wait()
    gain2_grad = jnp.zeros((1, width), F32)
    items = [slice(i * ITEM_ROWS, (i + 1) * ITEM_ROWS) for i in range(ITEMS)]
    a = ga
    for m in range(batches):
        row0 = m * ROWS

        def p_load(hp, m=m):
            return pltpu.make_async_copy(
                p_in.at[m, :, pl.ds(2 * hp, 2)], p.at[hp % 2], p_sem.at[hp % 2]
            )

        p_load(0).start()
        own_loads[m].wait()
        nearer[m].wait_recv()
        along[m].wait_recv()
        if m + 1 < batches:
            along.append(send(gb_far.at[m + 1], gb_x.at[m + 1], near_by.x))
        for rows in items:
            at = slice(row0 + rows.start, row0 + rows.stop)
            gb = (
                gb_own[m, rows].astype(F32)
                + gb_core[m, rows].astype(F32)
                + gb_x[m, rows].astype(F32)
            )
            unit2, inverse2 = normalize_parts(y[rows])
            gain2_grad = gain2_grad + jnp.sum(gb * unit2, axis=0, keepdims=True)
            gy_rows = cot[rows].astype(F32) + normalize_back(gb * gain2_ref[...], unit2, inverse2)
            gy[at] = gy_rows
            ga[at] = gy_rows.astype(BF16)
            go[rows] = dot(ga[at], wo[...], 1, 1).astype(BF16)
        if m + 1 < batches:
            first_loads = [load(y_in.at[m + 1], y), load(cot_in.at[m + 1], cot)]
        z_loads = z_load(m)

        def heads(hp, carry, row0=row0, p_load=p_load):
            @pl.when(hp + 1 < PAIRS)
            def _():
                p_load(hp + 1).start()

            p_load(hp).wait()
            slot = hp % 2
            head_gradients(
                lambda rows, cols: qkv[rows, cols],
                lambda rows, cols: go[rows, cols],
                lambda item, half: p[slot, item, half],
                gqkv, row0, hp, width, left,
            )
            return carry

        if m + 1 < batches:
            lax.fori_loop(0, PAIRS, heads, 0)
            first_loads.append(load(qkv_in.at[m + 1], qkv))
            z_send(m, z_loads)
            reduce_piece(1 + m)
            for copy in first_loads:
                copy.wait()
        else:
            z_send(m, z_loads)
            lax.fori_loop(0, FIRST_PAIRS, heads, 0)
            for copy in last_loads:
                copy.wait()
            weight_gradients(0, (3,))
            weight_gradients(1, (3,))
            for micro in range(batches):
                at = slice(micro * ROWS, (micro + 1) * ROWS)
                unit, _ = normalize_parts(x[at].astype(F32))
                a[at] = (unit * gain1_ref[...]).astype(BF16)
            weight_gradients(0, (0, 1, 2))
            sums[0].start()
            reduce_piece(2)
            lax.fori_loop(FIRST_PAIRS, PAIRS, heads, 0)
    sums[0].one()
    weight_gradients(1, (0, 1, 2))
    sums[1].start()

    gain1_grad = jnp.zeros((1, width), F32)
    between = [sums[0].two, sums[1].one, sums[0].three, sums[1].two]
    for m in range(batches):
        for rows in items:
            at = slice(m * ROWS + rows.start, m * ROWS + rows.stop)
            unit, inverse = normalize_parts(x[at].astype(F32))
            gnorm = dot(gqkv[at], wqkv[...], 1, 1)
            gain1_grad = gain1_grad + jnp.sum(gnorm * unit, axis=0, keepdims=True)
            go[rows] = (gy[at] + normalize_back(gnorm * gain1_ref[...], unit, inverse)).astype(BF16)
            if between:
                between.pop(0)()
        tok[:, m] = dot(pick_rows(group_ref, m, length).astype(BF16), go[...], 0, 0).astype(BF16)
    token_store = load(tok, tg_out)
    gsum[0] = jnp.concatenate([gain1_grad, gain2_grad, jnp.zeros((6, width), F32)], axis=0)
    gain_partners = [near_by.x, near_by.y, near_by.z_pair, near_by.z[2], near_by.core]
    gain_sent = [send(gsum.at[0], gain_in.at[0], gain_partners[0])]

    def gain_step():
        at = len(gain_sent)
        gain_sent[-1].wait_recv()
        gsum[at] = gsum[at - 1] + gain_in[at - 1]
        if at < len(gain_partners):
            gain_sent.append(send(gsum.at[at], gain_in.at[at], gain_partners[at]))

    sums[1].three()
    reduce_piece(3)

    def join(to, own):
        at = rows_at(expert * part_rows, part_rows)
        return [own(held.at[3, :, 1], eout.at[:, at], *to), own(held.at[3, :, 0], ein.at[:, at], *to)]

    part_rows = held.shape[3]
    joined = join((near_by.x,), send)
    join_near = join((near_by.core,), send)
    join_own = join((), load)
    gain_step()

    for m in range(batches):
        z_nearer[m].wait_recv()
        z_along[m].wait_recv()
        loads = [
            load(z_parts.at[0, m], gb_own.at[m]),
            load(z_core.at[0, m], gb_core.at[m]),
            load(z_far.at[m], gb_x.at[m]),
            load(y_in.at[m], y),
        ]
        for copy in loads:
            copy.wait()
        for rows in items:
            chosen = pick_rows(group_ref, m, length, rows)
            keep = jnp.sum(jnp.where(chosen, keep_ref[m], 0.0), axis=1, keepdims=True)
            z = (
                gb_own[m, rows].astype(F32)
                + gb_core[m, rows].astype(F32)
                + gb_x[m, rows].astype(F32)
            )
            go[rows] = (y[rows] + jnp.where(keep > 0, z, 0.0)).astype(BF16)
        if m == 0:
            token_store.wait()
        tok[:, m] = dot(pick_rows(group_ref, m, length).astype(BF16), go[...], 0, 0).astype(BF16)
        if m == 0:
            sums[0].back_three()
        gain_step()
    copies.keep(tok, result_out)
    sums[1].back_three()

    gain_step()
    for block_sum in sums:
        block_sum.back_two()
    gain_step()
    copies.keep(gsum.at[len(gain_partners)], gains_out)
    opposite = rows_at((expert + 2) % 4 * part_rows, part_rows)
    for copy in joined:
        copy.wait_recv()
    join_near += [
        send(ref.at[:, opposite], ref.at[:, opposite], near_by.core) for ref in (eout, ein)
    ]
    for block_sum in sums:
        block_sum.back_one()
    for block_sum in sums:
        block_sum.settle()
    for copy in join_own:
        copy.wait()
    for copy in join_near:
        copy.wait_recv()
    hidden = ein.shape[1]
    for k in range(3):
        cols = pl.ds(0, hidden)
        grads[k, :, cols] = ein[k].astype(F32).T.astype(BF16)
        copies.keep(grads.at[k, :, cols], ein_out.at[k])
    for block_sum in sums:
        block_sum.back_core()
    for block_sum in sums:
        block_sum.finish()
    copies.finish()


def back(gb_parts, z_parts, gw, cot, group, keep, x, o, y, qkv, p, gain1, gain2, wqkv, wo):
    batches, rows, width = x.shape
    length = keep.shape[2]
    out = jax.ShapeDtypeStruct
    vmem = pl.BlockSpec(memory_space=pltpu.VMEM)
    anywhere = pl.BlockSpec(memory_space=pl.ANY)
    piece = gw.shape[1:]
    both = batches * rows
    half = width // 2
    tokens_shape = (batches, rows, width)
    slots = [tokens_shape] * 5
    scratch = [
        ((width, 3 * width), BF16),
        ((width, width), BF16),
        ((both, width), BF16),
        ((both, width), BF16),
        ((rows, width), F32),
        ((rows, width), BF16),
        ((rows, 3 * width), BF16),
        ((2, ITEMS, 2, ITEM_ROWS, ITEM_ROWS), BF16),
        *[(slot, BF16) for slot in slots],
        ((both, width), F32),
        ((both, width), BF16),
        ((rows, width), BF16),
        ((both, 3 * width), BF16),
        ((4, width, width), BF16),
        *[
            (shape, BF16)
            for low, high in grad_columns(width)
            for shape in (
                (4, half, high - low),
                (2, 2, half // 2, high - low),
                (2, 2, half // 4, high - low),
                (2, 3, half // 4, (high - low) // 2),
                (2, half // 4, (high - low) // 2),
            )
        ],
        ((4,) + piece, BF16),
        ((4,) + piece, BF16),
        ((3, 4 * piece[2], width), BF16),
        ((6, 8, width), F32),
        ((5, 8, width), F32),
        ((length, batches, width), BF16),
    ]
    return pl.pallas_call(
        functools.partial(back_kernel, batches),
        in_specs=[anywhere] * 4 + [vmem] * 2 + [anywhere] * 5 + [vmem] * 2 + [anywhere] * 2,
        out_specs=[anywhere] * 9,
        out_shape=[
            out((length, batches, width), BF16),
            out((length, batches, width), BF16),
            out((4, width, width), BF16),
            out((3, width, 4 * piece[2]), BF16),
            out((3, 4 * piece[2], width), BF16),
            out((8, width), F32),
            out((2,) + tokens_shape, BF16),
            out(tokens_shape, BF16),
            out((3,) + piece, BF16),
        ],
        scratch_shapes=[pltpu.VMEM(*k) for k in scratch]
        + [
            pltpu.SemaphoreType.DMA((80,)),
            pltpu.SemaphoreType.DMA((80,)),
            pltpu.SemaphoreType.DMA((64,)),
            pltpu.SemaphoreType.DMA((2,)),
        ],
        compiler_params=pltpu.CompilerParams(
            vmem_limit_bytes=VMEM_LIMIT, has_side_effects=True, collective_id=1
        ),
        cost_estimate=pl.CostEstimate(
            flops=batches
            * (2 * rows * width * width * 8 + 16 * HEADS * ITEMS * ITEM_ROWS**2 * 128),
            bytes_accessed=80_000_000,
            transcendentals=0,
        ),
        name="back",
    )(
        gb_parts, z_parts, gw, cot, group, keep,
        x.reshape(both, width), o.reshape(both, width), y, qkv, p, gain1, gain2, wqkv, wo,
    )


def attention_backward_kernel(n_parts, n_carry, *refs):
    parts = refs[:n_parts]
    (cot_ref, x_ref, y_ref, qkv_ref, p_ref, o_ref, gain1_ref, gain2_ref, wqkv_ref, wo_ref) = refs[
        n_parts : n_parts + 10
    ]
    carried = refs[n_parts + 10 : n_parts + 10 + n_carry]
    tg_ref, gwqkv_ref, gwo_ref, ggain_ref, gmix_ref, gqkv_ref = refs[n_parts + 10 + n_carry :]
    width = x_ref.shape[1]
    head_dim = width // HEADS
    gb = parts[0][...].astype(F32)
    for part in parts[1:]:
        gb = gb + part[...].astype(F32)
    unit2, inverse2 = normalize_parts(y_ref[...])
    gain2_grad = jnp.sum(gb * unit2, axis=0, keepdims=True)
    gy = cot_ref[...].astype(F32) + normalize_back(gb * gain2_ref[...], unit2, inverse2)
    ga = gy.astype(BF16)
    gwo = dot(o_ref[...], ga, 0, 0)
    if n_carry:
        gwo = gwo + carried[1][...]
    gwo_ref[...] = gwo
    gmix_ref[...] = dot(ga, wo_ref[...], 1, 1).astype(BF16)
    pair = 2 * head_dim
    left = lax.broadcasted_iota(jnp.int32, (ITEM_ROWS, pair), 1) < head_dim

    def heads(hp, carry):
        head_gradients(
            lambda rows, cols: qkv_ref[rows, cols],
            lambda rows, cols: gmix_ref[rows, cols],
            lambda item, half: p_ref[item, hp * 2 + half],
            gqkv_ref, 0, hp, width, left,
        )
        return carry

    lax.fori_loop(0, HEADS // 2, heads, 0)
    unit, inverse = normalize_parts(x_ref[...].astype(F32))
    a = (unit * gain1_ref[...]).astype(BF16)
    for part in range(3):
        cols = slice(part * width, (part + 1) * width)
        gw = dot(a, gqkv_ref[:, cols], 0, 0)
        if n_carry:
            gw = gw + carried[0][:, cols]
        gwqkv_ref[:, cols] = gw
    gnorm = dot(gqkv_ref[...], wqkv_ref[...], 1, 1)
    gain1_grad = jnp.sum(gnorm * unit, axis=0, keepdims=True)
    gains = jnp.concatenate([gain1_grad, gain2_grad, jnp.zeros((6, width), F32)], axis=0)
    if n_carry:
        gains = gains + carried[2][...]
    ggain_ref[...] = gains
    tg_ref[...] = (gy + normalize_back(gnorm * gain1_ref[...], unit, inverse)).astype(BF16)


def attention_backward(parts, cot, x, y, qkv, p, o, gain1, gain2, wqkv, wo, carried):
    rows, width = x.shape
    out = jax.ShapeDtypeStruct
    return pl.pallas_call(
        functools.partial(attention_backward_kernel, len(parts), len(carried)),
        out_shape=(
            out((rows, width), BF16),
            out((width, 3 * width), F32),
            out((width, width), F32),
            out((8, width), F32),
        ),
        scratch_shapes=[pltpu.VMEM((rows, width), BF16), pltpu.VMEM((rows, 3 * width), BF16)],
        compiler_params=pltpu.CompilerParams(vmem_limit_bytes=VMEM_LIMIT),
        cost_estimate=pl.CostEstimate(
            flops=2 * rows * width * width * 8 + 16 * HEADS * ITEMS * ITEM_ROWS**2 * 128,
            bytes_accessed=30_000_000,
            transcendentals=0,
        ),
        name="attention_backward",
    )(*parts, cot, x, y, qkv, p, o, gain1, gain2, wqkv, wo, *carried)


def expert_kernel(groups, batches, pieces, *refs):
    flags, own_ref, more_ref, b_in, g_in, z_out, gb_out, gw_out = refs[:8]
    rows_b, rows_g, w, grads, in_sem, w_sem, out_sem, gw_sem = refs[8:]
    part = own_ref.shape[2]

    def rounded(rows):
        return (rows + TILE - 1) // TILE * TILE

    merged = [
        flags[g, 0, micro * ITEMS + item]
        for g in range(groups)
        for micro in range(batches)
        for item in range(ITEMS)
    ]
    n_merged = sum(merged)
    n_plain = len(merged) - n_merged
    sizes = [n_plain * IMAGE_ROWS, n_plain * CAPTION, n_merged * ITEM_ROWS]
    starts = [0, rounded(sizes[0]), rounded(sizes[0]) + rounded(sizes[1])]
    ends = [start + rounded(size) for start, size in zip(starts, sizes)]
    blocks = []
    plain, joined = 0, 0
    for flat, flag in enumerate(merged):
        g, micro, item = flat // (batches * ITEMS), flat // ITEMS % batches, flat % ITEMS
        base = item * ITEM_ROWS
        image = jnp.where(flag == 1, starts[2] + joined * ITEM_ROWS, plain * IMAGE_ROWS)
        caption = jnp.where(
            flag == 1, image + IMAGE_ROWS, starts[1] + plain * CAPTION
        )
        blocks.append((g, micro, base, IMAGE_ROWS, image, flag, 0))
        blocks.append((g, micro, base + IMAGE_ROWS, CAPTION, caption, flag, 1))
        plain, joined = plain + 1 - flag, joined + flag

    def copy_of(which, number, outward):
        g, micro, base, size, at, _, _ = blocks[number]
        held = (rows_b, rows_g)[which].at[pl.ds(pl.multiple_of(at, 16), size)]
        if outward:
            far = (gb_out, z_out)[which].at[g, micro, pl.ds(base, size)]
            return pltpu.make_async_copy(held, far, out_sem.at[which, number])
        far = (b_in, g_in)[which].at[g, micro, pl.ds(base, size)]
        return pltpu.make_async_copy(far, held, in_sem.at[which, number])

    def of_expert(expert, act, numbers=None):
        for number, (_, _, _, _, _, flag, kind) in enumerate(blocks):
            if numbers is not None and number not in numbers:
                continue
            if expert == 2 or kind == expert:
                @pl.when(flag == (1 if expert == 2 else 0))
                def _(number=number):
                    for which in range(2):
                        act(which, number)

    def weight_copy(k, i):
        piece = own_ref if i == 0 else more_ref.at[i - 1]
        return pltpu.make_async_copy(
            piece.at[k], w.at[k, :, pl.ds(i * part, part), :], w_sem.at[k, i]
        )

    for k in range(3):
        tail = pl.multiple_of(jnp.maximum(ends[k] - TILE, 0), TILE)
        rows_b[pl.ds(tail, TILE), :] = jnp.zeros((TILE, rows_b.shape[1]), BF16)
        rows_g[pl.ds(tail, TILE), :] = jnp.zeros((TILE, rows_g.shape[1]), BF16)
    def start_rows(k, numbers):
        of_expert(k, lambda which, number: copy_of(which, number, False).start(), numbers)

    early = range(len(blocks) // 2)
    late = range(len(blocks) // 2, len(blocks))
    early_plain = sum(1 - flag for flag in merged[: len(merged) // 2])
    middle = early_plain * IMAGE_ROWS // (2 * TILE)

    def wait_rows(k, numbers):
        of_expert(k, lambda which, number: copy_of(which, number, False).wait(), numbers)

    for i in range(pieces):
        weight_copy(0, i).start()
    start_rows(0, early)
    start_rows(0, late)
    for k in range(3):
        grads[...] = jnp.zeros(grads.shape, F32)
        for i in range(pieces):
            weight_copy(k, i).wait()
        wait_rows(k, early)
        if k == 0:
            for other in (1, 2):
                for i in range(pieces):
                    weight_copy(other, i).start()
                start_rows(other, early)
                start_rows(other, late)
        if k > 0:
            wait_rows(k, late)

        def tile(start, size, k=k):
            at = pl.ds(pl.multiple_of(start, TILE), size)
            b, gz = rows_b[at, :], rows_g[at, :]
            u, slope = gelu_and_slope(dot(b, w[k, 0], 1, 1))
            gh = (dot(gz, w[k, 1], 1, 1) * slope).astype(BF16)
            u = u.astype(BF16)
            z, gb = dot(u, w[k, 1], 1, 0), dot(gh, w[k, 0], 1, 0)
            grads[0] += dot(gh, b, 0, 0)
            grads[1] += dot(u, gz, 0, 0)
            rows_b[at, :] = gb.astype(BF16)
            rows_g[at, :] = z.astype(BF16)

        doubles = (ends[k] - starts[k]) // (2 * TILE)

        def double(t, carry, k=k):
            if k == 0:
                @pl.when(t == middle)
                def _():
                    wait_rows(0, late)

            tile(starts[k] + t * 2 * TILE, 2 * TILE)
            return carry

        lax.fori_loop(0, doubles, double, 0)
        if k == 0:
            @pl.when(middle >= doubles)
            def _():
                wait_rows(0, late)

        @pl.when((ends[k] - starts[k]) // TILE > 2 * doubles)
        def _(k=k):
            tile(ends[k] - TILE, TILE)

        of_expert(k, lambda which, number: copy_of(which, number, True).start())
        w[k] = grads[...].astype(BF16)
        for i in range(pieces):
            pltpu.make_async_copy(
                w.at[k, :, pl.ds(i * part, part), :], gw_out.at[i, k], gw_sem.at[k, i]
            ).start()
    for number in range(len(blocks)):
        for which in range(2):
            copy_of(which, number, True).wait()
    for k in range(3):
        for i in range(pieces):
            pltpu.make_async_copy(
                w.at[k, :, pl.ds(i * part, part), :], gw_out.at[i, k], gw_sem.at[k, i]
            ).wait()


def experts(flags, own, more, b_groups, g_groups):
    groups, batches, rows, width = b_groups.shape
    part = own.shape[2]
    pieces = 1 + (more.shape[0] if more.ndim == 5 else 0)
    hidden = part * pieces
    count = groups * batches * ITEMS
    capacity = (count * ITEM_ROWS // TILE + 4) * TILE
    out = jax.ShapeDtypeStruct
    anywhere = pl.BlockSpec(memory_space=pl.ANY)
    return pl.pallas_call(
        functools.partial(expert_kernel, groups, batches, pieces),
        in_specs=[pl.BlockSpec(memory_space=pltpu.SMEM)] + [anywhere] * 4,
        out_specs=[anywhere] * 3,
        out_shape=[out(b_groups.shape, BF16)] * 2 + [out((pieces,) + own.shape, BF16)],
        scratch_shapes=[
            pltpu.VMEM((capacity, width), BF16),
            pltpu.VMEM((capacity, width), BF16),
            pltpu.VMEM((3, 2, hidden, width), BF16),
            pltpu.VMEM((2, hidden, width), F32),
            pltpu.SemaphoreType.DMA((2, 2 * count)),
            pltpu.SemaphoreType.DMA((3, pieces)),
            pltpu.SemaphoreType.DMA((2, 2 * count)),
            pltpu.SemaphoreType.DMA((3, pieces)),
        ],
        compiler_params=pltpu.CompilerParams(vmem_limit_bytes=VMEM_LIMIT),
        cost_estimate=pl.CostEstimate(
            flops=2 * 6 * count * ITEM_ROWS * width * hidden,
            bytes_accessed=45_000_000,
            transcendentals=count * ITEM_ROWS * hidden,
        ),
        name="experts",
    )(flags, own, more, b_groups, g_groups)


def from_items(rows, first):
    one, two = rows[IMAGE_ROWS:ITEM_ROWS], rows[ITEM_ROWS + IMAGE_ROWS :]
    return jnp.concatenate(
        [
            rows[:PATCHES],
            rows[ITEM_ROWS : ITEM_ROWS + PATCHES],
            jnp.where(first, one, two),
            jnp.where(first, two, one),
        ],
        axis=0,
    )


class Links:
    def __init__(self):
        self.hosts = lax.axis_size("expert")
        self.dp = lax.axis_size("dp")
        self.direct = self.hosts == 4 and self.dp == 8
        self.me = lax.axis_index("expert")

    def flip(self, v, bit):
        return lax.ppermute(v, "expert", [(i, i ^ bit) for i in range(4)])

    def across_y(self, v):
        return lax.ppermute(v, "dp", [(i, i ^ 1) for i in range(8)])

    def along_z(self, v, shift):
        return lax.ppermute(v, "dp", [(i, (i + 2 * shift) % 8) for i in range(8)])

    def gather_tokens(self, v):
        if not self.direct:
            return list(lax.all_gather(v, "expert"))
        near, far = self.flip(v, 1), self.flip(v, 2)
        return [v, near, far, self.flip(far, 1)]

    def reduce_tokens(self, parts):
        if not self.direct:
            return [lax.psum_scatter(jnp.stack(parts), "expert", scatter_dimension=0)]
        far = (parts[2].astype(F32) + self.flip(parts[3], 1).astype(F32)).astype(BF16)
        return [parts[0], self.flip(parts[1], 1), self.flip(far, 2)]

    def reduce_weights(self, pieces):
        if not self.direct:
            return lax.psum_scatter(pieces[0], "dp", scatter_dimension=2, tiled=True)
        total = None
        for at, shift in enumerate((0, 1, 3, 2)):
            piece = pieces[2 * at].astype(F32) + self.across_y(pieces[2 * at + 1]).astype(F32)
            if shift:
                piece = self.along_z(piece.astype(BF16), -shift).astype(F32)
            total = piece if total is None else total + piece
        return total.astype(BF16)

    def join_hidden(self, v):
        if not self.direct:
            return lax.all_gather(v, "expert", axis=2, tiled=True)
        stacked = jnp.stack(self.gather_tokens(v))
        return jnp.concatenate(
            [
                lax.dynamic_index_in_dim(stacked, i ^ self.me, 0, keepdims=False)
                for i in range(4)
            ],
            axis=2,
        )


def shards(
    tokens,
    cotangent,
    item_group,
    routes,
    slot_order,
    attn_gain,
    ffn_gain,
    qkv_weight,
    out_weight,
    expert_in,
    expert_out,
):
    links = Links()
    hosts, me = links.hosts, links.me
    batches, length, width = tokens.shape
    shard = expert_in.shape[2]
    part = shard // hosts
    gain1, gain2 = attn_gain, ffn_gain

    own = jnp.stack(
        [
            jnp.swapaxes(lax.dynamic_slice_in_dim(expert_in, me * part, part, 2), 1, 2),
            lax.dynamic_slice_in_dim(expert_out, me * part, part, 1),
        ],
        axis=1,
    )
    first = item_group[:, ITEMS * PATCHES] == 0
    (
        w_all, gz_groups, flag_groups, b_groups, x_all, qkv_all, p_all, o_all, y_all, cot_all, kept
    ) = front(
        links.direct, hosts, own, jnp.swapaxes(tokens, 0, 1), jnp.swapaxes(cotangent, 0, 1),
        item_group, routes, slot_order, gain1, gain2, qkv_weight, out_weight,
    )
    if not links.direct:
        own = lax.all_gather(own, "dp", axis=2, tiled=True)
        gz_groups, flag_groups, b_groups = [
            lax.all_gather(v[0], "expert") for v in (gz_groups, flag_groups, b_groups)
        ]
    z_parts, gb_parts, gw_pieces = experts(flag_groups, own, w_all, b_groups, gz_groups)
    if links.direct:
        result, token_grad, gall, ein_sum, eout_sum, gains, *_ = back(
            gb_parts, z_parts, gw_pieces, cot_all, item_group, kept,
            x_all, o_all, y_all, qkv_all, p_all, gain1, gain2, qkv_weight, out_weight,
        )
        return (
            jnp.swapaxes(result, 0, 1),
            jnp.swapaxes(token_grad, 0, 1),
            gains[0],
            gains[1],
            jnp.concatenate([gall[i].astype(F32) for i in range(3)], axis=1),
            gall[3].astype(F32),
            ein_sum.astype(F32),
            eout_sum.astype(F32),
        )
    gb_terms = links.reduce_tokens(gb_parts)
    z_terms = links.reduce_tokens(z_parts)
    sums = links.join_hidden(links.reduce_weights(gw_pieces)).astype(F32)

    results, token_grads, carried = [], [], ()
    for m in range(batches):
        x, qkv, p, o, y = x_all[m], qkv_all[m], p_all[m], o_all[m], y_all[m]
        at = m
        tg, *carried = attention_backward(
            [t[at] for t in gb_terms],
            cot_all[m], x, y, qkv, p, o, gain1, gain2, qkv_weight, out_weight,
            tuple(carried),
        )
        token_grads.append(from_items(tg, first[m]))
        z = z_terms[0][at].astype(F32)
        for term in z_terms[1:]:
            z = z + term[at].astype(F32)
        branch = jnp.where(kept[m, 0][:, None] > 0, from_items(z, first[m]), 0.0)
        results.append((from_items(y, first[m]) + branch).astype(BF16))
    gw_qkv, gw_out, gains = carried
    packed = jnp.concatenate(
        [
            jnp.concatenate([gw_qkv, gw_out], axis=1),
            jnp.pad(gains[:2].reshape(1, 2 * width), ((0, 7), (0, 2 * width))),
        ],
        axis=0,
    ).astype(BF16)
    packed = lax.psum(packed, ("dp", "expert")).astype(F32)
    return (
        jnp.stack(results),
        jnp.stack(token_grads),
        packed[width, :width],
        packed[width, width : 2 * width],
        packed[:width, : 3 * width],
        packed[:width, 3 * width :],
        jnp.swapaxes(sums[:, 0], 1, 2),
        sums[:, 1],
    )


def solution(mesh):
    in_specs = (
        P(None, ("dp", "expert"), None),
        P(None, ("dp", "expert"), None),
        P(None, ("dp", "expert")),
        P(None, ("dp", "expert")),
        P(None, ("dp", "expert"), None),
        P(),
        P(),
        P(),
        P(),
        P(None, None, "dp"),
        P(None, "dp", None),
    )
    out_specs = (
        P(None, ("dp", "expert"), None),
        P(None, ("dp", "expert"), None),
        P(),
        P(),
        P(),
        P(),
        P(None, None, "dp"),
        P(None, "dp", None),
    )
    return jax.shard_map(shards, mesh=mesh, in_specs=in_specs, out_specs=out_specs, check_vma=False)
```
